32 devices in a mesh: seq: 4 (over y, x), item: 8 (over z, core).
Axes of the slice: x: 2, y: 2, z: 4, core: 2. Of those that a mesh axis runs over, the one named last changes fastest.
Arguments:
- hidden: float32 [8, 4096, 768], P('item', 'seq'), may hold values from -6 to 6
- block_lists: int32 [8, 2, 64, 12, 3], P('item', None, 'seq'), may hold values from 0 to 63, as said below
- w_qkv: bfloat16 [2, 768, 2304], P(None, 'item'), may hold values from -0.3125 to 0.3125
- bias_query: bfloat16 [2, 768], P(None, 'item'), may hold values from -1.75 to 1.75
- bias_value: bfloat16 [2, 768], P(None, 'item'), may hold values from -0.1875 to 0.1875
- w_attn_out: bfloat16 [2, 768, 768], P(None, 'item'), may hold values from -1.75 to 1.75
- bias_attn_out: bfloat16 [2, 768], P(None, 'item'), may hold values from -0.625 to 0.625
- norm1_gain: bfloat16 [2, 768], P(None, 'item'), may hold values from 0.5 to 1.5
- norm1_shift: bfloat16 [2, 768], P(None, 'item'), may hold values from -0.625 to 0.625
- w_ffn_in: bfloat16 [2, 768, 3072], P(None, 'item'), may hold values from -0.21875 to 0.21875
- bias_ffn_in: bfloat16 [2, 3072], P(None, 'item'), may hold values from -0.625 to 0.625
- w_ffn_out: bfloat16 [2, 3072, 768], P(None, 'item'), may hold values from -0.15625 to 0.15625
- bias_ffn_out: bfloat16 [2, 768], P(None, 'item'), may hold values from -0.625 to 0.625
- norm2_gain: bfloat16 [2, 768], P(None, 'item'), may hold values from 0.5 to 1.5
- norm2_shift: bfloat16 [2, 768], P(None, 'item'), may hold values from -0.625 to 0.625
- cotangent: float32 [8, 4096, 768], P('item', 'seq'), may hold values from -6 to 6
Outputs:
- layer_output: float32 [8, 4096, 768], P('item', 'seq')
- input_grad: float32 [8, 4096, 768], P('item', 'seq')
- grad_w_qkv: float32 [2, 768, 2304], P(None, 'item')
- grad_bias_query: float32 [2, 768], P(None, 'item')
- grad_bias_value: float32 [2, 768], P(None, 'item')
- grad_w_attn_out: float32 [2, 768, 768], P(None, 'item')
- grad_bias_attn_out: float32 [2, 768], P(None, 'item')
- grad_norm1_gain: float32 [2, 768], P(None, 'item')
- grad_norm1_shift: float32 [2, 768], P(None, 'item')
- grad_w_ffn_in: float32 [2, 768, 3072], P(None, 'item')
- grad_bias_ffn_in: float32 [2, 3072], P(None, 'item')
- grad_w_ffn_out: float32 [2, 3072, 768], P(None, 'item')
- grad_bias_ffn_out: float32 [2, 768], P(None, 'item')
- grad_norm2_gain: float32 [2, 768], P(None, 'item')
- grad_norm2_shift: float32 [2, 768], P(None, 'item')
The draws below stay inside these ranges and needn't reach their ends.
Inputs may be any that keep to these rules, and one draw needn't show every extreme that they name: `block_lists`: for one item, layer and head, of the random blocks listed by the 16 query blocks of one run of 16 consecutive blocks (runs aligned at multiples of 16), at most 12 lie in any one such run.
All inputs are finite; a program needn't handle non-finite values.
Results may differ from the reference program's by a relative error of at most 0.038.
The reference program's roundings to bfloat16 on the way count: a program that leaves them out, or rounds other values in their place, can miss the bound.
Values may be sent and summed in bfloat16 or wider, within the bound.
A program may use at most 768 MiB of HBM per device.

```python
import jax
import jax.numpy as jnp
from jax import lax

D = 768
H = 12
HD = 64
FF = 3072
BLK = 64
RAND = 3
LEN = 4096
LAYERS = 2
ITEMS = 8
LOCAL = 16


def draw_block_lists(key, part):
    entries = LOCAL * RAND
    runs = LEN // (BLK * LOCAL)
    first_key, second_key = jax.random.split(jax.random.fold_in(key, 7))
    raw = jax.random.randint(first_key, (ITEMS, LAYERS, runs, H, entries), 0, 1 << 20, dtype=jnp.int32)
    scores = raw * entries + jnp.arange(entries, dtype=jnp.int32)
    order = jnp.argsort(scores, axis=-1).astype(jnp.int32)
    owners = order % runs
    within = jax.random.randint(second_key, (ITEMS, LAYERS, runs, H, entries), 0, LOCAL, dtype=jnp.int32)
    picked = owners * LOCAL + within
    picked = picked.reshape(ITEMS, LAYERS, runs, H, LOCAL, RAND).transpose(0, 1, 2, 4, 3, 5)
    return picked.reshape(ITEMS, LAYERS, LEN // BLK, H, RAND).astype(jnp.int32)


def shard_levels(stream_key, dims, pieces, least, high):
    level, own = 1.0, jax.random.fold_in(stream_key, 6)
    for position, shards_of in pieces:
        heights = jnp.exp(jax.random.uniform(jax.random.fold_in(own, position), (shards_of,), jnp.float32, least / len(pieces), high / len(pieces)))
        level = level * jnp.repeat(heights, dims[position] // shards_of).reshape([-1 if axis == position else 1 for axis in range(len(dims))])
    return level


def noise(key, extent, scale, most, pieces=(), kind=jnp.bfloat16):
    result = jax.random.normal(key, extent, jnp.float32) * scale
    if len(pieces) > 0:
        result = shard_levels(key, extent, pieces, -0.22, 0.18) * result
    return jnp.clip(result, min=-most, max=most).astype(kind)


def setup_inputs(seed: int = 0) -> dict:
    arg_keys = jax.random.split(jax.random.key(seed), 17)
    return {
        "hidden": noise(arg_keys[0], (ITEMS, LEN, D), 1.0, 6.0, ((0, 8), (1, 4)), jnp.float32),
        "block_lists": draw_block_lists(jax.random.fold_in(arg_keys[16], 71), 0),
        "w_qkv": noise(arg_keys[2], (LAYERS, D, 3 * D), (D // 2) ** -0.5, 0.3125, ((1, 8),)),
        "bias_query": noise(arg_keys[3], (LAYERS, D), 0.3, 1.75, ((1, 8),)),
        "bias_value": noise(arg_keys[4], (LAYERS, D), 0.03, 0.1875, ((1, 8),)),
        "w_attn_out": noise(arg_keys[5], (LAYERS, D, D), (max(D // 64, 1)) ** -0.5, 1.75, ((1, 8),)),
        "bias_attn_out": noise(arg_keys[6], (LAYERS, D), 0.1, 0.625, ((1, 8),)),
        "norm1_gain": jnp.clip(1.0 + 0.1 * jax.random.normal(arg_keys[7], (LAYERS, D), jnp.float32), 0.5, 1.5).astype(jnp.bfloat16),
        "norm1_shift": noise(arg_keys[8], (LAYERS, D), 0.1, 0.625, ((1, 8),)),
        "w_ffn_in": noise(arg_keys[9], (LAYERS, D, FF), D ** -0.5, 0.21875, ((1, 8),)),
        "bias_ffn_in": noise(arg_keys[10], (LAYERS, FF), 0.1, 0.625, ((1, 8),)),
        "w_ffn_out": noise(arg_keys[11], (LAYERS, FF, D), (FF // 2) ** -0.5, 0.15625, ((1, 8),)),
        "bias_ffn_out": noise(arg_keys[12], (LAYERS, D), 0.1, 0.625, ((1, 8),)),
        "norm2_gain": jnp.clip(1.0 + 0.1 * jax.random.normal(arg_keys[13], (LAYERS, D), jnp.float32), 0.5, 1.5).astype(jnp.bfloat16),
        "norm2_shift": noise(arg_keys[14], (LAYERS, D), 0.1, 0.625, ((1, 8),)),
        "cotangent": noise(arg_keys[15], (ITEMS, LEN, D), 1.0, 6.0, ((0, 8), (1, 4)), jnp.float32),
    }


exact_mode = lax.Precision.HIGHEST
epsilon = 1e-05

@jax.custom_vjp
def low(v):
    return lax.optimization_barrier(v.astype(jnp.bfloat16)).astype(jnp.float32)

@jax.custom_vjp
def low_back(v):
    return v

def low_keep(v):
    return (low(v), None)

def low_pass(kept, grad):
    return (grad,)

def back_keep(v):
    return (v, None)

def back_low(kept, grad):
    return (low(grad),)
low.defvjp(low_keep, low_pass)
low_back.defvjp(back_keep, back_low)

def layer_norm(resid, gain, shift):
    centre = resid - lax.optimization_barrier(jnp.mean(resid, -1, keepdims=True))
    spread = lax.optimization_barrier(jnp.mean(centre * centre, -1, keepdims=True))
    return centre * lax.rsqrt(spread + epsilon) * gain + shift

def softmax_rows(scores):
    row_max = lax.optimization_barrier(jnp.max(scores, -1, keepdims=True))
    exponent = jnp.exp(scores - row_max)
    return exponent / lax.optimization_barrier(jnp.sum(exponent, -1, keepdims=True))

def head_attention(query_head, key_head, value_head, block_sets):
    blocks = query_head.shape[0]
    score_scale = HD ** (-0.5)
    block_ids = jnp.arange(blocks, dtype=jnp.int32)
    shared = jnp.stack([(block_ids - 1) % blocks, block_ids, (block_ids + 1) % blocks, jnp.zeros_like(block_ids), jnp.full_like(block_ids, blocks - 1)], 1)
    chosen = jnp.concatenate([shared, block_sets.astype(jnp.int32)], 1)
    key_rows = key_head[chosen].reshape(blocks, -1, HD)
    value_rows = value_head[chosen].reshape(blocks, -1, HD)
    scores = low_back(jnp.einsum('nqd,nkd->nqk', query_head, key_rows, precision=exact_mode) * score_scale)
    chances = softmax_rows(scores)
    context = jnp.einsum('nqk,nkd->nqd', low(chances), value_rows, precision=exact_mode)
    glob_query = jnp.concatenate([query_head[0], query_head[blocks - 1]], 0)
    key_all = key_head.reshape(-1, HD)
    value_all = value_head.reshape(-1, HD)
    glob_scores = low_back(jnp.dot(glob_query, key_all.T, precision=exact_mode) * score_scale)
    glob_context = jnp.dot(softmax_rows(glob_scores), value_all, precision=exact_mode)
    context = context.at[0].set(glob_context[:BLK]).at[blocks - 1].set(glob_context[BLK:])
    return context

def attention_head(packed):
    return jax.checkpoint(head_attention)(*packed)

def layer_forward(current, params, block_sets):
    qkv_weight, query_bias, value_bias, out_weight, out_bias, gain_one, shift_one, inner_weight, inner_bias, outer_weight, outer_bias, gain_two, shift_two = params
    blocks = LEN // BLK
    projected = jnp.dot(low(current), qkv_weight, precision=exact_mode)
    projected = low(low_back(projected + jnp.concatenate([query_bias, jnp.zeros_like(query_bias), value_bias])))

    def split_heads(part):
        return part.reshape(blocks, BLK, H, HD).transpose(2, 0, 1, 3)
    queries = split_heads(projected[:, :D])
    key_part = split_heads(projected[:, D:2 * D])
    value_part = split_heads(projected[:, 2 * D:])
    context = lax.map(attention_head, (queries, key_part, value_part, jnp.transpose(block_sets, (1, 0, 2))))
    context = low(low_back(context.transpose(1, 2, 0, 3).reshape(LEN, D)))
    attn_out = low_back(jnp.dot(context, out_weight, precision=exact_mode) + out_bias)
    normed = layer_norm(current + attn_out, gain_one, shift_one)
    pre_act = low_back(jnp.dot(low(normed), inner_weight, precision=exact_mode) + inner_bias)
    activated = low(jax.nn.gelu(pre_act, approximate=True))
    ffn_out = low_back(jnp.dot(activated, outer_weight, precision=exact_mode) + outer_bias)
    return layer_norm(normed + ffn_out, gain_two, shift_two)

def reference(hidden, block_lists, w_qkv, bias_query, bias_value, w_attn_out, bias_attn_out, norm1_gain, norm1_shift, w_ffn_in, bias_ffn_in, w_ffn_out, bias_ffn_out, norm2_gain, norm2_shift, cotangent):
    weights = tuple((weight_in.astype(jnp.float32) for weight_in in (w_qkv, bias_query, bias_value, w_attn_out, bias_attn_out, norm1_gain, norm1_shift, w_ffn_in, bias_ffn_in, w_ffn_out, bias_ffn_out, norm2_gain, norm2_shift)))

    def network(sequence, block_sets, *params):
        current = sequence
        for section_index in range(LAYERS):
            current = layer_forward(current, tuple((weight_in[section_index] for weight_in in params)), block_sets[section_index])
        return current

    def item_step(running, packed):
        sequence, block_sets, grad_out = packed

        def item_network(seq_in, *params):
            return network(seq_in, block_sets, *params)
        output, pullback = jax.vjp(item_network, sequence, *weights)
        gradients = pullback(grad_out)
        summed = tuple((run_sum + gradient for run_sum, gradient in zip(running, gradients[1:])))
        return (summed, (output, gradients[0]))
    start = tuple((jnp.zeros_like(weight_in) for weight_in in weights))
    totals, (outputs, input_grads) = lax.scan(item_step, start, (hidden, block_lists, cotangent))
    return (outputs, input_grads, totals[0], totals[1], totals[2], totals[3], totals[4], totals[5], totals[6], totals[7], totals[8], totals[9], totals[10], totals[11], totals[12])
```

```python
from functools import partial

import jax
import jax.numpy as jnp
from jax import lax
from jax.experimental import pallas as pl
from jax.experimental.pallas import tpu as pltpu
from jax.sharding import PartitionSpec as P

D = 768
H = 12
LAYERS = 2
epsilon = 1e-05

HD = 64
BLK = 64
RAND = 3
F32=jnp.float32; BF=jnp.bfloat16
LOG2E=1.4426950408889634
NT=(((1,),(1,)),((),()))
TN=(((0,),(0,)),((),()))
NN=(((1,),(0,)),((),()))
def dot(a,b,dn): return lax.dot_general(a,b,dn,preferred_element_type=F32)
KEYS=(5+RAND)*BLK
CH=512

def low(v): return jnp.concatenate([v,jnp.zeros_like(v)],1)
def high(v): return jnp.concatenate([jnp.zeros_like(v),v],1)
def diag(a,b):
    return jnp.concatenate([jnp.concatenate([a,jnp.zeros_like(b)],1),jnp.concatenate([jnp.zeros_like(a),b],1)],0)

def places(hp,h):
    base=hp*2*HD+h*HD
    return slice(h*2*HD,(h+1)*2*HD), slice(base,base+HD), slice(h*HD,(h+1)*HD)

def listed(x_ref,lists_ref,lanes,h,j):
    length=x_ref.shape[0]; nb=length//BLK
    row=pl.multiple_of(j*BLK,BLK); prev=pl.multiple_of(row-BLK,BLK)
    rows=[pl.multiple_of(lists_ref[(h*nb+j)*RAND+r]*BLK,BLK) for r in range(RAND)]
    parts=[x_ref[pl.ds(prev,3*BLK),lanes],x_ref[0:BLK,lanes],x_ref[length-BLK:length,lanes]]
    parts+=[x_ref[pl.ds(k,BLK),lanes] for k in rows]
    return jnp.concatenate(parts,0), row, prev, rows

def pair_of(x_ref,lists_ref,lanes,h,i):
    kva,rowa,preva,ra=listed(x_ref,lists_ref,lanes,h,1+2*i)
    kvb,rowb,prevb,rb=listed(x_ref,lists_ref,lanes,h,2+2*i)
    return jnp.concatenate([kva,kvb],1),(rowa,preva,ra),(rowb,prevb,rb)

def run_pairs(half,hp,first,second,third):
    for h in range(hp): first(0,h,0)
    def body(i,carry):
        for u in range(2):
            t=2*i+u
            for h in range(hp):
                first(jnp.minimum(t+1,half-1),h,1-u)
                second(h,u)
                third(t-1,h,1-u)
        return carry
    return body

def fwd_kernel(hp, lists_ref, x_ref, o_ref, s_ref, p_ref, g_ref):
    length=x_ref.shape[0]; nb=length//BLK
    c=LOG2E*HD**-0.5
    half=(nb-2)//2
    def stage_s(i,h,slot):
        lanes,qs,_=places(hp,h)
        kv,(rowa,_,_),(rowb,_,_)=pair_of(x_ref,lists_ref,lanes,h,i)
        w=diag(low(x_ref[pl.ds(rowa,BLK),qs]),low(x_ref[pl.ds(rowb,BLK),qs]))
        s_ref[slot,h]=dot(kv,w,NT)
    def stage_p(h,slot):
        s=s_ref[slot,h]
        m=jnp.max(s,0,keepdims=True)
        e=jnp.exp2(s*c-m*c)
        inv=1.0/jnp.sum(e,0,keepdims=True)
        p_ref[slot,h]=(e*inv).astype(BF)
    def stage_c(i,h,slot):
        lanes,_,ds_=places(hp,h)
        kv,(rowa,_,_),(rowb,_,_)=pair_of(x_ref,lists_ref,lanes,h,jnp.maximum(i,0))
        ctx=dot(p_ref[slot,h],kv,TN)
        o_ref[pl.ds(rowa,BLK),ds_]=ctx[:BLK,HD:2*HD].astype(BF)
        o_ref[pl.ds(rowb,BLK),ds_]=ctx[BLK:,3*HD:].astype(BF)
    p_ref[...]=jnp.zeros_like(p_ref)
    body=run_pairs(half,hp,stage_s,stage_p,stage_c)
    lax.fori_loop(0,(half+1)//2,body,0)
    for h in range(hp): stage_c(half-1,h,(half-1)%2)
    heads=range(hp)
    ws=[]
    for h in heads:
        _,qs,_=places(hp,h)
        ws.append(low(jnp.concatenate([x_ref[0:BLK,qs],x_ref[length-BLK:length,qs]],0)))
    def chunk(i): return pl.ds(pl.multiple_of(i*CH,CH),CH)
    def one(i,ms):
        out=[]
        for h in heads:
            s=dot(x_ref[chunk(i),places(hp,h)[0]],ws[h],NT)
            g_ref[h,chunk(i),:]=s
            out.append(jnp.maximum(ms[h],jnp.max(s,0,keepdims=True)))
        return tuple(out)
    ms=lax.fori_loop(0,length//CH,one,tuple(jnp.full((1,2*BLK),-jnp.inf,F32) for h in heads),unroll=2)
    def two(i,ls):
        out=[]
        for h in heads:
            e=jnp.exp2(g_ref[h,chunk(i),:]*c-ms[h]*c)
            g_ref[h,chunk(i),:]=e
            out.append(ls[h]+jnp.sum(e,0,keepdims=True))
        return tuple(out)
    ls=lax.fori_loop(0,length//CH,two,tuple(jnp.zeros((1,2*BLK),F32) for h in heads))
    invs=[1.0/l for l in ls]
    acc_ref=s_ref
    for h in heads: s_ref[0,h]=jnp.zeros((KEYS,2*BLK),F32)
    def three(i,carry):
        for h in heads:
            p=g_ref[h,chunk(i),:]*invs[h]
            hi=p.astype(BF); lo=(p-hi.astype(F32)).astype(BF)
            s_ref[0,h,0:4*BLK,:]+=dot(jnp.concatenate([hi,lo],1),x_ref[chunk(i),places(hp,h)[0]],TN)
        return carry
    lax.fori_loop(0,length//CH,three,0,unroll=2)
    for h in heads:
        ds_=places(hp,h)[2]
        ctx=(s_ref[0,h,0:2*BLK,:]+s_ref[0,h,2*BLK:4*BLK,:])[:,HD:].astype(BF)
        o_ref[0:BLK,ds_]=ctx[:BLK]
        o_ref[length-BLK:length,ds_]=ctx[BLK:]

def attn_fwd(lists,x):
    length=x.shape[0]; hp=x.shape[1]//(3*HD)
    return pl.pallas_call(lambda *a: fwd_kernel(hp,*a),
        out_shape=jax.ShapeDtypeStruct((length,hp*HD),BF),
        in_specs=[pl.BlockSpec(memory_space=pltpu.SMEM),pl.BlockSpec(memory_space=pltpu.VMEM)],
        out_specs=pl.BlockSpec(memory_space=pltpu.VMEM),
        scratch_shapes=[pltpu.VMEM((2,hp,KEYS,2*BLK),F32),pltpu.VMEM((2,hp,KEYS,2*BLK),BF),pltpu.VMEM((hp,length,2*BLK),F32)],
        compiler_params=pltpu.CompilerParams(vmem_limit_bytes=48<<20),
        name="attn_fwd")(lists.reshape(-1),x)

def bwd_kernel(hp, lists_ref, x_ref, d_ref, o_ref, win_ref, rnd_ref, s_ref, p_ref, g_ref):
    length=x_ref.shape[0]; nb=length//BLK
    scale=HD**-0.5; c=LOG2E*scale
    half=(nb-2)//2
    win_ref[...]=jnp.zeros_like(win_ref)
    rnd_ref[...]=jnp.zeros_like(rnd_ref)
    def weights(rowa,rowb,qs,ds_):
        return jnp.concatenate([diag(low(x_ref[pl.ds(rowa,BLK),qs]),low(x_ref[pl.ds(rowb,BLK),qs])),
                                diag(high(d_ref[pl.ds(rowa,BLK),ds_]),high(d_ref[pl.ds(rowb,BLK),ds_]))],0)
    def stage_s(i,h,slot):
        lanes,qs,ds_=places(hp,h)
        kv,(rowa,_,_),(rowb,_,_)=pair_of(x_ref,lists_ref,lanes,h,i)
        s_ref[slot,h]=dot(kv,weights(rowa,rowb,qs,ds_),NT)
    def stage_p(h,slot):
        s=s_ref[slot,h,:,:2*BLK]; g=s_ref[slot,h,:,2*BLK:]
        m=jnp.max(s,0,keepdims=True)
        e=jnp.exp2(s*c-m*c)
        inv=1.0/jnp.sum(e,0,keepdims=True)
        delta=jnp.sum(e*g,0,keepdims=True)*inv
        p=e*inv
        p_ref[slot,h,:,:2*BLK]=(p*(g-delta)).astype(BF)
        p_ref[slot,h,:,2*BLK:]=p.astype(BF)
    def stage_c(i,h,slot):
        lanes,qs,ds_=places(hp,h)
        kv,(rowa,preva,ra),(rowb,prevb,rb)=pair_of(x_ref,lists_ref,lanes,h,jnp.maximum(i,0))
        dq=dot(p_ref[slot,h,:,:2*BLK],kv,TN)*scale
        o_ref[pl.ds(rowa,BLK),qs]=dq[:BLK,:HD].astype(BF)
        o_ref[pl.ds(rowb,BLK),qs]=dq[BLK:,2*HD:3*HD].astype(BF)
        dkv=dot(p_ref[slot,h],weights(rowa,rowb,qs,ds_),NN)
        for prev,rows,col in ((preva,ra,0),(prevb,rb,2*HD)):
            part=dkv[:,col:col+2*HD]
            win_ref[h,pl.ds(prev,3*BLK),:]+=part[:3*BLK]
            win_ref[h,length:length+2*BLK,:]+=part[3*BLK:5*BLK]
            for r in range(RAND):
                rnd_ref[h,pl.ds(rows[r],BLK),:]+=part[(5+r)*BLK:(6+r)*BLK]
    p_ref[...]=jnp.zeros_like(p_ref)
    body=run_pairs(half,hp,stage_s,stage_p,stage_c)
    lax.fori_loop(0,half//2,body,0)
    if half%2:
        for h in range(hp):
            stage_p(h,0); stage_c(half-2,h,1)
        for h in range(hp): stage_c(half-1,h,0)
    else:
        for h in range(hp): stage_c(half-1,h,1)
    lane_scale=jnp.where(lax.broadcasted_iota(jnp.int32,(1,2*HD),1)<HD,scale,1.0).astype(F32)
    heads=range(hp)
    ws=[];threes=[]
    for h in heads:
        _,qs,ds_=places(hp,h)
        q=low(jnp.concatenate([x_ref[0:BLK,qs],x_ref[length-BLK:length,qs]],0))
        d=high(jnp.concatenate([d_ref[0:BLK,ds_],d_ref[length-BLK:length,ds_]],0))
        ws.append(jnp.concatenate([q,d],0)); threes.append(jnp.concatenate([q,d,d],0))
    def chunk(i): return pl.ds(pl.multiple_of(i*CH,CH),CH)
    for h in heads:
        win_ref[h,0:BLK,:]+=win_ref[h,length:length+BLK,:]
        win_ref[h,length-BLK:length,:]+=win_ref[h,length+BLK:length+2*BLK,:]
    for h in heads:
        lanes,qs,ds_=places(hp,h)
        def one(i,m):
            s=dot(x_ref[chunk(i),lanes],ws[h],NT)
            g_ref[chunk(i),:]=s
            return jnp.maximum(m,jnp.max(s[:,:2*BLK],0,keepdims=True))
        m=lax.fori_loop(0,length//CH,one,jnp.full((1,2*BLK),-jnp.inf,F32),unroll=4)
        def two(i,st):
            l,eg=st
            e=jnp.exp2(g_ref[chunk(i),:2*BLK]*c-m*c)
            g_ref[chunk(i),:2*BLK]=e
            return l+jnp.sum(e,0,keepdims=True), eg+jnp.sum(e*g_ref[chunk(i),2*BLK:],0,keepdims=True)
        l,eg=lax.fori_loop(0,length//CH,two,(jnp.zeros((1,2*BLK),F32),)*2,unroll=2)
        inv=1.0/l; delta=eg*inv
        def three(i,dq):
            p=g_ref[chunk(i),:2*BLK]*inv
            ds=(p*(g_ref[chunk(i),2*BLK:]-delta)).astype(BF)
            hi=p.astype(BF); lo=(p-hi.astype(F32)).astype(BF)
            dkv=dot(jnp.concatenate([ds,hi,lo],1),threes[h],NN)
            tot=win_ref[h,chunk(i),:]+rnd_ref[h,chunk(i),:]+dkv
            o_ref[chunk(i),lanes]=(tot*lane_scale).astype(BF)
            return dq+dot(ds,x_ref[chunk(i),lanes],TN)
        dq=lax.fori_loop(0,length//CH,three,jnp.zeros((2*BLK,2*HD),F32),unroll=4)
        dq=(dq[:,:HD]*scale).astype(BF)
        o_ref[0:BLK,qs]=dq[:BLK]
        o_ref[length-BLK:length,qs]=dq[BLK:]

def attn_bwd(lists,x,d):
    length=x.shape[0]; hp=x.shape[1]//(3*HD)
    return pl.pallas_call(lambda *a: bwd_kernel(hp,*a),
        out_shape=jax.ShapeDtypeStruct(x.shape,BF),
        in_specs=[pl.BlockSpec(memory_space=pltpu.SMEM),pl.BlockSpec(memory_space=pltpu.VMEM),pl.BlockSpec(memory_space=pltpu.VMEM)],
        out_specs=pl.BlockSpec(memory_space=pltpu.VMEM),
        scratch_shapes=[pltpu.VMEM((hp,length+2*BLK,2*HD),F32),pltpu.VMEM((hp,length,2*HD),F32),pltpu.VMEM((2,hp,KEYS,4*BLK),F32),pltpu.VMEM((2,hp,KEYS,4*BLK),BF),pltpu.VMEM((length,4*BLK),F32)],
        compiler_params=pltpu.CompilerParams(vmem_limit_bytes=56<<20),
        name="attn_bwd")(lists.reshape(-1),x,d)


def layer_norm(resid, gain, shift):
    centre = resid - jnp.mean(resid, -1, keepdims=True)
    spread = jnp.mean(centre * centre, -1, keepdims=True)
    return centre * lax.rsqrt(spread + epsilon) * gain + shift


def to_groups(w, groups, hp):
    lead = w.shape[:-1]
    w = w.reshape(lead + (3, H, HD))
    w = jnp.pad(w, [(0, 0)] * (len(lead) + 1) + [(0, groups * hp - H), (0, 0)])
    w = w.reshape(lead + (3, groups, hp, HD))
    q, k, v = (w[..., n, :, :, :] for n in range(3))
    kv = jnp.stack([k, v], -2).reshape(lead + (groups, hp * 2 * HD))
    return jnp.concatenate([kv, q.reshape(lead + (groups, hp * HD))], -1).reshape(
        lead + (groups * hp * 3 * HD,)
    )


def from_groups(w, groups, hp):
    lead = w.shape[:-1]
    w = w.reshape(lead + (groups, hp * 3 * HD))
    kv = w[..., : hp * 2 * HD].reshape(lead + (groups, hp, 2, HD))
    q = w[..., hp * 2 * HD :].reshape(lead + (groups * hp, HD))
    k = kv[..., 0, :].reshape(lead + (groups * hp, HD))
    v = kv[..., 1, :].reshape(lead + (groups * hp, HD))
    return jnp.concatenate(
        [p[..., :H, :].reshape(lead + (H * HD,)) for p in (q, k, v)], -1
    )


def exchange(x):
    return lax.all_to_all(x, "seq", split_axis=0, concat_axis=0, tiled=True)


def mm(spec, a, b):
    return jnp.einsum(spec, a, b, preferred_element_type=jnp.float32)


def local(
    hidden,
    block_lists,
    w_qkv,
    bias_query,
    bias_value,
    w_attn_out,
    bias_attn_out,
    norm1_gain,
    norm1_shift,
    w_ffn_in,
    bias_ffn_in,
    w_ffn_out,
    bias_ffn_out,
    norm2_gain,
    norm2_shift,
    cotangent,
):
    groups = lax.axis_size("seq")
    hp = -(-H // groups)
    wide = groups * hp * HD
    tokens = hidden.shape[1]
    blocks_here = tokens // BLK
    ids = jnp.pad(block_lists[0], ((0, 0), (0, 0), (0, groups * hp - H), (0, 0)))
    ids = ids.reshape(LAYERS, blocks_here, groups, hp * RAND).transpose(2, 0, 1, 3)
    ids = exchange(ids.reshape(groups, -1)).reshape(groups, LAYERS, blocks_here, hp, RAND)
    ids = ids.transpose(1, 3, 0, 2, 4).reshape(LAYERS, -1)

    small = (bias_query, bias_value, bias_attn_out, norm1_gain, norm1_shift, bias_ffn_in, bias_ffn_out, norm2_gain, norm2_shift)
    sizes = [s.shape[1] for s in small]
    packed = lax.all_gather(jnp.concatenate(small, 1), "item", axis=0)
    rows = packed.shape[0]
    vectors = []
    for layer in range(LAYERS):
        at, out = 0, []
        for size in sizes:
            out.append(packed[:, layer, at : at + size].reshape(rows * size).astype(jnp.float32))
            at += size
        vectors.append(out)
    shards = (to_groups(w_qkv, groups, hp), w_attn_out, w_ffn_in, w_ffn_out)
    weights = [
        tuple(lax.all_gather(s[layer], "item", axis=0, tiled=True) for s in shards)
        for layer in range(LAYERS)
    ]
    current = hidden[0]
    saved = []
    for layer in range(LAYERS):
        qkv_weight, out_weight, inner_weight, outer_weight = weights[layer]
        query_bias, value_bias, out_bias, gain_one, shift_one, inner_bias, outer_bias, gain_two, shift_two = vectors[layer]
        bias = to_groups(jnp.concatenate([query_bias, jnp.zeros_like(query_bias), value_bias]), groups, hp)
        input_low = current.astype(BF)
        qkv_split = qkv_weight.reshape(D, groups, hp * 3 * HD)
        out_split = jnp.pad(out_weight, ((0, wide - D), (0, 0))).reshape(groups, hp * HD, D)
        proj = mm("td,dne->nte", input_low, qkv_split) + bias.reshape(groups, 1, hp * 3 * HD)
        x = exchange(proj.astype(BF)).reshape(groups * tokens, hp * 3 * HD)
        ctx = attn_fwd(ids[layer], x)
        context = exchange(ctx.reshape(groups, tokens, hp * HD))
        attn_out = mm("nte,ned->td", context, out_split)
        resid_one = current + attn_out + out_bias
        normed = layer_norm(resid_one, gain_one, shift_one)
        normed_low = normed.astype(BF)
        pre_act = mm("td,df->tf", normed_low, inner_weight) + inner_bias
        activated = jax.nn.gelu(pre_act, approximate=True).astype(BF)
        resid_two = normed + mm("tf,fd->td", activated, outer_weight) + outer_bias
        current = layer_norm(resid_two, gain_two, shift_two)
        saved.append((input_low, qkv_split, out_split, x, context, resid_one, normed_low, pre_act, activated, resid_two))
    grad_state = cotangent[0]
    collected = [None] * LAYERS
    for layer in reversed(range(LAYERS)):
        qkv_weight, out_weight, inner_weight, outer_weight = weights[layer]
        query_bias, value_bias, out_bias, gain_one, shift_one, inner_bias, outer_bias, gain_two, shift_two = vectors[layer]
        input_low, qkv_split, out_split, x, context, resid_one, normed_low, pre_act, activated, resid_two = saved[layer]
        unused, pull_two = jax.vjp(layer_norm, resid_two, gain_two, shift_two)
        grad_resid_two, grad_gain_two, grad_shift_two = pull_two(grad_state)
        grad_ffn = grad_resid_two.astype(BF)
        grad_act = mm("td,fd->tf", grad_ffn, outer_weight)
        unused, pull_gelu = jax.vjp(partial(jax.nn.gelu, approximate=True), pre_act)
        grad_pre = pull_gelu(grad_act)[0].astype(BF)
        grad_normed = grad_resid_two + mm("tf,df->td", grad_pre, inner_weight)
        unused, pull_one = jax.vjp(layer_norm, resid_one, gain_one, shift_one)
        grad_resid_one, grad_gain_one, grad_shift_one = pull_one(grad_normed)
        grad_attn = grad_resid_one.astype(BF)
        grad_context = mm("td,ned->nte", grad_attn, out_split).astype(BF)
        dctx = exchange(grad_context).reshape(groups * tokens, hp * HD)
        dx = attn_bwd(ids[layer], x, dctx)
        dproj = exchange(dx.reshape(groups, tokens, hp * 3 * HD))
        grad_outer_weight = mm("tf,td->fd", activated, grad_ffn)
        grad_inner_weight = mm("td,tf->df", normed_low, grad_pre)
        grad_out_weight = mm("nte,td->ned", context, grad_attn).reshape(wide, D)[:D]
        grad_qkv_weight = mm("td,nte->dne", input_low, dproj).reshape(D, -1)
        grad_state = grad_resid_one + mm("nte,dne->td", dproj, qkv_split)
        total = lambda g: jnp.sum(g.astype(jnp.float32), tuple(range(g.ndim - 1)))
        dbias = from_groups(jnp.sum(dproj.astype(jnp.float32), 1).reshape(-1), groups, hp)
        flat = (dbias[:D], dbias[2 * D :], total(grad_attn), grad_gain_one, grad_shift_one, total(grad_pre), total(grad_ffn), grad_gain_two, grad_shift_two)
        big = tuple(
            lax.psum(lax.psum_scatter(g.astype(BF), "item", scatter_dimension=0, tiled=True), "seq").astype(jnp.float32)
            for g in (grad_qkv_weight, grad_out_weight, grad_inner_weight, grad_outer_weight)
        )
        collected[layer] = (from_groups(big[0], groups, hp),) + big[1:], flat
    parts = [
        jnp.concatenate([g.reshape(rows, -1) for g in collected[layer][1]], 1) for layer in range(LAYERS)
    ]
    part = jnp.stack(parts, 1)
    part = part.reshape(rows, -1).astype(BF)
    mine = lax.psum(lax.psum_scatter(part, "item", scatter_dimension=0, tiled=True), "seq")
    mine = mine.astype(jnp.float32).reshape(LAYERS, -1)
    at, vecs = 0, []
    for size in sizes:
        vecs.append(mine[:, at : at + size])
        at += size
    gq, go, gi, gf = (jnp.stack([collected[layer][0][n] for layer in range(LAYERS)]) for n in range(4))
    return (
        current[None],
        grad_state[None],
        gq,
        vecs[0],
        vecs[1],
        go,
        vecs[2],
        vecs[3],
        vecs[4],
        gi,
        vecs[5],
        gf,
        vecs[6],
        vecs[7],
        vecs[8],
    )


def solution(mesh):
    placed = (
        P("item", "seq", None),
        P("item", None, "seq", None, None),
        P(None, "item", None),
        P(None, "item"),
        P(None, "item"),
        P(None, "item", None),
        P(None, "item"),
        P(None, "item"),
        P(None, "item"),
        P(None, "item", None),
        P(None, "item"),
        P(None, "item", None),
        P(None, "item"),
        P(None, "item"),
        P(None, "item"),
        P("item", "seq", None),
    )
    return jax.shard_map(
        local,
        mesh=mesh,
        in_specs=placed,
        out_specs=(
            P("item", "seq", None),
            P("item", "seq", None),
            P(None, "item", None),
            P(None, "item"),
            P(None, "item"),
            P(None, "item", None),
            P(None, "item"),
            P(None, "item"),
            P(None, "item"),
            P(None, "item", None),
            P(None, "item"),
            P(None, "item", None),
            P(None, "item"),
            P(None, "item"),
            P(None, "item"),
        ),
        check_vma=False,
    )
```

```python
from functools import partial

import jax
import jax.numpy as jnp
from jax import lax
from jax.experimental import pallas as pl
from jax.experimental.pallas import tpu as pltpu
from jax.sharding import PartitionSpec as P

D = 768
H = 12
LAYERS = 2
epsilon = 1e-05

HD = 64
BLK = 64
RAND = 3
F32=jnp.float32; BF=jnp.bfloat16
LOG2E=1.4426950408889634
NT=(((1,),(1,)),((),()))
TN=(((0,),(0,)),((),()))
NN=(((1,),(0,)),((),()))
def dot(a,b,dn): return lax.dot_general(a,b,dn,preferred_element_type=F32)
KEYS=(5+RAND)*BLK
CH=512

def low(v): return jnp.concatenate([v,jnp.zeros_like(v)],1)
def high(v): return jnp.concatenate([jnp.zeros_like(v),v],1)
def diag(a,b):
    return jnp.concatenate([jnp.concatenate([a,jnp.zeros_like(b)],1),jnp.concatenate([jnp.zeros_like(a),b],1)],0)

def places(hp,h):
    base=hp*2*HD+h*HD
    return slice(h*2*HD,(h+1)*2*HD), slice(base,base+HD), slice(h*HD,(h+1)*HD)

def listed(x_ref,lists_ref,lanes,h,j):
    length=x_ref.shape[0]; nb=length//BLK
    row=pl.multiple_of(j*BLK,BLK); prev=pl.multiple_of(row-BLK,BLK)
    rows=[pl.multiple_of(lists_ref[(h*nb+j)*RAND+r]*BLK,BLK) for r in range(RAND)]
    parts=[x_ref[pl.ds(prev,3*BLK),lanes],x_ref[0:BLK,lanes],x_ref[length-BLK:length,lanes]]
    parts+=[x_ref[pl.ds(k,BLK),lanes] for k in rows]
    return jnp.concatenate(parts,0), row, prev, rows

def pair_of(x_ref,lists_ref,lanes,h,i):
    kva,rowa,preva,ra=listed(x_ref,lists_ref,lanes,h,1+2*i)
    kvb,rowb,prevb,rb=listed(x_ref,lists_ref,lanes,h,2+2*i)
    return jnp.concatenate([kva,kvb],1),(rowa,preva,ra),(rowb,prevb,rb)

def run_pairs(half,hp,first,second,third):
    for h in range(hp): first(0,h,0)
    def body(i,carry):
        for u in range(2):
            t=2*i+u
            for h in range(hp):
                first(jnp.minimum(t+1,half-1),h,1-u)
                second(h,u)
                third(t-1,h,1-u)
        return carry
    return body

def fwd_kernel(hp, lists_ref, x_ref, o_ref, s_ref, p_ref, g_ref):
    length=x_ref.shape[0]; nb=length//BLK
    c=LOG2E*HD**-0.5
    half=(nb-2)//2
    def stage_s(i,h,slot):
        lanes,qs,_=places(hp,h)
        kv,(rowa,_,_),(rowb,_,_)=pair_of(x_ref,lists_ref,lanes,h,i)
        w=diag(low(x_ref[pl.ds(rowa,BLK),qs]),low(x_ref[pl.ds(rowb,BLK),qs]))
        s_ref[slot,h]=dot(kv,w,NT)
    def stage_p(h,slot):
        s=s_ref[slot,h]
        m=jnp.max(s,0,keepdims=True)
        e=jnp.exp2(s*c-m*c)
        inv=1.0/jnp.sum(e,0,keepdims=True)
        p_ref[slot,h]=(e*inv).astype(BF)
    def stage_c(i,h,slot):
        lanes,_,ds_=places(hp,h)
        kv,(rowa,_,_),(rowb,_,_)=pair_of(x_ref,lists_ref,lanes,h,jnp.maximum(i,0))
        ctx=dot(p_ref[slot,h],kv,TN)
        o_ref[pl.ds(rowa,BLK),ds_]=ctx[:BLK,HD:2*HD].astype(BF)
        o_ref[pl.ds(rowb,BLK),ds_]=ctx[BLK:,3*HD:].astype(BF)
    p_ref[...]=jnp.zeros_like(p_ref)
    body=run_pairs(half,hp,stage_s,stage_p,stage_c)
    lax.fori_loop(0,(half+1)//2,body,0)
    for h in range(hp): stage_c(half-1,h,(half-1)%2)
    heads=range(hp)
    ws=[]
    for h in heads:
        _,qs,_=places(hp,h)
        ws.append(low(jnp.concatenate([x_ref[0:BLK,qs],x_ref[length-BLK:length,qs]],0)))
    def chunk(i): return pl.ds(pl.multiple_of(i*CH,CH),CH)
    def one(i,ms):
        out=[]
        for h in heads:
            s=dot(x_ref[chunk(i),places(hp,h)[0]],ws[h],NT)
            g_ref[h,chunk(i),:]=s
            out.append(jnp.maximum(ms[h],jnp.max(s,0,keepdims=True)))
        return tuple(out)
    ms=lax.fori_loop(0,length//CH,one,tuple(jnp.full((1,2*BLK),-jnp.inf,F32) for h in heads),unroll=2)
    def two(i,ls):
        out=[]
        for h in heads:
            e=jnp.exp2(g_ref[h,chunk(i),:]*c-ms[h]*c)
            g_ref[h,chunk(i),:]=e
            out.append(ls[h]+jnp.sum(e,0,keepdims=True))
        return tuple(out)
    ls=lax.fori_loop(0,length//CH,two,tuple(jnp.zeros((1,2*BLK),F32) for h in heads))
    invs=[1.0/l for l in ls]
    acc_ref=s_ref
    for h in heads: s_ref[0,h]=jnp.zeros((KEYS,2*BLK),F32)
    def three(i,carry):
        for h in heads:
            p=g_ref[h,chunk(i),:]*invs[h]
            hi=p.astype(BF); lo=(p-hi.astype(F32)).astype(BF)
            s_ref[0,h,0:4*BLK,:]+=dot(jnp.concatenate([hi,lo],1),x_ref[chunk(i),places(hp,h)[0]],TN)
        return carry
    lax.fori_loop(0,length//CH,three,0,unroll=2)
    for h in heads:
        ds_=places(hp,h)[2]
        ctx=(s_ref[0,h,0:2*BLK,:]+s_ref[0,h,2*BLK:4*BLK,:])[:,HD:].astype(BF)
        o_ref[0:BLK,ds_]=ctx[:BLK]
        o_ref[length-BLK:length,ds_]=ctx[BLK:]

def attn_fwd(lists,x):
    length=x.shape[0]; hp=x.shape[1]//(3*HD)
    return pl.pallas_call(lambda *a: fwd_kernel(hp,*a),
        out_shape=jax.ShapeDtypeStruct((length,hp*HD),BF),
        in_specs=[pl.BlockSpec(memory_space=pltpu.SMEM),pl.BlockSpec(memory_space=pltpu.VMEM)],
        out_specs=pl.BlockSpec(memory_space=pltpu.VMEM),
        scratch_shapes=[pltpu.VMEM((2,hp,KEYS,2*BLK),F32),pltpu.VMEM((2,hp,KEYS,2*BLK),BF),pltpu.VMEM((hp,length,2*BLK),F32)],
        compiler_params=pltpu.CompilerParams(vmem_limit_bytes=48<<20),
        cost_estimate=pl.CostEstimate(flops=26*10**9,bytes_accessed=6*10**6,transcendentals=6*10**6),
        name="attn_fwd")(lists.reshape(-1),x)

def bwd_kernel(hp, lists_ref, x_ref, d_ref, o_ref, win_ref, rnd_ref, s_ref, p_ref, g_ref):
    length=x_ref.shape[0]; nb=length//BLK
    scale=HD**-0.5; c=LOG2E*scale
    half=(nb-2)//2
    win_ref[...]=jnp.zeros_like(win_ref)
    rnd_ref[...]=jnp.zeros_like(rnd_ref)
    def weights(rowa,rowb,qs,ds_):
        return jnp.concatenate([diag(low(x_ref[pl.ds(rowa,BLK),qs]),low(x_ref[pl.ds(rowb,BLK),qs])),
                                diag(high(d_ref[pl.ds(rowa,BLK),ds_]),high(d_ref[pl.ds(rowb,BLK),ds_]))],0)
    def stage_s(i,h,slot):
        lanes,qs,ds_=places(hp,h)
        kv,(rowa,_,_),(rowb,_,_)=pair_of(x_ref,lists_ref,lanes,h,i)
        s_ref[slot,h]=dot(kv,weights(rowa,rowb,qs,ds_),NT)
    def stage_p(h,slot):
        s=s_ref[slot,h,:,:2*BLK]; g=s_ref[slot,h,:,2*BLK:]
        m=jnp.max(s,0,keepdims=True)
        e=jnp.exp2(s*c-m*c)
        inv=1.0/jnp.sum(e,0,keepdims=True)
        delta=jnp.sum(e*g,0,keepdims=True)*inv
        p=e*inv
        p_ref[slot,h,:,:2*BLK]=(p*(g-delta)).astype(BF)
        p_ref[slot,h,:,2*BLK:]=p.astype(BF)
    def stage_c(i,h,slot):
        lanes,qs,ds_=places(hp,h)
        kv,(rowa,preva,ra),(rowb,prevb,rb)=pair_of(x_ref,lists_ref,lanes,h,jnp.maximum(i,0))
        dq=dot(p_ref[slot,h,:,:2*BLK],kv,TN)*scale
        o_ref[pl.ds(rowa,BLK),qs]=dq[:BLK,:HD].astype(BF)
        o_ref[pl.ds(rowb,BLK),qs]=dq[BLK:,2*HD:3*HD].astype(BF)
        dkv=dot(p_ref[slot,h],weights(rowa,rowb,qs,ds_),NN)
        for prev,rows,col in ((preva,ra,0),(prevb,rb,2*HD)):
            part=dkv[:,col:col+2*HD]
            win_ref[h,pl.ds(prev,3*BLK),:]+=part[:3*BLK]
            win_ref[h,length:length+2*BLK,:]+=part[3*BLK:5*BLK]
            for r in range(RAND):
                rnd_ref[h,pl.ds(rows[r],BLK),:]+=part[(5+r)*BLK:(6+r)*BLK]
    p_ref[...]=jnp.zeros_like(p_ref)
    body=run_pairs(half,hp,stage_s,stage_p,stage_c)
    lax.fori_loop(0,half//2,body,0)
    if half%2:
        for h in range(hp):
            stage_p(h,0); stage_c(half-2,h,1)
        for h in range(hp): stage_c(half-1,h,0)
    else:
        for h in range(hp): stage_c(half-1,h,1)
    lane_scale=jnp.where(lax.broadcasted_iota(jnp.int32,(1,2*HD),1)<HD,scale,1.0).astype(F32)
    heads=range(hp)
    ws=[];threes=[]
    for h in heads:
        _,qs,ds_=places(hp,h)
        q=low(jnp.concatenate([x_ref[0:BLK,qs],x_ref[length-BLK:length,qs]],0))
        d=high(jnp.concatenate([d_ref[0:BLK,ds_],d_ref[length-BLK:length,ds_]],0))
        ws.append(jnp.concatenate([q,d],0)); threes.append(jnp.concatenate([q,d,d],0))
    def chunk(i): return pl.ds(pl.multiple_of(i*CH,CH),CH)
    for h in heads:
        win_ref[h,0:BLK,:]+=win_ref[h,length:length+BLK,:]
        win_ref[h,length-BLK:length,:]+=win_ref[h,length+BLK:length+2*BLK,:]
    for h in heads:
        lanes,qs,ds_=places(hp,h)
        def one(i,m):
            s=dot(x_ref[chunk(i),lanes],ws[h],NT)
            g_ref[chunk(i),:]=s
            return jnp.maximum(m,jnp.max(s[:,:2*BLK],0,keepdims=True))
        m=lax.fori_loop(0,length//CH,one,jnp.full((1,2*BLK),-jnp.inf,F32),unroll=4)
        def two(i,st):
            l,eg=st
            e=jnp.exp2(g_ref[chunk(i),:2*BLK]*c-m*c)
            g_ref[chunk(i),:2*BLK]=e
            return l+jnp.sum(e,0,keepdims=True), eg+jnp.sum(e*g_ref[chunk(i),2*BLK:],0,keepdims=True)
        l,eg=lax.fori_loop(0,length//CH,two,(jnp.zeros((1,2*BLK),F32),)*2,unroll=2)
        inv=1.0/l; delta=eg*inv
        def three(i,dq):
            p=g_ref[chunk(i),:2*BLK]*inv
            ds=(p*(g_ref[chunk(i),2*BLK:]-delta)).astype(BF)
            hi=p.astype(BF); lo=(p-hi.astype(F32)).astype(BF)
            dkv=dot(jnp.concatenate([ds,hi,lo],1),threes[h],NN)
            tot=win_ref[h,chunk(i),:]+rnd_ref[h,chunk(i),:]+dkv
            o_ref[chunk(i),lanes]=(tot*lane_scale).astype(BF)
            return dq+dot(ds,x_ref[chunk(i),lanes],TN)
        dq=lax.fori_loop(0,length//CH,three,jnp.zeros((2*BLK,2*HD),F32),unroll=4)
        dq=(dq[:,:HD]*scale).astype(BF)
        o_ref[0:BLK,qs]=dq[:BLK]
        o_ref[length-BLK:length,qs]=dq[BLK:]

def attn_bwd(lists,x,d):
    length=x.shape[0]; hp=x.shape[1]//(3*HD)
    return pl.pallas_call(lambda *a: bwd_kernel(hp,*a),
        out_shape=jax.ShapeDtypeStruct(x.shape,BF),
        in_specs=[pl.BlockSpec(memory_space=pltpu.SMEM),pl.BlockSpec(memory_space=pltpu.VMEM),pl.BlockSpec(memory_space=pltpu.VMEM)],
        out_specs=pl.BlockSpec(memory_space=pltpu.VMEM),
        scratch_shapes=[pltpu.VMEM((hp,length+2*BLK,2*HD),F32),pltpu.VMEM((hp,length,2*HD),F32),pltpu.VMEM((2,hp,KEYS,4*BLK),F32),pltpu.VMEM((2,hp,KEYS,4*BLK),BF),pltpu.VMEM((length,4*BLK),F32)],
        compiler_params=pltpu.CompilerParams(vmem_limit_bytes=56<<20),
        cost_estimate=pl.CostEstimate(flops=46*10**9,bytes_accessed=12*10**6,transcendentals=6*10**6),
        name="attn_bwd")(lists.reshape(-1),x,d)


def layer_norm(resid, gain, shift):
    centre = resid - jnp.mean(resid, -1, keepdims=True)
    spread = jnp.mean(centre * centre, -1, keepdims=True)
    return centre * lax.rsqrt(spread + epsilon) * gain + shift


def to_groups(w, groups, hp):
    lead = w.shape[:-1]
    w = w.reshape(lead + (3, H, HD))
    w = jnp.pad(w, [(0, 0)] * (len(lead) + 1) + [(0, groups * hp - H), (0, 0)])
    w = w.reshape(lead + (3, groups, hp, HD))
    q, k, v = (w[..., n, :, :, :] for n in range(3))
    kv = jnp.stack([k, v], -2).reshape(lead + (groups, hp * 2 * HD))
    return jnp.concatenate([kv, q.reshape(lead + (groups, hp * HD))], -1).reshape(
        lead + (groups * hp * 3 * HD,)
    )


def from_groups(w, groups, hp):
    lead = w.shape[:-1]
    w = w.reshape(lead + (groups, hp * 3 * HD))
    kv = w[..., : hp * 2 * HD].reshape(lead + (groups, hp, 2, HD))
    q = w[..., hp * 2 * HD :].reshape(lead + (groups * hp, HD))
    k = kv[..., 0, :].reshape(lead + (groups * hp, HD))
    v = kv[..., 1, :].reshape(lead + (groups * hp, HD))
    return jnp.concatenate(
        [p[..., :H, :].reshape(lead + (H * HD,)) for p in (q, k, v)], -1
    )


def exchange(x):
    return lax.all_to_all(x, "seq", split_axis=0, concat_axis=0, tiled=True)


def mm(spec, a, b):
    return jnp.einsum(spec, a, b, preferred_element_type=jnp.float32)


def local(
    hidden,
    block_lists,
    w_qkv,
    bias_query,
    bias_value,
    w_attn_out,
    bias_attn_out,
    norm1_gain,
    norm1_shift,
    w_ffn_in,
    bias_ffn_in,
    w_ffn_out,
    bias_ffn_out,
    norm2_gain,
    norm2_shift,
    cotangent,
):
    groups = lax.axis_size("seq")
    hp = -(-H // groups)
    wide = groups * hp * HD
    tokens = hidden.shape[1]
    blocks_here = tokens // BLK
    ids = jnp.pad(block_lists[0], ((0, 0), (0, 0), (0, groups * hp - H), (0, 0)))
    ids = ids.reshape(LAYERS, blocks_here, groups, hp * RAND).transpose(2, 0, 1, 3)
    ids = exchange(ids.reshape(groups, -1)).reshape(groups, LAYERS, blocks_here, hp, RAND)
    ids = ids.transpose(1, 3, 0, 2, 4).reshape(LAYERS, -1)

    small = (bias_query, bias_value, bias_attn_out, norm1_gain, norm1_shift, bias_ffn_in, bias_ffn_out, norm2_gain, norm2_shift)
    sizes = [s.shape[1] for s in small]
    packed = lax.all_gather(jnp.concatenate(small, 1), "item", axis=0)
    rows = packed.shape[0]
    vectors = []
    for layer in range(LAYERS):
        at, out = 0, []
        for size in sizes:
            out.append(packed[:, layer, at : at + size].reshape(rows * size).astype(jnp.float32))
            at += size
        vectors.append(out)
    shards = (to_groups(w_qkv, groups, hp), w_attn_out, w_ffn_in, w_ffn_out)
    weights = [
        tuple(lax.all_gather(s[layer], "item", axis=0, tiled=True) for s in shards)
        for layer in range(LAYERS)
    ]
    current = hidden[0]
    seq_rank = lax.axis_index("seq")
    item_rank = lax.axis_index("item")
    cols = hp * 3 * HD
    hidden_all = exchange(jnp.broadcast_to(current.astype(BF)[None], (groups, tokens, D))).reshape(groups * tokens, D)
    own_shard = lax.dynamic_index_in_dim(shards[0][0].reshape(-1, groups, cols), seq_rank, 1, False)
    own_weight = lax.all_gather(own_shard, "item", axis=0, tiled=True)
    saved = []
    for layer in range(LAYERS):
        qkv_weight, out_weight, inner_weight, outer_weight = weights[layer]
        query_bias, value_bias, out_bias, gain_one, shift_one, inner_bias, outer_bias, gain_two, shift_two = vectors[layer]
        bias = to_groups(jnp.concatenate([query_bias, jnp.zeros_like(query_bias), value_bias]), groups, hp)
        input_low = current.astype(BF)
        qkv_split = qkv_weight.reshape(D, groups, hp * 3 * HD)
        out_split = jnp.pad(out_weight, ((0, wide - D), (0, 0))).reshape(groups, hp * HD, D)
        if layer == 0:
            own_bias = lax.dynamic_index_in_dim(bias.reshape(groups, cols), seq_rank, 0, True)
            x = (mm("td,de->te", hidden_all, own_weight) + own_bias).astype(BF)
        else:
            proj = mm("td,dne->nte", input_low, qkv_split) + bias.reshape(groups, 1, cols)
            x = exchange(proj.astype(BF)).reshape(groups * tokens, cols)
        ctx = attn_fwd(ids[layer], x)
        context = exchange(ctx.reshape(groups, tokens, hp * HD))
        attn_out = mm("nte,ned->td", context, out_split)
        resid_one = current + attn_out + out_bias
        normed = layer_norm(resid_one, gain_one, shift_one)
        normed_low = normed.astype(BF)
        pre_act = mm("td,df->tf", normed_low, inner_weight) + inner_bias
        activated = jax.nn.gelu(pre_act, approximate=True).astype(BF)
        resid_two = normed + mm("tf,fd->td", activated, outer_weight) + outer_bias
        current = layer_norm(resid_two, gain_two, shift_two)
        saved.append((input_low, qkv_split, out_split, x, context, resid_one, normed_low, pre_act, activated, resid_two))
    grad_state = cotangent[0]
    collected = [None] * LAYERS
    flats = [None] * LAYERS
    previous = None

    def scattered(g):
        return lax.psum_scatter(g, "item", scatter_dimension=0, tiled=True)

    def seq_total(shares):
        flat = jnp.concatenate([p.reshape(-1, D) for p in shares])
        flat = jnp.pad(flat, ((0, -flat.shape[0] % (8 * groups)), (0, 0)))
        parts = exchange(flat.reshape(groups, -1, D))
        own = jnp.sum(parts.astype(jnp.float32), 0).astype(BF)
        whole = exchange(jnp.broadcast_to(own[None], (groups,) + own.shape)).reshape(-1, D).astype(jnp.float32)
        at, out = 0, []
        for p in shares:
            n = p.size // D
            out.append(whole[at : at + n].reshape(p.shape))
            at += n
        return out

    def with_rows(grad, vectors):
        width = grad.shape[1]
        part = jnp.concatenate([v.reshape(rows, -1) for v in vectors], 1)
        part = jnp.pad(part, ((0, 0), (0, 8 * width - part.shape[1]))).reshape(rows, 8, width)
        return jnp.concatenate([grad.reshape(rows, -1, width), part.astype(BF)], 1).reshape(-1, width)

    def split_rows(share, counts):
        flat, at, out = share[-8:].reshape(-1), 0, []
        for n in counts:
            out.append(flat[at : at + n])
            at += n
        return share[:-8], out

    for layer in reversed(range(LAYERS)):
        qkv_weight, out_weight, inner_weight, outer_weight = weights[layer]
        query_bias, value_bias, out_bias, gain_one, shift_one, inner_bias, outer_bias, gain_two, shift_two = vectors[layer]
        input_low, qkv_split, out_split, x, context, resid_one, normed_low, pre_act, activated, resid_two = saved[layer]
        unused, pull_two = jax.vjp(layer_norm, resid_two, gain_two, shift_two)
        grad_resid_two, grad_gain_two, grad_shift_two = pull_two(grad_state)
        grad_ffn = grad_resid_two.astype(BF)
        grad_act = mm("td,fd->tf", grad_ffn, outer_weight)
        unused, pull_gelu = jax.vjp(partial(jax.nn.gelu, approximate=True), pre_act)
        grad_pre = pull_gelu(grad_act)[0].astype(BF)
        grad_normed = grad_resid_two + mm("tf,df->td", grad_pre, inner_weight)
        unused, pull_one = jax.vjp(layer_norm, resid_one, gain_one, shift_one)
        grad_resid_one, grad_gain_one, grad_shift_one = pull_one(grad_normed)
        grad_attn = grad_resid_one.astype(BF)
        grad_context = mm("td,ned->nte", grad_attn, out_split).astype(BF)
        dctx = exchange(grad_context).reshape(groups * tokens, hp * HD)
        grad_outer_weight = mm("tf,td->fd", activated, grad_ffn).astype(BF)
        grad_inner_weight = mm("td,tf->df", normed_low, grad_pre).astype(BF)
        grad_out_weight = mm("nte,td->ned", context, grad_attn).reshape(wide, D)[:D].astype(BF)
        total = lambda g: jnp.sum(g.astype(jnp.float32), tuple(range(g.ndim - 1)))
        early = (total(grad_attn), grad_gain_one, grad_shift_one, total(grad_pre), total(grad_ffn), grad_gain_two, grad_shift_two)
        counts = [v.size // rows for v in early]
        grad_out_weight = with_rows(grad_out_weight, early)
        dctx, grad_outer_weight, grad_inner_weight, grad_out_weight = lax.optimization_barrier((dctx, grad_outer_weight, grad_inner_weight, grad_out_weight))
        ffn_shares = (scattered(grad_inner_weight), scattered(grad_outer_weight), scattered(grad_out_weight))
        if previous is None:
            dctx, early_weight = lax.optimization_barrier((dctx, weights[0][0]))
            saved[0] = (saved[0][0], early_weight.reshape(D, groups, cols)) + saved[0][2:]
        else:
            dctx, previous = lax.optimization_barrier((dctx, previous))
            qkv, inner, outer, attn = seq_total(previous)
            qkv, late_one = split_rows(qkv, [D // rows] * 2)
            attn, early_one = split_rows(attn, counts)
            collected[layer + 1] = (from_groups(qkv, groups, hp), attn, inner, outer)
            flats[layer + 1] = late_one + early_one
        dx = attn_bwd(ids[layer], x, dctx)
        if layer == 0:
            dx, collected[1], flats[1] = lax.optimization_barrier((dx, collected[1], flats[1]))
            own_grad = mm("td,te->de", hidden_all, dx).reshape(rows, -1, cols)
            own_sum = jnp.broadcast_to(total(dx)[None, None], (rows, 8, cols))
            packed_grad = jnp.concatenate([own_grad, own_sum], 1).astype(BF)
            dproj = exchange(dx.reshape(groups, tokens, cols))
            packed_grad, ffn_shares = lax.optimization_barrier((packed_grad, ffn_shares))
            share = scattered(packed_grad.reshape(-1, cols))
            inner, outer, attn = seq_total(ffn_shares)
            share = exchange(jnp.broadcast_to(share[None], (groups,) + share.shape)).astype(jnp.float32)
            gq0 = from_groups(share[:, :-8].transpose(1, 0, 2).reshape(-1, groups * cols), groups, hp)
            db = from_groups(share[:, -8].reshape(-1), groups, hp)
            attn, flats[0] = split_rows(attn, counts)
            collected[0] = (gq0, attn, inner, outer)
            late = [lax.dynamic_slice_in_dim(db, part * D + item_rank * (D // rows), D // rows) for part in (0, 2)]
        else:
            dproj = exchange(dx.reshape(groups, tokens, cols))
            grad_qkv_weight = mm("td,nte->dne", input_low, dproj).reshape(D, -1).astype(BF)
            dbias = from_groups(jnp.sum(dproj.astype(jnp.float32), 1).reshape(-1), groups, hp)
            previous = (scattered(with_rows(grad_qkv_weight, (dbias[:D], dbias[2 * D :]))),) + ffn_shares
        grad_state = grad_resid_one + mm("nte,dne->td", dproj, qkv_split)
    first, second = flats
    vecs = [jnp.stack([late[n], second[n]]) for n in range(2)]
    vecs += [jnp.stack([first[n], second[n + 2]]) for n in range(7)]
    gq, go, gi, gf = (jnp.stack([collected[layer][n] for layer in range(LAYERS)]) for n in range(4))
    return (
        current[None],
        grad_state[None],
        gq,
        vecs[0],
        vecs[1],
        go,
        vecs[2],
        vecs[3],
        vecs[4],
        gi,
        vecs[5],
        gf,
        vecs[6],
        vecs[7],
        vecs[8],
    )


def solution(mesh):
    placed = (
        P("item", "seq", None),
        P("item", None, "seq", None, None),
        P(None, "item", None),
        P(None, "item"),
        P(None, "item"),
        P(None, "item", None),
        P(None, "item"),
        P(None, "item"),
        P(None, "item"),
        P(None, "item", None),
        P(None, "item"),
        P(None, "item", None),
        P(None, "item"),
        P(None, "item"),
        P(None, "item"),
        P("item", "seq", None),
    )
    return jax.shard_map(
        local,
        mesh=mesh,
        in_specs=placed,
        out_specs=(
            P("item", "seq", None),
            P("item", "seq", None),
            P(None, "item", None),
            P(None, "item"),
            P(None, "item"),
            P(None, "item", None),
            P(None, "item"),
            P(None, "item"),
            P(None, "item"),
            P(None, "item", None),
            P(None, "item"),
            P(None, "item", None),
            P(None, "item"),
            P(None, "item"),
            P(None, "item"),
        ),
        check_vma=False,
    )
```

```python
from functools import partial

import jax
import jax.numpy as jnp
from jax import lax
from jax.experimental import pallas as pl
from jax.experimental.pallas import tpu as pltpu
from jax.sharding import PartitionSpec as P

D = 768
H = 12
HD = 64
BLK = 64
RAND = 3
LAYERS = 2
LISTED = 5 + RAND
KEYS = LISTED * BLK
WIDE = 2 * HD
F32 = jnp.float32
BF = jnp.bfloat16
LOG2E = 1.4426950408889634
epsilon = 1e-05
NT = (((1,), (1,)), ((), ()))
TN = (((0,), (0,)), ((), ()))
NN = (((1,), (0,)), ((), ()))
VMEM = pltpu.VMEM


def dot(a, b, dims):
    return lax.dot_general(a, b, dims, preferred_element_type=F32)


class Plan:
    def __init__(self, groups, tokens, half=128):
        self.groups = groups
        self.tokens = tokens
        self.hp = -(-H // groups)
        self.pairs = self.hp // 2
        self.odd = self.hp % 2
        self.half = min(half, tokens // 2)
        self.chunks = tokens // 2 // self.half
        self.per = self.half // BLK
        self.rows = 2 * self.half
        self.xp = 2 * self.hp + 2 * self.pairs + self.odd
        self.cp = 2 * self.pairs + self.odd
        self.blocks = groups * tokens // BLK
        self.own = (2 * self.hp + self.hp) * HD
        self.cols = groups * self.own
        self.ctx = groups * self.hp * HD

    def x_shape(self):
        return (self.groups, self.chunks, self.xp, self.per, BLK, WIDE)

    def c_shape(self):
        return (self.groups, self.chunks, self.cp, self.per, BLK, WIDE)


def low(v):
    return jnp.concatenate([v, jnp.zeros_like(v)], 1)


def high(v):
    return jnp.concatenate([jnp.zeros_like(v), v], 1)


def diag(a, b):
    return jnp.concatenate(
        [jnp.concatenate([a, jnp.zeros_like(b)], 1), jnp.concatenate([jnp.zeros_like(a), b], 1)], 0
    )


def spots(plan, h, i):
    per = plan.per
    xb = (i // per) * (plan.xp * per) + i % per
    cb = (i // per) * (plan.cp * per) + i % per
    if h < 2 * plan.pairs:
        lanes = slice((h % 2) * HD, (h % 2 + 1) * HD)
        x0 = xb + (2 * plan.hp + 2 * (h // 2)) * per
        c0 = cb + 2 * (h // 2) * per
        return ((x0, lanes), (x0 + per, lanes)), ((c0, lanes), (c0 + per, lanes))
    x0 = xb + (2 * plan.hp + 2 * plan.pairs) * per
    c0 = cb + 2 * plan.pairs * per
    first, second = slice(0, HD), slice(HD, WIDE)
    return ((x0, first), (x0, second)), ((c0, first), (c0, second))


def listed(plan, x_ref, lists_ref, h, i):
    sides, places = [], []
    for side in range(2):
        at = ((h * (plan.blocks // 2) + i) * 2 + side) * LISTED
        ids = [lists_ref[at + n] for n in range(LISTED)]
        sides.append(jnp.concatenate([x_ref[n] for n in ids], 0))
        places.append(ids)
    return jnp.concatenate(sides, 1), places


def run_pairs(count, hp, first, second, third):
    for h in range(hp):
        first(0, h, 0)

    def body(i, carry):
        for u in range(2):
            t = 2 * i + u
            for h in range(hp):
                first(jnp.minimum(t + 1, count - 1), h, 1 - u)
                second(h, u)
                third(jnp.maximum(t - 1, 0), h, 1 - u)
        return carry

    lax.fori_loop(0, count // 2, body, 0)
    for h in range(hp):
        third(count - 1, h, 1)


def keys_of(plan, x_ref, h, n):
    per = plan.per
    at = (n * plan.xp + 2 * h) * per
    return pl.ds(at, 2 * per)


def attn_fwd_kernel(plan, lists_ref, x_ref, o_ref, s_ref, p_ref, g_ref, a_ref):
    c = LOG2E * HD**-0.5
    hp, count = plan.hp, plan.blocks // 2
    heads = range(hp)

    def stage_s(i, h, slot):
        kv, _ = listed(plan, x_ref, lists_ref, h, i)
        ((xa, la), (xb, lb)), _ = spots(plan, h, i)
        s_ref[slot, h] = dot(kv, diag(low(x_ref[xa, :, la]), low(x_ref[xb, :, lb])), NT)

    def stage_p(h, slot):
        s = s_ref[slot, h]
        m = jnp.max(s, 0, keepdims=True)
        e = jnp.exp2(s * c - m * c)
        inv = 1.0 / jnp.sum(e, 0, keepdims=True)
        p_ref[slot, h] = (e * inv).astype(BF)

    def stage_c(i, h, slot):
        kv, _ = listed(plan, x_ref, lists_ref, h, i)
        _, ((ca, la), (cb, lb)) = spots(plan, h, i)
        ctx = dot(p_ref[slot, h], kv, TN)
        o_ref[ca, :, la] = ctx[:BLK, HD:WIDE].astype(BF)
        o_ref[cb, :, lb] = ctx[BLK:, WIDE + HD :].astype(BF)

    p_ref[...] = jnp.zeros_like(p_ref)
    run_pairs(count, hp, stage_s, stage_p, stage_c)
    size = plan.rows
    steps = plan.groups * plan.chunks
    ws, outs = [], []
    for h in heads:
        ((xa, la), _), (c_first, _) = spots(plan, h, 0)
        (_, (xb, lb)), (_, c_last) = spots(plan, h, count - 1)
        ws.append(low(jnp.concatenate([x_ref[xa, :, la], x_ref[xb, :, lb]], 0)))
        outs.append((c_first, c_last))

    def chunk(n):
        return pl.ds(pl.multiple_of(n * size, size), size)

    def keys(h, n):
        return x_ref[keys_of(plan, x_ref, h, n)].reshape(size, WIDE)

    def one(n, ms):
        out = []
        for h in heads:
            s = dot(keys(h, n), ws[h], NT)
            g_ref[h, chunk(n), :] = s
            out.append(jnp.maximum(ms[h], jnp.max(s, 0, keepdims=True)))
        return tuple(out)

    ms = lax.fori_loop(
        0, steps, one, tuple(jnp.full((1, 2 * BLK), -jnp.inf, F32) for h in heads), unroll=2
    )

    def two(n, ls):
        out = []
        for h in heads:
            e = jnp.exp2(g_ref[h, chunk(n), :] * c - ms[h] * c)
            g_ref[h, chunk(n), :] = e
            out.append(ls[h] + jnp.sum(e, 0, keepdims=True))
        return tuple(out)

    ls = lax.fori_loop(0, steps, two, tuple(jnp.zeros((1, 2 * BLK), F32) for h in heads), unroll=2)
    invs = [1.0 / l for l in ls]
    a_ref[...] = jnp.zeros_like(a_ref)

    def three(n, carry):
        for h in heads:
            p = g_ref[h, chunk(n), :] * invs[h]
            hi = p.astype(BF)
            lo = (p - hi.astype(F32)).astype(BF)
            a_ref[h] += dot(jnp.concatenate([hi, lo], 1), keys(h, n), TN)
        return carry

    lax.fori_loop(0, steps, three, 0, unroll=2)
    for h in heads:
        ctx = (a_ref[h, : 2 * BLK, :] + a_ref[h, 2 * BLK :, :])[:, HD:].astype(BF)
        (ca, la), (cb, lb) = outs[h]
        o_ref[ca, :, la] = ctx[:BLK]
        o_ref[cb, :, lb] = ctx[BLK:]


def attn_fwd(plan, lists, x):
    flat = x.reshape(-1, BLK, WIDE)
    blocks = plan.groups * plan.chunks * plan.cp * plan.per
    keys = plan.blocks * BLK
    return pl.pallas_call(
        partial(attn_fwd_kernel, plan),
        out_shape=jax.ShapeDtypeStruct((blocks, BLK, WIDE), BF),
        in_specs=[pl.BlockSpec(memory_space=pltpu.SMEM), pl.BlockSpec(memory_space=VMEM)],
        out_specs=pl.BlockSpec(memory_space=VMEM),
        scratch_shapes=[
            VMEM((2, plan.hp, KEYS, 2 * BLK), F32),
            VMEM((2, plan.hp, KEYS, 2 * BLK), BF),
            VMEM((plan.hp, keys, 2 * BLK), F32),
            VMEM((plan.hp, 4 * BLK, WIDE), F32),
        ],
        compiler_params=pltpu.CompilerParams(vmem_limit_bytes=48 << 20),
        cost_estimate=pl.CostEstimate(flops=26 * 10**9, bytes_accessed=6 * 10**6, transcendentals=6 * 10**6),
        name="attn_fwd",
    )(lists, flat).reshape(plan.c_shape())


def attn_bwd_kernel(plan, lists_ref, x_ref, d_ref, o_ref, acc_ref, s_ref, p_ref, g_ref):
    scale = HD**-0.5
    c = LOG2E * scale
    hp, count = plan.hp, plan.blocks // 2
    heads = range(hp)
    acc_ref[...] = jnp.zeros_like(acc_ref)

    def weights(i, h):
        ((xa, xla), (xb, xlb)), ((ca, cla), (cb, clb)) = spots(plan, h, i)
        da, db = d_ref[ca, :, cla], d_ref[cb, :, clb]
        da = jnp.where(i == 0, jnp.zeros_like(da), da)
        db = jnp.where(i == count - 1, jnp.zeros_like(db), db)
        return jnp.concatenate(
            [diag(low(x_ref[xa, :, xla]), low(x_ref[xb, :, xlb])), diag(high(da), high(db))], 0
        )

    def stage_s(i, h, slot):
        kv, _ = listed(plan, x_ref, lists_ref, h, i)
        s_ref[slot, h] = dot(kv, weights(i, h), NT)

    def stage_p(h, slot):
        s = s_ref[slot, h, :, : 2 * BLK]
        g = s_ref[slot, h, :, 2 * BLK :]
        m = jnp.max(s, 0, keepdims=True)
        e = jnp.exp2(s * c - m * c)
        inv = 1.0 / jnp.sum(e, 0, keepdims=True)
        delta = jnp.sum(e * g, 0, keepdims=True) * inv
        p = e * inv
        p_ref[slot, h, :, : 2 * BLK] = (p * (g - delta)).astype(BF)
        p_ref[slot, h, :, 2 * BLK :] = p.astype(BF)

    def stage_c(i, h, slot):
        kv, places = listed(plan, x_ref, lists_ref, h, i)
        ((xa, la), (xb, lb)), _ = spots(plan, h, i)
        dq = dot(p_ref[slot, h, :, : 2 * BLK], kv, TN) * scale
        o_ref[xa, :, la] = dq[:BLK, :HD].astype(BF)
        o_ref[xb, :, lb] = dq[BLK:, WIDE : WIDE + HD].astype(BF)
        dkv = dot(p_ref[slot, h], weights(i, h), NN)
        for side in range(2):
            part = dkv[:, side * WIDE : (side + 1) * WIDE]
            for n in range(LISTED):
                acc_ref[places[side][n]] += part[n * BLK : (n + 1) * BLK]

    p_ref[...] = jnp.zeros_like(p_ref)
    run_pairs(count, hp, stage_s, stage_p, stage_c)
    lane_scale = jnp.where(
        lax.broadcasted_iota(jnp.int32, (1, WIDE), 1) < HD, scale, 1.0
    ).astype(F32)
    size = plan.rows
    steps = plan.groups * plan.chunks

    def chunk(n):
        return pl.ds(pl.multiple_of(n * size, size), size)

    for h in heads:
        ((xa, xla), _), ((ca, cla), _) = spots(plan, h, 0)
        (_, (xb, xlb)), (_, (cb, clb)) = spots(plan, h, count - 1)
        q = low(jnp.concatenate([x_ref[xa, :, xla], x_ref[xb, :, xlb]], 0))
        d = high(jnp.concatenate([d_ref[ca, :, cla], d_ref[cb, :, clb]], 0))
        w = jnp.concatenate([q, d], 0)
        three_w = jnp.concatenate([q, d, d], 0)

        def keys(n):
            return x_ref[keys_of(plan, x_ref, h, n)].reshape(size, WIDE)

        def one(n, m):
            s = dot(keys(n), w, NT)
            g_ref[chunk(n), :] = s
            return jnp.maximum(m, jnp.max(s[:, : 2 * BLK], 0, keepdims=True))

        m = lax.fori_loop(0, steps, one, jnp.full((1, 2 * BLK), -jnp.inf, F32), unroll=4)

        def two(n, state):
            l, eg = state
            e = jnp.exp2(g_ref[chunk(n), : 2 * BLK] * c - m * c)
            g_ref[chunk(n), : 2 * BLK] = e
            return (
                l + jnp.sum(e, 0, keepdims=True),
                eg + jnp.sum(e * g_ref[chunk(n), 2 * BLK :], 0, keepdims=True),
            )

        l, eg = lax.fori_loop(0, steps, two, (jnp.zeros((1, 2 * BLK), F32),) * 2, unroll=4)
        inv = 1.0 / l
        delta = eg * inv

        def three(n, dq):
            p = g_ref[chunk(n), : 2 * BLK] * inv
            ds = (p * (g_ref[chunk(n), 2 * BLK :] - delta)).astype(BF)
            hi = p.astype(BF)
            lo = (p - hi.astype(F32)).astype(BF)
            dkv = dot(jnp.concatenate([ds, hi, lo], 1), three_w, NN)
            where = keys_of(plan, x_ref, h, n)
            total = acc_ref[where].reshape(size, WIDE) + dkv
            o_ref[where] = (total * lane_scale).astype(BF).reshape(2 * plan.per, BLK, WIDE)
            return dq + dot(ds, keys(n), TN)

        dq = lax.fori_loop(0, steps, three, jnp.zeros((2 * BLK, WIDE), F32), unroll=4)
        dq = (dq[:, :HD] * scale).astype(BF)
        o_ref[xa, :, xla] = dq[:BLK]
        o_ref[xb, :, xlb] = dq[BLK:]


def attn_bwd(plan, lists, x, d):
    flat = x.reshape(-1, BLK, WIDE)
    keys = plan.blocks * BLK
    return pl.pallas_call(
        partial(attn_bwd_kernel, plan),
        out_shape=jax.ShapeDtypeStruct(flat.shape, BF),
        in_specs=[pl.BlockSpec(memory_space=pltpu.SMEM)] + [pl.BlockSpec(memory_space=VMEM)] * 2,
        out_specs=pl.BlockSpec(memory_space=VMEM),
        scratch_shapes=[
            VMEM(flat.shape, F32),
            VMEM((2, plan.hp, KEYS, 4 * BLK), F32),
            VMEM((2, plan.hp, KEYS, 4 * BLK), BF),
            VMEM((keys, 4 * BLK), F32),
        ],
        compiler_params=pltpu.CompilerParams(vmem_limit_bytes=56 << 20),
        cost_estimate=pl.CostEstimate(flops=46 * 10**9, bytes_accessed=12 * 10**6, transcendentals=6 * 10**6),
        name="attn_bwd",
    )(lists, flat, d.reshape(-1, BLK, WIDE)).reshape(plan.x_shape())


def mean(v):
    return jnp.sum(v, -1, keepdims=True) * (1.0 / v.shape[-1])


def normalise(resid):
    centre = resid - mean(resid)
    inv = lax.rsqrt(mean(centre * centre) + epsilon)
    return centre * inv, inv


def norm_back(unit, inv, gain, grad):
    g = grad * gain
    return inv * (g - mean(g) - unit * mean(g * unit))


def gelu_parts(u):
    k = 0.7978845608028654
    sq = u * u
    t = jnp.tanh(k * (u + 0.044715 * (u * sq)))
    half = 0.5 * (1.0 + t)
    return half * u, half + 0.5 * u * (1.0 - t * t) * (k + (3 * 0.044715 * k) * sq)


def rows_of(ref):
    return ref[...].reshape(-1, ref.shape[-1])


def pick_context(plan, pieces):
    half = plan.half
    tiles = []
    for g in range(plan.groups):
        for p in range(plan.pairs):
            tiles.append(pieces[g, 2 * p : 2 * p + 2].reshape(plan.rows, WIDE))
        if plan.odd:
            both = pieces[g, 2 * plan.pairs].reshape(half, WIDE)
            tiles.append(jnp.concatenate([both[:, :HD], both[:, HD:]], 0))
    return jnp.concatenate(tiles, 1)[:, :D]


def put_context(plan, value, ref):
    half, per = plan.half, plan.per
    if plan.ctx > D:
        value = jnp.concatenate([value, jnp.zeros((value.shape[0], plan.ctx - D), value.dtype)], 1)
    for g in range(plan.groups):
        at = g * plan.hp * HD
        for p in range(plan.pairs):
            ref[g, 2 * p : 2 * p + 2] = value[:, at : at + WIDE].reshape(2, per, BLK, WIDE)
            at += WIDE
        if plan.odd:
            one = value[:, at : at + HD]
            ref[g, 2 * plan.pairs] = jnp.concatenate([one[:half], one[half:]], 1).reshape(per, BLK, WIDE)


def put_heads(plan, value, ref):
    half, per, hp = plan.half, plan.per, plan.hp
    pairs_at = plan.groups * hp * WIDE
    single_at = pairs_at + plan.groups * plan.pairs * WIDE
    for g in range(plan.groups):
        for h in range(hp):
            at = (g * hp + h) * WIDE
            ref[g, 2 * h : 2 * h + 2] = value[:, at : at + WIDE].reshape(2, per, BLK, WIDE)
        for p in range(plan.pairs):
            at = pairs_at + (g * plan.pairs + p) * WIDE
            ref[g, 2 * hp + 2 * p : 2 * hp + 2 * p + 2] = value[:, at : at + WIDE].reshape(2, per, BLK, WIDE)
        if plan.odd:
            at = single_at + g * HD
            one = value[:, at : at + HD]
            ref[g, plan.xp - 1] = jnp.concatenate([one[:half], one[half:]], 1).reshape(per, BLK, WIDE)


def pick_heads(plan, pieces):
    half, hp = plan.half, plan.hp
    kv, pairs, singles = [], [], []
    for g in range(pieces.shape[0]):
        for h in range(hp):
            kv.append(pieces[g, 2 * h : 2 * h + 2].reshape(plan.rows, WIDE))
        for p in range(plan.pairs):
            pairs.append(pieces[g, 2 * hp + 2 * p : 2 * hp + 2 * p + 2].reshape(plan.rows, WIDE))
        if plan.odd:
            both = pieces[g, plan.xp - 1].reshape(half, WIDE)
            singles.append(jnp.concatenate([both[:, :HD], both[:, HD:]], 0))
    return jnp.concatenate(kv + pairs + singles, 1)


def whole(shape):
    return pl.BlockSpec(shape, lambda *i: (0,) * len(shape), pipeline_mode=pl.Buffered(1))


def own_kernel(plan, a_ref, w_ref, b_ref, o_ref):
    a = a_ref[...].reshape(plan.rows, D)
    y = (dot(a, rows_of(w_ref), NN) + b_ref[...]).astype(BF)
    one = Plan.__new__(Plan)
    one.__dict__.update(plan.__dict__)
    one.groups = 1
    put_heads(one, y, o_ref.at[:, 0])


def own_heads(plan, hidden_all, weight, bias):
    a = hidden_all.reshape(plan.groups, 2, plan.chunks, plan.half, D)
    return pl.pallas_call(
        partial(own_kernel, plan),
        out_shape=jax.ShapeDtypeStruct(plan.x_shape(), BF),
        grid=(plan.groups, plan.chunks),
        in_specs=[
            pl.BlockSpec((1, 2, 1, plan.half, D), lambda g, c: (g, 0, c, 0, 0)),
            whole(weight.shape),
            whole(bias.shape),
        ],
        out_specs=pl.BlockSpec((1, 1) + plan.x_shape()[2:], lambda g, c: (g, c, 0, 0, 0, 0)),
        compiler_params=pltpu.CompilerParams(vmem_limit_bytes=48 << 20),
        cost_estimate=pl.CostEstimate(flops=7 * 10**9, bytes_accessed=12 * 10**6, transcendentals=0),
        name="own_heads",
    )(a, weight, bias)


def own_grad_kernel(plan, item, steps, a_ref, d_ref, o_ref, acc_ref, sum_ref):
    n = pl.program_id(0) * plan.chunks + pl.program_id(1)

    @pl.when(n == 0)
    def _():
        acc_ref[...] = jnp.zeros_like(acc_ref)
        sum_ref[...] = jnp.zeros_like(sum_ref)

    d = pick_heads(plan, d_ref[:, 0])
    acc_ref[...] += dot(a_ref[...].reshape(plan.rows, D), d, TN)
    sum_ref[...] += jnp.sum(d.astype(F32).reshape(-1, 8, d.shape[1]), 0)

    @pl.when(n == steps - 1)
    def _():
        share = D // item
        total = jnp.broadcast_to(jnp.sum(sum_ref[...], 0, keepdims=True), (16, sum_ref.shape[1])).astype(BF)
        for r in range(item):
            o_ref[r, :share] = acc_ref[r * share : (r + 1) * share].astype(BF)
            o_ref[r, share:] = total


def own_grad(plan, item, hidden_all, dx):
    a = hidden_all.reshape(plan.groups, 2, plan.chunks, plan.half, D)
    return pl.pallas_call(
        partial(own_grad_kernel, plan, item, plan.groups * plan.chunks),
        out_shape=jax.ShapeDtypeStruct((item, D // item + 16, plan.own), BF),
        grid=(plan.groups, plan.chunks),
        in_specs=[
            pl.BlockSpec((1, 2, 1, plan.half, D), lambda g, c: (g, 0, c, 0, 0)),
            pl.BlockSpec((1, 1) + plan.x_shape()[2:], lambda g, c: (g, c, 0, 0, 0, 0)),
        ],
        out_specs=whole((item, D // item + 16, plan.own)),
        scratch_shapes=[VMEM((D, plan.own), F32), VMEM((8, plan.own), F32)],
        compiler_params=pltpu.CompilerParams(vmem_limit_bytes=48 << 20),
        cost_estimate=pl.CostEstimate(flops=7 * 10**9, bytes_accessed=12 * 10**6, transcendentals=0),
        name="own_grad",
    )(a, dx)


def halves(plan, width):
    return pl.BlockSpec((2, plan.half, width), lambda c: (0, c, 0))


def cut(plan, v):
    return v.reshape(2, plan.tokens // 2, v.shape[-1])


def read(ref):
    return ref[...].reshape(-1, ref.shape[-1])


def write(ref, value):
    ref[...] = value.reshape(ref.shape).astype(ref.dtype)


class Packed:
    def __init__(self, ref, ff):
        self.ref = ref
        self.item = ref.shape[0]
        self.share = D // self.item
        self.parts = ff // D

    def rows(self, first):
        return self.ref[:, first : first + self.share].reshape(D, D)

    def out(self):
        return self.rows(0)

    def ffn_in(self, n):
        return self.rows(self.share * (1 + n))

    def ffn_out(self, n):
        ranks = self.item // self.parts
        first = self.share * (1 + self.parts)
        return self.ref[n * ranks : (n + 1) * ranks, first : first + self.share * self.parts].reshape(D, D)

    def columns(self, n):
        return self.rows(self.share * (1 + 2 * self.parts + n))


def wide_parts(w):
    return jnp.concatenate([w[:, n : n + D] for n in range(0, w.shape[1], D)])


OUT_BIAS, GAIN1, SHIFT1, FFN_BIAS, GAIN2, SHIFT2 = range(6)


def first_half(plan, ctx, h, w, vec_ref):
    r1 = h + dot(ctx, w.out(), NN) + vec_ref[OUT_BIAS : OUT_BIAS + 1]
    unit1, inv1 = normalise(r1)
    y1 = unit1 * vec_ref[GAIN1 : GAIN1 + 1] + vec_ref[SHIFT1 : SHIFT1 + 1]
    return r1, unit1, inv1, y1, y1.astype(BF)


def part_of(n):
    return slice(n * D, (n + 1) * D)


def put(ref, n, value):
    ref[:, :, part_of(n)] = value.reshape(ref.shape[:2] + (D,)).astype(ref.dtype)


def get(ref, n):
    return ref[:, :, part_of(n)].reshape(-1, D)


def fwd_kernel(plan, ff, c_ref, h_ref, w_ref, vec_ref, inner_ref, bias_ref,
               x_ref, next_ref, next_low_ref, r1_ref, r2_ref, u_ref, y_ref, ctx_ref):
    w = Packed(w_ref, ff)
    ctx = pick_context(plan, c_ref[:, 0])
    write(ctx_ref, ctx)
    r1, _, _, y1, y1_low = first_half(plan, ctx, read(h_ref), w, vec_ref)
    write(r1_ref, r1)
    write(y_ref, y1_low)
    r2 = y1 + vec_ref[FFN_BIAS : FFN_BIAS + 1]
    for n in range(w.parts):
        u = dot(y1_low, w.ffn_in(n), NN) + inner_ref[:, part_of(n)]
        put(u_ref, n, u)
        r2 = r2 + dot(gelu_parts(u)[0].astype(BF), w.ffn_out(n), NN)
    write(r2_ref, r2)
    unit2, _ = normalise(r2)
    nxt = unit2 * vec_ref[GAIN2 : GAIN2 + 1] + vec_ref[SHIFT2 : SHIFT2 + 1]
    low_ = nxt.astype(BF)
    write(next_ref, nxt)
    write(next_low_ref, low_)
    y = [
        (dot(low_, w.columns(n), NN) + bias_ref[:, part_of(n)]).astype(BF) for n in range(plan.cols // D)
    ]
    put_heads(plan, jnp.concatenate(y, 1), x_ref.at[:, 0])


def piece_spec(shape):
    return pl.BlockSpec((shape[0], 1) + shape[2:], lambda c: (0, c, 0, 0, 0, 0))


def layer_fwd(plan, ctx, h, packed, vec, inner, bias):
    t = (2, plan.tokens // 2)
    ff = inner.shape[-1]
    shapes = [(D, F32), (D, BF), (D, F32), (D, F32), (ff, F32), (D, BF), (D, BF)]
    return pl.pallas_call(
        partial(fwd_kernel, plan, ff),
        out_shape=[jax.ShapeDtypeStruct(plan.x_shape(), BF)] + [jax.ShapeDtypeStruct(t + (n,), d) for n, d in shapes],
        grid=(plan.chunks,),
        in_specs=[piece_spec(plan.c_shape()), halves(plan, D)]
        + [whole(w.shape) for w in (packed, vec, inner, bias)],
        out_specs=[piece_spec(plan.x_shape())] + [halves(plan, n) for n, _ in shapes],
        compiler_params=pltpu.CompilerParams(vmem_limit_bytes=60 << 20),
        cost_estimate=pl.CostEstimate(flops=30 * 10**9, bytes_accessed=50 * 10**6, transcendentals=3 * 10**6),
        name="layer_fwd",
    )(ctx, cut(plan, h), packed, vec, inner, bias)


SUM_DO, D_GAIN1, D_SHIFT1, SUM_DF, D_GAIN2, D_SHIFT2 = range(6)


def add_sums(ref, at, value):
    ref[at] += jnp.sum(value.reshape(-1, 8, value.shape[-1]), 0)


def back_chunk(plan, gy, unit1, inv1, unit2, inv2, gate, w, vec_ref, sums_ref, inner_sum_ref, du_ref):
    @pl.when(pl.program_id(0) == 0)
    def _():
        sums_ref[...] = jnp.zeros_like(sums_ref)
        inner_sum_ref[...] = jnp.zeros_like(inner_sum_ref)

    dr2 = norm_back(unit2, inv2, vec_ref[GAIN2 : GAIN2 + 1], gy)
    df = dr2.astype(BF)
    dy1 = dr2
    for n in range(w.parts):
        du = (dot(df, w.ffn_out(n), NT) * gate(n)).astype(BF)
        put(du_ref, n, du)
        dy1 = dy1 + dot(du, w.ffn_in(n), NT)
        inner_sum_ref[:, part_of(n)] += jnp.sum(du.astype(F32).reshape(-1, 8, D), 0)
    dr1 = norm_back(unit1, inv1, vec_ref[GAIN1 : GAIN1 + 1], dy1)
    do = dr1.astype(BF)
    dc = dot(do, w.out(), NT).astype(BF)
    add_sums(sums_ref, SUM_DO, do.astype(F32))
    add_sums(sums_ref, D_GAIN1, dy1 * unit1)
    add_sums(sums_ref, D_SHIFT1, dy1)
    add_sums(sums_ref, SUM_DF, df.astype(F32))
    add_sums(sums_ref, D_GAIN2, gy * unit2)
    add_sums(sums_ref, D_SHIFT2, gy)
    return df, dr1, do, dc


def mid_kernel(plan, ff, c_ref, h_ref, gy_ref, w_ref, vec_ref, inner_ref,
               d_ref, out_ref, dr1_ref, gz_ref, du_ref, df_ref, do_ref, y_ref, ctx_ref, sums_ref, inner_sum_ref, gate_ref):
    w = Packed(w_ref, ff)
    ctx = pick_context(plan, c_ref[:, 0])
    write(ctx_ref, ctx)
    _, unit1, inv1, y1, y1_low = first_half(plan, ctx, read(h_ref), w, vec_ref)
    write(y_ref, y1_low)
    r2 = y1 + vec_ref[FFN_BIAS : FFN_BIAS + 1]
    for n in range(w.parts):
        u = dot(y1_low, w.ffn_in(n), NN) + inner_ref[:, part_of(n)]
        gz, gate_ref[n] = gelu_parts(u)
        gz = gz.astype(BF)
        put(gz_ref, n, gz)
        r2 = r2 + dot(gz, w.ffn_out(n), NN)
    unit2, inv2 = normalise(r2)
    write(out_ref, unit2 * vec_ref[GAIN2 : GAIN2 + 1] + vec_ref[SHIFT2 : SHIFT2 + 1])
    df, dr1, do, dc = back_chunk(plan, read(gy_ref), unit1, inv1, unit2, inv2, lambda n: gate_ref[n],
                                 w, vec_ref, sums_ref, inner_sum_ref, du_ref)
    put_context(plan, dc, d_ref.at[:, 0])
    write(dr1_ref, dr1)
    write(df_ref, df)
    write(do_ref, do)


def sum_specs(ff):
    return (
        [jax.ShapeDtypeStruct((6, 8, D), F32), jax.ShapeDtypeStruct((8, ff), F32)],
        [pl.BlockSpec((6, 8, D), lambda c: (0, 0, 0)), pl.BlockSpec((8, ff), lambda c: (0, 0))],
    )


def layer_mid(plan, ctx, h, gy, packed, vec, inner):
    t = (2, plan.tokens // 2)
    ff = inner.shape[-1]
    shapes = [(D, F32), (D, F32), (ff, BF), (ff, BF), (D, BF), (D, BF), (D, BF), (D, BF)]
    sums, sums_at = sum_specs(ff)
    return pl.pallas_call(
        partial(mid_kernel, plan, ff),
        out_shape=[jax.ShapeDtypeStruct(plan.c_shape(), BF)] + [jax.ShapeDtypeStruct(t + (n,), d) for n, d in shapes] + sums,
        grid=(plan.chunks,),
        in_specs=[piece_spec(plan.c_shape()), halves(plan, D), halves(plan, D)]
        + [whole(w.shape) for w in (packed, vec, inner)],
        out_specs=[piece_spec(plan.c_shape())] + [halves(plan, n) for n, _ in shapes] + sums_at,
        scratch_shapes=[VMEM((ff // D, plan.rows, D), F32)],
        compiler_params=pltpu.CompilerParams(vmem_limit_bytes=60 << 20),
        cost_estimate=pl.CostEstimate(flops=45 * 10**9, bytes_accessed=50 * 10**6, transcendentals=3 * 10**6),
        name="layer_mid",
    )(ctx, cut(plan, h), cut(plan, gy), packed, vec, inner)


def bwd_kernel(plan, ff, dx_ref, up_ref, r1_ref, r2_ref, u_ref, w_ref, vec_ref,
               d_ref, dr1_ref, gz_ref, du_ref, df_ref, do_ref, dqkv_ref, sums_ref, inner_sum_ref, qkv_sum_ref):
    w = Packed(w_ref, ff)
    dqkv = pick_heads(plan, dx_ref[:, 0])
    write(dqkv_ref, dqkv)
    gy = read(up_ref)
    for n in range(plan.cols // D):
        gy = gy + dot(dqkv[:, part_of(n)], w.columns(n), NT)

    @pl.when(pl.program_id(0) == 0)
    def _():
        qkv_sum_ref[...] = jnp.zeros_like(qkv_sum_ref)

    qkv_sum_ref[...] += jnp.sum(dqkv.astype(F32).reshape(-1, 8, dqkv.shape[-1]), 0)
    unit1, inv1 = normalise(read(r1_ref))
    unit2, inv2 = normalise(read(r2_ref))

    def gate(n):
        gz, value = gelu_parts(get(u_ref, n))
        put(gz_ref, n, gz)
        return value

    df, dr1, do, dc = back_chunk(plan, gy, unit1, inv1, unit2, inv2, gate, w, vec_ref, sums_ref, inner_sum_ref, du_ref)
    put_context(plan, dc, d_ref.at[:, 0])
    write(dr1_ref, dr1)
    write(df_ref, df)
    write(do_ref, do)


def layer_bwd(plan, dx, up, r1, r2, u, packed, vec):
    t = (2, plan.tokens // 2)
    ff = u.shape[-1]
    shapes = [(D, F32), (ff, BF), (ff, BF), (D, BF), (D, BF), (plan.cols, BF)]
    sums, sums_at = sum_specs(ff)
    sums = sums + [jax.ShapeDtypeStruct((8, plan.cols), F32)]
    sums_at = sums_at + [pl.BlockSpec((8, plan.cols), lambda c: (0, 0))]
    return pl.pallas_call(
        partial(bwd_kernel, plan, ff),
        out_shape=[jax.ShapeDtypeStruct(plan.c_shape(), BF)] + [jax.ShapeDtypeStruct(t + (n,), d) for n, d in shapes] + sums,
        grid=(plan.chunks,),
        in_specs=[piece_spec(plan.x_shape()), halves(plan, D), halves(plan, D), halves(plan, D), halves(plan, ff)]
        + [whole(w.shape) for w in (packed, vec)],
        out_specs=[piece_spec(plan.c_shape())] + [halves(plan, n) for n, _ in shapes] + sums_at,
        compiler_params=pltpu.CompilerParams(vmem_limit_bytes=60 << 20),
        cost_estimate=pl.CostEstimate(flops=40 * 10**9, bytes_accessed=50 * 10**6, transcendentals=3 * 10**6),
        name="layer_bwd",
    )(dx, up, r1, r2, u, packed, vec)


def dense_grad_kernel(item, gz_ref, df_ref, y_ref, du_ref, ctx_ref, do_ref, vec_ref, fo_ref, rest_ref):
    n = pl.program_id(0)
    parts = pl.num_programs(0)
    share = D // item
    ranks = item // parts
    fo_ref[...] = dot(gz_ref[...], df_ref[...], TN).astype(BF).reshape(fo_ref.shape)
    first = pl.multiple_of(n * share, 16)
    rest_ref[:, pl.ds(first, share)] = dot(y_ref[...], du_ref[...], TN).astype(BF).reshape(item, share, D)

    @pl.when(n == parts - 1)
    def _():
        at = parts * share
        rest_ref[:, at : at + share] = dot(ctx_ref[...], do_ref[...], TN).astype(BF).reshape(item, share, D)
        rest_ref[:, at + share :] = vec_ref[...]


def dense_grads(item, gz, df, y, du, ctx, do, vecs):
    tokens, ff = gz.shape
    parts = ff // D
    share = D // item
    rest = parts * share + share + vecs.shape[1]
    column = pl.BlockSpec((tokens, D), lambda n: (0, n))
    return pl.pallas_call(
        partial(dense_grad_kernel, item),
        out_shape=[jax.ShapeDtypeStruct((item, ff // item, D), BF), jax.ShapeDtypeStruct((item, rest, D), BF)],
        grid=(parts,),
        in_specs=[column, whole(df.shape), whole(y.shape), column, whole(ctx.shape), whole(do.shape), whole(vecs.shape)],
        out_specs=[pl.BlockSpec((item // parts, ff // item, D), lambda n: (n, 0, 0)), whole((item, rest, D))],
        compiler_params=pltpu.CompilerParams(vmem_limit_bytes=56 << 20),
        cost_estimate=pl.CostEstimate(flops=14 * 10**9, bytes_accessed=30 * 10**6, transcendentals=0),
        name="dense_grads",
    )(gz, df, y, du, ctx, do, vecs)


def column_grad_kernel(item, a_ref, d_ref, vec_ref, o_ref):
    n = pl.program_id(0)
    share = D // item
    first = pl.multiple_of(n * share, 16)
    o_ref[:, pl.ds(first, share)] = dot(a_ref[...], d_ref[...], TN).astype(BF).reshape(item, share, D)

    @pl.when(n == pl.num_programs(0) - 1)
    def _():
        o_ref[:, o_ref.shape[1] - vec_ref.shape[1] :] = vec_ref[...]


def column_grads(item, a, d, vecs):
    tokens = a.shape[0]
    parts = d.shape[1] // D
    out = (item, parts * (D // item) + vecs.shape[1], D)
    return pl.pallas_call(
        partial(column_grad_kernel, item),
        out_shape=jax.ShapeDtypeStruct(out, BF),
        grid=(parts,),
        in_specs=[whole(a.shape), pl.BlockSpec((tokens, D), lambda n: (0, n)), whole(vecs.shape)],
        out_specs=whole(out),
        compiler_params=pltpu.CompilerParams(vmem_limit_bytes=48 << 20),
        cost_estimate=pl.CostEstimate(flops=6 * 10**9, bytes_accessed=10 * 10**6, transcendentals=0),
        name="column_grads",
    )(a, d, vecs)


def tail_kernel(plan, dx_ref, up_ref, w_ref, o_ref):
    dqkv = pick_heads(plan, dx_ref[:, 0])
    share = D // w_ref.shape[0]
    out = read(up_ref)
    for n in range(plan.cols // D):
        out = out + dot(dqkv[:, part_of(n)], w_ref[:, n * share : (n + 1) * share].reshape(D, D), NT)
    write(o_ref, out)


def layer_tail(plan, dx, up, w_qkv):
    return pl.pallas_call(
        partial(tail_kernel, plan),
        out_shape=jax.ShapeDtypeStruct(up.shape, F32),
        grid=(plan.chunks,),
        in_specs=[piece_spec(plan.x_shape()), halves(plan, D), whole(w_qkv.shape)],
        out_specs=halves(plan, D),
        compiler_params=pltpu.CompilerParams(vmem_limit_bytes=48 << 20),
        cost_estimate=pl.CostEstimate(flops=8 * 10**9, bytes_accessed=12 * 10**6, transcendentals=0),
        name="layer_tail",
    )(dx, up, w_qkv)


def column_parts(plan, w):
    lead = w.shape[:-1]
    g, hp = plan.groups, plan.hp
    w = w.reshape(lead + (3, H, HD))
    w = jnp.pad(w, [(0, 0)] * (len(lead) + 1) + [(0, g * hp - H), (0, 0)])
    q, k, v = (w[..., n, :, :] for n in range(3))
    kv = jnp.stack([k, v], -2).reshape(lead + (g, hp * WIDE))
    q = q.reshape(lead + (g, hp, HD))
    pairs = q[..., : 2 * plan.pairs, :].reshape(lead + (g, plan.pairs * WIDE))
    last = q[..., 2 * plan.pairs :, :].reshape(lead + (g, plan.odd * HD))
    return kv, pairs, last


def all_columns(plan, w):
    lead = w.shape[:-1]
    return jnp.concatenate([p.reshape(lead + (-1,)) for p in column_parts(plan, w)], -1)


def own_columns(plan, w, rank):
    axis = w.ndim - 1
    return jnp.concatenate(
        [lax.dynamic_index_in_dim(p, rank, axis, False) for p in column_parts(plan, w)], -1
    )


def natural(plan, kv, pairs, last):
    lead = kv.shape[:-2]
    g, hp = plan.groups, plan.hp
    kv = kv.reshape(lead + (g * hp, 2, HD))
    q = jnp.concatenate(
        [pairs.reshape(lead + (g, 2 * plan.pairs, HD)), last.reshape(lead + (g, plan.odd, HD))], -2
    ).reshape(lead + (g * hp, HD))
    return jnp.concatenate(
        [p[..., :H, :].reshape(lead + (H * HD,)) for p in (q, kv[..., 0, :], kv[..., 1, :])], -1
    )


def from_all(plan, w):
    lead = w.shape[:-1]
    a = plan.groups * plan.hp * WIDE
    b = a + plan.groups * plan.pairs * WIDE
    return natural(plan, *(p.reshape(lead + (plan.groups, -1)) for p in (w[..., :a], w[..., a:b], w[..., b:])))


def from_own(plan, w):
    a = plan.hp * WIDE
    b = a + plan.pairs * WIDE
    w = jnp.moveaxis(w, 0, -2)
    return natural(plan, w[..., :a], w[..., a:b], w[..., b:])


def exchange(x):
    y = x.reshape((x.shape[0], -1, x.shape[-1]))
    return lax.all_to_all(y, "seq", split_axis=0, concat_axis=0, tiled=True).reshape(x.shape)


def tie(*args):
    return lax.optimization_barrier(args)


def key_table(plan, random_ids):
    n = plan.blocks
    here = n // plan.groups
    j = jnp.arange(n, dtype=jnp.int32)
    shared = jnp.stack(
        [jnp.maximum(j - 1, 0), j, jnp.minimum(j + 1, n - 1), jnp.zeros_like(j), jnp.full_like(j, n - 1)], 1
    )
    ids = jnp.concatenate([jnp.broadcast_to(shared[None], (plan.hp, n, 5)), random_ids], 2)
    inside = ids % here
    r = inside % (here // 2)
    head = jnp.arange(plan.hp, dtype=jnp.int32)[:, None, None]
    piece = 2 * head + inside // (here // 2)
    place = (((ids // here) * plan.chunks + r // plan.per) * plan.xp + piece) * plan.per + r % plan.per
    place = place.reshape(plan.hp, plan.groups, 2, here // 2, LISTED).transpose(0, 1, 3, 2, 4)
    return place.reshape(-1)


def local(
    hidden,
    block_lists,
    w_qkv,
    bias_query,
    bias_value,
    w_attn_out,
    bias_attn_out,
    norm1_gain,
    norm1_shift,
    w_ffn_in,
    bias_ffn_in,
    w_ffn_out,
    bias_ffn_out,
    norm2_gain,
    norm2_shift,
    cotangent,
):
    groups = lax.axis_size("seq")
    item = lax.axis_size("item")
    seq_rank = lax.axis_index("seq")
    item_rank = lax.axis_index("item")
    tokens = hidden.shape[1]
    plan = Plan(groups, tokens)
    here = tokens // BLK
    share = D // item
    hidden_low = hidden[0].astype(BF)
    hidden_all = exchange(jnp.broadcast_to(hidden_low[None], (groups, tokens, D)))
    hidden_all, block_lists = tie(hidden_all, block_lists)

    ids = jnp.pad(block_lists[0], ((0, 0), (0, 0), (0, groups * plan.hp - H), (0, 0)))
    ids = ids.reshape(LAYERS, here, groups, plan.hp * RAND).transpose(2, 0, 1, 3)
    ids = exchange(ids.reshape(groups, 1, -1)).reshape(groups, LAYERS, here, plan.hp, RAND)
    ids = ids.transpose(1, 3, 0, 2, 4).reshape(LAYERS, plan.hp, plan.blocks, RAND)
    tables = [key_table(plan, ids[layer]) for layer in range(LAYERS)]

    small = (bias_query, bias_value, bias_attn_out, norm1_gain, norm1_shift, bias_ffn_in, bias_ffn_out, norm2_gain, norm2_shift)
    packed = lax.all_gather(jnp.concatenate(small, 1), "item", axis=0).astype(F32)
    vectors = []
    for layer in range(LAYERS):
        at, out = 0, []
        for s in small:
            out.append(packed[:, layer, at : at + s.shape[1]].reshape(-1))
            at += s.shape[1]
        vectors.append(out)
    stacked = [jnp.stack(v[2:5] + v[6:9] + [v[2]] * 2) for v in vectors]
    inner = [v[5][None] for v in vectors]
    qkv_bias = [jnp.concatenate([v[0], jnp.zeros_like(v[0]), v[1]])[None] for v in vectors]

    own_weight = lax.all_gather(own_columns(plan, w_qkv[0], seq_rank), "item", axis=0)
    own_bias = own_columns(plan, qkv_bias[0], seq_rank)
    columns = wide_parts(all_columns(plan, w_qkv[0])), wide_parts(all_columns(plan, w_qkv[1]))

    def dense(layer):
        return [w_attn_out[layer], wide_parts(w_ffn_in[layer]), w_ffn_out[layer]]

    packed0 = lax.all_gather(jnp.concatenate(dense(0) + [columns[1]]), "item", axis=0)
    packed1 = lax.all_gather(jnp.concatenate(dense(1)), "item", axis=0)
    columns0 = lax.all_gather(columns[0], "item", axis=0)

    x0 = own_heads(plan, hidden_all, own_weight, own_bias)
    ctx0 = exchange(attn_fwd(plan, tables[0], x0))
    x1, h1, h1_low, r1, r2, u, y0, ctx0 = layer_fwd(
        plan, ctx0, hidden[0], packed0, stacked[0], inner[0], all_columns(plan, qkv_bias[1])
    )
    x1 = exchange(x1)
    ctx1 = exchange(attn_fwd(plan, tables[1], x1))
    d1, output, up1, gz1, du1, df1, do1, y1, ctx1, sums1, inner1 = layer_mid(
        plan, ctx1, h1, cotangent[0], packed1, stacked[1], inner[1]
    )

    def flat(a):
        return a.reshape(tokens, -1)

    def scattered(g):
        return lax.psum_scatter(g, "item", scatter_dimension=0, tiled=False)

    def rows_for(vecs):
        part = jnp.concatenate([v.reshape(item, -1) for v in vecs], 1)
        return jnp.pad(part, ((0, 0), (0, 16 * D - part.shape[1]))).reshape(item, 16, D).astype(BF)

    def split_rows(part, counts):
        values, at, out = part.reshape(-1), 0, []
        for n in counts:
            out.append(values[at : at + n])
            at += n
        return out

    def grads(gz, du, df, do, y, ctx, sums, inner_sum):
        sums = jnp.sum(sums, 1)
        vecs = (sums[SUM_DO], sums[D_GAIN1], sums[D_SHIFT1], jnp.sum(inner_sum, 0), sums[SUM_DF], sums[D_GAIN2], sums[D_SHIFT2])
        return dense_grads(item, flat(gz), flat(df), flat(y), flat(du), flat(ctx), flat(do), rows_for(vecs))

    def seq_parts(shares):
        rows = jnp.concatenate(shares)
        rows = jnp.pad(rows, ((0, -rows.shape[0] % (16 * groups)), (0, 0)))
        return jnp.sum(exchange(rows.reshape(groups, -1, D)).astype(F32), 0).astype(BF)

    def seq_gather(part):
        return exchange(jnp.broadcast_to(part[None], (groups,) + part.shape))

    def taken(full, shares):
        rows, at, out = full.reshape(-1, D), 0, []
        for p in shares:
            out.append(rows[at : at + p.shape[0]].astype(F32))
            at += p.shape[0]
        return out

    def unpart(rows):
        return jnp.concatenate([rows[n : n + share] for n in range(0, rows.shape[0], share)], 1)

    parts = w_ffn_in.shape[2] // D
    counts = [share] * 3 + [w_ffn_in.shape[2] // item] + [share] * 3
    dc1 = exchange(d1)
    fo1, rest1 = grads(gz1, du1, df1, do1, y1, ctx1, sums1, inner1)
    dc1, fo1, rest1 = tie(dc1, fo1, rest1)
    fo1, rest1 = scattered(fo1), scattered(rest1)
    dc1, columns0 = tie(dc1, columns0)
    dx1 = attn_bwd(plan, tables[1], x1, dc1)
    dx1 = exchange(dx1)
    dx1, fo1 = tie(dx1, fo1)
    d0, up0, gz0, du0, df0, do0, dqkv1, sums0, inner0, qkv_sum1 = layer_bwd(
        plan, dx1, up1, r1, r2, u, packed0, stacked[0]
    )
    d0, rest1 = tie(d0, rest1)
    dc0 = exchange(d0)
    bias1 = from_all(plan, jnp.sum(qkv_sum1, 0))
    qkv1 = column_grads(item, flat(h1_low), flat(dqkv1), rows_for((bias1[:D], bias1[2 * D :])))
    fo0, rest0 = grads(gz0, du0, df0, do0, y0, ctx0, sums0, inner0)
    dc0, qkv1, fo0, rest0 = tie(dc0, qkv1, fo0, rest0)
    qkv1, fo0, rest0 = scattered(qkv1), scattered(fo0), scattered(rest0)
    part1 = seq_parts([fo1, rest1])
    dx0 = attn_bwd(plan, tables[0], x0, dc0)
    dx0, qkv1, part1 = tie(dx0, qkv1, part1)
    own0 = own_grad(plan, item, hidden_all, dx0)
    dx0 = exchange(dx0)
    own0, dx0 = tie(own0, dx0)
    own0 = lax.all_to_all(own0, "item", split_axis=0, concat_axis=0, tiled=True)
    input_grad = layer_tail(plan, dx0, up0, columns0)
    input_grad, own0, fo0 = tie(input_grad, own0, fo0)
    own0 = seq_gather(jnp.sum(own0.astype(F32), 0).astype(BF)).astype(F32)
    part0 = seq_parts([qkv1, fo0])
    early, own0 = tie(jnp.concatenate([part1, part0]), own0)
    full = seq_gather(early)
    full, rest0 = tie(full, rest0)
    late = seq_gather(seq_parts([rest0]))
    outer_1, rest_1 = taken(full[:, : part1.shape[0]], [fo1, rest1])
    qkv_1, outer_0 = taken(full[:, part1.shape[0] :], [qkv1, fo0])
    (rest_0,) = taken(late, [rest0])
    qkv_0 = from_own(plan, own0[:, :-16])
    bias0 = from_own(plan, own0[:, -16])
    late0 = [lax.dynamic_slice_in_dim(bias0, part * D + item_rank * share, share) for part in (0, 2)]
    late1 = split_rows(qkv_1[-16:], [share] * 2)
    qkv_1 = from_all(plan, unpart(qkv_1[:-16]))
    inner_1, attn_1, early1 = unpart(rest_1[: parts * share]), rest_1[parts * share : -16], split_rows(rest_1[-16:], counts)
    inner_0, attn_0, early0 = unpart(rest_0[: parts * share]), rest_0[parts * share : -16], split_rows(rest_0[-16:], counts)
    vecs = [jnp.stack(pair) for pair in zip(late0 + early0, late1 + early1)]
    return (
        output.reshape(hidden.shape),
        input_grad.reshape(hidden.shape),
        jnp.stack([qkv_0, qkv_1]),
        vecs[0],
        vecs[1],
        jnp.stack([attn_0, attn_1]),
        vecs[2],
        vecs[3],
        vecs[4],
        jnp.stack([inner_0, inner_1]),
        vecs[5],
        jnp.stack([outer_0, outer_1]),
        vecs[6],
        vecs[7],
        vecs[8],
    )


def solution(mesh):
    placed = (
        P("item", "seq", None),
        P("item", None, "seq", None, None),
        P(None, "item", None),
        P(None, "item"),
        P(None, "item"),
        P(None, "item", None),
        P(None, "item"),
        P(None, "item"),
        P(None, "item"),
        P(None, "item", None),
        P(None, "item"),
        P(None, "item", None),
        P(None, "item"),
        P(None, "item"),
        P(None, "item"),
        P("item", "seq", None),
    )
    return jax.shard_map(
        local,
        mesh=mesh,
        in_specs=placed,
        out_specs=(
            P("item", "seq", None),
            P("item", "seq", None),
            P(None, "item", None),
            P(None, "item"),
            P(None, "item"),
            P(None, "item", None),
            P(None, "item"),
            P(None, "item"),
            P(None, "item"),
            P(None, "item", None),
            P(None, "item"),
            P(None, "item", None),
            P(None, "item"),
            P(None, "item"),
            P(None, "item"),
        ),
        check_vma=False,
    )
```

```python
from functools import partial

import jax
import jax.numpy as jnp
from jax import lax
from jax.experimental import pallas as pl
from jax.experimental.pallas import tpu as pltpu
from jax.sharding import PartitionSpec as P

D = 768
H = 12
HD = 64
BLK = 64
RAND = 3
LAYERS = 2
LISTED = 5 + RAND
KEYS = LISTED * BLK
WIDE = 2 * HD
F32 = jnp.float32
BF = jnp.bfloat16
LOG2E = 1.4426950408889634
epsilon = 1e-05
NT = (((1,), (1,)), ((), ()))
TN = (((0,), (0,)), ((), ()))
NN = (((1,), (0,)), ((), ()))
VMEM = pltpu.VMEM


def dot(a, b, dims):
    return lax.dot_general(a, b, dims, preferred_element_type=F32)


class Plan:
    def __init__(self, groups, tokens, half=128):
        self.groups = groups
        self.tokens = tokens
        self.hp = -(-H // groups)
        self.pairs = self.hp // 2
        self.odd = self.hp % 2
        self.half = min(half, tokens // 2)
        self.chunks = tokens // 2 // self.half
        self.per = self.half // BLK
        self.rows = 2 * self.half
        self.xp = 2 * self.hp + 2 * self.pairs + self.odd
        self.cp = 2 * self.pairs + self.odd
        self.blocks = groups * tokens // BLK
        self.own = (2 * self.hp + self.hp) * HD
        self.cols = groups * self.own
        self.ctx = groups * self.hp * HD

    def x_shape(self):
        return (self.groups, self.chunks, self.xp, self.per, BLK, WIDE)

    def c_shape(self):
        return (self.groups, self.chunks, self.cp, self.per, BLK, WIDE)


def low(v):
    return jnp.concatenate([v, jnp.zeros_like(v)], 1)


def high(v):
    return jnp.concatenate([jnp.zeros_like(v), v], 1)


def diag(a, b):
    return jnp.concatenate(
        [jnp.concatenate([a, jnp.zeros_like(b)], 1), jnp.concatenate([jnp.zeros_like(a), b], 1)], 0
    )


def spots(plan, h, i):
    per = plan.per
    xb = (i // per) * (plan.xp * per) + i % per
    cb = (i // per) * (plan.cp * per) + i % per
    if h < 2 * plan.pairs:
        lanes = slice((h % 2) * HD, (h % 2 + 1) * HD)
        x0 = xb + (2 * plan.hp + 2 * (h // 2)) * per
        c0 = cb + 2 * (h // 2) * per
        return ((x0, lanes), (x0 + per, lanes)), ((c0, lanes), (c0 + per, lanes))
    x0 = xb + (2 * plan.hp + 2 * plan.pairs) * per
    c0 = cb + 2 * plan.pairs * per
    first, second = slice(0, HD), slice(HD, WIDE)
    return ((x0, first), (x0, second)), ((c0, first), (c0, second))


def listed(plan, x_ref, lists_ref, h, i):
    sides, places = [], []
    for side in range(2):
        at = ((h * (plan.blocks // 2) + i) * 2 + side) * LISTED
        ids = [lists_ref[at + n] for n in range(LISTED)]
        sides.append(jnp.concatenate([x_ref[n] for n in ids], 0))
        places.append(ids)
    return jnp.concatenate(sides, 1), places


def run_pairs(count, hp, first, second, third):
    for h in range(hp):
        first(0, h, 0)

    def body(i, carry):
        for u in range(2):
            t = 2 * i + u
            for h in range(hp):
                first(jnp.minimum(t + 1, count - 1), h, 1 - u)
                second(h, u)
                third(jnp.maximum(t - 1, 0), h, 1 - u)
        return carry

    lax.fori_loop(0, count // 2, body, 0)
    for h in range(hp):
        third(count - 1, h, 1)


def keys_of(plan, x_ref, h, n):
    per = plan.per
    at = (n * plan.xp + 2 * h) * per
    return pl.ds(at, 2 * per)


def attn_fwd_kernel(plan, lists_ref, x_ref, o_ref, s_ref, p_ref, g_ref, a_ref):
    c = LOG2E * HD**-0.5
    hp, count = plan.hp, plan.blocks // 2
    heads = range(hp)

    def stage_s(i, h, slot):
        kv, _ = listed(plan, x_ref, lists_ref, h, i)
        ((xa, la), (xb, lb)), _ = spots(plan, h, i)
        s_ref[slot, h] = dot(kv, diag(low(x_ref[xa, :, la]), low(x_ref[xb, :, lb])), NT)

    def stage_p(h, slot):
        s = s_ref[slot, h]
        m = jnp.max(s, 0, keepdims=True)
        e = jnp.exp2(s * c - m * c)
        inv = 1.0 / jnp.sum(e, 0, keepdims=True)
        p_ref[slot, h] = (e * inv).astype(BF)

    def stage_c(i, h, slot):
        kv, _ = listed(plan, x_ref, lists_ref, h, i)
        _, ((ca, la), (cb, lb)) = spots(plan, h, i)
        ctx = dot(p_ref[slot, h], kv, TN)
        o_ref[ca, :, la] = ctx[:BLK, HD:WIDE].astype(BF)
        o_ref[cb, :, lb] = ctx[BLK:, WIDE + HD :].astype(BF)

    p_ref[...] = jnp.zeros_like(p_ref)
    run_pairs(count, hp, stage_s, stage_p, stage_c)
    size = plan.rows
    steps = plan.groups * plan.chunks
    ws, outs = [], []
    for h in heads:
        ((xa, la), _), (c_first, _) = spots(plan, h, 0)
        (_, (xb, lb)), (_, c_last) = spots(plan, h, count - 1)
        ws.append(low(jnp.concatenate([x_ref[xa, :, la], x_ref[xb, :, lb]], 0)))
        outs.append((c_first, c_last))

    def chunk(n):
        return pl.ds(pl.multiple_of(n * size, size), size)

    def keys(h, n):
        return x_ref[keys_of(plan, x_ref, h, n)].reshape(size, WIDE)

    def one(n, ms):
        out = []
        for h in heads:
            s = dot(keys(h, n), ws[h], NT)
            g_ref[h, chunk(n), :] = s
            out.append(jnp.maximum(ms[h], jnp.max(s, 0, keepdims=True)))
        return tuple(out)

    ms = lax.fori_loop(
        0, steps, one, tuple(jnp.full((1, 2 * BLK), -jnp.inf, F32) for h in heads), unroll=2
    )

    def two(n, ls):
        out = []
        for h in heads:
            e = jnp.exp2(g_ref[h, chunk(n), :] * c - ms[h] * c)
            g_ref[h, chunk(n), :] = e
            out.append(ls[h] + jnp.sum(e, 0, keepdims=True))
        return tuple(out)

    ls = lax.fori_loop(0, steps, two, tuple(jnp.zeros((1, 2 * BLK), F32) for h in heads), unroll=2)
    invs = [1.0 / l for l in ls]
    a_ref[...] = jnp.zeros_like(a_ref)

    def three(n, carry):
        for h in heads:
            p = g_ref[h, chunk(n), :] * invs[h]
            hi = p.astype(BF)
            lo = (p - hi.astype(F32)).astype(BF)
            a_ref[h] += dot(jnp.concatenate([hi, lo], 1), keys(h, n), TN)
        return carry

    lax.fori_loop(0, steps, three, 0, unroll=2)
    for h in heads:
        ctx = (a_ref[h, : 2 * BLK, :] + a_ref[h, 2 * BLK :, :])[:, HD:].astype(BF)
        (ca, la), (cb, lb) = outs[h]
        o_ref[ca, :, la] = ctx[:BLK]
        o_ref[cb, :, lb] = ctx[BLK:]


def attn_fwd(plan, lists, x):
    flat = x.reshape(-1, BLK, WIDE)
    blocks = plan.groups * plan.chunks * plan.cp * plan.per
    keys = plan.blocks * BLK
    return pl.pallas_call(
        partial(attn_fwd_kernel, plan),
        out_shape=jax.ShapeDtypeStruct((blocks, BLK, WIDE), BF),
        in_specs=[pl.BlockSpec(memory_space=pltpu.SMEM), pl.BlockSpec(memory_space=VMEM)],
        out_specs=pl.BlockSpec(memory_space=VMEM),
        scratch_shapes=[
            VMEM((2, plan.hp, KEYS, 2 * BLK), F32),
            VMEM((2, plan.hp, KEYS, 2 * BLK), BF),
            VMEM((plan.hp, keys, 2 * BLK), F32),
            VMEM((plan.hp, 4 * BLK, WIDE), F32),
        ],
        compiler_params=pltpu.CompilerParams(vmem_limit_bytes=48 << 20),
        cost_estimate=pl.CostEstimate(flops=26 * 10**9, bytes_accessed=6 * 10**6, transcendentals=6 * 10**6),
        name="attn_fwd",
    )(lists, flat).reshape(plan.c_shape())


def attn_bwd_kernel(plan, lists_ref, x_ref, d_ref, o_ref, acc_ref, s_ref, p_ref, g_ref):
    scale = HD**-0.5
    c = LOG2E * scale
    hp, count = plan.hp, plan.blocks // 2
    heads = range(hp)
    acc_ref[...] = jnp.zeros_like(acc_ref)

    def weights(i, h):
        ((xa, xla), (xb, xlb)), ((ca, cla), (cb, clb)) = spots(plan, h, i)
        da, db = d_ref[ca, :, cla], d_ref[cb, :, clb]
        da = jnp.where(i == 0, jnp.zeros_like(da), da)
        db = jnp.where(i == count - 1, jnp.zeros_like(db), db)
        return jnp.concatenate(
            [diag(low(x_ref[xa, :, xla]), low(x_ref[xb, :, xlb])), diag(high(da), high(db))], 0
        )

    def stage_s(i, h, slot):
        kv, _ = listed(plan, x_ref, lists_ref, h, i)
        s_ref[slot, h] = dot(kv, weights(i, h), NT)

    def stage_p(h, slot):
        s = s_ref[slot, h, :, : 2 * BLK]
        g = s_ref[slot, h, :, 2 * BLK :]
        m = jnp.max(s, 0, keepdims=True)
        e = jnp.exp2(s * c - m * c)
        inv = 1.0 / jnp.sum(e, 0, keepdims=True)
        delta = jnp.sum(e * g, 0, keepdims=True) * inv
        p = e * inv
        p_ref[slot, h, :, : 2 * BLK] = (p * (g - delta)).astype(BF)
        p_ref[slot, h, :, 2 * BLK :] = p.astype(BF)

    def stage_c(i, h, slot):
        kv, places = listed(plan, x_ref, lists_ref, h, i)
        ((xa, la), (xb, lb)), _ = spots(plan, h, i)
        dq = dot(p_ref[slot, h, :, : 2 * BLK], kv, TN) * scale
        o_ref[xa, :, la] = dq[:BLK, :HD].astype(BF)
        o_ref[xb, :, lb] = dq[BLK:, WIDE : WIDE + HD].astype(BF)
        dkv = dot(p_ref[slot, h], weights(i, h), NN)
        for side in range(2):
            part = dkv[:, side * WIDE : (side + 1) * WIDE]
            for n in range(LISTED):
                acc_ref[places[side][n]] += part[n * BLK : (n + 1) * BLK]

    p_ref[...] = jnp.zeros_like(p_ref)
    run_pairs(count, hp, stage_s, stage_p, stage_c)
    lane_scale = jnp.where(
        lax.broadcasted_iota(jnp.int32, (1, WIDE), 1) < HD, scale, 1.0
    ).astype(F32)
    size = plan.rows
    steps = plan.groups * plan.chunks

    def chunk(n):
        return pl.ds(pl.multiple_of(n * size, size), size)

    for h in heads:
        ((xa, xla), _), ((ca, cla), _) = spots(plan, h, 0)
        (_, (xb, xlb)), (_, (cb, clb)) = spots(plan, h, count - 1)
        q = low(jnp.concatenate([x_ref[xa, :, xla], x_ref[xb, :, xlb]], 0))
        d = high(jnp.concatenate([d_ref[ca, :, cla], d_ref[cb, :, clb]], 0))
        w = jnp.concatenate([q, d], 0)
        three_w = jnp.concatenate([q, d, d], 0)

        def keys(n):
            return x_ref[keys_of(plan, x_ref, h, n)].reshape(size, WIDE)

        def one(n, m):
            s = dot(keys(n), w, NT)
            g_ref[chunk(n), :] = s
            return jnp.maximum(m, jnp.max(s[:, : 2 * BLK], 0, keepdims=True))

        m = lax.fori_loop(0, steps, one, jnp.full((1, 2 * BLK), -jnp.inf, F32), unroll=4)

        def two(n, state):
            l, eg = state
            e = jnp.exp2(g_ref[chunk(n), : 2 * BLK] * c - m * c)
            g_ref[chunk(n), : 2 * BLK] = e
            return (
                l + jnp.sum(e, 0, keepdims=True),
                eg + jnp.sum(e * g_ref[chunk(n), 2 * BLK :], 0, keepdims=True),
            )

        l, eg = lax.fori_loop(0, steps, two, (jnp.zeros((1, 2 * BLK), F32),) * 2, unroll=4)
        inv = 1.0 / l
        delta = eg * inv

        def three(n, dq):
            p = g_ref[chunk(n), : 2 * BLK] * inv
            ds = (p * (g_ref[chunk(n), 2 * BLK :] - delta)).astype(BF)
            hi = p.astype(BF)
            lo = (p - hi.astype(F32)).astype(BF)
            dkv = dot(jnp.concatenate([ds, hi, lo], 1), three_w, NN)
            where = keys_of(plan, x_ref, h, n)
            total = acc_ref[where].reshape(size, WIDE) + dkv
            o_ref[where] = (total * lane_scale).astype(BF).reshape(2 * plan.per, BLK, WIDE)
            return dq + dot(ds, keys(n), TN)

        dq = lax.fori_loop(0, steps, three, jnp.zeros((2 * BLK, WIDE), F32), unroll=4)
        dq = (dq[:, :HD] * scale).astype(BF)
        o_ref[xa, :, xla] = dq[:BLK]
        o_ref[xb, :, xlb] = dq[BLK:]


def attn_bwd(plan, lists, x, d):
    flat = x.reshape(-1, BLK, WIDE)
    keys = plan.blocks * BLK
    return pl.pallas_call(
        partial(attn_bwd_kernel, plan),
        out_shape=jax.ShapeDtypeStruct(flat.shape, BF),
        in_specs=[pl.BlockSpec(memory_space=pltpu.SMEM)] + [pl.BlockSpec(memory_space=VMEM)] * 2,
        out_specs=pl.BlockSpec(memory_space=VMEM),
        scratch_shapes=[
            VMEM(flat.shape, F32),
            VMEM((2, plan.hp, KEYS, 4 * BLK), F32),
            VMEM((2, plan.hp, KEYS, 4 * BLK), BF),
            VMEM((keys, 4 * BLK), F32),
        ],
        compiler_params=pltpu.CompilerParams(vmem_limit_bytes=56 << 20),
        cost_estimate=pl.CostEstimate(flops=46 * 10**9, bytes_accessed=12 * 10**6, transcendentals=6 * 10**6),
        name="attn_bwd",
    )(lists, flat, d.reshape(-1, BLK, WIDE)).reshape(plan.x_shape())


def mean(v):
    return jnp.sum(v, -1, keepdims=True) * (1.0 / v.shape[-1])


def normalise(resid):
    centre = resid - mean(resid)
    inv = lax.rsqrt(mean(centre * centre) + epsilon)
    return centre * inv, inv


def norm_back(unit, inv, gain, grad):
    g = grad * gain
    return inv * (g - mean(g) - unit * mean(g * unit))


def gelu_parts(u):
    k = 0.7978845608028654
    sq = u * u
    t = jnp.tanh(k * (u + 0.044715 * (u * sq)))
    half = 0.5 * (1.0 + t)
    return half * u, half + 0.5 * u * (1.0 - t * t) * (k + (3 * 0.044715 * k) * sq)


def rows_of(ref):
    return ref[...].reshape(-1, ref.shape[-1])


def pick_context(plan, pieces):
    half = plan.half
    tiles = []
    for g in range(plan.groups):
        for p in range(plan.pairs):
            tiles.append(pieces[g, 2 * p : 2 * p + 2].reshape(plan.rows, WIDE))
        if plan.odd:
            both = pieces[g, 2 * plan.pairs].reshape(half, WIDE)
            tiles.append(jnp.concatenate([both[:, :HD], both[:, HD:]], 0))
    return jnp.concatenate(tiles, 1)[:, :D]


def put_context(plan, value, ref):
    half, per = plan.half, plan.per
    if plan.ctx > D:
        value = jnp.concatenate([value, jnp.zeros((value.shape[0], plan.ctx - D), value.dtype)], 1)
    for g in range(plan.groups):
        at = g * plan.hp * HD
        for p in range(plan.pairs):
            ref[g, 2 * p : 2 * p + 2] = value[:, at : at + WIDE].reshape(2, per, BLK, WIDE)
            at += WIDE
        if plan.odd:
            one = value[:, at : at + HD]
            ref[g, 2 * plan.pairs] = jnp.concatenate([one[:half], one[half:]], 1).reshape(per, BLK, WIDE)


def put_heads(plan, value, ref):
    half, per, hp = plan.half, plan.per, plan.hp
    pairs_at = plan.groups * hp * WIDE
    single_at = pairs_at + plan.groups * plan.pairs * WIDE
    for g in range(plan.groups):
        for h in range(hp):
            at = (g * hp + h) * WIDE
            ref[g, 2 * h : 2 * h + 2] = value[:, at : at + WIDE].reshape(2, per, BLK, WIDE)
        for p in range(plan.pairs):
            at = pairs_at + (g * plan.pairs + p) * WIDE
            ref[g, 2 * hp + 2 * p : 2 * hp + 2 * p + 2] = value[:, at : at + WIDE].reshape(2, per, BLK, WIDE)
        if plan.odd:
            at = single_at + g * HD
            one = value[:, at : at + HD]
            ref[g, plan.xp - 1] = jnp.concatenate([one[:half], one[half:]], 1).reshape(per, BLK, WIDE)


def pick_heads(plan, pieces):
    half, hp = plan.half, plan.hp
    kv, pairs, singles = [], [], []
    for g in range(pieces.shape[0]):
        for h in range(hp):
            kv.append(pieces[g, 2 * h : 2 * h + 2].reshape(plan.rows, WIDE))
        for p in range(plan.pairs):
            pairs.append(pieces[g, 2 * hp + 2 * p : 2 * hp + 2 * p + 2].reshape(plan.rows, WIDE))
        if plan.odd:
            both = pieces[g, plan.xp - 1].reshape(half, WIDE)
            singles.append(jnp.concatenate([both[:, :HD], both[:, HD:]], 0))
    return jnp.concatenate(kv + pairs + singles, 1)


def whole(shape):
    return pl.BlockSpec(shape, lambda *i: (0,) * len(shape), pipeline_mode=pl.Buffered(1))


def own_kernel(plan, a_ref, w_ref, b_ref, o_ref):
    a = a_ref[...].reshape(plan.rows, D)
    y = (dot(a, rows_of(w_ref), NN) + b_ref[...]).astype(BF)
    one = Plan.__new__(Plan)
    one.__dict__.update(plan.__dict__)
    one.groups = 1
    put_heads(one, y, o_ref.at[:, 0])


def own_heads(plan, hidden_all, weight, bias):
    a = hidden_all.reshape(plan.groups, 2, plan.chunks, plan.half, D)
    return pl.pallas_call(
        partial(own_kernel, plan),
        out_shape=jax.ShapeDtypeStruct(plan.x_shape(), BF),
        grid=(plan.groups, plan.chunks),
        in_specs=[
            pl.BlockSpec((1, 2, 1, plan.half, D), lambda g, c: (g, 0, c, 0, 0)),
            whole(weight.shape),
            whole(bias.shape),
        ],
        out_specs=pl.BlockSpec((1, 1) + plan.x_shape()[2:], lambda g, c: (g, c, 0, 0, 0, 0)),
        compiler_params=pltpu.CompilerParams(vmem_limit_bytes=48 << 20),
        cost_estimate=pl.CostEstimate(flops=7 * 10**9, bytes_accessed=12 * 10**6, transcendentals=0),
        name="own_heads",
    )(a, weight, bias)


def own_grad_kernel(plan, item, steps, a_ref, d_ref, o_ref, acc_ref, sum_ref):
    n = pl.program_id(0) * plan.chunks + pl.program_id(1)

    @pl.when(n == 0)
    def _():
        acc_ref[...] = jnp.zeros_like(acc_ref)
        sum_ref[...] = jnp.zeros_like(sum_ref)

    d = pick_heads(plan, d_ref[:, 0])
    acc_ref[...] += dot(a_ref[...].reshape(plan.rows, D), d, TN)
    sum_ref[...] += jnp.sum(d.astype(F32).reshape(-1, 8, d.shape[1]), 0)

    @pl.when(n == steps - 1)
    def _():
        share = D // item
        total = jnp.broadcast_to(jnp.sum(sum_ref[...], 0, keepdims=True), (16, sum_ref.shape[1])).astype(BF)
        for r in range(item):
            o_ref[r, :share] = acc_ref[r * share : (r + 1) * share].astype(BF)
            o_ref[r, share:] = total


def own_grad(plan, item, hidden_all, dx):
    a = hidden_all.reshape(plan.groups, 2, plan.chunks, plan.half, D)
    return pl.pallas_call(
        partial(own_grad_kernel, plan, item, plan.groups * plan.chunks),
        out_shape=jax.ShapeDtypeStruct((item, D // item + 16, plan.own), BF),
        grid=(plan.groups, plan.chunks),
        in_specs=[
            pl.BlockSpec((1, 2, 1, plan.half, D), lambda g, c: (g, 0, c, 0, 0)),
            pl.BlockSpec((1, 1) + plan.x_shape()[2:], lambda g, c: (g, c, 0, 0, 0, 0)),
        ],
        out_specs=whole((item, D // item + 16, plan.own)),
        scratch_shapes=[VMEM((D, plan.own), F32), VMEM((8, plan.own), F32)],
        compiler_params=pltpu.CompilerParams(vmem_limit_bytes=48 << 20),
        cost_estimate=pl.CostEstimate(flops=7 * 10**9, bytes_accessed=12 * 10**6, transcendentals=0),
        name="own_grad",
    )(a, dx)


def halves(plan, width):
    return pl.BlockSpec((2, plan.half, width), lambda c: (0, c, 0))


def cut(plan, v):
    return v.reshape(2, plan.tokens // 2, v.shape[-1])


def read(ref):
    return ref[...].reshape(-1, ref.shape[-1])


def write(ref, value):
    ref[...] = value.reshape(ref.shape).astype(ref.dtype)


class Packed:
    def __init__(self, ref, ff):
        self.ref = ref
        self.item = ref.shape[0]
        self.share = D // self.item
        self.parts = ff // D

    def rows(self, first):
        return self.ref[:, first : first + self.share].reshape(D, D)

    def out(self):
        return self.rows(0)

    def ffn_in(self, n):
        return self.rows(self.share * (1 + n))

    def ffn_out(self, n):
        ranks = self.item // self.parts
        first = self.share * (1 + self.parts)
        return self.ref[n * ranks : (n + 1) * ranks, first : first + self.share * self.parts].reshape(D, D)

    def columns(self, n):
        return self.rows(self.share * (1 + 2 * self.parts + n))


def wide_parts(w):
    return jnp.concatenate([w[:, n : n + D] for n in range(0, w.shape[1], D)])


OUT_BIAS, GAIN1, SHIFT1, FFN_BIAS, GAIN2, SHIFT2 = range(6)


def first_half(plan, ctx, h, w, vec_ref):
    r1 = h + dot(ctx, w.out(), NN) + vec_ref[OUT_BIAS : OUT_BIAS + 1]
    unit1, inv1 = normalise(r1)
    y1 = unit1 * vec_ref[GAIN1 : GAIN1 + 1] + vec_ref[SHIFT1 : SHIFT1 + 1]
    return r1, unit1, inv1, y1, y1.astype(BF)


def part_of(n):
    return slice(n * D, (n + 1) * D)


def put(ref, n, value):
    ref[:, :, part_of(n)] = value.reshape(ref.shape[:2] + (D,)).astype(ref.dtype)


def get(ref, n):
    return ref[:, :, part_of(n)].reshape(-1, D)


def fwd_kernel(plan, ff, c_ref, h_ref, w_ref, vec_ref, inner_ref, bias_ref,
               x_ref, next_ref, next_low_ref, r1_ref, r2_ref, u_ref, y_ref, ctx_ref):
    w = Packed(w_ref, ff)
    ctx = pick_context(plan, c_ref[:, 0])
    write(ctx_ref, ctx)
    r1, _, _, y1, y1_low = first_half(plan, ctx, read(h_ref), w, vec_ref)
    write(r1_ref, r1)
    write(y_ref, y1_low)
    r2 = y1 + vec_ref[FFN_BIAS : FFN_BIAS + 1]
    for n in range(w.parts):
        u = dot(y1_low, w.ffn_in(n), NN) + inner_ref[:, part_of(n)]
        put(u_ref, n, u)
        r2 = r2 + dot(gelu_parts(u)[0].astype(BF), w.ffn_out(n), NN)
    write(r2_ref, r2)
    unit2, _ = normalise(r2)
    nxt = unit2 * vec_ref[GAIN2 : GAIN2 + 1] + vec_ref[SHIFT2 : SHIFT2 + 1]
    low_ = nxt.astype(BF)
    write(next_ref, nxt)
    write(next_low_ref, low_)
    y = [
        (dot(low_, w.columns(n), NN) + bias_ref[:, part_of(n)]).astype(BF) for n in range(plan.cols // D)
    ]
    put_heads(plan, jnp.concatenate(y, 1), x_ref.at[:, 0])


def piece_spec(shape):
    return pl.BlockSpec((shape[0], 1) + shape[2:], lambda c: (0, c, 0, 0, 0, 0))


def layer_fwd(plan, ctx, h, packed, vec, inner, bias):
    t = (2, plan.tokens // 2)
    ff = inner.shape[-1]
    shapes = [(D, F32), (D, BF), (D, F32), (D, F32), (ff, F32), (D, BF), (D, BF)]
    return pl.pallas_call(
        partial(fwd_kernel, plan, ff),
        out_shape=[jax.ShapeDtypeStruct(plan.x_shape(), BF)] + [jax.ShapeDtypeStruct(t + (n,), d) for n, d in shapes],
        grid=(plan.chunks,),
        in_specs=[piece_spec(plan.c_shape()), halves(plan, D)]
        + [whole(w.shape) for w in (packed, vec, inner, bias)],
        out_specs=[piece_spec(plan.x_shape())] + [halves(plan, n) for n, _ in shapes],
        compiler_params=pltpu.CompilerParams(vmem_limit_bytes=60 << 20),
        cost_estimate=pl.CostEstimate(flops=30 * 10**9, bytes_accessed=50 * 10**6, transcendentals=3 * 10**6),
        name="layer_fwd",
    )(ctx, cut(plan, h), packed, vec, inner, bias)


SUM_DO, D_GAIN1, D_SHIFT1, SUM_DF, D_GAIN2, D_SHIFT2 = range(6)


def add_sums(ref, at, value):
    ref[at] += jnp.sum(value.reshape(-1, 8, value.shape[-1]), 0)


def back_chunk(plan, gy, unit1, inv1, unit2, inv2, gate, w, vec_ref, sums_ref, inner_sum_ref, du_ref):
    @pl.when(pl.program_id(0) == 0)
    def _():
        sums_ref[...] = jnp.zeros_like(sums_ref)
        inner_sum_ref[...] = jnp.zeros_like(inner_sum_ref)

    dr2 = norm_back(unit2, inv2, vec_ref[GAIN2 : GAIN2 + 1], gy)
    df = dr2.astype(BF)
    dy1 = dr2
    for n in range(w.parts):
        du = (dot(df, w.ffn_out(n), NT) * gate(n)).astype(BF)
        put(du_ref, n, du)
        dy1 = dy1 + dot(du, w.ffn_in(n), NT)
        inner_sum_ref[:, part_of(n)] += jnp.sum(du.astype(F32).reshape(-1, 8, D), 0)
    dr1 = norm_back(unit1, inv1, vec_ref[GAIN1 : GAIN1 + 1], dy1)
    do = dr1.astype(BF)
    dc = dot(do, w.out(), NT).astype(BF)
    add_sums(sums_ref, SUM_DO, do.astype(F32))
    add_sums(sums_ref, D_GAIN1, dy1 * unit1)
    add_sums(sums_ref, D_SHIFT1, dy1)
    add_sums(sums_ref, SUM_DF, df.astype(F32))
    add_sums(sums_ref, D_GAIN2, gy * unit2)
    add_sums(sums_ref, D_SHIFT2, gy)
    return df, dr1, do, dc


def mid_kernel(plan, ff, c_ref, h_ref, gy_ref, w_ref, vec_ref, inner_ref,
               d_ref, out_ref, dr1_ref, gz_ref, du_ref, df_ref, do_ref, y_ref, ctx_ref, sums_ref, inner_sum_ref, gate_ref):
    w = Packed(w_ref, ff)
    ctx = pick_context(plan, c_ref[:, 0])
    write(ctx_ref, ctx)
    _, unit1, inv1, y1, y1_low = first_half(plan, ctx, read(h_ref), w, vec_ref)
    write(y_ref, y1_low)
    r2 = y1 + vec_ref[FFN_BIAS : FFN_BIAS + 1]
    for n in range(w.parts):
        u = dot(y1_low, w.ffn_in(n), NN) + inner_ref[:, part_of(n)]
        gz, gate_ref[n] = gelu_parts(u)
        gz = gz.astype(BF)
        put(gz_ref, n, gz)
        r2 = r2 + dot(gz, w.ffn_out(n), NN)
    unit2, inv2 = normalise(r2)
    write(out_ref, unit2 * vec_ref[GAIN2 : GAIN2 + 1] + vec_ref[SHIFT2 : SHIFT2 + 1])
    df, dr1, do, dc = back_chunk(plan, read(gy_ref), unit1, inv1, unit2, inv2, lambda n: gate_ref[n],
                                 w, vec_ref, sums_ref, inner_sum_ref, du_ref)
    put_context(plan, dc, d_ref.at[:, 0])
    write(dr1_ref, dr1)
    write(df_ref, df)
    write(do_ref, do)


def sum_specs(ff):
    return (
        [jax.ShapeDtypeStruct((6, 8, D), F32), jax.ShapeDtypeStruct((8, ff), F32)],
        [pl.BlockSpec((6, 8, D), lambda c: (0, 0, 0)), pl.BlockSpec((8, ff), lambda c: (0, 0))],
    )


def layer_mid(plan, ctx, h, gy, packed, vec, inner):
    t = (2, plan.tokens // 2)
    ff = inner.shape[-1]
    shapes = [(D, F32), (D, F32), (ff, BF), (ff, BF), (D, BF), (D, BF), (D, BF), (D, BF)]
    sums, sums_at = sum_specs(ff)
    return pl.pallas_call(
        partial(mid_kernel, plan, ff),
        out_shape=[jax.ShapeDtypeStruct(plan.c_shape(), BF)] + [jax.ShapeDtypeStruct(t + (n,), d) for n, d in shapes] + sums,
        grid=(plan.chunks,),
        in_specs=[piece_spec(plan.c_shape()), halves(plan, D), halves(plan, D)]
        + [whole(w.shape) for w in (packed, vec, inner)],
        out_specs=[piece_spec(plan.c_shape())] + [halves(plan, n) for n, _ in shapes] + sums_at,
        scratch_shapes=[VMEM((ff // D, plan.rows, D), F32)],
        compiler_params=pltpu.CompilerParams(vmem_limit_bytes=60 << 20),
        cost_estimate=pl.CostEstimate(flops=45 * 10**9, bytes_accessed=50 * 10**6, transcendentals=3 * 10**6),
        name="layer_mid",
    )(ctx, cut(plan, h), cut(plan, gy), packed, vec, inner)


def bwd_kernel(plan, ff, dx_ref, up_ref, r1_ref, r2_ref, u_ref, w_ref, vec_ref,
               d_ref, dr1_ref, gz_ref, du_ref, df_ref, do_ref, sums_ref, inner_sum_ref):
    w = Packed(w_ref, ff)
    dqkv = pick_heads(plan, dx_ref[:, 0])
    gy = read(up_ref)
    for n in range(plan.cols // D):
        gy = gy + dot(dqkv[:, part_of(n)], w.columns(n), NT)

    unit1, inv1 = normalise(read(r1_ref))
    unit2, inv2 = normalise(read(r2_ref))

    def gate(n):
        gz, value = gelu_parts(get(u_ref, n))
        put(gz_ref, n, gz)
        return value

    df, dr1, do, dc = back_chunk(plan, gy, unit1, inv1, unit2, inv2, gate, w, vec_ref, sums_ref, inner_sum_ref, du_ref)
    put_context(plan, dc, d_ref.at[:, 0])
    write(dr1_ref, dr1)
    write(df_ref, df)
    write(do_ref, do)


def layer_bwd(plan, dx, up, r1, r2, u, packed, vec):
    t = (2, plan.tokens // 2)
    ff = u.shape[-1]
    shapes = [(D, F32), (ff, BF), (ff, BF), (D, BF), (D, BF)]
    sums, sums_at = sum_specs(ff)
    return pl.pallas_call(
        partial(bwd_kernel, plan, ff),
        out_shape=[jax.ShapeDtypeStruct(plan.c_shape(), BF)] + [jax.ShapeDtypeStruct(t + (n,), d) for n, d in shapes] + sums,
        grid=(plan.chunks,),
        in_specs=[piece_spec(plan.x_shape()), halves(plan, D), halves(plan, D), halves(plan, D), halves(plan, ff)]
        + [whole(w.shape) for w in (packed, vec)],
        out_specs=[piece_spec(plan.c_shape())] + [halves(plan, n) for n, _ in shapes] + sums_at,
        compiler_params=pltpu.CompilerParams(vmem_limit_bytes=60 << 20),
        cost_estimate=pl.CostEstimate(flops=40 * 10**9, bytes_accessed=50 * 10**6, transcendentals=3 * 10**6),
        name="layer_bwd",
    )(dx, up, r1, r2, u, packed, vec)


def dense_grad_kernel(item, gz_ref, df_ref, y_ref, du_ref, ctx_ref, do_ref, vec_ref, fo_ref, rest_ref):
    n = pl.program_id(0)
    parts = pl.num_programs(0)
    share = D // item
    ranks = item // parts
    fo_ref[...] = dot(gz_ref[...], df_ref[...], TN).astype(BF).reshape(fo_ref.shape)
    first = pl.multiple_of(n * share, 16)
    rest_ref[:, pl.ds(first, share)] = dot(y_ref[...], du_ref[...], TN).astype(BF).reshape(item, share, D)

    @pl.when(n == parts - 1)
    def _():
        at = parts * share
        rest_ref[:, at : at + share] = dot(ctx_ref[...], do_ref[...], TN).astype(BF).reshape(item, share, D)
        rest_ref[:, at + share :] = vec_ref[...]


def dense_grads(item, gz, df, y, du, ctx, do, vecs):
    tokens, ff = gz.shape
    parts = ff // D
    share = D // item
    rest = parts * share + share + vecs.shape[1]
    column = pl.BlockSpec((tokens, D), lambda n: (0, n))
    return pl.pallas_call(
        partial(dense_grad_kernel, item),
        out_shape=[jax.ShapeDtypeStruct((item, ff // item, D), BF), jax.ShapeDtypeStruct((item, rest, D), BF)],
        grid=(parts,),
        in_specs=[column, whole(df.shape), whole(y.shape), column, whole(ctx.shape), whole(do.shape), whole(vecs.shape)],
        out_specs=[pl.BlockSpec((item // parts, ff // item, D), lambda n: (n, 0, 0)), whole((item, rest, D))],
        compiler_params=pltpu.CompilerParams(vmem_limit_bytes=56 << 20),
        cost_estimate=pl.CostEstimate(flops=14 * 10**9, bytes_accessed=30 * 10**6, transcendentals=0),
        name="dense_grads",
    )(gz, df, y, du, ctx, do, vecs)


def tail_kernel(plan, dx_ref, up_ref, w_ref, o_ref):
    dqkv = pick_heads(plan, dx_ref[:, 0])
    share = D // w_ref.shape[0]
    out = read(up_ref)
    for n in range(plan.cols // D):
        out = out + dot(dqkv[:, part_of(n)], w_ref[:, n * share : (n + 1) * share].reshape(D, D), NT)
    write(o_ref, out)


def layer_tail(plan, dx, up, w_qkv):
    return pl.pallas_call(
        partial(tail_kernel, plan),
        out_shape=jax.ShapeDtypeStruct(up.shape, F32),
        grid=(plan.chunks,),
        in_specs=[piece_spec(plan.x_shape()), halves(plan, D), whole(w_qkv.shape)],
        out_specs=halves(plan, D),
        compiler_params=pltpu.CompilerParams(vmem_limit_bytes=48 << 20),
        cost_estimate=pl.CostEstimate(flops=8 * 10**9, bytes_accessed=12 * 10**6, transcendentals=0),
        name="layer_tail",
    )(dx, up, w_qkv)


def finish_kernel(plan, share, counts, *refs):
    fulls, owns, outs = refs[:LAYERS], refs[LAYERS], refs[LAYERS + 1 :]
    qkv_ref, bias_ref, attn_ref, inner_ref, outer_ref = outs[:5]
    small = outs[5:]
    outer = outer_ref.shape[1]
    parts = inner_ref.shape[2] // D
    each = owns.shape[1] // LAYERS
    for layer in range(LAYERS):
        flat = fulls[layer][...].reshape(-1, D)
        outer_ref[layer] = flat[:outer].astype(F32)
        at = outer
        for n in range(parts):
            inner_ref[layer, :, part_of(n)] = flat[at : at + share].astype(F32)
            at += share
        attn_ref[layer] = flat[at : at + share].astype(F32)
        at += share
        vecs = flat[at : at + 16].astype(F32)
        at = 0
        for ref, n in zip(small, counts):
            ref[layer : layer + 1, :] = vecs[at // D : at // D + 1, at % D : at % D + n]
            at += n
        pieces = {}
        for g in range(plan.groups):
            rows = owns[g, layer * each : (layer + 1) * each].astype(F32)
            for i in range(plan.hp):
                head = g * plan.hp + i
                pieces["k", head] = rows[:, i * WIDE : i * WIDE + HD]
                pieces["v", head] = rows[:, i * WIDE + HD : (i + 1) * WIDE]
                pieces["q", head] = rows[:, (2 * plan.hp + i) * HD : (2 * plan.hp + i + 1) * HD]
        value = jnp.concatenate([pieces[kind, head] for kind in "qkv" for head in range(H)], 1)
        qkv_ref[layer] = value[:share]
        bias_ref[layer : layer + 1, :] = value[share : share + 1]


def finish(plan, share, ff, item, counts, fulls, owns):
    out = [(share, 3 * D), (3 * D,), (share, D), (share, ff), (ff // item, D)] + [(n,) for n in counts]
    return pl.pallas_call(
        partial(finish_kernel, plan, share, counts),
        out_shape=[jax.ShapeDtypeStruct((LAYERS,) + s, F32) for s in out],
        in_specs=[pl.BlockSpec(memory_space=VMEM)] * (LAYERS + 1),
        out_specs=[pl.BlockSpec(memory_space=VMEM)] * len(out),
        compiler_params=pltpu.CompilerParams(vmem_limit_bytes=48 << 20),
        name="finish",
    )(*fulls, owns)


def column_parts(plan, w):
    lead = w.shape[:-1]
    g, hp = plan.groups, plan.hp
    w = w.reshape(lead + (3, H, HD))
    w = jnp.pad(w, [(0, 0)] * (len(lead) + 1) + [(0, g * hp - H), (0, 0)])
    q, k, v = (w[..., n, :, :] for n in range(3))
    kv = jnp.stack([k, v], -2).reshape(lead + (g, hp * WIDE))
    q = q.reshape(lead + (g, hp, HD))
    pairs = q[..., : 2 * plan.pairs, :].reshape(lead + (g, plan.pairs * WIDE))
    last = q[..., 2 * plan.pairs :, :].reshape(lead + (g, plan.odd * HD))
    return kv, pairs, last


def all_columns(plan, w):
    lead = w.shape[:-1]
    return jnp.concatenate([p.reshape(lead + (-1,)) for p in column_parts(plan, w)], -1)


def own_columns(plan, w, rank):
    axis = w.ndim - 1
    return jnp.concatenate(
        [lax.dynamic_index_in_dim(p, rank, axis, False) for p in column_parts(plan, w)], -1
    )


def exchange(x):
    y = x.reshape((x.shape[0], -1, x.shape[-1]))
    return lax.all_to_all(y, "seq", split_axis=0, concat_axis=0, tiled=True).reshape(x.shape)


def tie(*args):
    return lax.optimization_barrier(args)


def key_table(plan, random_ids):
    n = plan.blocks
    here = n // plan.groups
    j = jnp.arange(n, dtype=jnp.int32)
    shared = jnp.stack(
        [jnp.maximum(j - 1, 0), j, jnp.minimum(j + 1, n - 1), jnp.zeros_like(j), jnp.full_like(j, n - 1)], 1
    )
    ids = jnp.concatenate([jnp.broadcast_to(shared[None], (plan.hp, n, 5)), random_ids], 2)
    inside = ids % here
    r = inside % (here // 2)
    head = jnp.arange(plan.hp, dtype=jnp.int32)[:, None, None]
    piece = 2 * head + inside // (here // 2)
    place = (((ids // here) * plan.chunks + r // plan.per) * plan.xp + piece) * plan.per + r % plan.per
    place = place.reshape(plan.hp, plan.groups, 2, here // 2, LISTED).transpose(0, 1, 3, 2, 4)
    return place.reshape(-1)


def local(
    hidden,
    block_lists,
    w_qkv,
    bias_query,
    bias_value,
    w_attn_out,
    bias_attn_out,
    norm1_gain,
    norm1_shift,
    w_ffn_in,
    bias_ffn_in,
    w_ffn_out,
    bias_ffn_out,
    norm2_gain,
    norm2_shift,
    cotangent,
):
    groups = lax.axis_size("seq")
    item = lax.axis_size("item")
    seq_rank = lax.axis_index("seq")
    item_rank = lax.axis_index("item")
    tokens = hidden.shape[1]
    plan = Plan(groups, tokens)
    here = tokens // BLK
    share = D // item
    hidden_low = hidden[0].astype(BF)
    hidden_all = exchange(jnp.broadcast_to(hidden_low[None], (groups, tokens, D)))
    hidden_all, block_lists = tie(hidden_all, block_lists)

    ids = jnp.pad(block_lists[0], ((0, 0), (0, 0), (0, groups * plan.hp - H), (0, 0)))
    ids = ids.reshape(LAYERS, here, groups, plan.hp * RAND).transpose(2, 0, 1, 3)
    ids = exchange(ids.reshape(groups, 1, -1)).reshape(groups, LAYERS, here, plan.hp, RAND)
    ids = ids.transpose(1, 3, 0, 2, 4).reshape(LAYERS, plan.hp, plan.blocks, RAND)
    tables = [key_table(plan, ids[layer]) for layer in range(LAYERS)]

    small = (bias_query, bias_value, bias_attn_out, norm1_gain, norm1_shift, bias_ffn_in, bias_ffn_out, norm2_gain, norm2_shift)
    packed = lax.all_gather(jnp.concatenate(small, 1), "item", axis=0).astype(F32)
    vectors = []
    for layer in range(LAYERS):
        at, out = 0, []
        for s in small:
            out.append(packed[:, layer, at : at + s.shape[1]].reshape(-1))
            at += s.shape[1]
        vectors.append(out)
    stacked = [jnp.stack(v[2:5] + v[6:9] + [v[2]] * 2) for v in vectors]
    inner = [v[5][None] for v in vectors]
    qkv_bias = [jnp.concatenate([v[0], jnp.zeros_like(v[0]), v[1]])[None] for v in vectors]

    own_weight = lax.all_gather(own_columns(plan, w_qkv[0], seq_rank), "item", axis=0)
    own_bias = own_columns(plan, qkv_bias[0], seq_rank)
    columns = wide_parts(all_columns(plan, w_qkv[0])), wide_parts(all_columns(plan, w_qkv[1]))

    def dense(layer):
        return [w_attn_out[layer], wide_parts(w_ffn_in[layer]), w_ffn_out[layer]]

    packed0 = lax.all_gather(jnp.concatenate(dense(0) + [columns[1]]), "item", axis=0)
    packed1 = lax.all_gather(jnp.concatenate(dense(1)), "item", axis=0)
    columns0 = lax.all_gather(columns[0], "item", axis=0)

    x0 = own_heads(plan, hidden_all, own_weight, own_bias)
    ctx0 = exchange(attn_fwd(plan, tables[0], x0))
    x1, h1, h1_low, r1, r2, u, y0, ctx0 = layer_fwd(
        plan, ctx0, hidden[0], packed0, stacked[0], inner[0], all_columns(plan, qkv_bias[1])
    )
    x1 = exchange(x1)
    ctx1 = exchange(attn_fwd(plan, tables[1], x1))
    h1_all = lax.all_gather(h1_low.reshape(tokens, D), "seq", axis=0)
    d1, output, up1, gz1, du1, df1, do1, y1, ctx1, sums1, inner1 = layer_mid(
        plan, ctx1, h1, cotangent[0], packed1, stacked[1], inner[1]
    )

    def flat(a):
        return a.reshape(tokens, -1)

    def scattered(g):
        return lax.psum_scatter(g, "item", scatter_dimension=0, tiled=False)

    def rows_for(vecs):
        part = jnp.concatenate([v.reshape(item, -1) for v in vecs], 1)
        return jnp.pad(part, ((0, 0), (0, 16 * D - part.shape[1]))).reshape(item, 16, D).astype(BF)

    def grads(gz, du, df, do, y, ctx, sums, inner_sum):
        sums = jnp.sum(sums, 1)
        vecs = (sums[SUM_DO], sums[D_GAIN1], sums[D_SHIFT1], jnp.sum(inner_sum, 0), sums[SUM_DF], sums[D_GAIN2], sums[D_SHIFT2])
        return dense_grads(item, flat(gz), flat(df), flat(y), flat(du), flat(ctx), flat(do), rows_for(vecs))

    def seq_send(shares):
        rows = jnp.concatenate(shares)
        rows = jnp.pad(rows, ((0, -rows.shape[0] % (16 * groups)), (0, 0)))
        return exchange(rows.reshape(groups, -1, D))

    def seq_sum(sent):
        return jnp.sum(sent.astype(F32), 0).astype(BF)

    def seq_gather(part):
        return exchange(jnp.broadcast_to(part[None], (groups,) + part.shape))

    counts = [share] * 3 + [w_ffn_in.shape[2] // item] + [share] * 3
    dc1 = exchange(d1)
    fo1, rest1 = grads(gz1, du1, df1, do1, y1, ctx1, sums1, inner1)
    dc1, fo1, rest1 = tie(dc1, fo1, rest1)
    fo1, rest1 = scattered(fo1), scattered(rest1)
    dc1, columns0, h1_all = tie(dc1, columns0, h1_all)
    dx1 = attn_bwd(plan, tables[1], x1, dc1)
    own1 = own_grad(plan, item, h1_all, dx1)
    dx1 = exchange(dx1)
    dx1, own1 = tie(dx1, own1)
    own1 = scattered(own1)
    dx1, fo1 = tie(dx1, fo1)
    d0, up0, gz0, du0, df0, do0, sums0, inner0 = layer_bwd(plan, dx1, up1, r1, r2, u, packed0, stacked[0])
    d0, rest1 = tie(d0, rest1)
    dc0 = exchange(d0)
    fo0, rest0 = grads(gz0, du0, df0, do0, y0, ctx0, sums0, inner0)
    dc0, fo0, rest0, own1 = tie(dc0, fo0, rest0, own1)
    fo0, rest0 = scattered(fo0), scattered(rest0)
    sent1 = seq_send([fo1, rest1])
    dx0 = attn_bwd(plan, tables[0], x0, dc0)
    dx0, sent1 = tie(dx0, sent1)
    own0 = own_grad(plan, item, hidden_all, dx0)
    dx0 = exchange(dx0)
    dx0, own0, part1 = tie(dx0, own0, seq_sum(sent1))
    own0 = scattered(own0)
    full1 = seq_gather(part1)
    input_grad = layer_tail(plan, dx0, up0, columns0)
    full0 = seq_gather(seq_sum(seq_send([fo0, rest0])))
    owns = seq_gather(jnp.concatenate([own0, own1]))
    qkv, bias, attn, inner_grad, outer, *small_grads = finish(
        plan, share, w_ffn_in.shape[2], item, counts, (full0, full1), owns
    )
    bias_q, bias_v = (lax.dynamic_slice_in_dim(bias, part * D + item_rank * share, share, 1) for part in (0, 2))
    out_bias, gain1, shift1, inner_bias, ffn_bias, gain2, shift2 = small_grads
    return (
        output.reshape(hidden.shape),
        input_grad.reshape(hidden.shape),
        qkv,
        bias_q,
        bias_v,
        attn,
        out_bias,
        gain1,
        shift1,
        inner_grad,
        inner_bias,
        outer,
        ffn_bias,
        gain2,
        shift2,
    )


def solution(mesh):
    placed = (
        P("item", "seq", None),
        P("item", None, "seq", None, None),
        P(None, "item", None),
        P(None, "item"),
        P(None, "item"),
        P(None, "item", None),
        P(None, "item"),
        P(None, "item"),
        P(None, "item"),
        P(None, "item", None),
        P(None, "item"),
        P(None, "item", None),
        P(None, "item"),
        P(None, "item"),
        P(None, "item"),
        P("item", "seq", None),
    )
    return jax.shard_map(
        local,
        mesh=mesh,
        in_specs=placed,
        out_specs=(
            P("item", "seq", None),
            P("item", "seq", None),
            P(None, "item", None),
            P(None, "item"),
            P(None, "item"),
            P(None, "item", None),
            P(None, "item"),
            P(None, "item"),
            P(None, "item"),
            P(None, "item", None),
            P(None, "item"),
            P(None, "item", None),
            P(None, "item"),
            P(None, "item"),
            P(None, "item"),
        ),
        check_vma=False,
    )
```

```python
from functools import partial

import jax
import jax.numpy as jnp
from jax import lax
from jax.experimental import pallas as pl
from jax.experimental.pallas import tpu as pltpu
from jax.sharding import PartitionSpec as P

D = 768
H = 12
HD = 64
BLK = 64
RAND = 3
LAYERS = 2
LISTED = 5 + RAND
KEYS = LISTED * BLK
WIDE = 2 * HD
F32 = jnp.float32
BF = jnp.bfloat16
LOG2E = 1.4426950408889634
epsilon = 1e-05
NT = (((1,), (1,)), ((), ()))
TN = (((0,), (0,)), ((), ()))
NN = (((1,), (0,)), ((), ()))
VMEM = pltpu.VMEM


def dot(a, b, dims):
    return lax.dot_general(a, b, dims, preferred_element_type=F32)


class Plan:
    def __init__(self, groups, tokens, half=128):
        self.groups = groups
        self.tokens = tokens
        self.hp = -(-H // groups)
        self.pairs = self.hp // 2
        self.odd = self.hp % 2
        self.half = min(half, tokens // 2)
        self.chunks = tokens // 2 // self.half
        self.per = self.half // BLK
        self.rows = 2 * self.half
        self.xp = 2 * self.hp + 2 * self.pairs + self.odd
        self.cp = 2 * self.pairs + self.odd
        self.blocks = groups * tokens // BLK
        self.own = (2 * self.hp + self.hp) * HD
        self.cols = groups * self.own
        self.ctx = groups * self.hp * HD

    def x_shape(self):
        return (self.groups, self.chunks, self.xp, self.per, BLK, WIDE)

    def c_shape(self):
        return (self.groups, self.chunks, self.cp, self.per, BLK, WIDE)


def low(v):
    return jnp.concatenate([v, jnp.zeros_like(v)], 1)


def high(v):
    return jnp.concatenate([jnp.zeros_like(v), v], 1)


def diag(a, b):
    return jnp.concatenate(
        [jnp.concatenate([a, jnp.zeros_like(b)], 1), jnp.concatenate([jnp.zeros_like(a), b], 1)], 0
    )


def spots(plan, h, i):
    per = plan.per
    xb = (i // per) * (plan.xp * per) + i % per
    cb = (i // per) * (plan.cp * per) + i % per
    if h < 2 * plan.pairs:
        lanes = slice((h % 2) * HD, (h % 2 + 1) * HD)
        x0 = xb + (2 * plan.hp + 2 * (h // 2)) * per
        c0 = cb + 2 * (h // 2) * per
        return ((x0, lanes), (x0 + per, lanes)), ((c0, lanes), (c0 + per, lanes))
    x0 = xb + (2 * plan.hp + 2 * plan.pairs) * per
    c0 = cb + 2 * plan.pairs * per
    first, second = slice(0, HD), slice(HD, WIDE)
    return ((x0, first), (x0, second)), ((c0, first), (c0, second))


def listed(plan, x_ref, lists_ref, h, i):
    sides, places = [], []
    for side in range(2):
        at = ((h * (plan.blocks // 2) + i) * 2 + side) * LISTED
        ids = [lists_ref[at + n] for n in range(LISTED)]
        sides.append(jnp.concatenate([x_ref[n] for n in ids], 0))
        places.append(ids)
    return jnp.concatenate(sides, 1), places


def run_pairs(count, hp, first, second, third):
    for h in range(hp):
        first(0, h, 0)

    def body(i, carry):
        for u in range(2):
            t = 2 * i + u
            for h in range(hp):
                first(jnp.minimum(t + 1, count - 1), h, 1 - u)
                second(h, u)
                third(jnp.maximum(t - 1, 0), h, 1 - u)
        return carry

    lax.fori_loop(0, count // 2, body, 0)
    for h in range(hp):
        third(count - 1, h, 1)


def keys_of(plan, x_ref, h, n):
    per = plan.per
    at = (n * plan.xp + 2 * h) * per
    return pl.ds(at, 2 * per)


def attn_fwd_kernel(plan, lists_ref, x_ref, o_ref, s_ref, p_ref, g_ref, a_ref):
    c = LOG2E * HD**-0.5
    hp, count = plan.hp, plan.blocks // 2
    heads = range(hp)

    def stage_s(i, h, slot):
        kv, _ = listed(plan, x_ref, lists_ref, h, i)
        ((xa, la), (xb, lb)), _ = spots(plan, h, i)
        s_ref[slot, h] = dot(kv, diag(low(x_ref[xa, :, la]), low(x_ref[xb, :, lb])), NT)

    def stage_p(h, slot):
        s = s_ref[slot, h]
        m = jnp.max(s, 0, keepdims=True)
        e = jnp.exp2(s * c - m * c)
        inv = 1.0 / jnp.sum(e, 0, keepdims=True)
        p_ref[slot, h] = (e * inv).astype(BF)

    def stage_c(i, h, slot):
        kv, _ = listed(plan, x_ref, lists_ref, h, i)
        _, ((ca, la), (cb, lb)) = spots(plan, h, i)
        ctx = dot(p_ref[slot, h], kv, TN)
        o_ref[ca, :, la] = ctx[:BLK, HD:WIDE].astype(BF)
        o_ref[cb, :, lb] = ctx[BLK:, WIDE + HD :].astype(BF)

    p_ref[...] = jnp.zeros_like(p_ref)
    run_pairs(count, hp, stage_s, stage_p, stage_c)
    size = plan.rows
    steps = plan.groups * plan.chunks
    ws, outs = [], []
    for h in heads:
        ((xa, la), _), (c_first, _) = spots(plan, h, 0)
        (_, (xb, lb)), (_, c_last) = spots(plan, h, count - 1)
        ws.append(low(jnp.concatenate([x_ref[xa, :, la], x_ref[xb, :, lb]], 0)))
        outs.append((c_first, c_last))

    def chunk(n):
        return pl.ds(pl.multiple_of(n * size, size), size)

    def keys(h, n):
        return x_ref[keys_of(plan, x_ref, h, n)].reshape(size, WIDE)

    def one(n, ms):
        out = []
        for h in heads:
            s = dot(keys(h, n), ws[h], NT)
            g_ref[h, chunk(n), :] = s
            out.append(jnp.maximum(ms[h], jnp.max(s, 0, keepdims=True)))
        return tuple(out)

    ms = lax.fori_loop(
        0, steps, one, tuple(jnp.full((1, 2 * BLK), -jnp.inf, F32) for h in heads), unroll=2
    )

    def two(n, ls):
        out = []
        for h in heads:
            e = jnp.exp2(g_ref[h, chunk(n), :] * c - ms[h] * c)
            g_ref[h, chunk(n), :] = e
            out.append(ls[h] + jnp.sum(e, 0, keepdims=True))
        return tuple(out)

    ls = lax.fori_loop(0, steps, two, tuple(jnp.zeros((1, 2 * BLK), F32) for h in heads), unroll=2)
    invs = [1.0 / l for l in ls]
    a_ref[...] = jnp.zeros_like(a_ref)

    def three(n, carry):
        for h in heads:
            p = g_ref[h, chunk(n), :] * invs[h]
            hi = p.astype(BF)
            lo = (p - hi.astype(F32)).astype(BF)
            a_ref[h] += dot(jnp.concatenate([hi, lo], 1), keys(h, n), TN)
        return carry

    lax.fori_loop(0, steps, three, 0, unroll=2)
    for h in heads:
        ctx = (a_ref[h, : 2 * BLK, :] + a_ref[h, 2 * BLK :, :])[:, HD:].astype(BF)
        (ca, la), (cb, lb) = outs[h]
        o_ref[ca, :, la] = ctx[:BLK]
        o_ref[cb, :, lb] = ctx[BLK:]


def attn_fwd(plan, lists, x):
    flat = x.reshape(-1, BLK, WIDE)
    blocks = plan.groups * plan.chunks * plan.cp * plan.per
    keys = plan.blocks * BLK
    return pl.pallas_call(
        partial(attn_fwd_kernel, plan),
        out_shape=jax.ShapeDtypeStruct((blocks, BLK, WIDE), BF),
        in_specs=[pl.BlockSpec(memory_space=pltpu.SMEM), pl.BlockSpec(memory_space=VMEM)],
        out_specs=pl.BlockSpec(memory_space=VMEM),
        scratch_shapes=[
            VMEM((2, plan.hp, KEYS, 2 * BLK), F32),
            VMEM((2, plan.hp, KEYS, 2 * BLK), BF),
            VMEM((plan.hp, keys, 2 * BLK), F32),
            VMEM((plan.hp, 4 * BLK, WIDE), F32),
        ],
        compiler_params=pltpu.CompilerParams(vmem_limit_bytes=48 << 20),
        cost_estimate=pl.CostEstimate(flops=26 * 10**9, bytes_accessed=6 * 10**6, transcendentals=6 * 10**6),
        name="attn_fwd",
    )(lists, flat).reshape(plan.c_shape())


def attn_bwd_kernel(plan, lists_ref, x_ref, d_ref, o_ref, acc_ref, s_ref, p_ref, g_ref):
    scale = HD**-0.5
    c = LOG2E * scale
    hp, count = plan.hp, plan.blocks // 2
    heads = range(hp)
    acc_ref[...] = jnp.zeros_like(acc_ref)

    def weights(i, h):
        ((xa, xla), (xb, xlb)), ((ca, cla), (cb, clb)) = spots(plan, h, i)
        da, db = d_ref[ca, :, cla], d_ref[cb, :, clb]
        da = jnp.where(i == 0, jnp.zeros_like(da), da)
        db = jnp.where(i == count - 1, jnp.zeros_like(db), db)
        return jnp.concatenate(
            [diag(low(x_ref[xa, :, xla]), low(x_ref[xb, :, xlb])), diag(high(da), high(db))], 0
        )

    def stage_s(i, h, slot):
        kv, _ = listed(plan, x_ref, lists_ref, h, i)
        s_ref[slot, h] = dot(kv, weights(i, h), NT)

    def stage_p(h, slot):
        s = s_ref[slot, h, :, : 2 * BLK]
        g = s_ref[slot, h, :, 2 * BLK :]
        m = jnp.max(s, 0, keepdims=True)
        e = jnp.exp2(s * c - m * c)
        inv = 1.0 / jnp.sum(e, 0, keepdims=True)
        delta = jnp.sum(e * g, 0, keepdims=True) * inv
        p = e * inv
        p_ref[slot, h, :, : 2 * BLK] = (p * (g - delta)).astype(BF)
        p_ref[slot, h, :, 2 * BLK :] = p.astype(BF)

    def stage_c(i, h, slot):
        kv, places = listed(plan, x_ref, lists_ref, h, i)
        ((xa, la), (xb, lb)), _ = spots(plan, h, i)
        dq = dot(p_ref[slot, h, :, : 2 * BLK], kv, TN) * scale
        o_ref[xa, :, la] = dq[:BLK, :HD].astype(BF)
        o_ref[xb, :, lb] = dq[BLK:, WIDE : WIDE + HD].astype(BF)
        dkv = dot(p_ref[slot, h], weights(i, h), NN)
        for side in range(2):
            part = dkv[:, side * WIDE : (side + 1) * WIDE]
            for n in range(LISTED):
                acc_ref[places[side][n]] += part[n * BLK : (n + 1) * BLK]

    p_ref[...] = jnp.zeros_like(p_ref)
    run_pairs(count, hp, stage_s, stage_p, stage_c)
    lane_scale = jnp.where(
        lax.broadcasted_iota(jnp.int32, (1, WIDE), 1) < HD, scale, 1.0
    ).astype(F32)
    size = plan.rows
    steps = plan.groups * plan.chunks

    def chunk(n):
        return pl.ds(pl.multiple_of(n * size, size), size)

    for h in heads:
        ((xa, xla), _), ((ca, cla), _) = spots(plan, h, 0)
        (_, (xb, xlb)), (_, (cb, clb)) = spots(plan, h, count - 1)
        q = low(jnp.concatenate([x_ref[xa, :, xla], x_ref[xb, :, xlb]], 0))
        d = high(jnp.concatenate([d_ref[ca, :, cla], d_ref[cb, :, clb]], 0))
        w = jnp.concatenate([q, d], 0)
        three_w = jnp.concatenate([q, d, d], 0)

        def keys(n):
            return x_ref[keys_of(plan, x_ref, h, n)].reshape(size, WIDE)

        def one(n, m):
            s = dot(keys(n), w, NT)
            g_ref[chunk(n), :] = s
            return jnp.maximum(m, jnp.max(s[:, : 2 * BLK], 0, keepdims=True))

        m = lax.fori_loop(0, steps, one, jnp.full((1, 2 * BLK), -jnp.inf, F32), unroll=4)

        def two(n, state):
            l, eg = state
            e = jnp.exp2(g_ref[chunk(n), : 2 * BLK] * c - m * c)
            g_ref[chunk(n), : 2 * BLK] = e
            return (
                l + jnp.sum(e, 0, keepdims=True),
                eg + jnp.sum(e * g_ref[chunk(n), 2 * BLK :], 0, keepdims=True),
            )

        l, eg = lax.fori_loop(0, steps, two, (jnp.zeros((1, 2 * BLK), F32),) * 2, unroll=4)
        inv = 1.0 / l
        delta = eg * inv

        def three(n, dq):
            p = g_ref[chunk(n), : 2 * BLK] * inv
            ds = (p * (g_ref[chunk(n), 2 * BLK :] - delta)).astype(BF)
            hi = p.astype(BF)
            lo = (p - hi.astype(F32)).astype(BF)
            dkv = dot(jnp.concatenate([ds, hi, lo], 1), three_w, NN)
            where = keys_of(plan, x_ref, h, n)
            total = acc_ref[where].reshape(size, WIDE) + dkv
            o_ref[where] = (total * lane_scale).astype(BF).reshape(2 * plan.per, BLK, WIDE)
            return dq + dot(ds, keys(n), TN)

        dq = lax.fori_loop(0, steps, three, jnp.zeros((2 * BLK, WIDE), F32), unroll=4)
        dq = (dq[:, :HD] * scale).astype(BF)
        o_ref[xa, :, xla] = dq[:BLK]
        o_ref[xb, :, xlb] = dq[BLK:]


def attn_bwd(plan, lists, x, d):
    flat = x.reshape(-1, BLK, WIDE)
    keys = plan.blocks * BLK
    return pl.pallas_call(
        partial(attn_bwd_kernel, plan),
        out_shape=jax.ShapeDtypeStruct(flat.shape, BF),
        in_specs=[pl.BlockSpec(memory_space=pltpu.SMEM)] + [pl.BlockSpec(memory_space=VMEM)] * 2,
        out_specs=pl.BlockSpec(memory_space=VMEM),
        scratch_shapes=[
            VMEM(flat.shape, F32),
            VMEM((2, plan.hp, KEYS, 4 * BLK), F32),
            VMEM((2, plan.hp, KEYS, 4 * BLK), BF),
            VMEM((keys, 4 * BLK), F32),
        ],
        compiler_params=pltpu.CompilerParams(vmem_limit_bytes=56 << 20),
        cost_estimate=pl.CostEstimate(flops=46 * 10**9, bytes_accessed=12 * 10**6, transcendentals=6 * 10**6),
        name="attn_bwd",
    )(lists, flat, d.reshape(-1, BLK, WIDE)).reshape(plan.x_shape())


def mean(v):
    return jnp.sum(v, -1, keepdims=True) * (1.0 / v.shape[-1])


def normalise(resid):
    centre = resid - mean(resid)
    inv = lax.rsqrt(mean(centre * centre) + epsilon)
    return centre * inv, inv


def norm_back(unit, inv, gain, grad):
    g = grad * gain
    return inv * (g - mean(g) - unit * mean(g * unit))


def gelu_parts(u):
    k = 0.7978845608028654
    sq = u * u
    t = jnp.tanh(k * (u + 0.044715 * (u * sq)))
    half = 0.5 * (1.0 + t)
    return half * u, half + 0.5 * u * (1.0 - t * t) * (k + (3 * 0.044715 * k) * sq)


def rows_of(ref):
    return ref[...].reshape(-1, ref.shape[-1])


def pick_context(plan, pieces):
    half = plan.half
    tiles = []
    for g in range(plan.groups):
        for p in range(plan.pairs):
            tiles.append(pieces[g, 2 * p : 2 * p + 2].reshape(plan.rows, WIDE))
        if plan.odd:
            both = pieces[g, 2 * plan.pairs].reshape(half, WIDE)
            tiles.append(jnp.concatenate([both[:, :HD], both[:, HD:]], 0))
    return jnp.concatenate(tiles, 1)[:, :D]


def put_context(plan, value, ref):
    half, per = plan.half, plan.per
    if plan.ctx > D:
        value = jnp.concatenate([value, jnp.zeros((value.shape[0], plan.ctx - D), value.dtype)], 1)
    for g in range(plan.groups):
        at = g * plan.hp * HD
        for p in range(plan.pairs):
            ref[g, 2 * p : 2 * p + 2] = value[:, at : at + WIDE].reshape(2, per, BLK, WIDE)
            at += WIDE
        if plan.odd:
            one = value[:, at : at + HD]
            ref[g, 2 * plan.pairs] = jnp.concatenate([one[:half], one[half:]], 1).reshape(per, BLK, WIDE)


def put_heads(plan, value, ref):
    half, per, hp = plan.half, plan.per, plan.hp
    pairs_at = plan.groups * hp * WIDE
    single_at = pairs_at + plan.groups * plan.pairs * WIDE
    for g in range(plan.groups):
        for h in range(hp):
            at = (g * hp + h) * WIDE
            ref[g, 2 * h : 2 * h + 2] = value[:, at : at + WIDE].reshape(2, per, BLK, WIDE)
        for p in range(plan.pairs):
            at = pairs_at + (g * plan.pairs + p) * WIDE
            ref[g, 2 * hp + 2 * p : 2 * hp + 2 * p + 2] = value[:, at : at + WIDE].reshape(2, per, BLK, WIDE)
        if plan.odd:
            at = single_at + g * HD
            one = value[:, at : at + HD]
            ref[g, plan.xp - 1] = jnp.concatenate([one[:half], one[half:]], 1).reshape(per, BLK, WIDE)


def pick_heads(plan, pieces):
    half, hp = plan.half, plan.hp
    kv, pairs, singles = [], [], []
    for g in range(pieces.shape[0]):
        for h in range(hp):
            kv.append(pieces[g, 2 * h : 2 * h + 2].reshape(plan.rows, WIDE))
        for p in range(plan.pairs):
            pairs.append(pieces[g, 2 * hp + 2 * p : 2 * hp + 2 * p + 2].reshape(plan.rows, WIDE))
        if plan.odd:
            both = pieces[g, plan.xp - 1].reshape(half, WIDE)
            singles.append(jnp.concatenate([both[:, :HD], both[:, HD:]], 0))
    return jnp.concatenate(kv + pairs + singles, 1)


def whole(shape):
    return pl.BlockSpec(shape, lambda *i: (0,) * len(shape), pipeline_mode=pl.Buffered(1))


MESH = pl.DeviceIdType.MESH
SMALL = 32


def start_kernel(plan, item, hid_ref, shard_ref, small_ref, ids_ref, all_ref, x_ref, small_all_ref, ids_all_ref,
                 hall, wall, xall, h_send, h_recv, i_send, i_recv, w_send, w_recv, v_send, v_recv, local_sem):
    groups = plan.groups
    me = lax.axis_index("seq")
    rank = lax.axis_index("item")
    seq_peers = [lax.rem(me + k, groups) for k in range(1, groups)]
    item_peers = [lax.rem(rank + k, item) for k in range(1, item)]
    barrier = pltpu.get_barrier_semaphore()
    for p in seq_peers:
        pl.semaphore_signal(barrier, inc=1, device_id=(p, rank), device_id_type=MESH)
    for p in item_peers:
        pl.semaphore_signal(barrier, inc=1, device_id=(me, p), device_id_type=MESH)
    pl.semaphore_wait(barrier, len(seq_peers) + len(item_peers))

    def remote(src, dst, send, recv, seq, it):
        copy = pltpu.make_async_remote_copy(
            src_ref=src, dst_ref=dst, send_sem=send, recv_sem=recv, device_id=(seq, it), device_id_type=MESH
        )
        copy.start()
        return copy

    if groups == 4:
        xn = me + 1 - 2 * lax.rem(me, 2)
        yn = lax.rem(me + 2, 4)
        dn = lax.rem(xn + 2, 4)
        order = [xn, yn, dn]

        def to(n, half):
            return remote(hid_ref.at[half], hall.at[me, half], h_send.at[n, half], h_recv.at[n, half], (xn, yn)[n], rank)

        sent = {(0, 0): to(0, 0), (1, 1): to(1, 1)}
        sent[0, 1] = to(0, 1)
        sent[1, 0] = to(1, 0)
    else:
        order = [lax.rem(me + groups - k, groups) for k in range(1, groups)]
        sent = {}
        for k, p in enumerate(seq_peers):
            for half in range(2):
                sent[k, half] = remote(hid_ref.at[half], hall.at[me, half], h_send.at[k, half], h_recv.at[k, half], p, rank)
    shards = [remote(shard_ref, wall.at[rank], w_send.at[k], w_recv.at[k], me, p) for k, p in enumerate(item_peers)]
    smalls = [remote(small_ref, small_all_ref.at[rank], v_send.at[k], v_recv.at[k], me, p) for k, p in enumerate(item_peers)]
    lists = [remote(ids_ref.at[p], ids_all_ref.at[me], i_send.at[k], i_recv.at[k], p, rank) for k, p in enumerate(seq_peers)]
    mine = [
        pltpu.make_async_copy(hid_ref, all_ref.at[me], local_sem.at[0]),
        pltpu.make_async_copy(hid_ref, hall.at[me], local_sem.at[1]),
    ]
    for copy in mine:
        copy.start()
    wall[rank] = shard_ref[...]
    small_all_ref[rank] = small_ref[...]
    ids_all_ref[me] = ids_ref[me]
    for copy in shards:
        copy.wait()
    mine[1].wait()
    share = D // item
    one = Plan.__new__(Plan)
    one.__dict__.update(plan.__dict__)
    one.groups = 1
    out = []

    def project(source, n):
        weight = wall[:, :share].reshape(D, plan.own)
        bias = jnp.sum(wall[:, share : share + 1].astype(F32), 0)

        def chunk(c, carry):
            rows = pl.ds(pl.multiple_of(c * plan.half, plan.half), plan.half)
            a = jnp.concatenate([hall[source, 0, rows], hall[source, 1, rows]], 0)
            put_heads(one, (dot(a, weight, NN) + bias).astype(BF), xall.at[pl.ds(source, 1), c])
            return carry

        lax.fori_loop(0, plan.chunks, chunk, 0)
        copy = pltpu.make_async_copy(xall.at[source], x_ref.at[source], local_sem.at[2 + n])
        copy.start()
        out.append(copy)

    if groups == 4:
        sent[0, 0].wait_recv()
        forward = [remote(hall.at[xn, 0], hall.at[xn, 0], h_send.at[2, 0], h_recv.at[2, 0], yn, rank)]
        sent[1, 1].wait_recv()
        forward.append(remote(hall.at[yn, 1], hall.at[yn, 1], h_send.at[2, 1], h_recv.at[2, 1], xn, rank))
        project(me, 0)
        sent[0, 1].wait_recv()
        project(xn, 1)
        sent[1, 0].wait_recv()
        project(yn, 2)
        for copy in forward:
            copy.wait_recv()
        project(dn, 3)
        ends = list(sent.values()) + forward
    else:
        project(me, 0)
        for k in range(groups - 1):
            for half in range(2):
                sent[k, half].wait_recv()
            project(order[k], k + 1)
        ends = list(sent.values())
    for k, source in enumerate(order):
        copy = pltpu.make_async_copy(hall.at[source], all_ref.at[source], local_sem.at[2 + groups + k])
        copy.start()
        out.append(copy)
    for copy in ends:
        copy.wait_send()
    for copy in smalls + lists:
        copy.wait()
    mine[0].wait()
    for copy in out:
        copy.wait()


def start(plan, item, hidden_low, shard, small, ids):
    g = plan.groups
    dma = pltpu.SemaphoreType.DMA
    hid = hidden_low.reshape(2, plan.tokens // 2, D)
    return pl.pallas_call(
        partial(start_kernel, plan, item),
        out_shape=[
            jax.ShapeDtypeStruct((g,) + hid.shape, BF),
            jax.ShapeDtypeStruct(plan.x_shape(), BF),
            jax.ShapeDtypeStruct((item,) + small.shape, BF),
            jax.ShapeDtypeStruct(ids.shape, jnp.int32),
        ],
        in_specs=[pl.BlockSpec(memory_space=VMEM)] * 4,
        out_specs=[pl.BlockSpec(memory_space=pl.ANY)] * 2 + [pl.BlockSpec(memory_space=VMEM)] * 2,
        scratch_shapes=[
            VMEM((g,) + hid.shape, BF),
            VMEM((item,) + shard.shape, BF),
            VMEM(plan.x_shape(), BF),
            dma((g - 1, 2)),
            dma((g - 1, 2)),
            dma((g - 1,)),
            dma((g - 1,)),
            dma((item - 1,)),
            dma((item - 1,)),
            dma((item - 1,)),
            dma((item - 1,)),
            dma((2 + 2 * g,)),
        ],
        compiler_params=pltpu.CompilerParams(collective_id=1, has_side_effects=True, vmem_limit_bytes=40 << 20),
        cost_estimate=pl.CostEstimate(flops=55 * 10**9, bytes_accessed=12 * 10**6, transcendentals=0),
        name="start",
    )(hid, shard, small, ids)


def own_grad_kernel(plan, item, steps, a_ref, d_ref, o_ref, acc_ref, sum_ref):
    n = pl.program_id(0) * plan.chunks + pl.program_id(1)

    @pl.when(n == 0)
    def _():
        acc_ref[...] = jnp.zeros_like(acc_ref)
        sum_ref[...] = jnp.zeros_like(sum_ref)

    d = pick_heads(plan, d_ref[:, 0])
    acc_ref[...] += dot(a_ref[...].reshape(plan.rows, D), d, TN)
    sum_ref[...] += jnp.sum(d.astype(F32).reshape(-1, 8, d.shape[1]), 0)

    @pl.when(n == steps - 1)
    def _():
        share = D // item
        total = jnp.broadcast_to(jnp.sum(sum_ref[...], 0, keepdims=True), (16, sum_ref.shape[1])).astype(BF)
        own = sum_ref.shape[1]
        for r in range(item):
            o_ref[r, :share, :own] = acc_ref[r * share : (r + 1) * share].astype(BF)
            o_ref[r, share:, :own] = total
            o_ref[r, :, own:] = jnp.zeros((share + 16, o_ref.shape[2] - own), BF)


def own_grad(plan, item, hidden_all, dx):
    a = hidden_all.reshape(plan.groups, 2, plan.chunks, plan.half, D)
    return pl.pallas_call(
        partial(own_grad_kernel, plan, item, plan.groups * plan.chunks),
        out_shape=jax.ShapeDtypeStruct((item, D // item + 16, D), BF),
        grid=(plan.groups, plan.chunks),
        in_specs=[
            pl.BlockSpec((1, 2, 1, plan.half, D), lambda g, c: (g, 0, c, 0, 0)),
            pl.BlockSpec((1, 1) + plan.x_shape()[2:], lambda g, c: (g, c, 0, 0, 0, 0)),
        ],
        out_specs=whole((item, D // item + 16, D)),
        scratch_shapes=[VMEM((D, plan.own), F32), VMEM((8, plan.own), F32)],
        compiler_params=pltpu.CompilerParams(vmem_limit_bytes=48 << 20),
        cost_estimate=pl.CostEstimate(flops=7 * 10**9, bytes_accessed=12 * 10**6, transcendentals=0),
        name="own_grad",
    )(a, dx)


def halves(plan, width):
    return pl.BlockSpec((2, plan.half, width), lambda c: (0, c, 0))


def cut(plan, v):
    return v.reshape(2, plan.tokens // 2, v.shape[-1])


def read(ref):
    return ref[...].reshape(-1, ref.shape[-1])


def write(ref, value):
    ref[...] = value.reshape(ref.shape).astype(ref.dtype)


class Packed:
    def __init__(self, ref, ff):
        self.ref = ref
        self.item = ref.shape[0]
        self.share = D // self.item
        self.parts = ff // D

    def rows(self, first):
        return self.ref[:, first : first + self.share].reshape(D, D)

    def out(self):
        return self.rows(0)

    def ffn_in(self, n):
        return self.rows(self.share * (1 + n))

    def ffn_out(self, n):
        ranks = self.item // self.parts
        first = self.share * (1 + self.parts)
        return self.ref[n * ranks : (n + 1) * ranks, first : first + self.share * self.parts].reshape(D, D)


def column_part(ref, n):
    share = D // ref.shape[0]
    return ref[:, n * share : (n + 1) * share].reshape(D, D)


def wide_parts(w):
    return jnp.concatenate([w[:, n : n + D] for n in range(0, w.shape[1], D)])


OUT_BIAS, GAIN1, SHIFT1, FFN_BIAS, GAIN2, SHIFT2 = range(6)


def first_half(plan, ctx, h, w, vec_ref):
    r1 = h + dot(ctx, w.out(), NN) + vec_ref[OUT_BIAS : OUT_BIAS + 1]
    unit1, inv1 = normalise(r1)
    y1 = unit1 * vec_ref[GAIN1 : GAIN1 + 1] + vec_ref[SHIFT1 : SHIFT1 + 1]
    return r1, unit1, inv1, y1, y1.astype(BF)


def part_of(n):
    return slice(n * D, (n + 1) * D)


def put(ref, n, value):
    ref[:, :, part_of(n)] = value.reshape(ref.shape[:2] + (D,)).astype(ref.dtype)


def get(ref, n):
    return ref[:, :, part_of(n)].reshape(-1, D)


class Swap:
    def __init__(self, plan, src, buf, send, recv, own):
        self.plan, self.src, self.buf, self.send, self.recv, self.own = plan, src, buf, send, recv, own
        self.me = lax.axis_index("seq")
        self.rank = lax.axis_index("item")

    def copy(self, c, k):
        peer = lax.rem(self.me + k, self.plan.groups)
        return pltpu.make_async_remote_copy(
            src_ref=self.src.at[peer, c],
            dst_ref=self.buf.at[self.me, c],
            send_sem=self.send.at[c, k - 1],
            recv_sem=self.recv.at[c, k - 1],
            device_id=(peer, self.rank),
            device_id_type=MESH,
        )

    def local(self):
        return pltpu.make_async_copy(self.src.at[self.me], self.buf.at[self.me], self.own.at[0])

    def step(self):
        c, groups = pl.program_id(0), self.plan.groups

        @pl.when(c == 0)
        def _():
            barrier = pltpu.get_barrier_semaphore()
            for k in range(1, groups):
                peer = lax.rem(self.me + k, groups)
                pl.semaphore_signal(barrier, inc=1, device_id=(peer, self.rank), device_id_type=MESH)
            pl.semaphore_wait(barrier, groups - 1)
            self.local().start()
            for n in range(self.plan.chunks):
                for k in range(1, groups):
                    self.copy(n, k).start()
            self.local().wait()

        for k in range(1, groups):
            self.copy(c, k).wait_recv()
        return self.buf[:, c]

    def end(self):
        c = pl.program_id(0)
        for k in range(1, self.plan.groups):
            self.copy(c, k).wait_send()

    @staticmethod
    def scratch(plan, shape):
        sems = (plan.chunks, plan.groups - 1)
        dma = pltpu.SemaphoreType.DMA
        return [VMEM(shape, BF), dma(sems), dma(sems), dma((1,))]


def swap_params(number):
    return pltpu.CompilerParams(collective_id=number, has_side_effects=True, vmem_limit_bytes=60 << 20)


def fwd_kernel(plan, ff, c_ref, h_ref, w_ref, vec_ref, inner_ref,
               next_ref, next_low_ref, r1_ref, r2_ref, u_ref, y_ref, ctx_ref, *swapping):
    swap = Swap(plan, c_ref, *swapping)
    w = Packed(w_ref, ff)
    ctx = pick_context(plan, swap.step())
    write(ctx_ref, ctx)
    r1, _, _, y1, y1_low = first_half(plan, ctx, read(h_ref), w, vec_ref)
    write(r1_ref, r1)
    write(y_ref, y1_low)
    r2 = y1 + vec_ref[FFN_BIAS : FFN_BIAS + 1]
    for n in range(w.parts):
        u = dot(y1_low, w.ffn_in(n), NN) + inner_ref[:, part_of(n)]
        put(u_ref, n, u)
        r2 = r2 + dot(gelu_parts(u)[0].astype(BF), w.ffn_out(n), NN)
    write(r2_ref, r2)
    unit2, _ = normalise(r2)
    nxt = unit2 * vec_ref[GAIN2 : GAIN2 + 1] + vec_ref[SHIFT2 : SHIFT2 + 1]
    low_ = nxt.astype(BF)
    write(next_ref, nxt)
    write(next_low_ref, low_)
    swap.end()


def project_kernel(plan, a_ref, w_ref, bias_ref, x_ref):
    a = read(a_ref)
    y = [
        (dot(a, column_part(w_ref, n), NN) + bias_ref[:, part_of(n)]).astype(BF) for n in range(plan.cols // D)
    ]
    put_heads(plan, jnp.concatenate(y, 1), x_ref.at[:, 0])


def piece_spec(shape):
    return pl.BlockSpec((shape[0], 1) + shape[2:], lambda c: (0, c, 0, 0, 0, 0))


def layer_fwd(plan, ctx, h, packed, vec, inner):
    t = (2, plan.tokens // 2)
    ff = inner.shape[-1]
    shapes = [(D, F32), (D, BF), (D, F32), (D, F32), (ff, F32), (D, BF), (D, BF)]
    return pl.pallas_call(
        partial(fwd_kernel, plan, ff),
        out_shape=[jax.ShapeDtypeStruct(t + (n,), d) for n, d in shapes],
        grid=(plan.chunks,),
        in_specs=[pl.BlockSpec(memory_space=pl.ANY), halves(plan, D)] + [whole(w.shape) for w in (packed, vec, inner)],
        out_specs=[halves(plan, n) for n, _ in shapes],
        scratch_shapes=Swap.scratch(plan, plan.c_shape()),
        compiler_params=swap_params(2),
        cost_estimate=pl.CostEstimate(flops=24 * 10**9, bytes_accessed=50 * 10**6, transcendentals=3 * 10**6),
        name="layer_fwd",
    )(ctx, cut(plan, h), packed, vec, inner)


def project(plan, a, columns, bias):
    return pl.pallas_call(
        partial(project_kernel, plan),
        out_shape=jax.ShapeDtypeStruct(plan.x_shape(), BF),
        grid=(plan.chunks,),
        in_specs=[halves(plan, D), whole(columns.shape), whole(bias.shape)],
        out_specs=piece_spec(plan.x_shape()),
        compiler_params=pltpu.CompilerParams(vmem_limit_bytes=48 << 20),
        cost_estimate=pl.CostEstimate(flops=8 * 10**9, bytes_accessed=10 * 10**6, transcendentals=0),
        name="project",
    )(a, columns, bias)


SUM_DO, D_GAIN1, D_SHIFT1, SUM_DF, D_GAIN2, D_SHIFT2 = range(6)


def add_sums(ref, at, value):
    ref[at] += jnp.sum(value.reshape(-1, 8, value.shape[-1]), 0)


def back_chunk(plan, gy, unit1, inv1, unit2, inv2, gate, w, vec_ref, sums_ref, inner_sum_ref, du_ref):
    @pl.when(pl.program_id(0) == 0)
    def _():
        sums_ref[...] = jnp.zeros_like(sums_ref)
        inner_sum_ref[...] = jnp.zeros_like(inner_sum_ref)

    dr2 = norm_back(unit2, inv2, vec_ref[GAIN2 : GAIN2 + 1], gy)
    df = dr2.astype(BF)
    dy1 = dr2
    for n in range(w.parts):
        du = (dot(df, w.ffn_out(n), NT) * gate(n)).astype(BF)
        put(du_ref, n, du)
        dy1 = dy1 + dot(du, w.ffn_in(n), NT)
        inner_sum_ref[:, part_of(n)] += jnp.sum(du.astype(F32).reshape(-1, 8, D), 0)
    dr1 = norm_back(unit1, inv1, vec_ref[GAIN1 : GAIN1 + 1], dy1)
    do = dr1.astype(BF)
    dc = dot(do, w.out(), NT).astype(BF)
    add_sums(sums_ref, SUM_DO, do.astype(F32))
    add_sums(sums_ref, D_GAIN1, dy1 * unit1)
    add_sums(sums_ref, D_SHIFT1, dy1)
    add_sums(sums_ref, SUM_DF, df.astype(F32))
    add_sums(sums_ref, D_GAIN2, gy * unit2)
    add_sums(sums_ref, D_SHIFT2, gy)
    return df, dr1, do, dc


def mid_kernel(plan, ff, c_ref, h_ref, gy_ref, w_ref, vec_ref, inner_ref,
               d_ref, out_ref, dr1_ref, gz_ref, du_ref, df_ref, do_ref, y_ref, ctx_ref, sums_ref, inner_sum_ref, gate_ref, *swapping):
    swap = Swap(plan, c_ref, *swapping)
    w = Packed(w_ref, ff)
    ctx = pick_context(plan, swap.step())
    write(ctx_ref, ctx)
    _, unit1, inv1, y1, y1_low = first_half(plan, ctx, read(h_ref), w, vec_ref)
    write(y_ref, y1_low)
    r2 = y1 + vec_ref[FFN_BIAS : FFN_BIAS + 1]
    for n in range(w.parts):
        u = dot(y1_low, w.ffn_in(n), NN) + inner_ref[:, part_of(n)]
        gz, gate_ref[n] = gelu_parts(u)
        gz = gz.astype(BF)
        put(gz_ref, n, gz)
        r2 = r2 + dot(gz, w.ffn_out(n), NN)
    unit2, inv2 = normalise(r2)
    write(out_ref, unit2 * vec_ref[GAIN2 : GAIN2 + 1] + vec_ref[SHIFT2 : SHIFT2 + 1])
    df, dr1, do, dc = back_chunk(plan, read(gy_ref), unit1, inv1, unit2, inv2, lambda n: gate_ref[n],
                                 w, vec_ref, sums_ref, inner_sum_ref, du_ref)
    put_context(plan, dc, d_ref.at[:, 0])
    write(dr1_ref, dr1)
    write(df_ref, df)
    write(do_ref, do)
    swap.end()


def sum_specs(ff):
    return (
        [jax.ShapeDtypeStruct((6, 8, D), F32), jax.ShapeDtypeStruct((8, ff), F32)],
        [pl.BlockSpec((6, 8, D), lambda c: (0, 0, 0)), pl.BlockSpec((8, ff), lambda c: (0, 0))],
    )


def layer_mid(plan, ctx, h, gy, packed, vec, inner):
    t = (2, plan.tokens // 2)
    ff = inner.shape[-1]
    shapes = [(D, F32), (D, F32), (ff, BF), (ff, BF), (D, BF), (D, BF), (D, BF), (D, BF)]
    sums, sums_at = sum_specs(ff)
    return pl.pallas_call(
        partial(mid_kernel, plan, ff),
        out_shape=[jax.ShapeDtypeStruct(plan.c_shape(), BF)] + [jax.ShapeDtypeStruct(t + (n,), d) for n, d in shapes] + sums,
        grid=(plan.chunks,),
        in_specs=[pl.BlockSpec(memory_space=pl.ANY), halves(plan, D), halves(plan, D)]
        + [whole(w.shape) for w in (packed, vec, inner)],
        out_specs=[piece_spec(plan.c_shape())] + [halves(plan, n) for n, _ in shapes] + sums_at,
        scratch_shapes=[VMEM((ff // D, plan.rows, D), F32)] + Swap.scratch(plan, plan.c_shape()),
        compiler_params=swap_params(3),
        cost_estimate=pl.CostEstimate(flops=45 * 10**9, bytes_accessed=50 * 10**6, transcendentals=3 * 10**6),
        name="layer_mid",
    )(ctx, cut(plan, h), cut(plan, gy), packed, vec, inner)


def bwd_kernel(plan, ff, dx_ref, up_ref, r1_ref, r2_ref, u_ref, w_ref, cols_ref, vec_ref,
               d_ref, dr1_ref, gz_ref, du_ref, df_ref, do_ref, dqkv_ref, sums_ref, inner_sum_ref, qkv_sum_ref, *swapping):
    swap = Swap(plan, dx_ref, *swapping)
    w = Packed(w_ref, ff)
    dqkv = pick_heads(plan, swap.step())
    write(dqkv_ref, dqkv)

    @pl.when(pl.program_id(0) == 0)
    def _():
        qkv_sum_ref[...] = jnp.zeros_like(qkv_sum_ref)

    qkv_sum_ref[...] += jnp.sum(dqkv.astype(F32).reshape(-1, 8, dqkv.shape[-1]), 0)
    gy = read(up_ref)
    for n in range(plan.cols // D):
        gy = gy + dot(dqkv[:, part_of(n)], column_part(cols_ref, n), NT)

    unit1, inv1 = normalise(read(r1_ref))
    unit2, inv2 = normalise(read(r2_ref))

    def gate(n):
        gz, value = gelu_parts(get(u_ref, n))
        put(gz_ref, n, gz)
        return value

    df, dr1, do, dc = back_chunk(plan, gy, unit1, inv1, unit2, inv2, gate, w, vec_ref, sums_ref, inner_sum_ref, du_ref)
    put_context(plan, dc, d_ref.at[:, 0])
    write(dr1_ref, dr1)
    write(df_ref, df)
    write(do_ref, do)
    swap.end()


def layer_bwd(plan, dx, up, r1, r2, u, packed, columns, vec):
    t = (2, plan.tokens // 2)
    ff = u.shape[-1]
    shapes = [(D, F32), (ff, BF), (ff, BF), (D, BF), (D, BF), (plan.cols, BF)]
    sums, sums_at = sum_specs(ff)
    sums = sums + [jax.ShapeDtypeStruct((8, plan.cols), F32)]
    sums_at = sums_at + [pl.BlockSpec((8, plan.cols), lambda c: (0, 0))]
    return pl.pallas_call(
        partial(bwd_kernel, plan, ff),
        out_shape=[jax.ShapeDtypeStruct(plan.c_shape(), BF)] + [jax.ShapeDtypeStruct(t + (n,), d) for n, d in shapes] + sums,
        grid=(plan.chunks,),
        in_specs=[pl.BlockSpec(memory_space=pl.ANY), halves(plan, D), halves(plan, D), halves(plan, D), halves(plan, ff)]
        + [whole(w.shape) for w in (packed, columns, vec)],
        out_specs=[piece_spec(plan.c_shape())] + [halves(plan, n) for n, _ in shapes] + sums_at,
        scratch_shapes=Swap.scratch(plan, plan.x_shape()),
        compiler_params=swap_params(4),
        cost_estimate=pl.CostEstimate(flops=40 * 10**9, bytes_accessed=50 * 10**6, transcendentals=3 * 10**6),
        name="layer_bwd",
    )(dx, up, r1, r2, u, packed, columns, vec)


def dense_grad_kernel(item, gz_ref, df_ref, y_ref, du_ref, ctx_ref, do_ref, vec_ref, fo_ref, rest_ref):
    n = pl.program_id(0)
    parts = pl.num_programs(0)
    share = D // item
    ranks = item // parts
    fo = dot(gz_ref[...], df_ref[...], TN).astype(BF)
    if len(fo_ref.shape) == 3:
        fo_ref[...] = fo.reshape(fo_ref.shape)
    else:
        count, here, rows = fo_ref.shape[:3]
        for r in range(here):
            for g in range(count):
                first = (r * count + g) * rows
                fo_ref[g, r] = fo[first : first + rows]
    first = pl.multiple_of(n * share, 16)
    rest_ref[:, pl.ds(first, share)] = dot(y_ref[...], du_ref[...], TN).astype(BF).reshape(item, share, D)

    @pl.when(n == parts - 1)
    def _():
        at = parts * share
        rest_ref[:, at : at + share] = dot(ctx_ref[...], do_ref[...], TN).astype(BF).reshape(item, share, D)
        rest_ref[:, at + share :] = vec_ref[...]


def dense_grads(item, gz, df, y, du, ctx, do, vecs, cut_for=0):
    tokens, ff = gz.shape
    parts = ff // D
    share = D // item
    rest = parts * share + share + vecs.shape[1]
    column = pl.BlockSpec((tokens, D), lambda n: (0, n))
    fo_shape, fo_spec = (item, ff // item, D), pl.BlockSpec((item // parts, ff // item, D), lambda n: (n, 0, 0))
    if cut_for:
        fo_shape = (cut_for, item, ff // item // cut_for, D)
        fo_spec = pl.BlockSpec((cut_for, item // parts) + fo_shape[2:], lambda n: (0, n, 0, 0))
    return pl.pallas_call(
        partial(dense_grad_kernel, item),
        out_shape=[jax.ShapeDtypeStruct(fo_shape, BF), jax.ShapeDtypeStruct((item, rest, D), BF)],
        grid=(parts,),
        in_specs=[column, whole(df.shape), whole(y.shape), column, whole(ctx.shape), whole(do.shape), whole(vecs.shape)],
        out_specs=[fo_spec, whole((item, rest, D))],
        compiler_params=pltpu.CompilerParams(vmem_limit_bytes=56 << 20),
        cost_estimate=pl.CostEstimate(flops=14 * 10**9, bytes_accessed=30 * 10**6, transcendentals=0),
        name="dense_grads",
    )(gz, df, y, du, ctx, do, vecs)


def column_grad_kernel(item, a_ref, d_ref, vec_ref, o_ref):
    n = pl.program_id(0)
    share = D // item
    first = pl.multiple_of(n * share, 16)
    o_ref[:, pl.ds(first, share)] = dot(a_ref[...], d_ref[...], TN).astype(BF).reshape(item, share, D)

    @pl.when(n == pl.num_programs(0) - 1)
    def _():
        o_ref[:, o_ref.shape[1] - vec_ref.shape[1] :] = vec_ref[...]


def column_grads(item, a, d, vecs):
    tokens = a.shape[0]
    parts = d.shape[1] // D
    out = (item, parts * (D // item) + vecs.shape[1], D)
    return pl.pallas_call(
        partial(column_grad_kernel, item),
        out_shape=jax.ShapeDtypeStruct(out, BF),
        grid=(parts,),
        in_specs=[whole(a.shape), pl.BlockSpec((tokens, D), lambda n: (0, n)), whole(vecs.shape)],
        out_specs=whole(out),
        compiler_params=pltpu.CompilerParams(vmem_limit_bytes=48 << 20),
        cost_estimate=pl.CostEstimate(flops=6 * 10**9, bytes_accessed=10 * 10**6, transcendentals=0),
        name="column_grads",
    )(a, d, vecs)


def tail_kernel(plan, dx_ref, up_ref, w_ref, o_ref):
    dqkv = pick_heads(plan, dx_ref[:, 0])
    out = read(up_ref)
    for n in range(plan.cols // D):
        out = out + dot(dqkv[:, part_of(n)], column_part(w_ref, n), NT)
    write(o_ref, out)


def layer_tail(plan, dx, up, w_qkv):
    return pl.pallas_call(
        partial(tail_kernel, plan),
        out_shape=jax.ShapeDtypeStruct(up.shape, F32),
        grid=(plan.chunks,),
        in_specs=[piece_spec(plan.x_shape()), halves(plan, D), whole(w_qkv.shape)],
        out_specs=halves(plan, D),
        compiler_params=pltpu.CompilerParams(vmem_limit_bytes=48 << 20),
        cost_estimate=pl.CostEstimate(flops=8 * 10**9, bytes_accessed=12 * 10**6, transcendentals=0),
        name="layer_tail",
    )(dx, up, w_qkv)


def finish_kernel(plan, share, counts, seq_first, full_ref, owns_ref, *outs):
    qkv_ref, bias0_ref, biasq_ref, biasv_ref, attn_ref, inner_ref, outer_ref = outs[:7]
    small = outs[7:]
    outer = outer_ref.shape[1]
    parts = inner_ref.shape[2] // D
    hp, pairs, groups = plan.hp, plan.pairs, plan.groups

    def rest(layer, flat, at):
        for n in range(parts):
            inner_ref[layer, :, part_of(n)] = flat[at : at + share].astype(F32)
            at += share
        attn_ref[layer] = flat[at : at + share].astype(F32)
        at += share
        vecs = flat[at : at + 16].astype(F32)
        first = 0
        for ref, n in zip(small, counts):
            ref[layer : layer + 1, :] = vecs[first // D : first // D + 1, first % D : first % D + n]
            first += n
        return at + 16

    def in_order(pieces):
        return jnp.concatenate([pieces[kind, head] for kind in "qkv" for head in range(H)], 1)

    zero = full_ref[...].reshape(-1, D)
    outer_ref[1] = zero[:outer].astype(F32)
    zero = zero[rest(1, zero, outer) :]
    columns = plan.cols // D
    values = jnp.concatenate([zero[n * share : (n + 1) * share] for n in range(columns)], 1).astype(F32)
    at = columns * share
    vec = zero[at : at + 16].astype(F32)
    biasq_ref[...] = vec[:1, :share]
    biasv_ref[...] = vec[:1, share : 2 * share]
    pieces = {}
    for head in range(H):
        g, i = head // hp, head % hp
        pieces["k", head] = values[:, head * WIDE : head * WIDE + HD]
        pieces["v", head] = values[:, head * WIDE + HD : (head + 1) * WIDE]
        first = groups * hp * WIDE
        if i < 2 * pairs:
            first += (g * pairs + i // 2) * WIDE + (i % 2) * HD
        else:
            first += groups * pairs * WIDE + g * HD
        pieces["q", head] = values[:, first : first + HD]
    qkv_ref[1] = in_order(pieces)
    at = rest(0, zero, at + 16)
    own_at = 0
    if seq_first:
        own_at = outer // groups
        for g in range(groups):
            outer_ref[0, g * own_at : (g + 1) * own_at] = owns_ref[g, :own_at].astype(F32)
    else:
        outer_ref[0] = zero[at : at + outer].astype(F32)
    pieces = {}
    for head in range(H):
        g, i = head // hp, head % hp
        rows = owns_ref[g, own_at : own_at + share + 16].astype(F32)
        pieces["k", head] = rows[:, i * WIDE : i * WIDE + HD]
        pieces["v", head] = rows[:, i * WIDE + HD : (i + 1) * WIDE]
        pieces["q", head] = rows[:, (2 * hp + i) * HD : (2 * hp + i + 1) * HD]
    value = in_order(pieces)
    qkv_ref[0] = value[:share]
    bias0_ref[...] = value[share : share + 1]


def finish(plan, share, ff, item, counts, seq_first, full, owns):
    out = [(LAYERS, share, 3 * D), (1, 3 * D), (1, share), (1, share), (LAYERS, share, D), (LAYERS, share, ff), (LAYERS, ff // item, D)]
    out += [(LAYERS, n) for n in counts]
    return pl.pallas_call(
        partial(finish_kernel, plan, share, counts, seq_first),
        out_shape=[jax.ShapeDtypeStruct(s, F32) for s in out],
        in_specs=[pl.BlockSpec(memory_space=VMEM)] * 2,
        out_specs=[pl.BlockSpec(memory_space=VMEM)] * len(out),
        compiler_params=pltpu.CompilerParams(vmem_limit_bytes=48 << 20),
        name="finish",
    )(full, owns)


def column_parts(plan, w):
    lead = w.shape[:-1]
    g, hp = plan.groups, plan.hp
    w = w.reshape(lead + (3, H, HD))
    w = jnp.pad(w, [(0, 0)] * (len(lead) + 1) + [(0, g * hp - H), (0, 0)])
    q, k, v = (w[..., n, :, :] for n in range(3))
    kv = jnp.stack([k, v], -2).reshape(lead + (g, hp * WIDE))
    q = q.reshape(lead + (g, hp, HD))
    pairs = q[..., : 2 * plan.pairs, :].reshape(lead + (g, plan.pairs * WIDE))
    last = q[..., 2 * plan.pairs :, :].reshape(lead + (g, plan.odd * HD))
    return kv, pairs, last


def all_columns(plan, w):
    lead = w.shape[:-1]
    return jnp.concatenate([p.reshape(lead + (-1,)) for p in column_parts(plan, w)], -1)


def own_columns(plan, w, rank):
    axis = w.ndim - 1
    return jnp.concatenate(
        [lax.dynamic_index_in_dim(p, rank, axis, False) for p in column_parts(plan, w)], -1
    )


def natural(plan, kv, pairs, last):
    lead = kv.shape[:-2]
    g, hp = plan.groups, plan.hp
    kv = kv.reshape(lead + (g * hp, 2, HD))
    q = jnp.concatenate(
        [pairs.reshape(lead + (g, 2 * plan.pairs, HD)), last.reshape(lead + (g, plan.odd, HD))], -2
    ).reshape(lead + (g * hp, HD))
    return jnp.concatenate(
        [p[..., :H, :].reshape(lead + (H * HD,)) for p in (q, kv[..., 0, :], kv[..., 1, :])], -1
    )


def from_all(plan, w):
    lead = w.shape[:-1]
    a = plan.groups * plan.hp * WIDE
    b = a + plan.groups * plan.pairs * WIDE
    return natural(plan, *(p.reshape(lead + (plan.groups, -1)) for p in (w[..., :a], w[..., a:b], w[..., b:])))


def exchange(x):
    y = x.reshape((x.shape[0], -1, x.shape[-1]))
    return lax.all_to_all(y, "seq", split_axis=0, concat_axis=0, tiled=True).reshape(x.shape)


def tie(*args):
    return lax.optimization_barrier(args)


def key_table(plan, random_ids):
    n = plan.blocks
    here = n // plan.groups
    j = jnp.arange(n, dtype=jnp.int32)
    shared = jnp.stack(
        [jnp.maximum(j - 1, 0), j, jnp.minimum(j + 1, n - 1), jnp.zeros_like(j), jnp.full_like(j, n - 1)], 1
    )
    ids = jnp.concatenate([jnp.broadcast_to(shared[None], (plan.hp, n, 5)), random_ids], 2)
    inside = ids % here
    r = inside % (here // 2)
    head = jnp.arange(plan.hp, dtype=jnp.int32)[:, None, None]
    piece = 2 * head + inside // (here // 2)
    place = (((ids // here) * plan.chunks + r // plan.per) * plan.xp + piece) * plan.per + r % plan.per
    place = place.reshape(plan.hp, plan.groups, 2, here // 2, LISTED).transpose(0, 1, 3, 2, 4)
    return place.reshape(-1)


def local(
    hidden,
    block_lists,
    w_qkv,
    bias_query,
    bias_value,
    w_attn_out,
    bias_attn_out,
    norm1_gain,
    norm1_shift,
    w_ffn_in,
    bias_ffn_in,
    w_ffn_out,
    bias_ffn_out,
    norm2_gain,
    norm2_shift,
    cotangent,
):
    groups = lax.axis_size("seq")
    item = lax.axis_size("item")
    seq_rank = lax.axis_index("seq")
    item_rank = lax.axis_index("item")
    tokens = hidden.shape[1]
    plan = Plan(groups, tokens)
    here = tokens // BLK
    share = D // item
    ids = jnp.pad(block_lists[0], ((0, 0), (0, 0), (0, groups * plan.hp - H), (0, 0)))
    ids = ids.reshape(LAYERS, here, groups, plan.hp * RAND).transpose(2, 0, 1, 3).reshape(groups, -1)
    used = ids.shape[1]
    ids = jnp.pad(ids, ((0, 0), (0, -used % 1024))).reshape(groups, -1, 128)
    small = (bias_query, bias_value, bias_attn_out, norm1_gain, norm1_shift, bias_ffn_in, bias_ffn_out, norm2_gain, norm2_shift)
    flat_small = jnp.concatenate(small, 1).reshape(-1)
    own_bias = lax.dynamic_update_slice(jnp.zeros((3 * D,), BF), bias_query[0], (item_rank * share,))
    own_bias = lax.dynamic_update_slice(own_bias, bias_value[0], (2 * D + item_rank * share,))
    shard = jnp.concatenate([w_qkv[0], own_bias[None], jnp.zeros((15, 3 * D), BF)])
    hidden_all, x0, small_all, ids = start(
        plan,
        item,
        hidden[0].astype(BF),
        own_columns(plan, shard, seq_rank),
        jnp.pad(flat_small, (0, SMALL * 128 - flat_small.shape[0])).reshape(SMALL, 128),
        ids,
    )
    ids = ids.reshape(groups, -1)[:, :used].reshape(groups, LAYERS, here, plan.hp, RAND)
    ids = ids.transpose(1, 3, 0, 2, 4).reshape(LAYERS, plan.hp, plan.blocks, RAND)
    tables = [key_table(plan, ids[layer]) for layer in range(LAYERS)]
    packed = small_all.reshape(item, -1)[:, : flat_small.shape[0]].reshape(item, LAYERS, -1).astype(F32)
    vectors = []
    for layer in range(LAYERS):
        at, out = 0, []
        for s in small:
            out.append(packed[:, layer, at : at + s.shape[1]].reshape(-1))
            at += s.shape[1]
        vectors.append(out)
    stacked = [jnp.stack(v[2:5] + v[6:9] + [v[2]] * 2) for v in vectors]
    inner = [v[5][None] for v in vectors]
    qkv_bias = [jnp.concatenate([v[0], jnp.zeros_like(v[0]), v[1]])[None] for v in vectors]

    columns = wide_parts(all_columns(plan, w_qkv[0])), wide_parts(all_columns(plan, w_qkv[1]))

    def dense(layer):
        return [w_attn_out[layer], wide_parts(w_ffn_in[layer]), w_ffn_out[layer]]

    packed0 = lax.all_gather(jnp.concatenate(dense(0)), "item", axis=0)
    columns1 = lax.all_gather(columns[1], "item", axis=0)
    packed1 = lax.all_gather(jnp.concatenate(dense(1)), "item", axis=0)
    columns0 = lax.all_gather(columns[0], "item", axis=0)

    ctx0 = attn_fwd(plan, tables[0], x0)
    h1, h1_low, r1, r2, u, y0, ctx0 = layer_fwd(plan, ctx0, hidden[0], packed0, stacked[0], inner[0])
    x1 = exchange(project(plan, h1_low, columns1, all_columns(plan, qkv_bias[1])))
    ctx1 = attn_fwd(plan, tables[1], x1)
    d1, output, up1, gz1, du1, df1, do1, y1, ctx1, sums1, inner1 = layer_mid(
        plan, ctx1, h1, cotangent[0], packed1, stacked[1], inner[1]
    )

    def flat(a):
        return a.reshape(tokens, -1)

    def scattered(g):
        return lax.psum_scatter(g, "item", scatter_dimension=0, tiled=False)

    def rows_for(vecs):
        part = jnp.concatenate([v.reshape(item, -1) for v in vecs], 1)
        return jnp.pad(part, ((0, 0), (0, 16 * D - part.shape[1]))).reshape(item, 16, D).astype(BF)

    def grads(gz, du, df, do, y, ctx, sums, inner_sum, cut_for=0):
        sums = jnp.sum(sums, 1)
        vecs = (sums[SUM_DO], sums[D_GAIN1], sums[D_SHIFT1], jnp.sum(inner_sum, 0), sums[SUM_DF], sums[D_GAIN2], sums[D_SHIFT2])
        return dense_grads(item, flat(gz), flat(df), flat(y), flat(du), flat(ctx), flat(do), rows_for(vecs), cut_for)

    def seq_send(shares):
        rows = jnp.concatenate(shares)
        rows = jnp.pad(rows, ((0, -rows.shape[0] % (16 * groups)), (0, 0)))
        return exchange(rows.reshape(groups, -1, D))

    def seq_sum(sent):
        return jnp.sum(sent.astype(F32), 0).astype(BF)

    def seq_gather(part):
        return exchange(jnp.broadcast_to(part[None], (groups,) + part.shape))

    counts = [share] * 3 + [w_ffn_in.shape[2] // item] + [share] * 3
    dc1 = exchange(d1)
    fo1, rest1 = grads(gz1, du1, df1, do1, y1, ctx1, sums1, inner1)
    dc1, fo1, rest1 = tie(dc1, fo1, rest1)
    fo1, rest1 = scattered(fo1), scattered(rest1)
    dx1 = attn_bwd(plan, tables[1], x1, dc1)
    dx1, columns0 = tie(dx1, columns0)
    d0, up0, gz0, du0, df0, do0, dqkv1, sums0, inner0, qkv_sum1 = layer_bwd(
        plan, dx1, up1, r1, r2, u, packed0, columns1, stacked[0]
    )
    d0, fo1 = tie(d0, fo1)
    dc0 = exchange(d0)
    bias1 = from_all(plan, jnp.sum(qkv_sum1, 0))
    qkv1 = column_grads(item, flat(h1_low), flat(dqkv1), rows_for((bias1[:D], bias1[2 * D :])))
    seq_first = (w_ffn_out.shape[1] // groups) % 16 == 0
    fo0, rest0 = grads(gz0, du0, df0, do0, y0, ctx0, sums0, inner0, groups if seq_first else 0)
    dc0, qkv1, fo0, rest0, rest1 = tie(dc0, qkv1, fo0, rest0, rest1)
    qkv1, rest0 = scattered(qkv1), scattered(rest0)
    fo0 = exchange(fo0) if seq_first else scattered(fo0)
    dx0 = attn_bwd(plan, tables[0], x0, dc0)
    dx0, fo0, qkv1 = tie(dx0, fo0, qkv1)
    own0 = own_grad(plan, item, hidden_all, dx0)
    dx0 = exchange(dx0)
    if seq_first:
        own0 = jnp.concatenate([seq_sum(fo0), own0], 1)
    dx0, own0 = tie(dx0, own0)
    own0 = scattered(own0)
    sent = seq_send([fo1, rest1, qkv1, rest0] + ([] if seq_first else [fo0]))
    input_grad = layer_tail(plan, dx0, up0, columns0)
    full = seq_gather(seq_sum(sent))
    owns = seq_gather(own0)
    qkv, bias0, biasq1, biasv1, attn, inner_grad, outer, *small_grads = finish(
        plan, share, w_ffn_in.shape[2], item, counts, seq_first, full, owns
    )
    biasq0, biasv0 = (lax.dynamic_slice_in_dim(bias0, part * D + item_rank * share, share, 1) for part in (0, 2))
    bias_q, bias_v = jnp.concatenate([biasq0, biasq1]), jnp.concatenate([biasv0, biasv1])
    out_bias, gain1, shift1, inner_bias, ffn_bias, gain2, shift2 = small_grads
    return (
        output.reshape(hidden.shape),
        input_grad.reshape(hidden.shape),
        qkv,
        bias_q,
        bias_v,
        attn,
        out_bias,
        gain1,
        shift1,
        inner_grad,
        inner_bias,
        outer,
        ffn_bias,
        gain2,
        shift2,
    )


def solution(mesh):
    placed = (
        P("item", "seq", None),
        P("item", None, "seq", None, None),
        P(None, "item", None),
        P(None, "item"),
        P(None, "item"),
        P(None, "item", None),
        P(None, "item"),
        P(None, "item"),
        P(None, "item"),
        P(None, "item", None),
        P(None, "item"),
        P(None, "item", None),
        P(None, "item"),
        P(None, "item"),
        P(None, "item"),
        P("item", "seq", None),
    )
    return jax.shard_map(
        local,
        mesh=mesh,
        in_specs=placed,
        out_specs=(
            P("item", "seq", None),
            P("item", "seq", None),
            P(None, "item", None),
            P(None, "item"),
            P(None, "item"),
            P(None, "item", None),
            P(None, "item"),
            P(None, "item"),
            P(None, "item"),
            P(None, "item", None),
            P(None, "item"),
            P(None, "item", None),
            P(None, "item"),
            P(None, "item"),
            P(None, "item"),
        ),
        check_vma=False,
    )
```

```python
from functools import partial

import jax
import jax.numpy as jnp
from jax import lax
from jax.experimental import pallas as pl
from jax.experimental.pallas import tpu as pltpu
from jax.sharding import PartitionSpec as P

D = 768
H = 12
HD = 64
BLK = 64
RAND = 3
LAYERS = 2
LISTED = 5 + RAND
KEYS = LISTED * BLK
WIDE = 2 * HD
F32 = jnp.float32
BF = jnp.bfloat16
LOG2E = 1.4426950408889634
epsilon = 1e-05
NT = (((1,), (1,)), ((), ()))
TN = (((0,), (0,)), ((), ()))
NN = (((1,), (0,)), ((), ()))
VMEM = pltpu.VMEM


def dot(a, b, dims):
    return lax.dot_general(a, b, dims, preferred_element_type=F32)


class Plan:
    def __init__(self, groups, tokens, half=128):
        self.groups = groups
        self.tokens = tokens
        self.hp = -(-H // groups)
        self.pairs = self.hp // 2
        self.odd = self.hp % 2
        self.half = min(half, tokens // 2)
        self.chunks = tokens // 2 // self.half
        self.per = self.half // BLK
        self.rows = 2 * self.half
        self.xp = 2 * self.hp + 2 * self.pairs + self.odd
        self.cp = 2 * self.pairs + self.odd
        self.blocks = groups * tokens // BLK
        self.own = (2 * self.hp + self.hp) * HD
        self.cols = groups * self.own
        self.ctx = groups * self.hp * HD

    def x_shape(self):
        return (self.groups, self.chunks, self.xp, self.per, BLK, WIDE)

    def c_shape(self):
        return (self.groups, self.chunks, self.cp, self.per, BLK, WIDE)


def low(v):
    return jnp.concatenate([v, jnp.zeros_like(v)], 1)


def high(v):
    return jnp.concatenate([jnp.zeros_like(v), v], 1)


def diag(a, b):
    return jnp.concatenate(
        [jnp.concatenate([a, jnp.zeros_like(b)], 1), jnp.concatenate([jnp.zeros_like(a), b], 1)], 0
    )


def spots(plan, h, i):
    per = plan.per
    xb = (i // per) * (plan.xp * per) + i % per
    cb = (i // per) * (plan.cp * per) + i % per
    if h < 2 * plan.pairs:
        lanes = slice((h % 2) * HD, (h % 2 + 1) * HD)
        x0 = xb + (2 * plan.hp + 2 * (h // 2)) * per
        c0 = cb + 2 * (h // 2) * per
        return ((x0, lanes), (x0 + per, lanes)), ((c0, lanes), (c0 + per, lanes))
    x0 = xb + (2 * plan.hp + 2 * plan.pairs) * per
    c0 = cb + 2 * plan.pairs * per
    first, second = slice(0, HD), slice(HD, WIDE)
    return ((x0, first), (x0, second)), ((c0, first), (c0, second))


def listed(plan, x_ref, lists_ref, h, i):
    sides, places = [], []
    for side in range(2):
        at = ((h * (plan.blocks // 2) + i) * 2 + side) * LISTED
        ids = [lists_ref[at + n] for n in range(LISTED)]
        sides.append(jnp.concatenate([x_ref[n] for n in ids], 0))
        places.append(ids)
    return jnp.concatenate(sides, 1), places


def run_pairs(count, hp, first, second, third):
    for h in range(hp):
        first(0, h, 0)

    def body(i, carry):
        for u in range(2):
            t = 2 * i + u
            for h in range(hp):
                first(jnp.minimum(t + 1, count - 1), h, 1 - u)
                second(h, u)
                third(jnp.maximum(t - 1, 0), h, 1 - u)
        return carry

    lax.fori_loop(0, count // 2, body, 0)
    for h in range(hp):
        third(count - 1, h, 1)


def keys_of(plan, x_ref, h, n):
    per = plan.per
    at = (n * plan.xp + 2 * h) * per
    return pl.ds(at, 2 * per)


def attn_fwd_kernel(plan, lists_ref, x_ref, o_ref, s_ref, p_ref, g_ref, a_ref):
    c = LOG2E * HD**-0.5
    hp, count = plan.hp, plan.blocks // 2
    heads = range(hp)

    def stage_s(i, h, slot):
        kv, _ = listed(plan, x_ref, lists_ref, h, i)
        ((xa, la), (xb, lb)), _ = spots(plan, h, i)
        s_ref[slot, h] = dot(kv, diag(low(x_ref[xa, :, la]), low(x_ref[xb, :, lb])), NT)

    def stage_p(h, slot):
        s = s_ref[slot, h]
        m = jnp.max(s, 0, keepdims=True)
        e = jnp.exp2(s * c - m * c)
        inv = 1.0 / jnp.sum(e, 0, keepdims=True)
        p_ref[slot, h] = (e * inv).astype(BF)

    def stage_c(i, h, slot):
        kv, _ = listed(plan, x_ref, lists_ref, h, i)
        _, ((ca, la), (cb, lb)) = spots(plan, h, i)
        ctx = dot(p_ref[slot, h], kv, TN)
        o_ref[ca, :, la] = ctx[:BLK, HD:WIDE].astype(BF)
        o_ref[cb, :, lb] = ctx[BLK:, WIDE + HD :].astype(BF)

    p_ref[...] = jnp.zeros_like(p_ref)
    run_pairs(count, hp, stage_s, stage_p, stage_c)
    size = plan.rows
    steps = plan.groups * plan.chunks
    ws, outs = [], []
    for h in heads:
        ((xa, la), _), (c_first, _) = spots(plan, h, 0)
        (_, (xb, lb)), (_, c_last) = spots(plan, h, count - 1)
        ws.append(low(jnp.concatenate([x_ref[xa, :, la], x_ref[xb, :, lb]], 0)))
        outs.append((c_first, c_last))

    def chunk(n):
        return pl.ds(pl.multiple_of(n * size, size), size)

    def keys(h, n):
        return x_ref[keys_of(plan, x_ref, h, n)].reshape(size, WIDE)

    def one(n, ms):
        out = []
        for h in heads:
            s = dot(keys(h, n), ws[h], NT)
            g_ref[h, chunk(n), :] = s
            out.append(jnp.maximum(ms[h], jnp.max(s, 0, keepdims=True)))
        return tuple(out)

    ms = lax.fori_loop(
        0, steps, one, tuple(jnp.full((1, 2 * BLK), -jnp.inf, F32) for h in heads), unroll=2
    )

    def two(n, ls):
        out = []
        for h in heads:
            e = jnp.exp2(g_ref[h, chunk(n), :] * c - ms[h] * c)
            g_ref[h, chunk(n), :] = e
            out.append(ls[h] + jnp.sum(e, 0, keepdims=True))
        return tuple(out)

    ls = lax.fori_loop(0, steps, two, tuple(jnp.zeros((1, 2 * BLK), F32) for h in heads), unroll=2)
    invs = [1.0 / l for l in ls]
    a_ref[...] = jnp.zeros_like(a_ref)

    def three(n, carry):
        for h in heads:
            p = g_ref[h, chunk(n), :] * invs[h]
            hi = p.astype(BF)
            lo = (p - hi.astype(F32)).astype(BF)
            a_ref[h] += dot(jnp.concatenate([hi, lo], 1), keys(h, n), TN)
        return carry

    lax.fori_loop(0, steps, three, 0, unroll=2)
    for h in heads:
        ctx = (a_ref[h, : 2 * BLK, :] + a_ref[h, 2 * BLK :, :])[:, HD:].astype(BF)
        (ca, la), (cb, lb) = outs[h]
        o_ref[ca, :, la] = ctx[:BLK]
        o_ref[cb, :, lb] = ctx[BLK:]


def attn_fwd(plan, lists, x):
    flat = x.reshape(-1, BLK, WIDE)
    blocks = plan.groups * plan.chunks * plan.cp * plan.per
    keys = plan.blocks * BLK
    return pl.pallas_call(
        partial(attn_fwd_kernel, plan),
        out_shape=jax.ShapeDtypeStruct((blocks, BLK, WIDE), BF),
        in_specs=[pl.BlockSpec(memory_space=pltpu.SMEM), pl.BlockSpec(memory_space=VMEM)],
        out_specs=pl.BlockSpec(memory_space=VMEM),
        scratch_shapes=[
            VMEM((2, plan.hp, KEYS, 2 * BLK), F32),
            VMEM((2, plan.hp, KEYS, 2 * BLK), BF),
            VMEM((plan.hp, keys, 2 * BLK), F32),
            VMEM((plan.hp, 4 * BLK, WIDE), F32),
        ],
        compiler_params=pltpu.CompilerParams(vmem_limit_bytes=48 << 20),
        cost_estimate=pl.CostEstimate(flops=26 * 10**9, bytes_accessed=6 * 10**6, transcendentals=6 * 10**6),
        name="attn_fwd",
    )(lists, flat).reshape(plan.c_shape())


def attn_bwd_kernel(plan, lists_ref, x_ref, d_ref, o_ref, acc_ref, s_ref, p_ref, g_ref, q_ref):
    scale = HD**-0.5
    c = LOG2E * scale
    hp, count = plan.hp, plan.blocks // 2
    heads = range(hp)
    acc_ref[...] = jnp.zeros_like(acc_ref)

    def weights(i, h):
        ((xa, xla), (xb, xlb)), ((ca, cla), (cb, clb)) = spots(plan, h, i)
        da, db = d_ref[ca, :, cla], d_ref[cb, :, clb]
        da = jnp.where(i == 0, jnp.zeros_like(da), da)
        db = jnp.where(i == count - 1, jnp.zeros_like(db), db)
        return jnp.concatenate(
            [diag(low(x_ref[xa, :, xla]), low(x_ref[xb, :, xlb])), diag(high(da), high(db))], 0
        )

    def stage_s(i, h, slot):
        kv, _ = listed(plan, x_ref, lists_ref, h, i)
        s_ref[slot, h] = dot(kv, weights(i, h), NT)

    def stage_p(h, slot):
        s = s_ref[slot, h, :, : 2 * BLK]
        g = s_ref[slot, h, :, 2 * BLK :]
        m = jnp.max(s, 0, keepdims=True)
        e = jnp.exp2(s * c - m * c)
        inv = 1.0 / jnp.sum(e, 0, keepdims=True)
        delta = jnp.sum(e * g, 0, keepdims=True) * inv
        p = e * inv
        p_ref[slot, h, :, : 2 * BLK] = (p * (g - delta)).astype(BF)
        p_ref[slot, h, :, 2 * BLK :] = p.astype(BF)

    def stage_c(i, h, slot):
        kv, places = listed(plan, x_ref, lists_ref, h, i)
        ((xa, la), (xb, lb)), _ = spots(plan, h, i)
        dq = dot(p_ref[slot, h, :, : 2 * BLK], kv, TN) * scale
        o_ref[xa, :, la] = dq[:BLK, :HD].astype(BF)
        o_ref[xb, :, lb] = dq[BLK:, WIDE : WIDE + HD].astype(BF)
        dkv = dot(p_ref[slot, h], weights(i, h), NN)
        for side in range(2):
            part = dkv[:, side * WIDE : (side + 1) * WIDE]
            for n in range(LISTED):
                acc_ref[places[side][n]] += part[n * BLK : (n + 1) * BLK]

    p_ref[...] = jnp.zeros_like(p_ref)
    run_pairs(count, hp, stage_s, stage_p, stage_c)
    lane_scale = jnp.where(
        lax.broadcasted_iota(jnp.int32, (1, WIDE), 1) < HD, scale, 1.0
    ).astype(F32)
    size = plan.rows
    steps = plan.groups * plan.chunks

    def chunk(n):
        return pl.ds(pl.multiple_of(n * size, size), size)

    ws, threes, ends = [], [], []
    for h in heads:
        ((xa, xla), _), ((ca, cla), _) = spots(plan, h, 0)
        (_, (xb, xlb)), (_, (cb, clb)) = spots(plan, h, count - 1)
        q = low(jnp.concatenate([x_ref[xa, :, xla], x_ref[xb, :, xlb]], 0))
        d = high(jnp.concatenate([d_ref[ca, :, cla], d_ref[cb, :, clb]], 0))
        ws.append(jnp.concatenate([q, d], 0))
        threes.append(jnp.concatenate([q, d, d], 0))
        ends.append(((xa, xla), (xb, xlb)))

    def keys(h, n):
        return x_ref[keys_of(plan, x_ref, h, n)].reshape(size, WIDE)

    def one(n, ms):
        out = []
        for h in heads:
            s = dot(keys(h, n), ws[h], NT)
            g_ref[h, chunk(n), :] = s
            out.append(jnp.maximum(ms[h], jnp.max(s[:, : 2 * BLK], 0, keepdims=True)))
        return tuple(out)

    ms = lax.fori_loop(0, steps, one, tuple(jnp.full((1, 2 * BLK), -jnp.inf, F32) for h in heads), unroll=2)

    def two(n, state):
        out = []
        for h in heads:
            l, eg = state[h]
            e = jnp.exp2(g_ref[h, chunk(n), : 2 * BLK] * c - ms[h] * c)
            g_ref[h, chunk(n), : 2 * BLK] = e
            out.append(
                (
                    l + jnp.sum(e, 0, keepdims=True),
                    eg + jnp.sum(e * g_ref[h, chunk(n), 2 * BLK :], 0, keepdims=True),
                )
            )
        return tuple(out)

    sums = lax.fori_loop(0, steps, two, tuple((jnp.zeros((1, 2 * BLK), F32),) * 2 for h in heads), unroll=2)
    invs = [1.0 / l for l, _ in sums]
    deltas = [eg * inv for (_, eg), inv in zip(sums, invs)]
    q_ref[...] = jnp.zeros_like(q_ref)

    def three(n, carry):
        for h in heads:
            p = g_ref[h, chunk(n), : 2 * BLK] * invs[h]
            ds = (p * (g_ref[h, chunk(n), 2 * BLK :] - deltas[h])).astype(BF)
            hi = p.astype(BF)
            lo = (p - hi.astype(F32)).astype(BF)
            dkv = dot(jnp.concatenate([ds, hi, lo], 1), threes[h], NN)
            where = keys_of(plan, x_ref, h, n)
            total = acc_ref[where].reshape(size, WIDE) + dkv
            o_ref[where] = (total * lane_scale).astype(BF).reshape(2 * plan.per, BLK, WIDE)
            q_ref[h] += dot(ds, keys(h, n), TN)
        return carry

    lax.fori_loop(0, steps, three, 0, unroll=2)
    for h in heads:
        (xa, xla), (xb, xlb) = ends[h]
        dq = (q_ref[h, :, :HD] * scale).astype(BF)
        o_ref[xa, :, xla] = dq[:BLK]
        o_ref[xb, :, xlb] = dq[BLK:]


def attn_bwd(plan, lists, x, d):
    flat = x.reshape(-1, BLK, WIDE)
    keys = plan.blocks * BLK
    return pl.pallas_call(
        partial(attn_bwd_kernel, plan),
        out_shape=jax.ShapeDtypeStruct(flat.shape, BF),
        in_specs=[pl.BlockSpec(memory_space=pltpu.SMEM)] + [pl.BlockSpec(memory_space=VMEM)] * 2,
        out_specs=pl.BlockSpec(memory_space=VMEM),
        scratch_shapes=[
            VMEM(flat.shape, F32),
            VMEM((2, plan.hp, KEYS, 4 * BLK), F32),
            VMEM((2, plan.hp, KEYS, 4 * BLK), BF),
            VMEM((plan.hp, keys, 4 * BLK), F32),
            VMEM((plan.hp, 2 * BLK, WIDE), F32),
        ],
        compiler_params=pltpu.CompilerParams(vmem_limit_bytes=56 << 20),
        cost_estimate=pl.CostEstimate(flops=46 * 10**9, bytes_accessed=12 * 10**6, transcendentals=6 * 10**6),
        name="attn_bwd",
    )(lists, flat, d.reshape(-1, BLK, WIDE)).reshape(plan.x_shape())


def mean(v):
    return jnp.sum(v, -1, keepdims=True) * (1.0 / v.shape[-1])


def normalise(resid):
    centre = resid - mean(resid)
    inv = lax.rsqrt(mean(centre * centre) + epsilon)
    return centre * inv, inv


def norm_back(unit, inv, gain, grad):
    g = grad * gain
    return inv * (g - mean(g) - unit * mean(g * unit))


def gelu_parts(u):
    k = 0.7978845608028654
    sq = u * u
    t = jnp.tanh(k * (u + 0.044715 * (u * sq)))
    half = 0.5 * (1.0 + t)
    return half * u, half + 0.5 * u * (1.0 - t * t) * (k + (3 * 0.044715 * k) * sq)


def rows_of(ref):
    return ref[...].reshape(-1, ref.shape[-1])


def pick_context(plan, pieces):
    half = plan.half
    tiles = []
    for g in range(plan.groups):
        for p in range(plan.pairs):
            tiles.append(pieces[g, 2 * p : 2 * p + 2].reshape(plan.rows, WIDE))
        if plan.odd:
            both = pieces[g, 2 * plan.pairs].reshape(half, WIDE)
            tiles.append(jnp.concatenate([both[:, :HD], both[:, HD:]], 0))
    return jnp.concatenate(tiles, 1)[:, :D]


def put_context(plan, value, ref):
    half, per = plan.half, plan.per
    if plan.ctx > D:
        value = jnp.concatenate([value, jnp.zeros((value.shape[0], plan.ctx - D), value.dtype)], 1)
    for g in range(plan.groups):
        at = g * plan.hp * HD
        for p in range(plan.pairs):
            ref[g, 2 * p : 2 * p + 2] = value[:, at : at + WIDE].reshape(2, per, BLK, WIDE)
            at += WIDE
        if plan.odd:
            one = value[:, at : at + HD]
            ref[g, 2 * plan.pairs] = jnp.concatenate([one[:half], one[half:]], 1).reshape(per, BLK, WIDE)


def put_heads(plan, value, ref):
    half, per, hp = plan.half, plan.per, plan.hp
    pairs_at = plan.groups * hp * WIDE
    single_at = pairs_at + plan.groups * plan.pairs * WIDE
    for g in range(plan.groups):
        for h in range(hp):
            at = (g * hp + h) * WIDE
            ref[g, 2 * h : 2 * h + 2] = value[:, at : at + WIDE].reshape(2, per, BLK, WIDE)
        for p in range(plan.pairs):
            at = pairs_at + (g * plan.pairs + p) * WIDE
            ref[g, 2 * hp + 2 * p : 2 * hp + 2 * p + 2] = value[:, at : at + WIDE].reshape(2, per, BLK, WIDE)
        if plan.odd:
            at = single_at + g * HD
            one = value[:, at : at + HD]
            ref[g, plan.xp - 1] = jnp.concatenate([one[:half], one[half:]], 1).reshape(per, BLK, WIDE)


def pick_heads(plan, pieces):
    half, hp = plan.half, plan.hp
    kv, pairs, singles = [], [], []
    for g in range(pieces.shape[0]):
        for h in range(hp):
            kv.append(pieces[g, 2 * h : 2 * h + 2].reshape(plan.rows, WIDE))
        for p in range(plan.pairs):
            pairs.append(pieces[g, 2 * hp + 2 * p : 2 * hp + 2 * p + 2].reshape(plan.rows, WIDE))
        if plan.odd:
            both = pieces[g, plan.xp - 1].reshape(half, WIDE)
            singles.append(jnp.concatenate([both[:, :HD], both[:, HD:]], 0))
    return jnp.concatenate(kv + pairs + singles, 1)


def whole(shape):
    return pl.BlockSpec(shape, lambda *i: (0,) * len(shape), pipeline_mode=pl.Buffered(1))


MESH = pl.DeviceIdType.MESH
SMALL = 32


def start_kernel(plan, item, hid_ref, shard_ref, small_ref, ids_ref, all_ref, x_ref, small_all_ref, ids_all_ref,
                 hall, wall, xall, h_send, h_recv, i_send, i_recv, w_send, w_recv, v_send, v_recv, local_sem):
    groups = plan.groups
    me = lax.axis_index("seq")
    rank = lax.axis_index("item")
    seq_peers = [lax.rem(me + k, groups) for k in range(1, groups)]
    item_peers = [lax.rem(rank + k, item) for k in range(1, item)]
    barrier = pltpu.get_barrier_semaphore()
    for p in seq_peers:
        pl.semaphore_signal(barrier, inc=1, device_id=(p, rank), device_id_type=MESH)
    for p in item_peers:
        pl.semaphore_signal(barrier, inc=1, device_id=(me, p), device_id_type=MESH)
    pl.semaphore_wait(barrier, len(seq_peers) + len(item_peers))

    def remote(src, dst, send, recv, seq, it):
        copy = pltpu.make_async_remote_copy(
            src_ref=src, dst_ref=dst, send_sem=send, recv_sem=recv, device_id=(seq, it), device_id_type=MESH
        )
        copy.start()
        return copy

    if groups == 4:
        xn = me + 1 - 2 * lax.rem(me, 2)
        yn = lax.rem(me + 2, 4)
        dn = lax.rem(xn + 2, 4)
        order = [xn, yn, dn]

        def to(n, half):
            return remote(hid_ref.at[half], hall.at[me, half], h_send.at[n, half], h_recv.at[n, half], (xn, yn)[n], rank)

        sent = {(0, 0): to(0, 0), (1, 1): to(1, 1)}
        sent[0, 1] = to(0, 1)
        sent[1, 0] = to(1, 0)
    else:
        order = [lax.rem(me + groups - k, groups) for k in range(1, groups)]
        sent = {}
        for k, p in enumerate(seq_peers):
            for half in range(2):
                sent[k, half] = remote(hid_ref.at[half], hall.at[me, half], h_send.at[k, half], h_recv.at[k, half], p, rank)
    shards = [remote(shard_ref, wall.at[rank], w_send.at[k], w_recv.at[k], me, p) for k, p in enumerate(item_peers)]
    smalls = [remote(small_ref, small_all_ref.at[rank], v_send.at[k], v_recv.at[k], me, p) for k, p in enumerate(item_peers)]
    lists = [remote(ids_ref.at[p], ids_all_ref.at[me], i_send.at[k], i_recv.at[k], p, rank) for k, p in enumerate(seq_peers)]
    mine = [
        pltpu.make_async_copy(hid_ref, all_ref.at[me], local_sem.at[0]),
        pltpu.make_async_copy(hid_ref, hall.at[me], local_sem.at[1]),
    ]
    for copy in mine:
        copy.start()
    wall[rank] = shard_ref[...]
    small_all_ref[rank] = small_ref[...]
    ids_all_ref[me] = ids_ref[me]
    for copy in shards:
        copy.wait()
    mine[1].wait()
    share = D // item
    one = Plan.__new__(Plan)
    one.__dict__.update(plan.__dict__)
    one.groups = 1
    out = []

    def project(source, n):
        weight = wall[:, :share].reshape(D, plan.own)
        bias = jnp.sum(wall[:, share : share + 1].astype(F32), 0)

        def chunk(c, carry):
            rows = pl.ds(pl.multiple_of(c * plan.half, plan.half), plan.half)
            a = jnp.concatenate([hall[source, 0, rows], hall[source, 1, rows]], 0)
            put_heads(one, (dot(a, weight, NN) + bias).astype(BF), xall.at[pl.ds(source, 1), c])
            return carry

        lax.fori_loop(0, plan.chunks, chunk, 0)
        copy = pltpu.make_async_copy(xall.at[source], x_ref.at[source], local_sem.at[2 + n])
        copy.start()
        out.append(copy)

    if groups == 4:
        sent[0, 0].wait_recv()
        forward = [remote(hall.at[xn, 0], hall.at[xn, 0], h_send.at[2, 0], h_recv.at[2, 0], yn, rank)]
        sent[1, 1].wait_recv()
        forward.append(remote(hall.at[yn, 1], hall.at[yn, 1], h_send.at[2, 1], h_recv.at[2, 1], xn, rank))
        project(me, 0)
        sent[0, 1].wait_recv()
        project(xn, 1)
        sent[1, 0].wait_recv()
        project(yn, 2)
        for copy in forward:
            copy.wait_recv()
        project(dn, 3)
        ends = list(sent.values()) + forward
    else:
        project(me, 0)
        for k in range(groups - 1):
            for half in range(2):
                sent[k, half].wait_recv()
            project(order[k], k + 1)
        ends = list(sent.values())
    for k, source in enumerate(order):
        copy = pltpu.make_async_copy(hall.at[source], all_ref.at[source], local_sem.at[2 + groups + k])
        copy.start()
        out.append(copy)
    for copy in ends:
        copy.wait_send()
    for copy in smalls + lists:
        copy.wait()
    mine[0].wait()
    for copy in out:
        copy.wait()


def start(plan, item, hidden_low, shard, small, ids):
    g = plan.groups
    dma = pltpu.SemaphoreType.DMA
    hid = hidden_low.reshape(2, plan.tokens // 2, D)
    return pl.pallas_call(
        partial(start_kernel, plan, item),
        out_shape=[
            jax.ShapeDtypeStruct((g,) + hid.shape, BF),
            jax.ShapeDtypeStruct(plan.x_shape(), BF),
            jax.ShapeDtypeStruct((item,) + small.shape, BF),
            jax.ShapeDtypeStruct(ids.shape, jnp.int32),
        ],
        in_specs=[pl.BlockSpec(memory_space=VMEM)] * 4,
        out_specs=[pl.BlockSpec(memory_space=pl.ANY)] * 2 + [pl.BlockSpec(memory_space=VMEM)] * 2,
        scratch_shapes=[
            VMEM((g,) + hid.shape, BF),
            VMEM((item,) + shard.shape, BF),
            VMEM(plan.x_shape(), BF),
            dma((g - 1, 2)),
            dma((g - 1, 2)),
            dma((g - 1,)),
            dma((g - 1,)),
            dma((item - 1,)),
            dma((item - 1,)),
            dma((item - 1,)),
            dma((item - 1,)),
            dma((2 + 2 * g,)),
        ],
        compiler_params=pltpu.CompilerParams(collective_id=1, has_side_effects=True, vmem_limit_bytes=40 << 20),
        cost_estimate=pl.CostEstimate(flops=55 * 10**9, bytes_accessed=12 * 10**6, transcendentals=0),
        name="start",
    )(hid, shard, small, ids)


def put_own_grad(plan, item, acc_ref, sum_ref, o_ref):
    share, own = D // item, plan.own
    total = jnp.broadcast_to(jnp.sum(sum_ref[...], 0, keepdims=True), (16, own)).astype(BF)
    for r in range(item):
        o_ref[r, :share, :own] = acc_ref[r * share : (r + 1) * share].astype(BF)
        o_ref[r, share:, :own] = total
        o_ref[r, :, own:] = jnp.zeros((share + 16, o_ref.shape[2] - own), BF)


def own_grad_kernel(plan, item, steps, a_ref, d_ref, o_ref, acc_ref, sum_ref):
    n = pl.program_id(0) * plan.chunks + pl.program_id(1)

    @pl.when(n == 0)
    def _():
        acc_ref[...] = jnp.zeros_like(acc_ref)
        sum_ref[...] = jnp.zeros_like(sum_ref)

    d = pick_heads(plan, d_ref[:, 0])
    acc_ref[...] += dot(a_ref[...].reshape(plan.rows, D), d, TN)
    sum_ref[...] += jnp.sum(d.astype(F32).reshape(-1, 8, d.shape[1]), 0)

    @pl.when(n == steps - 1)
    def _():
        put_own_grad(plan, item, acc_ref, sum_ref, o_ref)


def own_grad(plan, item, hidden_all, dx):
    a = hidden_all.reshape(plan.groups, 2, plan.chunks, plan.half, D)
    return pl.pallas_call(
        partial(own_grad_kernel, plan, item, plan.groups * plan.chunks),
        out_shape=jax.ShapeDtypeStruct((item, D // item + 16, D), BF),
        grid=(plan.groups, plan.chunks),
        in_specs=[
            pl.BlockSpec((1, 2, 1, plan.half, D), lambda g, c: (g, 0, c, 0, 0)),
            pl.BlockSpec((1, 1) + plan.x_shape()[2:], lambda g, c: (g, c, 0, 0, 0, 0)),
        ],
        out_specs=whole((item, D // item + 16, D)),
        scratch_shapes=[VMEM((D, plan.own), F32), VMEM((8, plan.own), F32)],
        compiler_params=pltpu.CompilerParams(vmem_limit_bytes=48 << 20),
        cost_estimate=pl.CostEstimate(flops=7 * 10**9, bytes_accessed=12 * 10**6, transcendentals=0),
        name="own_grad",
    )(a, dx)


def halves(plan, width):
    return pl.BlockSpec((2, plan.half, width), lambda c: (0, c, 0))


def cut(plan, v):
    return v.reshape(2, plan.tokens // 2, v.shape[-1])


def read(ref):
    return ref[...].reshape(-1, ref.shape[-1])


def write(ref, value):
    ref[...] = value.reshape(ref.shape).astype(ref.dtype)


class Packed:
    def __init__(self, ref, ff):
        self.ref = ref
        self.item = ref.shape[0]
        self.share = D // self.item
        self.parts = ff // D

    def rows(self, first):
        return self.ref[:, first : first + self.share].reshape(D, D)

    def out(self):
        return self.rows(0)

    def ffn_in(self, n):
        return self.rows(self.share * (1 + n))

    def ffn_out(self, n):
        ranks = self.item // self.parts
        first = self.share * (1 + self.parts)
        return self.ref[n * ranks : (n + 1) * ranks, first : first + self.share * self.parts].reshape(D, D)


def column_part(ref, n):
    share = D // ref.shape[0]
    return ref[:, n * share : (n + 1) * share].reshape(D, D)


def wide_parts(w):
    return jnp.concatenate([w[:, n : n + D] for n in range(0, w.shape[1], D)])


OUT_BIAS, GAIN1, SHIFT1, FFN_BIAS, GAIN2, SHIFT2 = range(6)


def first_half(plan, ctx, h, w, vec_ref):
    r1 = h + dot(ctx, w.out(), NN) + vec_ref[OUT_BIAS : OUT_BIAS + 1]
    unit1, inv1 = normalise(r1)
    y1 = unit1 * vec_ref[GAIN1 : GAIN1 + 1] + vec_ref[SHIFT1 : SHIFT1 + 1]
    return r1, unit1, inv1, y1, y1.astype(BF)


def part_of(n):
    return slice(n * D, (n + 1) * D)


def put(ref, n, value):
    ref[:, :, part_of(n)] = value.reshape(ref.shape[:2] + (D,)).astype(ref.dtype)


def get(ref, n):
    return ref[:, :, part_of(n)].reshape(-1, D)


class Swap:
    def __init__(self, plan, src, buf, send, recv, own):
        self.plan, self.src, self.buf, self.send, self.recv, self.own = plan, src, buf, send, recv, own
        self.me = lax.axis_index("seq")
        self.rank = lax.axis_index("item")

    def copy(self, c, k):
        peer = lax.rem(self.me + k, self.plan.groups)
        return pltpu.make_async_remote_copy(
            src_ref=self.src.at[peer, c],
            dst_ref=self.buf.at[self.me, c],
            send_sem=self.send.at[c, k - 1],
            recv_sem=self.recv.at[c, k - 1],
            device_id=(peer, self.rank),
            device_id_type=MESH,
        )

    def local(self):
        return pltpu.make_async_copy(self.src.at[self.me], self.buf.at[self.me], self.own.at[0])

    def step(self):
        self.begin()
        return self.arrived()

    def begin(self):
        groups = self.plan.groups

        @pl.when(pl.program_id(0) == 0)
        def _():
            barrier = pltpu.get_barrier_semaphore()
            for k in range(1, groups):
                peer = lax.rem(self.me + k, groups)
                pl.semaphore_signal(barrier, inc=1, device_id=(peer, self.rank), device_id_type=MESH)
            pl.semaphore_wait(barrier, groups - 1)
            self.local().start()
            for n in range(self.plan.chunks):
                for k in range(1, groups):
                    self.copy(n, k).start()
            self.local().wait()

    def arrived(self):
        c = pl.program_id(0)
        for k in range(1, self.plan.groups):
            self.copy(c, k).wait_recv()
        return self.buf[:, c]

    def end(self):
        c = pl.program_id(0)
        for k in range(1, self.plan.groups):
            self.copy(c, k).wait_send()

    @staticmethod
    def scratch(plan, shape):
        sems = (plan.chunks, plan.groups - 1)
        dma = pltpu.SemaphoreType.DMA
        return [VMEM(shape, BF), dma(sems), dma(sems), dma((1,))]


class Give:
    def __init__(self, plan, out, stage, send, recv, own):
        self.plan, self.out, self.stage, self.send, self.recv, self.own = plan, out, stage, send, recv, own
        self.me = lax.axis_index("seq")
        self.rank = lax.axis_index("item")

    def copy(self, c, k):
        peer = lax.rem(self.me + k, self.plan.groups)
        return pltpu.make_async_remote_copy(
            src_ref=self.stage.at[c, peer],
            dst_ref=self.out.at[self.me, c],
            send_sem=self.send.at[c, k - 1],
            recv_sem=self.recv.at[c, k - 1],
            device_id=(peer, self.rank),
            device_id_type=MESH,
        )

    def local(self, c):
        return pltpu.make_async_copy(self.stage.at[c, self.me], self.out.at[self.me, c], self.own.at[c])

    def step(self, fill):
        c = pl.program_id(0)
        fill(self.stage.at[c])
        self.local(c).start()
        for k in range(1, self.plan.groups):
            self.copy(c, k).start()

    def end(self):
        @pl.when(pl.program_id(0) == self.plan.chunks - 1)
        def _():
            for n in range(self.plan.chunks):
                self.local(n).wait()
                for k in range(1, self.plan.groups):
                    self.copy(n, k).wait()

    @staticmethod
    def scratch(plan, shape):
        sems = (plan.chunks, plan.groups - 1)
        dma = pltpu.SemaphoreType.DMA
        return [VMEM((plan.chunks, plan.groups) + shape[2:], BF), dma(sems), dma(sems), dma((plan.chunks,))]


class Spread:
    def __init__(self, plan, out, stage, send, recv, own):
        self.plan, self.out, self.stage, self.send, self.recv, self.own = plan, out, stage, send, recv, own
        self.me = lax.axis_index("seq")
        self.rank = lax.axis_index("item")
        self.passing = plan.groups == 4
        if self.passing:
            self.peers = [self.me + 1 - 2 * lax.rem(self.me, 2), lax.rem(self.me + 2, 4)]
        else:
            self.peers = [lax.rem(self.me + k, plan.groups) for k in range(1, plan.groups)]

    def rows(self, c):
        half = self.plan.half
        return pl.ds(pl.multiple_of(c * half, half), half)

    def remote(self, src, dst, c, n, peer):
        return pltpu.make_async_remote_copy(
            src_ref=src,
            dst_ref=dst,
            send_sem=self.send.at[c, n],
            recv_sem=self.recv.at[c, n],
            device_id=(peer, self.rank),
            device_id_type=MESH,
        )

    def copy(self, c, n):
        return self.remote(self.stage.at[c], self.out.at[self.me, :, self.rows(c)], c, n, self.peers[n])

    def onward(self, c, n):
        part = self.out.at[self.peers[n], n, self.rows(c)]
        return self.remote(part, part, c, 2 + n, self.peers[1 - n])

    def local(self, c):
        return pltpu.make_async_copy(self.stage.at[c], self.out.at[self.me, :, self.rows(c)], self.own.at[c])

    def pass_on(self, c):
        for n in range(2):
            self.copy(c, n).wait_recv()
            self.onward(c, n).start()

    def step(self, value):
        c = pl.program_id(0)
        self.stage[c] = value.reshape(2, self.plan.half, value.shape[-1])
        self.local(c).start()
        for n in range(len(self.peers)):
            self.copy(c, n).start()
        if self.passing:

            @pl.when(c > 0)
            def _():
                self.pass_on(c - 1)

    def end(self):
        @pl.when(pl.program_id(0) == self.plan.chunks - 1)
        def _():
            if self.passing:
                self.pass_on(self.plan.chunks - 1)
            for c in range(self.plan.chunks):
                self.local(c).wait()
                for n in range(len(self.peers)):
                    self.copy(c, n).wait_send()
                    if self.passing:
                        self.onward(c, n).wait()
                    else:
                        self.copy(c, n).wait_recv()

    @staticmethod
    def scratch(plan):
        sems = (plan.chunks, max(plan.groups - 1, 4))
        dma = pltpu.SemaphoreType.DMA
        return [VMEM((plan.chunks, 2, plan.half, D), BF), dma(sems), dma(sems), dma((plan.chunks,))]


def swap_params(number):
    return pltpu.CompilerParams(collective_id=number, has_side_effects=True, vmem_limit_bytes=60 << 20)


def fwd_kernel(plan, ff, c_ref, h_ref, w_ref, vec_ref, inner_ref,
               all_ref, next_ref, r1_ref, r2_ref, u_ref, y_ref, ctx_ref, *swapping):
    swap = Swap(plan, c_ref, *swapping[:4])
    spread = Spread(plan, all_ref, *swapping[4:])
    w = Packed(w_ref, ff)
    ctx = pick_context(plan, swap.step())
    write(ctx_ref, ctx)
    r1, _, _, y1, y1_low = first_half(plan, ctx, read(h_ref), w, vec_ref)
    write(r1_ref, r1)
    write(y_ref, y1_low)
    r2 = y1 + vec_ref[FFN_BIAS : FFN_BIAS + 1]
    for n in range(w.parts):
        u = dot(y1_low, w.ffn_in(n), NN) + inner_ref[:, part_of(n)]
        put(u_ref, n, u)
        r2 = r2 + dot(gelu_parts(u)[0].astype(BF), w.ffn_out(n), NN)
    write(r2_ref, r2)
    unit2, _ = normalise(r2)
    nxt = unit2 * vec_ref[GAIN2 : GAIN2 + 1] + vec_ref[SHIFT2 : SHIFT2 + 1]
    low_ = nxt.astype(BF)
    write(next_ref, nxt)
    spread.step(low_)
    swap.end()
    spread.end()


def own_kernel(plan, a_ref, w_ref, o_ref):
    share = D // w_ref.shape[0]
    weight = w_ref[:, :share, : plan.own].reshape(D, plan.own)
    bias = jnp.sum(w_ref[:, share : share + 1, : plan.own].astype(F32), 0)
    y = (dot(a_ref[...].reshape(plan.rows, D), weight, NN) + bias).astype(BF)
    one = Plan.__new__(Plan)
    one.__dict__.update(plan.__dict__)
    one.groups = 1
    put_heads(one, y, o_ref.at[:, 0])


def own_heads(plan, every, weight):
    return pl.pallas_call(
        partial(own_kernel, plan),
        out_shape=jax.ShapeDtypeStruct(plan.x_shape(), BF),
        grid=(plan.groups, plan.chunks),
        in_specs=[
            pl.BlockSpec((1, 2, 1, plan.half, D), lambda g, c: (g, 0, c, 0, 0)),
            whole(weight.shape),
        ],
        out_specs=pl.BlockSpec((1, 1) + plan.x_shape()[2:], lambda g, c: (g, c, 0, 0, 0, 0)),
        compiler_params=pltpu.CompilerParams(vmem_limit_bytes=48 << 20),
        cost_estimate=pl.CostEstimate(flops=12 * 10**9, bytes_accessed=12 * 10**6, transcendentals=0),
        name="own_heads",
    )(every.reshape(plan.groups, 2, plan.chunks, plan.half, D), weight)


def piece_spec(shape):
    return pl.BlockSpec((shape[0], 1) + shape[2:], lambda c: (0, c, 0, 0, 0, 0))


def layer_fwd(plan, ctx, h, packed, vec, inner):
    t = (2, plan.tokens // 2)
    ff = inner.shape[-1]
    shapes = [(D, F32), (D, F32), (D, F32), (ff, F32), (D, BF), (D, BF)]
    return pl.pallas_call(
        partial(fwd_kernel, plan, ff),
        out_shape=[jax.ShapeDtypeStruct((plan.groups,) + t + (D,), BF)] + [jax.ShapeDtypeStruct(t + (n,), d) for n, d in shapes],
        grid=(plan.chunks,),
        in_specs=[pl.BlockSpec(memory_space=pl.ANY), halves(plan, D)] + [whole(w.shape) for w in (packed, vec, inner)],
        out_specs=[pl.BlockSpec(memory_space=pl.ANY)] + [halves(plan, n) for n, _ in shapes],
        scratch_shapes=Swap.scratch(plan, plan.c_shape()) + Spread.scratch(plan),
        compiler_params=swap_params(2),
        cost_estimate=pl.CostEstimate(flops=24 * 10**9, bytes_accessed=50 * 10**6, transcendentals=3 * 10**6),
        name="layer_fwd",
    )(ctx, cut(plan, h), packed, vec, inner)


SUM_DO, D_GAIN1, D_SHIFT1, SUM_DF, D_GAIN2, D_SHIFT2 = range(6)


def add_sums(ref, at, value):
    ref[at] += jnp.sum(value.reshape(-1, 8, value.shape[-1]), 0)


def back_chunk(plan, gy, unit1, inv1, unit2, inv2, gate, w, vec_ref, sums_ref, inner_sum_ref, du_ref):
    @pl.when(pl.program_id(0) == 0)
    def _():
        sums_ref[...] = jnp.zeros_like(sums_ref)
        inner_sum_ref[...] = jnp.zeros_like(inner_sum_ref)

    dr2 = norm_back(unit2, inv2, vec_ref[GAIN2 : GAIN2 + 1], gy)
    df = dr2.astype(BF)
    dy1 = dr2
    for n in range(w.parts):
        du = (dot(df, w.ffn_out(n), NT) * gate(n)).astype(BF)
        put(du_ref, n, du)
        dy1 = dy1 + dot(du, w.ffn_in(n), NT)
        inner_sum_ref[:, part_of(n)] += jnp.sum(du.astype(F32).reshape(-1, 8, D), 0)
    dr1 = norm_back(unit1, inv1, vec_ref[GAIN1 : GAIN1 + 1], dy1)
    do = dr1.astype(BF)
    dc = dot(do, w.out(), NT).astype(BF)
    add_sums(sums_ref, SUM_DO, do.astype(F32))
    add_sums(sums_ref, D_GAIN1, dy1 * unit1)
    add_sums(sums_ref, D_SHIFT1, dy1)
    add_sums(sums_ref, SUM_DF, df.astype(F32))
    add_sums(sums_ref, D_GAIN2, gy * unit2)
    add_sums(sums_ref, D_SHIFT2, gy)
    return df, dr1, do, dc


def mid_kernel(plan, ff, c_ref, h_ref, gy_ref, w_ref, vec_ref, inner_ref,
               d_ref, out_ref, dr1_ref, gz_ref, du_ref, df_ref, do_ref, y_ref, ctx_ref, sums_ref, inner_sum_ref, gate_ref, *swapping):
    swap = Swap(plan, c_ref, *swapping)
    w = Packed(w_ref, ff)
    ctx = pick_context(plan, swap.step())
    write(ctx_ref, ctx)
    _, unit1, inv1, y1, y1_low = first_half(plan, ctx, read(h_ref), w, vec_ref)
    write(y_ref, y1_low)
    r2 = y1 + vec_ref[FFN_BIAS : FFN_BIAS + 1]
    for n in range(w.parts):
        u = dot(y1_low, w.ffn_in(n), NN) + inner_ref[:, part_of(n)]
        gz, gate_ref[n] = gelu_parts(u)
        gz = gz.astype(BF)
        put(gz_ref, n, gz)
        r2 = r2 + dot(gz, w.ffn_out(n), NN)
    unit2, inv2 = normalise(r2)
    write(out_ref, unit2 * vec_ref[GAIN2 : GAIN2 + 1] + vec_ref[SHIFT2 : SHIFT2 + 1])
    df, dr1, do, dc = back_chunk(plan, read(gy_ref), unit1, inv1, unit2, inv2, lambda n: gate_ref[n],
                                 w, vec_ref, sums_ref, inner_sum_ref, du_ref)
    put_context(plan, dc, d_ref.at[:, 0])
    write(dr1_ref, dr1)
    write(df_ref, df)
    write(do_ref, do)
    swap.end()


def sum_specs(ff):
    return (
        [jax.ShapeDtypeStruct((6, 8, D), F32), jax.ShapeDtypeStruct((8, ff), F32)],
        [pl.BlockSpec((6, 8, D), lambda c: (0, 0, 0)), pl.BlockSpec((8, ff), lambda c: (0, 0))],
    )


def layer_mid(plan, ctx, h, gy, packed, vec, inner):
    t = (2, plan.tokens // 2)
    ff = inner.shape[-1]
    shapes = [(D, F32), (D, F32), (ff, BF), (ff, BF), (D, BF), (D, BF), (D, BF), (D, BF)]
    sums, sums_at = sum_specs(ff)
    return pl.pallas_call(
        partial(mid_kernel, plan, ff),
        out_shape=[jax.ShapeDtypeStruct(plan.c_shape(), BF)] + [jax.ShapeDtypeStruct(t + (n,), d) for n, d in shapes] + sums,
        grid=(plan.chunks,),
        in_specs=[pl.BlockSpec(memory_space=pl.ANY), halves(plan, D), halves(plan, D)]
        + [whole(w.shape) for w in (packed, vec, inner)],
        out_specs=[piece_spec(plan.c_shape())] + [halves(plan, n) for n, _ in shapes] + sums_at,
        scratch_shapes=[VMEM((ff // D, plan.rows, D), F32)] + Swap.scratch(plan, plan.c_shape()),
        compiler_params=swap_params(3),
        cost_estimate=pl.CostEstimate(flops=45 * 10**9, bytes_accessed=50 * 10**6, transcendentals=3 * 10**6),
        name="layer_mid",
    )(ctx, cut(plan, h), cut(plan, gy), packed, vec, inner)


def bwd_kernel(plan, ff, item, dx_ref, up_ref, r1_ref, r2_ref, u_ref, every_ref, own_ref, w_ref, cols_ref, vec_ref,
               d_ref, dr1_ref, gz_ref, du_ref, df_ref, do_ref, own_grad_ref, sums_ref, inner_sum_ref, acc_ref, sum_ref, *swapping):
    swap = Swap(plan, dx_ref, *swapping[:4])
    give = Give(plan, d_ref, *swapping[4:])
    w = Packed(w_ref, ff)
    swap.begin()
    one = Plan.__new__(Plan)
    one.__dict__.update(plan.__dict__)
    one.groups = 1
    c = pl.program_id(0)

    @pl.when(c == 0)
    def _():
        acc_ref[...] = jnp.zeros_like(acc_ref)
        sum_ref[...] = jnp.zeros_like(sum_ref)

    for s in range(plan.groups):
        d = pick_heads(one, own_ref[s : s + 1, 0])
        acc_ref[...] += dot(every_ref[s].reshape(plan.rows, D), d, TN)
        sum_ref[...] += jnp.sum(d.astype(F32).reshape(-1, 8, plan.own), 0)

    @pl.when(c == plan.chunks - 1)
    def _():
        put_own_grad(plan, item, acc_ref, sum_ref, own_grad_ref)

    dqkv = pick_heads(plan, swap.arrived())
    gy = read(up_ref)
    for n in range(plan.cols // D):
        gy = gy + dot(dqkv[:, part_of(n)], column_part(cols_ref, n), NT)

    unit1, inv1 = normalise(read(r1_ref))
    unit2, inv2 = normalise(read(r2_ref))

    def gate(n):
        gz, value = gelu_parts(get(u_ref, n))
        put(gz_ref, n, gz)
        return value

    df, dr1, do, dc = back_chunk(plan, gy, unit1, inv1, unit2, inv2, gate, w, vec_ref, sums_ref, inner_sum_ref, du_ref)
    give.step(lambda ref: put_context(plan, dc, ref))
    write(dr1_ref, dr1)
    write(df_ref, df)
    write(do_ref, do)
    swap.end()
    give.end()


def layer_bwd(plan, item, dx, up, r1, r2, u, every, packed, columns, vec):
    t = (2, plan.tokens // 2)
    ff = u.shape[-1]
    shapes = [(D, F32), (ff, BF), (ff, BF), (D, BF), (D, BF)]
    sums, sums_at = sum_specs(ff)
    own_grad_shape = (item, D // item + 16, D)
    return pl.pallas_call(
        partial(bwd_kernel, plan, ff, item),
        out_shape=[jax.ShapeDtypeStruct(plan.c_shape(), BF)]
        + [jax.ShapeDtypeStruct(t + (n,), d) for n, d in shapes]
        + [jax.ShapeDtypeStruct(own_grad_shape, BF)]
        + sums,
        grid=(plan.chunks,),
        in_specs=[pl.BlockSpec(memory_space=pl.ANY), halves(plan, D), halves(plan, D), halves(plan, D), halves(plan, ff)]
        + [pl.BlockSpec((plan.groups, 2, plan.half, D), lambda c: (0, 0, c, 0)), piece_spec(plan.x_shape())]
        + [whole(w.shape) for w in (packed, columns, vec)],
        out_specs=[pl.BlockSpec(memory_space=pl.ANY)] + [halves(plan, n) for n, _ in shapes] + [whole(own_grad_shape)] + sums_at,
        scratch_shapes=[VMEM((D, plan.own), F32), VMEM((8, plan.own), F32)]
        + Swap.scratch(plan, plan.x_shape())
        + Give.scratch(plan, plan.c_shape()),
        compiler_params=swap_params(4),
        cost_estimate=pl.CostEstimate(flops=70 * 10**9, bytes_accessed=60 * 10**6, transcendentals=3 * 10**6),
        name="layer_bwd",
    )(dx, up, r1, r2, u, every, dx, packed, columns, vec)


def dense_grad_kernel(item, gz_ref, df_ref, y_ref, du_ref, ctx_ref, do_ref, vec_ref, fo_ref, rest_ref):
    n = pl.program_id(0)
    parts = pl.num_programs(0)
    share = D // item
    ranks = item // parts
    fo = dot(gz_ref[...], df_ref[...], TN).astype(BF)
    if len(fo_ref.shape) == 3:
        fo_ref[...] = fo.reshape(fo_ref.shape)
    else:
        count, here, rows = fo_ref.shape[:3]
        for r in range(here):
            for g in range(count):
                first = (r * count + g) * rows
                fo_ref[g, r] = fo[first : first + rows]
    first = pl.multiple_of(n * share, 16)
    rest_ref[:, pl.ds(first, share)] = dot(y_ref[...], du_ref[...], TN).astype(BF).reshape(item, share, D)

    @pl.when(n == parts - 1)
    def _():
        at = parts * share
        rest_ref[:, at : at + share] = dot(ctx_ref[...], do_ref[...], TN).astype(BF).reshape(item, share, D)
        rest_ref[:, at + share : at + share + 16] = vec_ref[:, :16]
        if vec_ref.shape[1] > 16:
            rest_ref[:, at + share + 16 :] = vec_ref[:, 16:]


def dense_grads(item, gz, df, y, du, ctx, do, vecs, cut_for=0):
    tokens, ff = gz.shape
    parts = ff // D
    share = D // item
    rest = parts * share + share + vecs.shape[1]
    column = pl.BlockSpec((tokens, D), lambda n: (0, n))
    fo_shape, fo_spec = (item, ff // item, D), pl.BlockSpec((item // parts, ff // item, D), lambda n: (n, 0, 0))
    if cut_for:
        fo_shape = (cut_for, item, ff // item // cut_for, D)
        fo_spec = pl.BlockSpec((cut_for, item // parts) + fo_shape[2:], lambda n: (0, n, 0, 0))
    return pl.pallas_call(
        partial(dense_grad_kernel, item),
        out_shape=[jax.ShapeDtypeStruct(fo_shape, BF), jax.ShapeDtypeStruct((item, rest, D), BF)],
        grid=(parts,),
        in_specs=[column, whole(df.shape), whole(y.shape), column, whole(ctx.shape), whole(do.shape), whole(vecs.shape)],
        out_specs=[fo_spec, whole((item, rest, D))],
        compiler_params=pltpu.CompilerParams(vmem_limit_bytes=56 << 20),
        cost_estimate=pl.CostEstimate(flops=14 * 10**9, bytes_accessed=30 * 10**6, transcendentals=0),
        name="dense_grads",
    )(gz, df, y, du, ctx, do, vecs)


def tail_kernel(plan, dx_ref, up_ref, w_ref, o_ref):
    dqkv = pick_heads(plan, dx_ref[:, 0])
    out = read(up_ref)
    for n in range(plan.cols // D):
        out = out + dot(dqkv[:, part_of(n)], column_part(w_ref, n), NT)
    write(o_ref, out)


def layer_tail(plan, dx, up, w_qkv):
    return pl.pallas_call(
        partial(tail_kernel, plan),
        out_shape=jax.ShapeDtypeStruct(up.shape, F32),
        grid=(plan.chunks,),
        in_specs=[piece_spec(plan.x_shape()), halves(plan, D), whole(w_qkv.shape)],
        out_specs=halves(plan, D),
        compiler_params=pltpu.CompilerParams(vmem_limit_bytes=48 << 20),
        cost_estimate=pl.CostEstimate(flops=8 * 10**9, bytes_accessed=12 * 10**6, transcendentals=0),
        name="layer_tail",
    )(dx, up, w_qkv)


def finish_kernel(plan, share, counts, seq_first, sizes, full_ref, *outs):
    qkv_ref, bias_ref, attn_ref, inner_ref, outer_ref = outs[:5]
    small = outs[5:]
    outer = outer_ref.shape[1]
    parts = inner_ref.shape[2] // D
    hp, groups = plan.hp, plan.groups

    def rest(layer, flat, at):
        for n in range(parts):
            inner_ref[layer, :, part_of(n)] = flat[at : at + share].astype(F32)
            at += share
        attn_ref[layer] = flat[at : at + share].astype(F32)
        at += share
        vecs = flat[at : at + 16].astype(F32)
        first = 0
        for ref, n in zip(small, counts):
            ref[layer : layer + 1, :] = vecs[first // D : first // D + 1, first % D : first % D + n]
            first += n
        return at + 16

    def own(layer, first):
        pieces = {}
        for head in range(H):
            g, i = head // hp, head % hp
            rows = full_ref[g, first : first + share + 16].astype(F32)
            pieces["k", head] = rows[:, i * WIDE : i * WIDE + HD]
            pieces["v", head] = rows[:, i * WIDE + HD : (i + 1) * WIDE]
            pieces["q", head] = rows[:, (2 * hp + i) * HD : (2 * hp + i + 1) * HD]
        value = jnp.concatenate([pieces[kind, head] for kind in "qkv" for head in range(H)], 1)
        qkv_ref[layer] = value[:share]
        bias_ref[layer : layer + 1, :] = value[share : share + 1]

    first, second, third = sizes
    one = full_ref[:, :first].reshape(-1, D)
    outer_ref[1] = one[:outer].astype(F32)
    rest(1, one, outer)
    zero = full_ref[:, first : first + second].reshape(-1, D)
    at = rest(0, zero, 0)
    own(1, first + second)
    own_at = first + second + third
    if seq_first:
        here = outer // groups
        for g in range(groups):
            outer_ref[0, g * here : (g + 1) * here] = full_ref[g, own_at : own_at + here].astype(F32)
        own_at += here
    else:
        outer_ref[0] = zero[at : at + outer].astype(F32)
    own(0, own_at)


def finish(plan, share, ff, item, counts, seq_first, sizes, full):
    out = [(share, 3 * D), (3 * D,), (share, D), (share, ff), (ff // item, D)] + [(n,) for n in counts]
    return pl.pallas_call(
        partial(finish_kernel, plan, share, counts, seq_first, sizes),
        out_shape=[jax.ShapeDtypeStruct((LAYERS,) + s, F32) for s in out],
        in_specs=[pl.BlockSpec(memory_space=VMEM)],
        out_specs=[pl.BlockSpec(memory_space=VMEM)] * len(out),
        compiler_params=pltpu.CompilerParams(vmem_limit_bytes=48 << 20),
        name="finish",
    )(full)


def column_parts(plan, w):
    lead = w.shape[:-1]
    g, hp = plan.groups, plan.hp
    w = w.reshape(lead + (3, H, HD))
    w = jnp.pad(w, [(0, 0)] * (len(lead) + 1) + [(0, g * hp - H), (0, 0)])
    q, k, v = (w[..., n, :, :] for n in range(3))
    kv = jnp.stack([k, v], -2).reshape(lead + (g, hp * WIDE))
    q = q.reshape(lead + (g, hp, HD))
    pairs = q[..., : 2 * plan.pairs, :].reshape(lead + (g, plan.pairs * WIDE))
    last = q[..., 2 * plan.pairs :, :].reshape(lead + (g, plan.odd * HD))
    return kv, pairs, last


def all_columns(plan, w):
    lead = w.shape[:-1]
    return jnp.concatenate([p.reshape(lead + (-1,)) for p in column_parts(plan, w)], -1)


def own_columns(plan, w, rank):
    axis = w.ndim - 1
    return jnp.concatenate(
        [lax.dynamic_index_in_dim(p, rank, axis, False) for p in column_parts(plan, w)], -1
    )


def exchange(x):
    y = x.reshape((x.shape[0], -1, x.shape[-1]))
    return lax.all_to_all(y, "seq", split_axis=0, concat_axis=0, tiled=True).reshape(x.shape)


def tie(*args):
    return lax.optimization_barrier(args)


def key_table(plan, random_ids):
    n = plan.blocks
    here = n // plan.groups
    j = jnp.arange(n, dtype=jnp.int32)
    shared = jnp.stack(
        [jnp.maximum(j - 1, 0), j, jnp.minimum(j + 1, n - 1), jnp.zeros_like(j), jnp.full_like(j, n - 1)], 1
    )
    ids = jnp.concatenate([jnp.broadcast_to(shared[None], (plan.hp, n, 5)), random_ids], 2)
    inside = ids % here
    r = inside % (here // 2)
    head = jnp.arange(plan.hp, dtype=jnp.int32)[:, None, None]
    piece = 2 * head + inside // (here // 2)
    place = (((ids // here) * plan.chunks + r // plan.per) * plan.xp + piece) * plan.per + r % plan.per
    place = place.reshape(plan.hp, plan.groups, 2, here // 2, LISTED).transpose(0, 1, 3, 2, 4)
    return place.reshape(-1)


def local(
    hidden,
    block_lists,
    w_qkv,
    bias_query,
    bias_value,
    w_attn_out,
    bias_attn_out,
    norm1_gain,
    norm1_shift,
    w_ffn_in,
    bias_ffn_in,
    w_ffn_out,
    bias_ffn_out,
    norm2_gain,
    norm2_shift,
    cotangent,
):
    groups = lax.axis_size("seq")
    item = lax.axis_size("item")
    seq_rank = lax.axis_index("seq")
    item_rank = lax.axis_index("item")
    tokens = hidden.shape[1]
    plan = Plan(groups, tokens)
    here = tokens // BLK
    share = D // item
    ids = jnp.pad(block_lists[0], ((0, 0), (0, 0), (0, groups * plan.hp - H), (0, 0)))
    ids = ids.reshape(LAYERS, here, groups, plan.hp * RAND).transpose(2, 0, 1, 3).reshape(groups, -1)
    used = ids.shape[1]
    ids = jnp.pad(ids, ((0, 0), (0, -used % 1024))).reshape(groups, -1, 128)
    small = (bias_query, bias_value, bias_attn_out, norm1_gain, norm1_shift, bias_ffn_in, bias_ffn_out, norm2_gain, norm2_shift)
    flat_small = jnp.concatenate(small, 1).reshape(-1)

    def own_shard(layer):
        bias = lax.dynamic_update_slice(jnp.zeros((3 * D,), BF), bias_query[layer], (item_rank * share,))
        bias = lax.dynamic_update_slice(bias, bias_value[layer], (2 * D + item_rank * share,))
        rows = jnp.concatenate([w_qkv[layer], bias[None], jnp.zeros((15, 3 * D), BF)])
        return own_columns(plan, rows, seq_rank)

    hidden_all, x0, small_all, ids = start(
        plan,
        item,
        hidden[0].astype(BF),
        own_shard(0),
        jnp.pad(flat_small, (0, SMALL * 128 - flat_small.shape[0])).reshape(SMALL, 128),
        ids,
    )
    ids = ids.reshape(groups, -1)[:, :used].reshape(groups, LAYERS, here, plan.hp, RAND)
    ids = ids.transpose(1, 3, 0, 2, 4).reshape(LAYERS, plan.hp, plan.blocks, RAND)
    tables = [key_table(plan, ids[layer]) for layer in range(LAYERS)]
    packed = small_all.reshape(item, -1)[:, : flat_small.shape[0]].reshape(item, LAYERS, -1).astype(F32)
    vectors = []
    for layer in range(LAYERS):
        at, out = 0, []
        for s in small:
            out.append(packed[:, layer, at : at + s.shape[1]].reshape(-1))
            at += s.shape[1]
        vectors.append(out)
    stacked = [jnp.stack(v[2:5] + v[6:9] + [v[2]] * 2) for v in vectors]
    inner = [v[5][None] for v in vectors]

    columns = wide_parts(all_columns(plan, w_qkv[0])), wide_parts(all_columns(plan, w_qkv[1]))

    def dense(layer):
        return [w_attn_out[layer], wide_parts(w_ffn_in[layer]), w_ffn_out[layer]]

    packed0 = lax.all_gather(jnp.concatenate(dense(0)), "item", axis=0)
    own_weight1 = jnp.pad(own_shard(1), ((0, 0), (0, D - plan.own)))
    own_weight1 = lax.all_gather(own_weight1, "item", axis=0)
    packed1 = lax.all_gather(jnp.concatenate(dense(1)), "item", axis=0)
    columns1 = lax.all_gather(columns[1], "item", axis=0)
    columns0 = lax.all_gather(columns[0], "item", axis=0)

    ctx0 = attn_fwd(plan, tables[0], x0)
    h1_all, h1, r1, r2, u, y0, ctx0 = layer_fwd(plan, ctx0, hidden[0], packed0, stacked[0], inner[0])
    x1 = own_heads(plan, h1_all, own_weight1)
    ctx1 = attn_fwd(plan, tables[1], x1)
    d1, output, up1, gz1, du1, df1, do1, y1, ctx1, sums1, inner1 = layer_mid(
        plan, ctx1, h1, cotangent[0], packed1, stacked[1], inner[1]
    )

    def flat(a):
        return a.reshape(tokens, -1)

    def scattered(g):
        return lax.psum_scatter(g, "item", scatter_dimension=0, tiled=False)

    def rows_for(vecs):
        part = jnp.concatenate([v.reshape(item, -1) for v in vecs], 1)
        return jnp.pad(part, ((0, 0), (0, 16 * D - part.shape[1]))).reshape(item, 16, D).astype(BF)

    def grads(gz, du, df, do, y, ctx, sums, inner_sum, cut_for=0, more=()):
        sums = jnp.sum(sums, 1)
        vecs = (sums[SUM_DO], sums[D_GAIN1], sums[D_SHIFT1], jnp.sum(inner_sum, 0), sums[SUM_DF], sums[D_GAIN2], sums[D_SHIFT2])
        rows = jnp.concatenate([rows_for(vecs)] + list(more), 1)
        return dense_grads(item, flat(gz), flat(df), flat(y), flat(du), flat(ctx), flat(do), rows, cut_for)

    def seq_send(shares):
        rows = jnp.concatenate(shares)
        rows = jnp.pad(rows, ((0, -rows.shape[0] % (16 * groups)), (0, 0)))
        return exchange(rows.reshape(groups, -1, D))

    def seq_sum(sent):
        return jnp.sum(sent.astype(F32), 0).astype(BF)

    def seq_gather(part):
        return exchange(jnp.broadcast_to(part[None], (groups,) + part.shape))

    counts = [share] * 3 + [w_ffn_in.shape[2] // item] + [share] * 3
    dc1 = exchange(d1)
    fo1, rest1 = grads(gz1, du1, df1, do1, y1, ctx1, sums1, inner1)
    dc1, fo1, rest1 = tie(dc1, fo1, rest1)
    fo1, rest1 = scattered(fo1), scattered(rest1)
    dx1 = attn_bwd(plan, tables[1], x1, dc1)
    dx1, columns0 = tie(dx1, columns0)
    d0, up0, gz0, du0, df0, do0, own1, sums0, inner0 = layer_bwd(
        plan, item, dx1, up1, r1, r2, u, h1_all, packed0, columns1, stacked[0]
    )
    dc0, fo1, rest1, own1 = tie(d0, fo1, rest1, own1)
    own1 = scattered(own1)
    sent1 = seq_send([fo1, rest1])
    seq_first = (w_ffn_out.shape[1] // groups) % 16 == 0
    fo0, rest0 = grads(gz0, du0, df0, do0, y0, ctx0, sums0, inner0, groups if seq_first else 0)
    dc0, fo0, rest0, sent1 = tie(dc0, fo0, rest0, sent1)
    part1 = seq_sum(sent1)
    rest0 = scattered(rest0)
    fo0 = exchange(fo0) if seq_first else scattered(fo0)
    dx0 = attn_bwd(plan, tables[0], x0, dc0)
    dx0, fo0, own1 = tie(dx0, fo0, own1)
    own0 = own_grad(plan, item, hidden_all, dx0)
    dx0 = exchange(dx0)
    if seq_first:
        own0 = jnp.concatenate([seq_sum(fo0), own0], 1)
    own_share = scattered(own0)
    dx0, own0 = tie(dx0, own0)
    part0 = seq_sum(seq_send([rest0] + ([] if seq_first else [fo0])))
    input_grad = layer_tail(plan, dx0, up0, columns0)
    sizes = part1.shape[0], part0.shape[0], own1.shape[0]
    full = seq_gather(jnp.concatenate([part1, part0, own1, own_share]))
    qkv, bias, attn, inner_grad, outer, *small_grads = finish(
        plan, share, w_ffn_in.shape[2], item, counts, seq_first, sizes, full
    )
    bias_q, bias_v = (lax.dynamic_slice_in_dim(bias, part * D + item_rank * share, share, 1) for part in (0, 2))
    out_bias, gain1, shift1, inner_bias, ffn_bias, gain2, shift2 = small_grads
    return (
        output.reshape(hidden.shape),
        input_grad.reshape(hidden.shape),
        qkv,
        bias_q,
        bias_v,
        attn,
        out_bias,
        gain1,
        shift1,
        inner_grad,
        inner_bias,
        outer,
        ffn_bias,
        gain2,
        shift2,
    )


def solution(mesh):
    placed = (
        P("item", "seq", None),
        P("item", None, "seq", None, None),
        P(None, "item", None),
        P(None, "item"),
        P(None, "item"),
        P(None, "item", None),
        P(None, "item"),
        P(None, "item"),
        P(None, "item"),
        P(None, "item", None),
        P(None, "item"),
        P(None, "item", None),
        P(None, "item"),
        P(None, "item"),
        P(None, "item"),
        P("item", "seq", None),
    )
    return jax.shard_map(
        local,
        mesh=mesh,
        in_specs=placed,
        out_specs=(
            P("item", "seq", None),
            P("item", "seq", None),
            P(None, "item", None),
            P(None, "item"),
            P(None, "item"),
            P(None, "item", None),
            P(None, "item"),
            P(None, "item"),
            P(None, "item"),
            P(None, "item", None),
            P(None, "item"),
            P(None, "item", None),
            P(None, "item"),
            P(None, "item"),
            P(None, "item"),
        ),
        check_vma=False,
    )
```

```python
from functools import partial

import jax
import jax.numpy as jnp
from jax import lax
from jax.experimental import pallas as pl
from jax.experimental.pallas import tpu as pltpu
from jax.sharding import PartitionSpec as P

D = 768
H = 12
HD = 64
BLK = 64
RAND = 3
LAYERS = 2
LISTED = 5 + RAND
KEYS = LISTED * BLK
WIDE = 2 * HD
F32 = jnp.float32
BF = jnp.bfloat16
LOG2E = 1.4426950408889634
epsilon = 1e-05
NT = (((1,), (1,)), ((), ()))
TN = (((0,), (0,)), ((), ()))
NN = (((1,), (0,)), ((), ()))
VMEM = pltpu.VMEM


def dot(a, b, dims):
    return lax.dot_general(a, b, dims, preferred_element_type=F32)


class Plan:
    def __init__(self, groups, tokens, half=128):
        self.groups = groups
        self.tokens = tokens
        self.hp = -(-H // groups)
        self.pairs = self.hp // 2
        self.odd = self.hp % 2
        self.half = min(half, tokens // 2)
        self.chunks = tokens // 2 // self.half
        self.per = self.half // BLK
        self.rows = 2 * self.half
        self.xp = 2 * self.hp + 2 * self.pairs + self.odd
        self.cp = 2 * self.pairs + self.odd
        self.blocks = groups * tokens // BLK
        self.own = (2 * self.hp + self.hp) * HD
        self.cols = groups * self.own
        self.ctx = groups * self.hp * HD

    def x_shape(self):
        return (self.groups, self.chunks, self.xp, self.per, BLK, WIDE)

    def c_shape(self):
        return (self.groups, self.chunks, self.cp, self.per, BLK, WIDE)


def low(v):
    return jnp.concatenate([v, jnp.zeros_like(v)], 1)


def high(v):
    return jnp.concatenate([jnp.zeros_like(v), v], 1)


def diag(a, b):
    return jnp.concatenate(
        [jnp.concatenate([a, jnp.zeros_like(b)], 1), jnp.concatenate([jnp.zeros_like(a), b], 1)], 0
    )


def spots(plan, h, i):
    per = plan.per
    xb = (i // per) * (plan.xp * per) + i % per
    cb = (i // per) * (plan.cp * per) + i % per
    if h < 2 * plan.pairs:
        lanes = slice((h % 2) * HD, (h % 2 + 1) * HD)
        x0 = xb + (2 * plan.hp + 2 * (h // 2)) * per
        c0 = cb + 2 * (h // 2) * per
        return ((x0, lanes), (x0 + per, lanes)), ((c0, lanes), (c0 + per, lanes))
    x0 = xb + (2 * plan.hp + 2 * plan.pairs) * per
    c0 = cb + 2 * plan.pairs * per
    first, second = slice(0, HD), slice(HD, WIDE)
    return ((x0, first), (x0, second)), ((c0, first), (c0, second))


def listed(plan, x_ref, lists_ref, h, i):
    sides, places = [], []
    for side in range(2):
        at = ((h * (plan.blocks // 2) + i) * 2 + side) * LISTED
        ids = [lists_ref[at + n] for n in range(LISTED)]
        sides.append(jnp.concatenate([x_ref[n] for n in ids], 0))
        places.append(ids)
    return jnp.concatenate(sides, 1), places


def run_pairs(count, hp, first, second, third):
    for h in range(hp):
        first(0, h, 0)

    def body(i, carry):
        for u in range(2):
            t = 2 * i + u
            for h in range(hp):
                first(jnp.minimum(t + 1, count - 1), h, 1 - u)
                second(h, u)
                third(jnp.maximum(t - 1, 0), h, 1 - u)
        return carry

    lax.fori_loop(0, count // 2, body, 0)
    for h in range(hp):
        third(count - 1, h, 1)


def keys_of(plan, x_ref, h, n):
    per = plan.per
    at = (n * plan.xp + 2 * h) * per
    return pl.ds(at, 2 * per)


def attn_fwd_kernel(plan, lists_ref, x_ref, o_ref, s_ref, p_ref, g_ref, a_ref):
    c = LOG2E * HD**-0.5
    hp, count = plan.hp, plan.blocks // 2
    heads = range(hp)

    def stage_s(i, h, slot):
        kv, _ = listed(plan, x_ref, lists_ref, h, i)
        ((xa, la), (xb, lb)), _ = spots(plan, h, i)
        s_ref[slot, h] = dot(kv, diag(low(x_ref[xa, :, la]), low(x_ref[xb, :, lb])), NT)

    def stage_p(h, slot):
        s = s_ref[slot, h]
        m = jnp.max(s, 0, keepdims=True)
        e = jnp.exp2(s * c - m * c)
        inv = 1.0 / jnp.sum(e, 0, keepdims=True)
        p_ref[slot, h] = (e * inv).astype(BF)

    def stage_c(i, h, slot):
        kv, _ = listed(plan, x_ref, lists_ref, h, i)
        _, ((ca, la), (cb, lb)) = spots(plan, h, i)
        ctx = dot(p_ref[slot, h], kv, TN)
        o_ref[ca, :, la] = ctx[:BLK, HD:WIDE].astype(BF)
        o_ref[cb, :, lb] = ctx[BLK:, WIDE + HD :].astype(BF)

    p_ref[...] = jnp.zeros_like(p_ref)
    run_pairs(count, hp, stage_s, stage_p, stage_c)
    size = plan.rows
    steps = plan.groups * plan.chunks
    ws, outs = [], []
    for h in heads:
        ((xa, la), _), (c_first, _) = spots(plan, h, 0)
        (_, (xb, lb)), (_, c_last) = spots(plan, h, count - 1)
        ws.append(low(jnp.concatenate([x_ref[xa, :, la], x_ref[xb, :, lb]], 0)))
        outs.append((c_first, c_last))

    def chunk(n):
        return pl.ds(pl.multiple_of(n * size, size), size)

    def keys(h, n):
        return x_ref[keys_of(plan, x_ref, h, n)].reshape(size, WIDE)

    def one(n, ms):
        out = []
        for h in heads:
            s = dot(keys(h, n), ws[h], NT)
            g_ref[h, chunk(n), :] = s
            out.append(jnp.maximum(ms[h], jnp.max(s, 0, keepdims=True)))
        return tuple(out)

    ms = lax.fori_loop(
        0, steps, one, tuple(jnp.full((1, 2 * BLK), -jnp.inf, F32) for h in heads), unroll=2
    )

    def two(n, ls):
        out = []
        for h in heads:
            e = jnp.exp2(g_ref[h, chunk(n), :] * c - ms[h] * c)
            g_ref[h, chunk(n), :] = e
            out.append(ls[h] + jnp.sum(e, 0, keepdims=True))
        return tuple(out)

    ls = lax.fori_loop(0, steps, two, tuple(jnp.zeros((1, 2 * BLK), F32) for h in heads), unroll=2)
    invs = [1.0 / l for l in ls]
    a_ref[...] = jnp.zeros_like(a_ref)

    def three(n, carry):
        for h in heads:
            p = g_ref[h, chunk(n), :] * invs[h]
            hi = p.astype(BF)
            lo = (p - hi.astype(F32)).astype(BF)
            a_ref[h] += dot(jnp.concatenate([hi, lo], 1), keys(h, n), TN)
        return carry

    lax.fori_loop(0, steps, three, 0, unroll=2)
    for h in heads:
        ctx = (a_ref[h, : 2 * BLK, :] + a_ref[h, 2 * BLK :, :])[:, HD:].astype(BF)
        (ca, la), (cb, lb) = outs[h]
        o_ref[ca, :, la] = ctx[:BLK]
        o_ref[cb, :, lb] = ctx[BLK:]


def attn_fwd(plan, lists, x):
    flat = x.reshape(-1, BLK, WIDE)
    blocks = plan.groups * plan.chunks * plan.cp * plan.per
    keys = plan.blocks * BLK
    return pl.pallas_call(
        partial(attn_fwd_kernel, plan),
        out_shape=jax.ShapeDtypeStruct((blocks, BLK, WIDE), BF),
        in_specs=[pl.BlockSpec(memory_space=pltpu.SMEM), pl.BlockSpec(memory_space=VMEM)],
        out_specs=pl.BlockSpec(memory_space=VMEM),
        scratch_shapes=[
            VMEM((2, plan.hp, KEYS, 2 * BLK), F32),
            VMEM((2, plan.hp, KEYS, 2 * BLK), BF),
            VMEM((plan.hp, keys, 2 * BLK), F32),
            VMEM((plan.hp, 4 * BLK, WIDE), F32),
        ],
        compiler_params=pltpu.CompilerParams(vmem_limit_bytes=48 << 20),
        cost_estimate=pl.CostEstimate(flops=26 * 10**9, bytes_accessed=6 * 10**6, transcendentals=6 * 10**6),
        name="attn_fwd",
    )(lists, flat).reshape(plan.c_shape())


def attn_bwd_kernel(plan, lists_ref, x_ref, d_ref, o_ref, acc_ref, s_ref, p_ref, g_ref, q_ref):
    scale = HD**-0.5
    c = LOG2E * scale
    hp, count = plan.hp, plan.blocks // 2
    heads = range(hp)
    acc_ref[...] = jnp.zeros_like(acc_ref)

    def weights(i, h):
        ((xa, xla), (xb, xlb)), ((ca, cla), (cb, clb)) = spots(plan, h, i)
        da, db = d_ref[ca, :, cla], d_ref[cb, :, clb]
        da = jnp.where(i == 0, jnp.zeros_like(da), da)
        db = jnp.where(i == count - 1, jnp.zeros_like(db), db)
        return jnp.concatenate(
            [diag(low(x_ref[xa, :, xla]), low(x_ref[xb, :, xlb])), diag(high(da), high(db))], 0
        )

    def stage_s(i, h, slot):
        kv, _ = listed(plan, x_ref, lists_ref, h, i)
        s_ref[slot, h] = dot(kv, weights(i, h), NT)

    def stage_p(h, slot):
        s = s_ref[slot, h, :, : 2 * BLK]
        g = s_ref[slot, h, :, 2 * BLK :]
        m = jnp.max(s, 0, keepdims=True)
        e = jnp.exp2(s * c - m * c)
        inv = 1.0 / jnp.sum(e, 0, keepdims=True)
        delta = jnp.sum(e * g, 0, keepdims=True) * inv
        p = e * inv
        p_ref[slot, h, :, : 2 * BLK] = (p * (g - delta)).astype(BF)
        p_ref[slot, h, :, 2 * BLK :] = p.astype(BF)

    def stage_c(i, h, slot):
        kv, places = listed(plan, x_ref, lists_ref, h, i)
        ((xa, la), (xb, lb)), _ = spots(plan, h, i)
        dq = dot(p_ref[slot, h, :, : 2 * BLK], kv, TN) * scale
        o_ref[xa, :, la] = dq[:BLK, :HD].astype(BF)
        o_ref[xb, :, lb] = dq[BLK:, WIDE : WIDE + HD].astype(BF)
        dkv = dot(p_ref[slot, h], weights(i, h), NN)
        for side in range(2):
            part = dkv[:, side * WIDE : (side + 1) * WIDE]
            for n in range(LISTED):
                acc_ref[places[side][n]] += part[n * BLK : (n + 1) * BLK]

    p_ref[...] = jnp.zeros_like(p_ref)
    run_pairs(count, hp, stage_s, stage_p, stage_c)
    lane_scale = jnp.where(
        lax.broadcasted_iota(jnp.int32, (1, WIDE), 1) < HD, scale, 1.0
    ).astype(F32)
    size = plan.rows
    steps = plan.groups * plan.chunks

    def chunk(n):
        return pl.ds(pl.multiple_of(n * size, size), size)

    ws, threes, ends = [], [], []
    for h in heads:
        ((xa, xla), _), ((ca, cla), _) = spots(plan, h, 0)
        (_, (xb, xlb)), (_, (cb, clb)) = spots(plan, h, count - 1)
        q = low(jnp.concatenate([x_ref[xa, :, xla], x_ref[xb, :, xlb]], 0))
        d = high(jnp.concatenate([d_ref[ca, :, cla], d_ref[cb, :, clb]], 0))
        ws.append(jnp.concatenate([q, d], 0))
        threes.append(jnp.concatenate([q, d, d], 0))
        ends.append(((xa, xla), (xb, xlb)))

    def keys(h, n):
        return x_ref[keys_of(plan, x_ref, h, n)].reshape(size, WIDE)

    def one(n, ms):
        out = []
        for h in heads:
            s = dot(keys(h, n), ws[h], NT)
            g_ref[h, chunk(n), :] = s
            out.append(jnp.maximum(ms[h], jnp.max(s[:, : 2 * BLK], 0, keepdims=True)))
        return tuple(out)

    ms = lax.fori_loop(0, steps, one, tuple(jnp.full((1, 2 * BLK), -jnp.inf, F32) for h in heads), unroll=2)

    def two(n, state):
        out = []
        for h in heads:
            l, eg = state[h]
            e = jnp.exp2(g_ref[h, chunk(n), : 2 * BLK] * c - ms[h] * c)
            g_ref[h, chunk(n), : 2 * BLK] = e
            out.append(
                (
                    l + jnp.sum(e, 0, keepdims=True),
                    eg + jnp.sum(e * g_ref[h, chunk(n), 2 * BLK :], 0, keepdims=True),
                )
            )
        return tuple(out)

    sums = lax.fori_loop(0, steps, two, tuple((jnp.zeros((1, 2 * BLK), F32),) * 2 for h in heads), unroll=2)
    invs = [1.0 / l for l, _ in sums]
    deltas = [eg * inv for (_, eg), inv in zip(sums, invs)]
    q_ref[...] = jnp.zeros_like(q_ref)

    def three(n, carry):
        for h in heads:
            p = g_ref[h, chunk(n), : 2 * BLK] * invs[h]
            ds = (p * (g_ref[h, chunk(n), 2 * BLK :] - deltas[h])).astype(BF)
            hi = p.astype(BF)
            lo = (p - hi.astype(F32)).astype(BF)
            dkv = dot(jnp.concatenate([ds, hi, lo], 1), threes[h], NN)
            where = keys_of(plan, x_ref, h, n)
            total = acc_ref[where].reshape(size, WIDE) + dkv
            o_ref[where] = (total * lane_scale).astype(BF).reshape(2 * plan.per, BLK, WIDE)
            q_ref[h] += dot(ds, keys(h, n), TN)
        return carry

    lax.fori_loop(0, steps, three, 0, unroll=2)
    for h in heads:
        (xa, xla), (xb, xlb) = ends[h]
        dq = (q_ref[h, :, :HD] * scale).astype(BF)
        o_ref[xa, :, xla] = dq[:BLK]
        o_ref[xb, :, xlb] = dq[BLK:]


def attn_bwd(plan, lists, x, d):
    flat = x.reshape(-1, BLK, WIDE)
    keys = plan.blocks * BLK
    return pl.pallas_call(
        partial(attn_bwd_kernel, plan),
        out_shape=jax.ShapeDtypeStruct(flat.shape, BF),
        in_specs=[pl.BlockSpec(memory_space=pltpu.SMEM)] + [pl.BlockSpec(memory_space=VMEM)] * 2,
        out_specs=pl.BlockSpec(memory_space=VMEM),
        scratch_shapes=[
            VMEM(flat.shape, F32),
            VMEM((2, plan.hp, KEYS, 4 * BLK), F32),
            VMEM((2, plan.hp, KEYS, 4 * BLK), BF),
            VMEM((plan.hp, keys, 4 * BLK), F32),
            VMEM((plan.hp, 2 * BLK, WIDE), F32),
        ],
        compiler_params=pltpu.CompilerParams(vmem_limit_bytes=56 << 20),
        cost_estimate=pl.CostEstimate(flops=46 * 10**9, bytes_accessed=12 * 10**6, transcendentals=6 * 10**6),
        name="attn_bwd",
    )(lists, flat, d.reshape(-1, BLK, WIDE)).reshape(plan.x_shape())


def mean(v):
    return jnp.sum(v, -1, keepdims=True) * (1.0 / v.shape[-1])


def normalise(resid):
    centre = resid - mean(resid)
    inv = lax.rsqrt(mean(centre * centre) + epsilon)
    return centre * inv, inv


def norm_back(unit, inv, gain, grad):
    g = grad * gain
    return inv * (g - mean(g) - unit * mean(g * unit))


def gelu_parts(u):
    k = 0.7978845608028654
    sq = u * u
    t = jnp.tanh(k * (u + 0.044715 * (u * sq)))
    half = 0.5 * (1.0 + t)
    return half * u, half + 0.5 * u * (1.0 - t * t) * (k + (3 * 0.044715 * k) * sq)


def rows_of(ref):
    return ref[...].reshape(-1, ref.shape[-1])


def pick_context(plan, pieces):
    half = plan.half
    tiles = []
    for g in range(plan.groups):
        for p in range(plan.pairs):
            tiles.append(pieces[g, 2 * p : 2 * p + 2].reshape(plan.rows, WIDE))
        if plan.odd:
            both = pieces[g, 2 * plan.pairs].reshape(half, WIDE)
            tiles.append(jnp.concatenate([both[:, :HD], both[:, HD:]], 0))
    return jnp.concatenate(tiles, 1)[:, :D]


def put_context(plan, value, ref):
    half, per = plan.half, plan.per
    if plan.ctx > D:
        value = jnp.concatenate([value, jnp.zeros((value.shape[0], plan.ctx - D), value.dtype)], 1)
    for g in range(plan.groups):
        at = g * plan.hp * HD
        for p in range(plan.pairs):
            ref[g, 2 * p : 2 * p + 2] = value[:, at : at + WIDE].reshape(2, per, BLK, WIDE)
            at += WIDE
        if plan.odd:
            one = value[:, at : at + HD]
            ref[g, 2 * plan.pairs] = jnp.concatenate([one[:half], one[half:]], 1).reshape(per, BLK, WIDE)


def put_heads(plan, value, ref):
    half, per, hp = plan.half, plan.per, plan.hp
    pairs_at = plan.groups * hp * WIDE
    single_at = pairs_at + plan.groups * plan.pairs * WIDE
    for g in range(plan.groups):
        for h in range(hp):
            at = (g * hp + h) * WIDE
            ref[g, 2 * h : 2 * h + 2] = value[:, at : at + WIDE].reshape(2, per, BLK, WIDE)
        for p in range(plan.pairs):
            at = pairs_at + (g * plan.pairs + p) * WIDE
            ref[g, 2 * hp + 2 * p : 2 * hp + 2 * p + 2] = value[:, at : at + WIDE].reshape(2, per, BLK, WIDE)
        if plan.odd:
            at = single_at + g * HD
            one = value[:, at : at + HD]
            ref[g, plan.xp - 1] = jnp.concatenate([one[:half], one[half:]], 1).reshape(per, BLK, WIDE)


def pick_heads(plan, pieces):
    half, hp = plan.half, plan.hp
    kv, pairs, singles = [], [], []
    for g in range(pieces.shape[0]):
        for h in range(hp):
            kv.append(pieces[g, 2 * h : 2 * h + 2].reshape(plan.rows, WIDE))
        for p in range(plan.pairs):
            pairs.append(pieces[g, 2 * hp + 2 * p : 2 * hp + 2 * p + 2].reshape(plan.rows, WIDE))
        if plan.odd:
            both = pieces[g, plan.xp - 1].reshape(half, WIDE)
            singles.append(jnp.concatenate([both[:, :HD], both[:, HD:]], 0))
    return jnp.concatenate(kv + pairs + singles, 1)


def whole(shape):
    return pl.BlockSpec(shape, lambda *i: (0,) * len(shape), pipeline_mode=pl.Buffered(1))


MESH = pl.DeviceIdType.MESH
SMALL = 32


def start_kernel(plan, item, hid_ref, shard_ref, small_ref, ids_ref, all_ref, x_ref, small_all_ref, ids_all_ref,
                 hall, wall, xall, h_send, h_recv, i_send, i_recv, w_send, w_recv, v_send, v_recv, local_sem):
    groups = plan.groups
    me = lax.axis_index("seq")
    rank = lax.axis_index("item")
    seq_peers = [lax.rem(me + k, groups) for k in range(1, groups)]
    item_peers = [lax.rem(rank + k, item) for k in range(1, item)]
    barrier = pltpu.get_barrier_semaphore()
    for p in seq_peers:
        pl.semaphore_signal(barrier, inc=1, device_id=(p, rank), device_id_type=MESH)
    for p in item_peers:
        pl.semaphore_signal(barrier, inc=1, device_id=(me, p), device_id_type=MESH)
    pl.semaphore_wait(barrier, len(seq_peers) + len(item_peers))

    def remote(src, dst, send, recv, seq, it):
        copy = pltpu.make_async_remote_copy(
            src_ref=src, dst_ref=dst, send_sem=send, recv_sem=recv, device_id=(seq, it), device_id_type=MESH
        )
        copy.start()
        return copy

    if groups == 4:
        xn = me + 1 - 2 * lax.rem(me, 2)
        yn = lax.rem(me + 2, 4)
        dn = lax.rem(xn + 2, 4)
        order = [xn, yn, dn]

        def to(n, half):
            return remote(hid_ref.at[half], hall.at[me, half], h_send.at[n, half], h_recv.at[n, half], (xn, yn)[n], rank)

        sent = {(0, 0): to(0, 0), (1, 1): to(1, 1)}
        sent[0, 1] = to(0, 1)
        sent[1, 0] = to(1, 0)
    else:
        order = [lax.rem(me + groups - k, groups) for k in range(1, groups)]
        sent = {}
        for k, p in enumerate(seq_peers):
            for half in range(2):
                sent[k, half] = remote(hid_ref.at[half], hall.at[me, half], h_send.at[k, half], h_recv.at[k, half], p, rank)
    shards = [remote(shard_ref, wall.at[rank], w_send.at[k], w_recv.at[k], me, p) for k, p in enumerate(item_peers)]
    smalls = [remote(small_ref, small_all_ref.at[rank], v_send.at[k], v_recv.at[k], me, p) for k, p in enumerate(item_peers)]
    lists = [remote(ids_ref.at[p], ids_all_ref.at[me], i_send.at[k], i_recv.at[k], p, rank) for k, p in enumerate(seq_peers)]
    mine = [
        pltpu.make_async_copy(hid_ref, all_ref.at[me], local_sem.at[0]),
        pltpu.make_async_copy(hid_ref, hall.at[me], local_sem.at[1]),
    ]
    for copy in mine:
        copy.start()
    wall[rank] = shard_ref[...]
    small_all_ref[rank] = small_ref[...]
    ids_all_ref[me] = ids_ref[me]
    for copy in shards:
        copy.wait()
    mine[1].wait()
    share = D // item
    one = Plan.__new__(Plan)
    one.__dict__.update(plan.__dict__)
    one.groups = 1
    out = []

    def project(source, n):
        weight = wall[:, :share].reshape(D, plan.own)
        bias = jnp.sum(wall[:, share : share + 1].astype(F32), 0)

        def chunk(c, carry):
            rows = pl.ds(pl.multiple_of(c * plan.half, plan.half), plan.half)
            a = jnp.concatenate([hall[source, 0, rows], hall[source, 1, rows]], 0)
            put_heads(one, (dot(a, weight, NN) + bias).astype(BF), xall.at[pl.ds(source, 1), c])
            return carry

        lax.fori_loop(0, plan.chunks, chunk, 0)
        copy = pltpu.make_async_copy(xall.at[source], x_ref.at[source], local_sem.at[2 + n])
        copy.start()
        out.append(copy)

    if groups == 4:
        sent[0, 0].wait_recv()
        forward = [remote(hall.at[xn, 0], hall.at[xn, 0], h_send.at[2, 0], h_recv.at[2, 0], yn, rank)]
        sent[1, 1].wait_recv()
        forward.append(remote(hall.at[yn, 1], hall.at[yn, 1], h_send.at[2, 1], h_recv.at[2, 1], xn, rank))
        project(me, 0)
        sent[0, 1].wait_recv()
        project(xn, 1)
        sent[1, 0].wait_recv()
        project(yn, 2)
        for copy in forward:
            copy.wait_recv()
        project(dn, 3)
        ends = list(sent.values()) + forward
    else:
        project(me, 0)
        for k in range(groups - 1):
            for half in range(2):
                sent[k, half].wait_recv()
            project(order[k], k + 1)
        ends = list(sent.values())
    for k, source in enumerate(order):
        copy = pltpu.make_async_copy(hall.at[source], all_ref.at[source], local_sem.at[2 + groups + k])
        copy.start()
        out.append(copy)
    for copy in ends:
        copy.wait_send()
    for copy in smalls + lists:
        copy.wait()
    mine[0].wait()
    for copy in out:
        copy.wait()


def start(plan, item, hidden_low, shard, small, ids):
    g = plan.groups
    dma = pltpu.SemaphoreType.DMA
    hid = hidden_low.reshape(2, plan.tokens // 2, D)
    return pl.pallas_call(
        partial(start_kernel, plan, item),
        out_shape=[
            jax.ShapeDtypeStruct((g,) + hid.shape, BF),
            jax.ShapeDtypeStruct(plan.x_shape(), BF),
            jax.ShapeDtypeStruct((item,) + small.shape, BF),
            jax.ShapeDtypeStruct(ids.shape, jnp.int32),
        ],
        in_specs=[pl.BlockSpec(memory_space=VMEM)] * 4,
        out_specs=[pl.BlockSpec(memory_space=pl.ANY)] * 2 + [pl.BlockSpec(memory_space=VMEM)] * 2,
        scratch_shapes=[
            VMEM((g,) + hid.shape, BF),
            VMEM((item,) + shard.shape, BF),
            VMEM(plan.x_shape(), BF),
            dma((g - 1, 2)),
            dma((g - 1, 2)),
            dma((g - 1,)),
            dma((g - 1,)),
            dma((item - 1,)),
            dma((item - 1,)),
            dma((item - 1,)),
            dma((item - 1,)),
            dma((2 + 2 * g,)),
        ],
        compiler_params=pltpu.CompilerParams(collective_id=1, has_side_effects=True, vmem_limit_bytes=40 << 20),
        cost_estimate=pl.CostEstimate(flops=55 * 10**9, bytes_accessed=12 * 10**6, transcendentals=0),
        name="start",
    )(hid, shard, small, ids)


def put_own_grad(plan, item, acc_ref, sum_ref, o_ref):
    share, own = D // item, plan.own
    total = jnp.broadcast_to(jnp.sum(sum_ref[...], 0, keepdims=True), (16, own)).astype(BF)
    for r in range(item):
        o_ref[r, :share, :own] = acc_ref[r * share : (r + 1) * share].astype(BF)
        o_ref[r, share:, :own] = total
        o_ref[r, :, own:] = jnp.zeros((share + 16, o_ref.shape[2] - own), BF)


def own_grad_kernel(plan, item, steps, a_ref, d_ref, o_ref, acc_ref, sum_ref):
    n = pl.program_id(0) * plan.chunks + pl.program_id(1)

    @pl.when(n == 0)
    def _():
        acc_ref[...] = jnp.zeros_like(acc_ref)
        sum_ref[...] = jnp.zeros_like(sum_ref)

    d = pick_heads(plan, d_ref[:, 0])
    acc_ref[...] += dot(a_ref[...].reshape(plan.rows, D), d, TN)
    sum_ref[...] += jnp.sum(d.astype(F32).reshape(-1, 8, d.shape[1]), 0)

    @pl.when(n == steps - 1)
    def _():
        put_own_grad(plan, item, acc_ref, sum_ref, o_ref)


def own_grad(plan, item, hidden_all, dx):
    a = hidden_all.reshape(plan.groups, 2, plan.chunks, plan.half, D)
    return pl.pallas_call(
        partial(own_grad_kernel, plan, item, plan.groups * plan.chunks),
        out_shape=jax.ShapeDtypeStruct((item, D // item + 16, D), BF),
        grid=(plan.groups, plan.chunks),
        in_specs=[
            pl.BlockSpec((1, 2, 1, plan.half, D), lambda g, c: (g, 0, c, 0, 0)),
            pl.BlockSpec((1, 1) + plan.x_shape()[2:], lambda g, c: (g, c, 0, 0, 0, 0)),
        ],
        out_specs=whole((item, D // item + 16, D)),
        scratch_shapes=[VMEM((D, plan.own), F32), VMEM((8, plan.own), F32)],
        compiler_params=pltpu.CompilerParams(vmem_limit_bytes=48 << 20),
        cost_estimate=pl.CostEstimate(flops=7 * 10**9, bytes_accessed=12 * 10**6, transcendentals=0),
        name="own_grad",
    )(a, dx)


def halves(plan, width):
    return pl.BlockSpec((2, plan.half, width), lambda c: (0, c, 0))


def cut(plan, v):
    return v.reshape(2, plan.tokens // 2, v.shape[-1])


def read(ref):
    return ref[...].reshape(-1, ref.shape[-1])


def write(ref, value):
    ref[...] = value.reshape(ref.shape).astype(ref.dtype)


class Packed:
    def __init__(self, ref, ff):
        self.ref = ref
        self.item = ref.shape[0]
        self.share = D // self.item
        self.parts = ff // D

    def rows(self, first):
        return self.ref[:, first : first + self.share].reshape(D, D)

    def out(self):
        return self.rows(0)

    def ffn_in(self, n):
        return self.rows(self.share * (1 + n))

    def ffn_out(self, n):
        ranks = self.item // self.parts
        first = self.share * (1 + self.parts)
        return self.ref[n * ranks : (n + 1) * ranks, first : first + self.share * self.parts].reshape(D, D)


def column_part(ref, n):
    share = D // ref.shape[0]
    return ref[:, n * share : (n + 1) * share].reshape(D, D)


def wide_parts(w):
    return jnp.concatenate([w[:, n : n + D] for n in range(0, w.shape[1], D)])


OUT_BIAS, GAIN1, SHIFT1, FFN_BIAS, GAIN2, SHIFT2 = range(6)


def first_half(plan, ctx, h, w, vec_ref):
    r1 = h + dot(ctx, w.out(), NN) + vec_ref[OUT_BIAS : OUT_BIAS + 1]
    unit1, inv1 = normalise(r1)
    y1 = unit1 * vec_ref[GAIN1 : GAIN1 + 1] + vec_ref[SHIFT1 : SHIFT1 + 1]
    return r1, unit1, inv1, y1, y1.astype(BF)


def part_of(n):
    return slice(n * D, (n + 1) * D)


def put(ref, n, value):
    ref[:, :, part_of(n)] = value.reshape(ref.shape[:2] + (D,)).astype(ref.dtype)


def get(ref, n):
    return ref[:, :, part_of(n)].reshape(-1, D)


class Swap:
    def __init__(self, plan, src, buf, send, recv, own):
        self.plan, self.src, self.buf, self.send, self.recv, self.own = plan, src, buf, send, recv, own
        self.me = lax.axis_index("seq")
        self.rank = lax.axis_index("item")

    def copy(self, c, k):
        peer = lax.rem(self.me + k, self.plan.groups)
        return pltpu.make_async_remote_copy(
            src_ref=self.src.at[peer, c],
            dst_ref=self.buf.at[self.me, c],
            send_sem=self.send.at[c, k - 1],
            recv_sem=self.recv.at[c, k - 1],
            device_id=(peer, self.rank),
            device_id_type=MESH,
        )

    def local(self):
        return pltpu.make_async_copy(self.src.at[self.me], self.buf.at[self.me], self.own.at[0])

    def step(self):
        self.begin()
        return self.arrived()

    def begin(self):
        groups = self.plan.groups

        @pl.when(pl.program_id(0) == 0)
        def _():
            barrier = pltpu.get_barrier_semaphore()
            for k in range(1, groups):
                peer = lax.rem(self.me + k, groups)
                pl.semaphore_signal(barrier, inc=1, device_id=(peer, self.rank), device_id_type=MESH)
            pl.semaphore_wait(barrier, groups - 1)
            self.local().start()
            for n in range(self.plan.chunks):
                for k in range(1, groups):
                    self.copy(n, k).start()
            self.local().wait()

    def arrived(self):
        c = pl.program_id(0)
        for k in range(1, self.plan.groups):
            self.copy(c, k).wait_recv()
        return self.buf[:, c]

    def end(self):
        c = pl.program_id(0)
        for k in range(1, self.plan.groups):
            self.copy(c, k).wait_send()

    @staticmethod
    def scratch(plan, shape):
        sems = (plan.chunks, plan.groups - 1)
        dma = pltpu.SemaphoreType.DMA
        return [VMEM(shape, BF), dma(sems), dma(sems), dma((1,))]


class Give:
    def __init__(self, plan, out, stage, send, recv, own):
        self.plan, self.out, self.stage, self.send, self.recv, self.own = plan, out, stage, send, recv, own
        self.me = lax.axis_index("seq")
        self.rank = lax.axis_index("item")

    def copy(self, c, k):
        peer = lax.rem(self.me + k, self.plan.groups)
        return pltpu.make_async_remote_copy(
            src_ref=self.stage.at[c, peer],
            dst_ref=self.out.at[self.me, c],
            send_sem=self.send.at[c, k - 1],
            recv_sem=self.recv.at[c, k - 1],
            device_id=(peer, self.rank),
            device_id_type=MESH,
        )

    def local(self, c):
        return pltpu.make_async_copy(self.stage.at[c, self.me], self.out.at[self.me, c], self.own.at[c])

    def step(self, fill):
        c = pl.program_id(0)
        fill(self.stage.at[c])
        self.local(c).start()
        for k in range(1, self.plan.groups):
            self.copy(c, k).start()

    def end(self):
        @pl.when(pl.program_id(0) == self.plan.chunks - 1)
        def _():
            for n in range(self.plan.chunks):
                self.local(n).wait()
                for k in range(1, self.plan.groups):
                    self.copy(n, k).wait()

    @staticmethod
    def scratch(plan, shape):
        sems = (plan.chunks, plan.groups - 1)
        dma = pltpu.SemaphoreType.DMA
        return [VMEM((plan.chunks, plan.groups) + shape[2:], BF), dma(sems), dma(sems), dma((plan.chunks,))]


class Spread:
    def __init__(self, plan, out, stage, send, recv, own):
        self.plan, self.out, self.stage, self.send, self.recv, self.own = plan, out, stage, send, recv, own
        self.me = lax.axis_index("seq")
        self.rank = lax.axis_index("item")
        self.passing = plan.groups == 4
        if self.passing:
            self.peers = [self.me + 1 - 2 * lax.rem(self.me, 2), lax.rem(self.me + 2, 4)]
        else:
            self.peers = [lax.rem(self.me + k, plan.groups) for k in range(1, plan.groups)]

    def rows(self, c):
        half = self.plan.half
        return pl.ds(pl.multiple_of(c * half, half), half)

    def remote(self, src, dst, c, n, peer):
        return pltpu.make_async_remote_copy(
            src_ref=src,
            dst_ref=dst,
            send_sem=self.send.at[c, n],
            recv_sem=self.recv.at[c, n],
            device_id=(peer, self.rank),
            device_id_type=MESH,
        )

    def copy(self, c, n):
        return self.remote(self.stage.at[c], self.out.at[self.me, :, self.rows(c)], c, n, self.peers[n])

    def onward(self, c, n):
        part = self.out.at[self.peers[n], n, self.rows(c)]
        return self.remote(part, part, c, 2 + n, self.peers[1 - n])

    def local(self, c):
        return pltpu.make_async_copy(self.stage.at[c], self.out.at[self.me, :, self.rows(c)], self.own.at[c])

    def pass_on(self, c):
        for n in range(2):
            self.copy(c, n).wait_recv()
            self.onward(c, n).start()

    def step(self, value):
        c = pl.program_id(0)
        self.stage[c] = value.reshape(2, self.plan.half, value.shape[-1])
        self.local(c).start()
        for n in range(len(self.peers)):
            self.copy(c, n).start()
        if self.passing:

            @pl.when(c > 0)
            def _():
                self.pass_on(c - 1)

    def end(self):
        @pl.when(pl.program_id(0) == self.plan.chunks - 1)
        def _():
            if self.passing:
                self.pass_on(self.plan.chunks - 1)
            for c in range(self.plan.chunks):
                self.local(c).wait()
                for n in range(len(self.peers)):
                    self.copy(c, n).wait_send()
                    if self.passing:
                        self.onward(c, n).wait()
                    else:
                        self.copy(c, n).wait_recv()

    @staticmethod
    def scratch(plan):
        sems = (plan.chunks, max(plan.groups - 1, 4))
        dma = pltpu.SemaphoreType.DMA
        return [VMEM((plan.chunks, 2, plan.half, D), BF), dma(sems), dma(sems), dma((plan.chunks,))]


def swap_params(number):
    return pltpu.CompilerParams(collective_id=number, has_side_effects=True, vmem_limit_bytes=60 << 20)


def fwd_kernel(plan, ff, c_ref, h_ref, w_ref, vec_ref, inner_ref,
               all_ref, next_ref, r1_ref, r2_ref, u_ref, y_ref, ctx_ref, *swapping):
    swap = Swap(plan, c_ref, *swapping[:4])
    spread = Spread(plan, all_ref, *swapping[4:])
    w = Packed(w_ref, ff)
    ctx = pick_context(plan, swap.step())
    write(ctx_ref, ctx)
    r1, _, _, y1, y1_low = first_half(plan, ctx, read(h_ref), w, vec_ref)
    write(r1_ref, r1)
    write(y_ref, y1_low)
    r2 = y1 + vec_ref[FFN_BIAS : FFN_BIAS + 1]
    for n in range(w.parts):
        u = dot(y1_low, w.ffn_in(n), NN) + inner_ref[:, part_of(n)]
        put(u_ref, n, u)
        r2 = r2 + dot(gelu_parts(u)[0].astype(BF), w.ffn_out(n), NN)
    write(r2_ref, r2)
    unit2, _ = normalise(r2)
    nxt = unit2 * vec_ref[GAIN2 : GAIN2 + 1] + vec_ref[SHIFT2 : SHIFT2 + 1]
    low_ = nxt.astype(BF)
    write(next_ref, nxt)
    spread.step(low_)
    swap.end()
    spread.end()


def own_kernel(plan, a_ref, w_ref, o_ref):
    share = D // w_ref.shape[0]
    weight = w_ref[:, :share, : plan.own].reshape(D, plan.own)
    bias = jnp.sum(w_ref[:, share : share + 1, : plan.own].astype(F32), 0)
    y = (dot(a_ref[...].reshape(plan.rows, D), weight, NN) + bias).astype(BF)
    one = Plan.__new__(Plan)
    one.__dict__.update(plan.__dict__)
    one.groups = 1
    put_heads(one, y, o_ref.at[:, 0])


def own_heads(plan, every, weight):
    return pl.pallas_call(
        partial(own_kernel, plan),
        out_shape=jax.ShapeDtypeStruct(plan.x_shape(), BF),
        grid=(plan.groups, plan.chunks),
        in_specs=[
            pl.BlockSpec((1, 2, 1, plan.half, D), lambda g, c: (g, 0, c, 0, 0)),
            whole(weight.shape),
        ],
        out_specs=pl.BlockSpec((1, 1) + plan.x_shape()[2:], lambda g, c: (g, c, 0, 0, 0, 0)),
        compiler_params=pltpu.CompilerParams(vmem_limit_bytes=48 << 20),
        cost_estimate=pl.CostEstimate(flops=12 * 10**9, bytes_accessed=12 * 10**6, transcendentals=0),
        name="own_heads",
    )(every.reshape(plan.groups, 2, plan.chunks, plan.half, D), weight)


def piece_spec(shape):
    return pl.BlockSpec((shape[0], 1) + shape[2:], lambda c: (0, c, 0, 0, 0, 0))


def layer_fwd(plan, ctx, h, packed, vec, inner):
    t = (2, plan.tokens // 2)
    ff = inner.shape[-1]
    shapes = [(D, F32), (D, F32), (D, F32), (ff, F32), (D, BF), (D, BF)]
    return pl.pallas_call(
        partial(fwd_kernel, plan, ff),
        out_shape=[jax.ShapeDtypeStruct((plan.groups,) + t + (D,), BF)] + [jax.ShapeDtypeStruct(t + (n,), d) for n, d in shapes],
        grid=(plan.chunks,),
        in_specs=[pl.BlockSpec(memory_space=pl.ANY), halves(plan, D)] + [whole(w.shape) for w in (packed, vec, inner)],
        out_specs=[pl.BlockSpec(memory_space=pl.ANY)] + [halves(plan, n) for n, _ in shapes],
        scratch_shapes=Swap.scratch(plan, plan.c_shape()) + Spread.scratch(plan),
        compiler_params=swap_params(2),
        cost_estimate=pl.CostEstimate(flops=24 * 10**9, bytes_accessed=50 * 10**6, transcendentals=3 * 10**6),
        name="layer_fwd",
    )(ctx, cut(plan, h), packed, vec, inner)


SUM_DO, D_GAIN1, D_SHIFT1, SUM_DF, D_GAIN2, D_SHIFT2 = range(6)


def add_sums(ref, at, value):
    ref[at] += jnp.sum(value.reshape(-1, 8, value.shape[-1]), 0)


def back_chunk(plan, gy, unit1, inv1, unit2, inv2, gate, w, vec_ref, sums_ref, inner_sum_ref, du_ref):
    @pl.when(pl.program_id(0) == 0)
    def _():
        sums_ref[...] = jnp.zeros_like(sums_ref)
        inner_sum_ref[...] = jnp.zeros_like(inner_sum_ref)

    dr2 = norm_back(unit2, inv2, vec_ref[GAIN2 : GAIN2 + 1], gy)
    df = dr2.astype(BF)
    dy1 = dr2
    for n in range(w.parts):
        du = (dot(df, w.ffn_out(n), NT) * gate(n)).astype(BF)
        put(du_ref, n, du)
        dy1 = dy1 + dot(du, w.ffn_in(n), NT)
        inner_sum_ref[:, part_of(n)] += jnp.sum(du.astype(F32).reshape(-1, 8, D), 0)
    dr1 = norm_back(unit1, inv1, vec_ref[GAIN1 : GAIN1 + 1], dy1)
    do = dr1.astype(BF)
    dc = dot(do, w.out(), NT).astype(BF)
    add_sums(sums_ref, SUM_DO, do.astype(F32))
    add_sums(sums_ref, D_GAIN1, dy1 * unit1)
    add_sums(sums_ref, D_SHIFT1, dy1)
    add_sums(sums_ref, SUM_DF, df.astype(F32))
    add_sums(sums_ref, D_GAIN2, gy * unit2)
    add_sums(sums_ref, D_SHIFT2, gy)
    return df, dr1, do, dc


def mid_kernel(plan, ff, c_ref, h_ref, gy_ref, w_ref, vec_ref, inner_ref,
               d_ref, out_ref, dr1_ref, gz_ref, du_ref, df_ref, do_ref, y_ref, ctx_ref, sums_ref, inner_sum_ref, gate_ref, *swapping):
    swap = Swap(plan, c_ref, *swapping)
    w = Packed(w_ref, ff)
    ctx = pick_context(plan, swap.step())
    write(ctx_ref, ctx)
    _, unit1, inv1, y1, y1_low = first_half(plan, ctx, read(h_ref), w, vec_ref)
    write(y_ref, y1_low)
    r2 = y1 + vec_ref[FFN_BIAS : FFN_BIAS + 1]
    for n in range(w.parts):
        u = dot(y1_low, w.ffn_in(n), NN) + inner_ref[:, part_of(n)]
        gz, gate_ref[n] = gelu_parts(u)
        gz = gz.astype(BF)
        put(gz_ref, n, gz)
        r2 = r2 + dot(gz, w.ffn_out(n), NN)
    unit2, inv2 = normalise(r2)
    write(out_ref, unit2 * vec_ref[GAIN2 : GAIN2 + 1] + vec_ref[SHIFT2 : SHIFT2 + 1])
    df, dr1, do, dc = back_chunk(plan, read(gy_ref), unit1, inv1, unit2, inv2, lambda n: gate_ref[n],
                                 w, vec_ref, sums_ref, inner_sum_ref, du_ref)
    put_context(plan, dc, d_ref.at[:, 0])
    write(dr1_ref, dr1)
    write(df_ref, df)
    write(do_ref, do)
    swap.end()


def sum_specs(ff):
    return (
        [jax.ShapeDtypeStruct((6, 8, D), F32), jax.ShapeDtypeStruct((8, ff), F32)],
        [pl.BlockSpec((6, 8, D), lambda c: (0, 0, 0)), pl.BlockSpec((8, ff), lambda c: (0, 0))],
    )


def layer_mid(plan, ctx, h, gy, packed, vec, inner):
    t = (2, plan.tokens // 2)
    ff = inner.shape[-1]
    shapes = [(D, F32), (D, F32), (ff, BF), (ff, BF), (D, BF), (D, BF), (D, BF), (D, BF)]
    sums, sums_at = sum_specs(ff)
    return pl.pallas_call(
        partial(mid_kernel, plan, ff),
        out_shape=[jax.ShapeDtypeStruct(plan.c_shape(), BF)] + [jax.ShapeDtypeStruct(t + (n,), d) for n, d in shapes] + sums,
        grid=(plan.chunks,),
        in_specs=[pl.BlockSpec(memory_space=pl.ANY), halves(plan, D), halves(plan, D)]
        + [whole(w.shape) for w in (packed, vec, inner)],
        out_specs=[piece_spec(plan.c_shape())] + [halves(plan, n) for n, _ in shapes] + sums_at,
        scratch_shapes=[VMEM((ff // D, plan.rows, D), F32)] + Swap.scratch(plan, plan.c_shape()),
        compiler_params=swap_params(3),
        cost_estimate=pl.CostEstimate(flops=45 * 10**9, bytes_accessed=50 * 10**6, transcendentals=3 * 10**6),
        name="layer_mid",
    )(ctx, cut(plan, h), cut(plan, gy), packed, vec, inner)


def bwd_kernel(plan, ff, item, dx_ref, up_ref, r1_ref, r2_ref, u_ref, every_ref, own_ref, w_ref, cols_ref, vec_ref,
               d_ref, dr1_ref, gz_ref, du_ref, df_ref, do_ref, own_grad_ref, sums_ref, inner_sum_ref, acc_ref, sum_ref, *swapping):
    swap = Swap(plan, dx_ref, *swapping[:4])
    give = Give(plan, d_ref, *swapping[4:])
    w = Packed(w_ref, ff)
    swap.begin()
    one = Plan.__new__(Plan)
    one.__dict__.update(plan.__dict__)
    one.groups = 1
    c = pl.program_id(0)

    @pl.when(c == 0)
    def _():
        acc_ref[...] = jnp.zeros_like(acc_ref)
        sum_ref[...] = jnp.zeros_like(sum_ref)

    for s in range(plan.groups):
        d = pick_heads(one, own_ref[s : s + 1, 0])
        acc_ref[...] += dot(every_ref[s].reshape(plan.rows, D), d, TN)
        sum_ref[...] += jnp.sum(d.astype(F32).reshape(-1, 8, plan.own), 0)

    @pl.when(c == plan.chunks - 1)
    def _():
        put_own_grad(plan, item, acc_ref, sum_ref, own_grad_ref)

    dqkv = pick_heads(plan, swap.arrived())
    gy = read(up_ref)
    for n in range(plan.cols // D):
        gy = gy + dot(dqkv[:, part_of(n)], column_part(cols_ref, n), NT)

    unit1, inv1 = normalise(read(r1_ref))
    unit2, inv2 = normalise(read(r2_ref))

    def gate(n):
        gz, value = gelu_parts(get(u_ref, n))
        put(gz_ref, n, gz)
        return value

    df, dr1, do, dc = back_chunk(plan, gy, unit1, inv1, unit2, inv2, gate, w, vec_ref, sums_ref, inner_sum_ref, du_ref)
    give.step(lambda ref: put_context(plan, dc, ref))
    write(dr1_ref, dr1)
    write(df_ref, df)
    write(do_ref, do)
    swap.end()
    give.end()


def layer_bwd(plan, item, dx, up, r1, r2, u, every, packed, columns, vec):
    t = (2, plan.tokens // 2)
    ff = u.shape[-1]
    shapes = [(D, F32), (ff, BF), (ff, BF), (D, BF), (D, BF)]
    sums, sums_at = sum_specs(ff)
    own_grad_shape = (item, D // item + 16, D)
    return pl.pallas_call(
        partial(bwd_kernel, plan, ff, item),
        out_shape=[jax.ShapeDtypeStruct(plan.c_shape(), BF)]
        + [jax.ShapeDtypeStruct(t + (n,), d) for n, d in shapes]
        + [jax.ShapeDtypeStruct(own_grad_shape, BF)]
        + sums,
        grid=(plan.chunks,),
        in_specs=[pl.BlockSpec(memory_space=pl.ANY), halves(plan, D), halves(plan, D), halves(plan, D), halves(plan, ff)]
        + [pl.BlockSpec((plan.groups, 2, plan.half, D), lambda c: (0, 0, c, 0)), piece_spec(plan.x_shape())]
        + [whole(w.shape) for w in (packed, columns, vec)],
        out_specs=[pl.BlockSpec(memory_space=pl.ANY)] + [halves(plan, n) for n, _ in shapes] + [whole(own_grad_shape)] + sums_at,
        scratch_shapes=[VMEM((D, plan.own), F32), VMEM((8, plan.own), F32)]
        + Swap.scratch(plan, plan.x_shape())
        + Give.scratch(plan, plan.c_shape()),
        compiler_params=swap_params(4),
        cost_estimate=pl.CostEstimate(flops=70 * 10**9, bytes_accessed=60 * 10**6, transcendentals=3 * 10**6),
        name="layer_bwd",
    )(dx, up, r1, r2, u, every, dx, packed, columns, vec)


def dense_grad_kernel(item, gz_ref, df_ref, y_ref, du_ref, ctx_ref, do_ref, vec_ref, fo_ref, rest_ref):
    n = pl.program_id(0)
    parts = pl.num_programs(0)
    share = D // item
    ranks = item // parts
    fo = dot(gz_ref[...], df_ref[...], TN).astype(BF)
    if len(fo_ref.shape) == 3:
        fo_ref[...] = fo.reshape(fo_ref.shape)
    else:
        count, here, rows = fo_ref.shape[:3]
        for r in range(here):
            for g in range(count):
                first = (r * count + g) * rows
                fo_ref[g, r] = fo[first : first + rows]
    first = pl.multiple_of(n * share, 16)
    rest_ref[:, pl.ds(first, share)] = dot(y_ref[...], du_ref[...], TN).astype(BF).reshape(item, share, D)

    @pl.when(n == parts - 1)
    def _():
        at = parts * share
        rest_ref[:, at : at + share] = dot(ctx_ref[...], do_ref[...], TN).astype(BF).reshape(item, share, D)
        rest_ref[:, at + share : at + share + 16] = vec_ref[:, :16]
        if vec_ref.shape[1] > 16:
            rest_ref[:, at + share + 16 :] = vec_ref[:, 16:]


def dense_grads(item, gz, df, y, du, ctx, do, vecs, cut_for=0):
    tokens, ff = gz.shape
    parts = ff // D
    share = D // item
    rest = parts * share + share + vecs.shape[1]
    column = pl.BlockSpec((tokens, D), lambda n: (0, n))
    fo_shape, fo_spec = (item, ff // item, D), pl.BlockSpec((item // parts, ff // item, D), lambda n: (n, 0, 0))
    if cut_for:
        fo_shape = (cut_for, item, ff // item // cut_for, D)
        fo_spec = pl.BlockSpec((cut_for, item // parts) + fo_shape[2:], lambda n: (0, n, 0, 0))
    return pl.pallas_call(
        partial(dense_grad_kernel, item),
        out_shape=[jax.ShapeDtypeStruct(fo_shape, BF), jax.ShapeDtypeStruct((item, rest, D), BF)],
        grid=(parts,),
        in_specs=[column, whole(df.shape), whole(y.shape), column, whole(ctx.shape), whole(do.shape), whole(vecs.shape)],
        out_specs=[fo_spec, whole((item, rest, D))],
        compiler_params=pltpu.CompilerParams(vmem_limit_bytes=56 << 20),
        cost_estimate=pl.CostEstimate(flops=14 * 10**9, bytes_accessed=30 * 10**6, transcendentals=0),
        name="dense_grads",
    )(gz, df, y, du, ctx, do, vecs)


def tail_kernel(plan, dx_ref, up_ref, w_ref, rows_ref, o_ref, got_ref, *scratch):
    swap = Swap(plan, dx_ref, *scratch[:4])
    send, recv, own = scratch[4:]
    me, rank, groups = swap.me, swap.rank, plan.groups

    def copy(k):
        peer = lax.rem(me + k, groups)
        return pltpu.make_async_remote_copy(
            src_ref=rows_ref.at[peer],
            dst_ref=got_ref.at[me],
            send_sem=send.at[k - 1],
            recv_sem=recv.at[k - 1],
            device_id=(peer, rank),
            device_id_type=MESH,
        )

    def local():
        return pltpu.make_async_copy(rows_ref.at[me], got_ref.at[me], own.at[0])

    swap.begin()

    @pl.when(pl.program_id(0) == 0)
    def _():
        local().start()
        for k in range(1, groups):
            copy(k).start()

    dqkv = pick_heads(plan, swap.arrived())
    out = read(up_ref)
    for n in range(plan.cols // D):
        out = out + dot(dqkv[:, part_of(n)], column_part(w_ref, n), NT)
    write(o_ref, out)
    swap.end()

    @pl.when(pl.program_id(0) == plan.chunks - 1)
    def _():
        local().wait()
        for k in range(1, groups):
            copy(k).wait()


def layer_tail(plan, dx, up, columns, rows):
    dma = pltpu.SemaphoreType.DMA
    return pl.pallas_call(
        partial(tail_kernel, plan),
        out_shape=[jax.ShapeDtypeStruct(up.shape, F32), jax.ShapeDtypeStruct(rows.shape, BF)],
        grid=(plan.chunks,),
        in_specs=[pl.BlockSpec(memory_space=pl.ANY), halves(plan, D), whole(columns.shape), pl.BlockSpec(memory_space=pl.ANY)],
        out_specs=[halves(plan, D), pl.BlockSpec(memory_space=pl.ANY)],
        scratch_shapes=Swap.scratch(plan, plan.x_shape()) + [dma((plan.groups - 1,)), dma((plan.groups - 1,)), dma((1,))],
        compiler_params=swap_params(5),
        cost_estimate=pl.CostEstimate(flops=55 * 10**9, bytes_accessed=12 * 10**6, transcendentals=0),
        name="layer_tail",
    )(dx, up, columns, rows)


def gather_kernel(groups, rows_ref, out_ref, send, recv, own):
    me = lax.axis_index("seq")
    rank = lax.axis_index("item")
    barrier = pltpu.get_barrier_semaphore()
    for k in range(1, groups):
        pl.semaphore_signal(barrier, inc=1, device_id=(lax.rem(me + k, groups), rank), device_id_type=MESH)
    pl.semaphore_wait(barrier, groups - 1)
    count = rows_ref.shape[0]
    first = count // 32 * 16
    parts = [pl.ds(0, first), pl.ds(first, count - first)]
    if groups == 4:
        peers = [me + 1 - 2 * lax.rem(me, 2), lax.rem(me + 2, 4)]
    else:
        peers = [lax.rem(me + k, groups) for k in range(1, groups)]

    def remote(src, dst, n, part, peer):
        return pltpu.make_async_remote_copy(
            src_ref=src, dst_ref=dst, send_sem=send.at[n, part], recv_sem=recv.at[n, part],
            device_id=(peer, rank), device_id_type=MESH,
        )

    def copy(n, part):
        return remote(rows_ref.at[parts[part]], out_ref.at[me, parts[part]], n, part, peers[n])

    def onward(n):
        piece = out_ref.at[peers[n], parts[n]]
        return remote(piece, piece, 2, n, peers[1 - n])

    local = pltpu.make_async_copy(rows_ref, out_ref.at[me], own.at[0])
    if groups == 4:
        order = [(0, 0), (1, 1), (0, 1), (1, 0)]
    else:
        order = [(n, part) for n in range(groups - 1) for part in range(2)]
    for n, part in order:
        copy(n, part).start()
    local.start()
    if groups == 4:
        for n in range(2):
            copy(n, n).wait_recv()
            onward(n).start()
        for n in range(2):
            copy(n, 1 - n).wait_recv()
            onward(n).wait()
        for n, part in order:
            copy(n, part).wait_send()
    else:
        for n, part in order:
            copy(n, part).wait()
    local.wait()


def gather(groups, rows):
    sems = (max(groups - 1, 3), 2)
    dma = pltpu.SemaphoreType.DMA
    return pl.pallas_call(
        partial(gather_kernel, groups),
        out_shape=jax.ShapeDtypeStruct((groups,) + rows.shape, BF),
        in_specs=[pl.BlockSpec(memory_space=pl.ANY)],
        out_specs=pl.BlockSpec(memory_space=pl.ANY),
        scratch_shapes=[dma(sems), dma(sems), dma((1,))],
        compiler_params=swap_params(6),
        cost_estimate=pl.CostEstimate(flops=35 * 10**9, bytes_accessed=6 * 10**6, transcendentals=0),
        name="gather",
    )(rows)


def finish_kernel(plan, share, counts, seq_first, sizes, full_ref, *outs):
    qkv_ref, bias_ref, attn_ref, inner_ref, outer_ref = outs[:5]
    small = outs[5:]
    outer = outer_ref.shape[1]
    parts = inner_ref.shape[2] // D
    hp, groups = plan.hp, plan.groups

    def rest(layer, flat, at):
        for n in range(parts):
            inner_ref[layer, :, part_of(n)] = flat[at : at + share].astype(F32)
            at += share
        attn_ref[layer] = flat[at : at + share].astype(F32)
        at += share
        vecs = flat[at : at + 16].astype(F32)
        first = 0
        for ref, n in zip(small, counts):
            ref[layer : layer + 1, :] = vecs[first // D : first // D + 1, first % D : first % D + n]
            first += n
        return at + 16

    def own(layer, first):
        pieces = {}
        for head in range(H):
            g, i = head // hp, head % hp
            rows = full_ref[g, first : first + share + 16].astype(F32)
            pieces["k", head] = rows[:, i * WIDE : i * WIDE + HD]
            pieces["v", head] = rows[:, i * WIDE + HD : (i + 1) * WIDE]
            pieces["q", head] = rows[:, (2 * hp + i) * HD : (2 * hp + i + 1) * HD]
        value = jnp.concatenate([pieces[kind, head] for kind in "qkv" for head in range(H)], 1)
        qkv_ref[layer] = value[:share]
        bias_ref[layer : layer + 1, :] = value[share : share + 1]

    first, second, third = sizes
    one = full_ref[:, :first].reshape(-1, D)
    outer_ref[1] = one[:outer].astype(F32)
    rest(1, one, outer)
    zero = full_ref[:, first : first + second].reshape(-1, D)
    at = rest(0, zero, 0)
    own(1, first + second)
    own_at = first + second + third
    if seq_first:
        here = outer // groups
        for g in range(groups):
            outer_ref[0, g * here : (g + 1) * here] = full_ref[g, own_at : own_at + here].astype(F32)
        own_at += here
    else:
        outer_ref[0] = zero[at : at + outer].astype(F32)
    own(0, own_at)


def finish(plan, share, ff, item, counts, seq_first, sizes, full):
    out = [(share, 3 * D), (3 * D,), (share, D), (share, ff), (ff // item, D)] + [(n,) for n in counts]
    return pl.pallas_call(
        partial(finish_kernel, plan, share, counts, seq_first, sizes),
        out_shape=[jax.ShapeDtypeStruct((LAYERS,) + s, F32) for s in out],
        in_specs=[pl.BlockSpec(memory_space=VMEM)],
        out_specs=[pl.BlockSpec(memory_space=VMEM)] * len(out),
        compiler_params=pltpu.CompilerParams(vmem_limit_bytes=48 << 20),
        name="finish",
    )(full)


def column_parts(plan, w):
    lead = w.shape[:-1]
    g, hp = plan.groups, plan.hp
    w = w.reshape(lead + (3, H, HD))
    w = jnp.pad(w, [(0, 0)] * (len(lead) + 1) + [(0, g * hp - H), (0, 0)])
    q, k, v = (w[..., n, :, :] for n in range(3))
    kv = jnp.stack([k, v], -2).reshape(lead + (g, hp * WIDE))
    q = q.reshape(lead + (g, hp, HD))
    pairs = q[..., : 2 * plan.pairs, :].reshape(lead + (g, plan.pairs * WIDE))
    last = q[..., 2 * plan.pairs :, :].reshape(lead + (g, plan.odd * HD))
    return kv, pairs, last


def all_columns(plan, w):
    lead = w.shape[:-1]
    return jnp.concatenate([p.reshape(lead + (-1,)) for p in column_parts(plan, w)], -1)


def own_columns(plan, w, rank):
    axis = w.ndim - 1
    return jnp.concatenate(
        [lax.dynamic_index_in_dim(p, rank, axis, False) for p in column_parts(plan, w)], -1
    )


def exchange(x):
    y = x.reshape((x.shape[0], -1, x.shape[-1]))
    return lax.all_to_all(y, "seq", split_axis=0, concat_axis=0, tiled=True).reshape(x.shape)


def tie(*args):
    return lax.optimization_barrier(args)


def key_table(plan, random_ids):
    n = plan.blocks
    here = n // plan.groups
    j = jnp.arange(n, dtype=jnp.int32)
    shared = jnp.stack(
        [jnp.maximum(j - 1, 0), j, jnp.minimum(j + 1, n - 1), jnp.zeros_like(j), jnp.full_like(j, n - 1)], 1
    )
    ids = jnp.concatenate([jnp.broadcast_to(shared[None], (plan.hp, n, 5)), random_ids], 2)
    inside = ids % here
    r = inside % (here // 2)
    head = jnp.arange(plan.hp, dtype=jnp.int32)[:, None, None]
    piece = 2 * head + inside // (here // 2)
    place = (((ids // here) * plan.chunks + r // plan.per) * plan.xp + piece) * plan.per + r % plan.per
    place = place.reshape(plan.hp, plan.groups, 2, here // 2, LISTED).transpose(0, 1, 3, 2, 4)
    return place.reshape(-1)


def local(
    hidden,
    block_lists,
    w_qkv,
    bias_query,
    bias_value,
    w_attn_out,
    bias_attn_out,
    norm1_gain,
    norm1_shift,
    w_ffn_in,
    bias_ffn_in,
    w_ffn_out,
    bias_ffn_out,
    norm2_gain,
    norm2_shift,
    cotangent,
):
    groups = lax.axis_size("seq")
    item = lax.axis_size("item")
    seq_rank = lax.axis_index("seq")
    item_rank = lax.axis_index("item")
    tokens = hidden.shape[1]
    plan = Plan(groups, tokens)
    here = tokens // BLK
    share = D // item
    ids = jnp.pad(block_lists[0], ((0, 0), (0, 0), (0, groups * plan.hp - H), (0, 0)))
    ids = ids.reshape(LAYERS, here, groups, plan.hp * RAND).transpose(2, 0, 1, 3).reshape(groups, -1)
    used = ids.shape[1]
    ids = jnp.pad(ids, ((0, 0), (0, -used % 1024))).reshape(groups, -1, 128)
    small = (bias_query, bias_value, bias_attn_out, norm1_gain, norm1_shift, bias_ffn_in, bias_ffn_out, norm2_gain, norm2_shift)
    flat_small = jnp.concatenate(small, 1).reshape(-1)

    def own_shard(layer):
        bias = lax.dynamic_update_slice(jnp.zeros((3 * D,), BF), bias_query[layer], (item_rank * share,))
        bias = lax.dynamic_update_slice(bias, bias_value[layer], (2 * D + item_rank * share,))
        rows = jnp.concatenate([w_qkv[layer], bias[None], jnp.zeros((15, 3 * D), BF)])
        return own_columns(plan, rows, seq_rank)

    hidden_all, x0, small_all, ids = start(
        plan,
        item,
        hidden[0].astype(BF),
        own_shard(0),
        jnp.pad(flat_small, (0, SMALL * 128 - flat_small.shape[0])).reshape(SMALL, 128),
        ids,
    )
    ids = ids.reshape(groups, -1)[:, :used].reshape(groups, LAYERS, here, plan.hp, RAND)
    ids = ids.transpose(1, 3, 0, 2, 4).reshape(LAYERS, plan.hp, plan.blocks, RAND)
    tables = [key_table(plan, ids[layer]) for layer in range(LAYERS)]
    packed = small_all.reshape(item, -1)[:, : flat_small.shape[0]].reshape(item, LAYERS, -1).astype(F32)
    vectors = []
    for layer in range(LAYERS):
        at, out = 0, []
        for s in small:
            out.append(packed[:, layer, at : at + s.shape[1]].reshape(-1))
            at += s.shape[1]
        vectors.append(out)
    stacked = [jnp.stack(v[2:5] + v[6:9] + [v[2]] * 2) for v in vectors]
    inner = [v[5][None] for v in vectors]

    columns = wide_parts(all_columns(plan, w_qkv[0])), wide_parts(all_columns(plan, w_qkv[1]))

    def dense(layer):
        return [w_attn_out[layer], wide_parts(w_ffn_in[layer]), w_ffn_out[layer]]

    packed0 = lax.all_gather(jnp.concatenate(dense(0)), "item", axis=0)
    own_weight1 = jnp.pad(own_shard(1), ((0, 0), (0, D - plan.own)))
    own_weight1 = lax.all_gather(own_weight1, "item", axis=0)
    packed1 = lax.all_gather(jnp.concatenate(dense(1)), "item", axis=0)
    columns1 = lax.all_gather(columns[1], "item", axis=0)
    columns0 = lax.all_gather(columns[0], "item", axis=0)

    ctx0 = attn_fwd(plan, tables[0], x0)
    h1_all, h1, r1, r2, u, y0, ctx0 = layer_fwd(plan, ctx0, hidden[0], packed0, stacked[0], inner[0])
    x1 = own_heads(plan, h1_all, own_weight1)
    ctx1 = attn_fwd(plan, tables[1], x1)
    d1, output, up1, gz1, du1, df1, do1, y1, ctx1, sums1, inner1 = layer_mid(
        plan, ctx1, h1, cotangent[0], packed1, stacked[1], inner[1]
    )

    def flat(a):
        return a.reshape(tokens, -1)

    def scattered(g):
        return lax.psum_scatter(g, "item", scatter_dimension=0, tiled=False)

    def rows_for(vecs):
        part = jnp.concatenate([v.reshape(item, -1) for v in vecs], 1)
        return jnp.pad(part, ((0, 0), (0, 16 * D - part.shape[1]))).reshape(item, 16, D).astype(BF)

    def grads(gz, du, df, do, y, ctx, sums, inner_sum, cut_for=0, more=()):
        sums = jnp.sum(sums, 1)
        vecs = (sums[SUM_DO], sums[D_GAIN1], sums[D_SHIFT1], jnp.sum(inner_sum, 0), sums[SUM_DF], sums[D_GAIN2], sums[D_SHIFT2])
        rows = jnp.concatenate([rows_for(vecs)] + list(more), 1)
        return dense_grads(item, flat(gz), flat(df), flat(y), flat(du), flat(ctx), flat(do), rows, cut_for)

    def for_groups(shares):
        rows = jnp.concatenate(shares)
        rows = jnp.pad(rows, ((0, -rows.shape[0] % (16 * groups)), (0, 0)))
        return rows.reshape(groups, -1, D)

    def seq_send(shares):
        return exchange(for_groups(shares))

    def seq_sum(sent):
        return jnp.sum(sent.astype(F32), 0).astype(BF)

    counts = [share] * 3 + [w_ffn_in.shape[2] // item] + [share] * 3
    dc1 = exchange(d1)
    fo1, rest1 = grads(gz1, du1, df1, do1, y1, ctx1, sums1, inner1)
    dc1, fo1, rest1 = tie(dc1, fo1, rest1)
    fo1, rest1 = scattered(fo1), scattered(rest1)
    dx1 = attn_bwd(plan, tables[1], x1, dc1)
    dx1, columns0 = tie(dx1, columns0)
    d0, up0, gz0, du0, df0, do0, own1, sums0, inner0 = layer_bwd(
        plan, item, dx1, up1, r1, r2, u, h1_all, packed0, columns1, stacked[0]
    )
    dc0, fo1, rest1, own1 = tie(d0, fo1, rest1, own1)
    own1 = scattered(own1)
    sent1 = seq_send([fo1, rest1])
    seq_first = (w_ffn_out.shape[1] // groups) % 16 == 0
    fo0, rest0 = grads(gz0, du0, df0, do0, y0, ctx0, sums0, inner0, groups if seq_first else 0)
    dc0, fo0, rest0, sent1 = tie(dc0, fo0, rest0, sent1)
    part1 = seq_sum(sent1)
    rest0 = scattered(rest0)
    fo0 = exchange(fo0) if seq_first else scattered(fo0)
    dx0 = attn_bwd(plan, tables[0], x0, dc0)
    dx0, fo0, own1 = tie(dx0, fo0, own1)
    own0 = own_grad(plan, item, hidden_all, dx0)
    if seq_first:
        own0 = jnp.concatenate([seq_sum(fo0), own0], 1)
    own_share = scattered(own0)
    dx0, own0 = tie(dx0, own0)
    rows0 = for_groups([rest0] + ([] if seq_first else [fo0]))
    input_grad, rows0 = layer_tail(plan, dx0, up0, columns0, rows0)
    part0 = seq_sum(rows0)
    sizes = part1.shape[0], part0.shape[0], own1.shape[0]
    full = gather(groups, jnp.concatenate([part1, part0, own1, own_share]))
    qkv, bias, attn, inner_grad, outer, *small_grads = finish(
        plan, share, w_ffn_in.shape[2], item, counts, seq_first, sizes, full
    )
    bias_q, bias_v = (lax.dynamic_slice_in_dim(bias, part * D + item_rank * share, share, 1) for part in (0, 2))
    out_bias, gain1, shift1, inner_bias, ffn_bias, gain2, shift2 = small_grads
    return (
        output.reshape(hidden.shape),
        input_grad.reshape(hidden.shape),
        qkv,
        bias_q,
        bias_v,
        attn,
        out_bias,
        gain1,
        shift1,
        inner_grad,
        inner_bias,
        outer,
        ffn_bias,
        gain2,
        shift2,
    )


def solution(mesh):
    placed = (
        P("item", "seq", None),
        P("item", None, "seq", None, None),
        P(None, "item", None),
        P(None, "item"),
        P(None, "item"),
        P(None, "item", None),
        P(None, "item"),
        P(None, "item"),
        P(None, "item"),
        P(None, "item", None),
        P(None, "item"),
        P(None, "item", None),
        P(None, "item"),
        P(None, "item"),
        P(None, "item"),
        P("item", "seq", None),
    )
    return jax.shard_map(
        local,
        mesh=mesh,
        in_specs=placed,
        out_specs=(
            P("item", "seq", None),
            P("item", "seq", None),
            P(None, "item", None),
            P(None, "item"),
            P(None, "item"),
            P(None, "item", None),
            P(None, "item"),
            P(None, "item"),
            P(None, "item"),
            P(None, "item", None),
            P(None, "item"),
            P(None, "item", None),
            P(None, "item"),
            P(None, "item"),
            P(None, "item"),
        ),
        check_vma=False,
    )
```

```python
from functools import partial

import jax
import jax.numpy as jnp
from jax import lax
from jax.experimental import pallas as pl
from jax.experimental.pallas import tpu as pltpu
from jax.sharding import PartitionSpec as P

D = 768
H = 12
HD = 64
BLK = 64
RAND = 3
LAYERS = 2
LISTED = 5 + RAND
KEYS = LISTED * BLK
WIDE = 2 * HD
F32 = jnp.float32
BF = jnp.bfloat16
LOG2E = 1.4426950408889634
epsilon = 1e-05
NT = (((1,), (1,)), ((), ()))
TN = (((0,), (0,)), ((), ()))
NN = (((1,), (0,)), ((), ()))
VMEM = pltpu.VMEM


def dot(a, b, dims):
    return lax.dot_general(a, b, dims, preferred_element_type=F32)


class Plan:
    def __init__(self, groups, tokens, half=128):
        self.groups = groups
        self.tokens = tokens
        self.hp = -(-H // groups)
        self.pairs = self.hp // 2
        self.odd = self.hp % 2
        self.half = min(half, tokens // 2)
        self.chunks = tokens // 2 // self.half
        self.per = self.half // BLK
        self.rows = 2 * self.half
        self.xp = 2 * self.hp + 2 * self.pairs + self.odd
        self.cp = 2 * self.pairs + self.odd
        self.blocks = groups * tokens // BLK
        self.own = (2 * self.hp + self.hp) * HD
        self.cols = groups * self.own
        self.ctx = groups * self.hp * HD

    def x_shape(self):
        return (self.groups, self.chunks, self.xp, self.per, BLK, WIDE)

    def c_shape(self):
        return (self.groups, self.chunks, self.cp, self.per, BLK, WIDE)


def low(v):
    return jnp.concatenate([v, jnp.zeros_like(v)], 1)


def high(v):
    return jnp.concatenate([jnp.zeros_like(v), v], 1)


def diag(a, b):
    return jnp.concatenate(
        [jnp.concatenate([a, jnp.zeros_like(b)], 1), jnp.concatenate([jnp.zeros_like(a), b], 1)], 0
    )


def spots(plan, h, i):
    per = plan.per
    xb = (i // per) * (plan.xp * per) + i % per
    cb = (i // per) * (plan.cp * per) + i % per
    if h < 2 * plan.pairs:
        lanes = slice((h % 2) * HD, (h % 2 + 1) * HD)
        x0 = xb + (2 * plan.hp + 2 * (h // 2)) * per
        c0 = cb + 2 * (h // 2) * per
        return ((x0, lanes), (x0 + per, lanes)), ((c0, lanes), (c0 + per, lanes))
    x0 = xb + (2 * plan.hp + 2 * plan.pairs) * per
    c0 = cb + 2 * plan.pairs * per
    first, second = slice(0, HD), slice(HD, WIDE)
    return ((x0, first), (x0, second)), ((c0, first), (c0, second))


def listed(plan, x_ref, lists_ref, h, i):
    sides, places = [], []
    for side in range(2):
        at = ((h * (plan.blocks // 2) + i) * 2 + side) * LISTED
        ids = [lists_ref[at + n] for n in range(LISTED)]
        sides.append(jnp.concatenate([x_ref[n] for n in ids], 0))
        places.append(ids)
    return jnp.concatenate(sides, 1), places


def run_pairs(count, hp, first, second, third):
    for h in range(hp):
        first(0, h, 0)

    def body(i, carry):
        for u in range(2):
            t = 2 * i + u
            for h in range(hp):
                first(jnp.minimum(t + 1, count - 1), h, 1 - u)
                second(h, u)
                third(jnp.maximum(t - 1, 0), h, 1 - u)
        return carry

    lax.fori_loop(0, count // 2, body, 0)
    for h in range(hp):
        third(count - 1, h, 1)


def keys_of(plan, x_ref, h, n):
    per = plan.per
    at = (n * plan.xp + 2 * h) * per
    return pl.ds(at, 2 * per)


def attn_fwd_kernel(plan, lists_ref, x_ref, o_ref, s_ref, p_ref, g_ref, a_ref):
    c = LOG2E * HD**-0.5
    hp, count = plan.hp, plan.blocks // 2
    heads = range(hp)

    def stage_s(i, h, slot):
        kv, _ = listed(plan, x_ref, lists_ref, h, i)
        ((xa, la), (xb, lb)), _ = spots(plan, h, i)
        s_ref[slot, h] = dot(kv, diag(low(x_ref[xa, :, la]), low(x_ref[xb, :, lb])), NT)

    def stage_p(h, slot):
        s = s_ref[slot, h]
        m = jnp.max(s, 0, keepdims=True)
        e = jnp.exp2(s * c - m * c)
        inv = 1.0 / jnp.sum(e, 0, keepdims=True)
        p_ref[slot, h] = (e * inv).astype(BF)

    def stage_c(i, h, slot):
        kv, _ = listed(plan, x_ref, lists_ref, h, i)
        _, ((ca, la), (cb, lb)) = spots(plan, h, i)
        ctx = dot(p_ref[slot, h], kv, TN)
        o_ref[ca, :, la] = ctx[:BLK, HD:WIDE].astype(BF)
        o_ref[cb, :, lb] = ctx[BLK:, WIDE + HD :].astype(BF)

    p_ref[...] = jnp.zeros_like(p_ref)
    run_pairs(count, hp, stage_s, stage_p, stage_c)
    size = plan.rows
    steps = plan.groups * plan.chunks
    ws, outs = [], []
    for h in heads:
        ((xa, la), _), (c_first, _) = spots(plan, h, 0)
        (_, (xb, lb)), (_, c_last) = spots(plan, h, count - 1)
        ws.append(low(jnp.concatenate([x_ref[xa, :, la], x_ref[xb, :, lb]], 0)))
        outs.append((c_first, c_last))

    def chunk(n):
        return pl.ds(pl.multiple_of(n * size, size), size)

    def keys(h, n):
        return x_ref[keys_of(plan, x_ref, h, n)].reshape(size, WIDE)

    def one(n, ms):
        out = []
        for h in heads:
            s = dot(keys(h, n), ws[h], NT)
            g_ref[h, chunk(n), :] = s
            out.append(jnp.maximum(ms[h], jnp.max(s, 0, keepdims=True)))
        return tuple(out)

    ms = lax.fori_loop(
        0, steps, one, tuple(jnp.full((1, 2 * BLK), -jnp.inf, F32) for h in heads), unroll=2
    )

    def two(n, ls):
        out = []
        for h in heads:
            e = jnp.exp2(g_ref[h, chunk(n), :] * c - ms[h] * c)
            g_ref[h, chunk(n), :] = e
            out.append(ls[h] + jnp.sum(e, 0, keepdims=True))
        return tuple(out)

    ls = lax.fori_loop(0, steps, two, tuple(jnp.zeros((1, 2 * BLK), F32) for h in heads), unroll=2)
    invs = [1.0 / l for l in ls]
    a_ref[...] = jnp.zeros_like(a_ref)

    def three(n, carry):
        for h in heads:
            p = g_ref[h, chunk(n), :] * invs[h]
            hi = p.astype(BF)
            lo = (p - hi.astype(F32)).astype(BF)
            a_ref[h] += dot(jnp.concatenate([hi, lo], 1), keys(h, n), TN)
        return carry

    lax.fori_loop(0, steps, three, 0, unroll=2)
    for h in heads:
        ctx = (a_ref[h, : 2 * BLK, :] + a_ref[h, 2 * BLK :, :])[:, HD:].astype(BF)
        (ca, la), (cb, lb) = outs[h]
        o_ref[ca, :, la] = ctx[:BLK]
        o_ref[cb, :, lb] = ctx[BLK:]


def attn_fwd(plan, lists, x):
    flat = x.reshape(-1, BLK, WIDE)
    blocks = plan.groups * plan.chunks * plan.cp * plan.per
    keys = plan.blocks * BLK
    return pl.pallas_call(
        partial(attn_fwd_kernel, plan),
        out_shape=jax.ShapeDtypeStruct((blocks, BLK, WIDE), BF),
        in_specs=[pl.BlockSpec(memory_space=pltpu.SMEM), pl.BlockSpec(memory_space=VMEM)],
        out_specs=pl.BlockSpec(memory_space=VMEM),
        scratch_shapes=[
            VMEM((2, plan.hp, KEYS, 2 * BLK), F32),
            VMEM((2, plan.hp, KEYS, 2 * BLK), BF),
            VMEM((plan.hp, keys, 2 * BLK), F32),
            VMEM((plan.hp, 4 * BLK, WIDE), F32),
        ],
        compiler_params=pltpu.CompilerParams(vmem_limit_bytes=48 << 20),
        cost_estimate=pl.CostEstimate(flops=26 * 10**9, bytes_accessed=6 * 10**6, transcendentals=6 * 10**6),
        name="attn_fwd",
    )(lists, flat).reshape(plan.c_shape())


def attn_bwd_kernel(plan, lists_ref, x_ref, d_ref, o_ref, acc_ref, s_ref, p_ref, g_ref, q_ref):
    scale = HD**-0.5
    c = LOG2E * scale
    hp, count = plan.hp, plan.blocks // 2
    heads = range(hp)
    acc_ref[...] = jnp.zeros_like(acc_ref)

    def weights(i, h):
        ((xa, xla), (xb, xlb)), ((ca, cla), (cb, clb)) = spots(plan, h, i)
        da, db = d_ref[ca, :, cla], d_ref[cb, :, clb]
        da = jnp.where(i == 0, jnp.zeros_like(da), da)
        db = jnp.where(i == count - 1, jnp.zeros_like(db), db)
        return jnp.concatenate(
            [diag(low(x_ref[xa, :, xla]), low(x_ref[xb, :, xlb])), diag(high(da), high(db))], 0
        )

    def stage_s(i, h, slot):
        kv, _ = listed(plan, x_ref, lists_ref, h, i)
        s_ref[slot, h] = dot(kv, weights(i, h), NT)

    def stage_p(h, slot):
        s = s_ref[slot, h, :, : 2 * BLK]
        g = s_ref[slot, h, :, 2 * BLK :]
        m = jnp.max(s, 0, keepdims=True)
        e = jnp.exp2(s * c - m * c)
        inv = 1.0 / jnp.sum(e, 0, keepdims=True)
        delta = jnp.sum(e * g, 0, keepdims=True) * inv
        p = e * inv
        p_ref[slot, h, :, : 2 * BLK] = (p * (g - delta)).astype(BF)
        p_ref[slot, h, :, 2 * BLK :] = p.astype(BF)

    def stage_c(i, h, slot):
        kv, places = listed(plan, x_ref, lists_ref, h, i)
        ((xa, la), (xb, lb)), _ = spots(plan, h, i)
        dq = dot(p_ref[slot, h, :, : 2 * BLK], kv, TN) * scale
        o_ref[xa, :, la] = dq[:BLK, :HD].astype(BF)
        o_ref[xb, :, lb] = dq[BLK:, WIDE : WIDE + HD].astype(BF)
        dkv = dot(p_ref[slot, h], weights(i, h), NN)
        for side in range(2):
            part = dkv[:, side * WIDE : (side + 1) * WIDE]
            for n in range(LISTED):
                acc_ref[places[side][n]] += part[n * BLK : (n + 1) * BLK]

    p_ref[...] = jnp.zeros_like(p_ref)
    run_pairs(count, hp, stage_s, stage_p, stage_c)
    lane_scale = jnp.where(
        lax.broadcasted_iota(jnp.int32, (1, WIDE), 1) < HD, scale, 1.0
    ).astype(F32)
    size = plan.rows
    steps = plan.groups * plan.chunks

    def chunk(n):
        return pl.ds(pl.multiple_of(n * size, size), size)

    ws, threes, ends = [], [], []
    for h in heads:
        ((xa, xla), _), ((ca, cla), _) = spots(plan, h, 0)
        (_, (xb, xlb)), (_, (cb, clb)) = spots(plan, h, count - 1)
        q = low(jnp.concatenate([x_ref[xa, :, xla], x_ref[xb, :, xlb]], 0))
        d = high(jnp.concatenate([d_ref[ca, :, cla], d_ref[cb, :, clb]], 0))
        ws.append(jnp.concatenate([q, d], 0))
        threes.append(jnp.concatenate([q, d, d], 0))
        ends.append(((xa, xla), (xb, xlb)))

    def keys(h, n):
        return x_ref[keys_of(plan, x_ref, h, n)].reshape(size, WIDE)

    def one(n, ms):
        out = []
        for h in heads:
            s = dot(keys(h, n), ws[h], NT)
            g_ref[h, chunk(n), :] = s
            out.append(jnp.maximum(ms[h], jnp.max(s[:, : 2 * BLK], 0, keepdims=True)))
        return tuple(out)

    ms = lax.fori_loop(0, steps, one, tuple(jnp.full((1, 2 * BLK), -jnp.inf, F32) for h in heads), unroll=2)

    def two(n, state):
        out = []
        for h in heads:
            l, eg = state[h]
            e = jnp.exp2(g_ref[h, chunk(n), : 2 * BLK] * c - ms[h] * c)
            g_ref[h, chunk(n), : 2 * BLK] = e
            out.append(
                (
                    l + jnp.sum(e, 0, keepdims=True),
                    eg + jnp.sum(e * g_ref[h, chunk(n), 2 * BLK :], 0, keepdims=True),
                )
            )
        return tuple(out)

    sums = lax.fori_loop(0, steps, two, tuple((jnp.zeros((1, 2 * BLK), F32),) * 2 for h in heads), unroll=2)
    invs = [1.0 / l for l, _ in sums]
    deltas = [eg * inv for (_, eg), inv in zip(sums, invs)]
    q_ref[...] = jnp.zeros_like(q_ref)

    def three(n, carry):
        for h in heads:
            p = g_ref[h, chunk(n), : 2 * BLK] * invs[h]
            ds = (p * (g_ref[h, chunk(n), 2 * BLK :] - deltas[h])).astype(BF)
            hi = p.astype(BF)
            lo = (p - hi.astype(F32)).astype(BF)
            dkv = dot(jnp.concatenate([ds, hi, lo], 1), threes[h], NN)
            where = keys_of(plan, x_ref, h, n)
            total = acc_ref[where].reshape(size, WIDE) + dkv
            o_ref[where] = (total * lane_scale).astype(BF).reshape(2 * plan.per, BLK, WIDE)
            q_ref[h] += dot(ds, keys(h, n), TN)
        return carry

    lax.fori_loop(0, steps, three, 0, unroll=2)
    for h in heads:
        (xa, xla), (xb, xlb) = ends[h]
        dq = (q_ref[h, :, :HD] * scale).astype(BF)
        o_ref[xa, :, xla] = dq[:BLK]
        o_ref[xb, :, xlb] = dq[BLK:]


def attn_bwd(plan, lists, x, d):
    flat = x.reshape(-1, BLK, WIDE)
    keys = plan.blocks * BLK
    return pl.pallas_call(
        partial(attn_bwd_kernel, plan),
        out_shape=jax.ShapeDtypeStruct(flat.shape, BF),
        in_specs=[pl.BlockSpec(memory_space=pltpu.SMEM)] + [pl.BlockSpec(memory_space=VMEM)] * 2,
        out_specs=pl.BlockSpec(memory_space=VMEM),
        scratch_shapes=[
            VMEM(flat.shape, F32),
            VMEM((2, plan.hp, KEYS, 4 * BLK), F32),
            VMEM((2, plan.hp, KEYS, 4 * BLK), BF),
            VMEM((plan.hp, keys, 4 * BLK), F32),
            VMEM((plan.hp, 2 * BLK, WIDE), F32),
        ],
        compiler_params=pltpu.CompilerParams(vmem_limit_bytes=56 << 20),
        cost_estimate=pl.CostEstimate(flops=46 * 10**9, bytes_accessed=12 * 10**6, transcendentals=6 * 10**6),
        name="attn_bwd",
    )(lists, flat, d.reshape(-1, BLK, WIDE)).reshape(plan.x_shape())


def mean(v):
    return jnp.sum(v, -1, keepdims=True) * (1.0 / v.shape[-1])


def normalise(resid):
    centre = resid - mean(resid)
    inv = lax.rsqrt(mean(centre * centre) + epsilon)
    return centre * inv, inv


def norm_back(unit, inv, gain, grad):
    g = grad * gain
    return inv * (g - mean(g) - unit * mean(g * unit))


def gelu_parts(u):
    k = 0.7978845608028654
    sq = u * u
    t = jnp.tanh(k * (u + 0.044715 * (u * sq)))
    half = 0.5 * (1.0 + t)
    return half * u, half + 0.5 * u * (1.0 - t * t) * (k + (3 * 0.044715 * k) * sq)


def rows_of(ref):
    return ref[...].reshape(-1, ref.shape[-1])


def pick_context(plan, pieces):
    half = plan.half
    tiles = []
    for g in range(plan.groups):
        for p in range(plan.pairs):
            tiles.append(pieces[g, 2 * p : 2 * p + 2].reshape(plan.rows, WIDE))
        if plan.odd:
            both = pieces[g, 2 * plan.pairs].reshape(half, WIDE)
            tiles.append(jnp.concatenate([both[:, :HD], both[:, HD:]], 0))
    return jnp.concatenate(tiles, 1)[:, :D]


def put_context(plan, value, ref):
    half, per = plan.half, plan.per
    if plan.ctx > D:
        value = jnp.concatenate([value, jnp.zeros((value.shape[0], plan.ctx - D), value.dtype)], 1)
    for g in range(plan.groups):
        at = g * plan.hp * HD
        for p in range(plan.pairs):
            ref[g, 2 * p : 2 * p + 2] = value[:, at : at + WIDE].reshape(2, per, BLK, WIDE)
            at += WIDE
        if plan.odd:
            one = value[:, at : at + HD]
            ref[g, 2 * plan.pairs] = jnp.concatenate([one[:half], one[half:]], 1).reshape(per, BLK, WIDE)


def put_heads(plan, value, ref):
    half, per, hp = plan.half, plan.per, plan.hp
    pairs_at = plan.groups * hp * WIDE
    single_at = pairs_at + plan.groups * plan.pairs * WIDE
    for g in range(plan.groups):
        for h in range(hp):
            at = (g * hp + h) * WIDE
            ref[g, 2 * h : 2 * h + 2] = value[:, at : at + WIDE].reshape(2, per, BLK, WIDE)
        for p in range(plan.pairs):
            at = pairs_at + (g * plan.pairs + p) * WIDE
            ref[g, 2 * hp + 2 * p : 2 * hp + 2 * p + 2] = value[:, at : at + WIDE].reshape(2, per, BLK, WIDE)
        if plan.odd:
            at = single_at + g * HD
            one = value[:, at : at + HD]
            ref[g, plan.xp - 1] = jnp.concatenate([one[:half], one[half:]], 1).reshape(per, BLK, WIDE)


def pick_heads(plan, pieces):
    half, hp = plan.half, plan.hp
    kv, pairs, singles = [], [], []
    for g in range(pieces.shape[0]):
        for h in range(hp):
            kv.append(pieces[g, 2 * h : 2 * h + 2].reshape(plan.rows, WIDE))
        for p in range(plan.pairs):
            pairs.append(pieces[g, 2 * hp + 2 * p : 2 * hp + 2 * p + 2].reshape(plan.rows, WIDE))
        if plan.odd:
            both = pieces[g, plan.xp - 1].reshape(half, WIDE)
            singles.append(jnp.concatenate([both[:, :HD], both[:, HD:]], 0))
    return jnp.concatenate(kv + pairs + singles, 1)


def whole(shape):
    return pl.BlockSpec(shape, lambda *i: (0,) * len(shape), pipeline_mode=pl.Buffered(1))


MESH = pl.DeviceIdType.MESH
SMALL = 32


def start_kernel(plan, item, hid_ref, shard_ref, small_ref, ids_ref, all_ref, x_ref, small_all_ref, ids_all_ref,
                 hall, wall, xall, h_send, h_recv, i_send, i_recv, w_send, w_recv, v_send, v_recv, local_sem):
    groups = plan.groups
    me = lax.axis_index("seq")
    rank = lax.axis_index("item")
    seq_peers = [lax.rem(me + k, groups) for k in range(1, groups)]
    item_peers = [lax.rem(rank + k, item) for k in range(1, item)]
    barrier = pltpu.get_barrier_semaphore()
    for p in seq_peers:
        pl.semaphore_signal(barrier, inc=1, device_id=(p, rank), device_id_type=MESH)
    for p in item_peers:
        pl.semaphore_signal(barrier, inc=1, device_id=(me, p), device_id_type=MESH)
    pl.semaphore_wait(barrier, len(seq_peers) + len(item_peers))

    def remote(src, dst, send, recv, seq, it):
        copy = pltpu.make_async_remote_copy(
            src_ref=src, dst_ref=dst, send_sem=send, recv_sem=recv, device_id=(seq, it), device_id_type=MESH
        )
        copy.start()
        return copy

    if groups == 4:
        xn = me + 1 - 2 * lax.rem(me, 2)
        yn = lax.rem(me + 2, 4)
        dn = lax.rem(xn + 2, 4)
        order = [xn, yn, dn]

        def to(n, half):
            return remote(hid_ref.at[half], hall.at[me, half], h_send.at[n, half], h_recv.at[n, half], (xn, yn)[n], rank)

        sent = {(0, 0): to(0, 0), (1, 1): to(1, 1)}
        sent[0, 1] = to(0, 1)
        sent[1, 0] = to(1, 0)
    else:
        order = [lax.rem(me + groups - k, groups) for k in range(1, groups)]
        sent = {}
        for k, p in enumerate(seq_peers):
            for half in range(2):
                sent[k, half] = remote(hid_ref.at[half], hall.at[me, half], h_send.at[k, half], h_recv.at[k, half], p, rank)
    shards = [remote(shard_ref, wall.at[rank], w_send.at[k], w_recv.at[k], me, p) for k, p in enumerate(item_peers)]
    smalls = [remote(small_ref, small_all_ref.at[rank], v_send.at[k], v_recv.at[k], me, p) for k, p in enumerate(item_peers)]
    lists = [remote(ids_ref.at[p], ids_all_ref.at[me], i_send.at[k], i_recv.at[k], p, rank) for k, p in enumerate(seq_peers)]
    mine = [
        pltpu.make_async_copy(hid_ref, all_ref.at[me], local_sem.at[0]),
        pltpu.make_async_copy(hid_ref, hall.at[me], local_sem.at[1]),
    ]
    for copy in mine:
        copy.start()
    wall[rank] = shard_ref[...]
    small_all_ref[rank] = small_ref[...]
    ids_all_ref[me] = ids_ref[me]
    for copy in shards:
        copy.wait()
    mine[1].wait()
    share = D // item
    one = Plan.__new__(Plan)
    one.__dict__.update(plan.__dict__)
    one.groups = 1
    out = []

    def project(source, n):
        weight = wall[:, :share].reshape(D, plan.own)
        bias = jnp.sum(wall[:, share : share + 1].astype(F32), 0)

        def chunk(c, carry):
            rows = pl.ds(pl.multiple_of(c * plan.half, plan.half), plan.half)
            a = jnp.concatenate([hall[source, 0, rows], hall[source, 1, rows]], 0)
            put_heads(one, (dot(a, weight, NN) + bias).astype(BF), xall.at[pl.ds(source, 1), c])
            return carry

        lax.fori_loop(0, plan.chunks, chunk, 0)
        copy = pltpu.make_async_copy(xall.at[source], x_ref.at[source], local_sem.at[2 + n])
        copy.start()
        out.append(copy)

    if groups == 4:
        sent[0, 0].wait_recv()
        forward = [remote(hall.at[xn, 0], hall.at[xn, 0], h_send.at[2, 0], h_recv.at[2, 0], yn, rank)]
        sent[1, 1].wait_recv()
        forward.append(remote(hall.at[yn, 1], hall.at[yn, 1], h_send.at[2, 1], h_recv.at[2, 1], xn, rank))
        project(me, 0)
        sent[0, 1].wait_recv()
        project(xn, 1)
        sent[1, 0].wait_recv()
        project(yn, 2)
        for copy in forward:
            copy.wait_recv()
        project(dn, 3)
        ends = list(sent.values()) + forward
    else:
        project(me, 0)
        for k in range(groups - 1):
            for half in range(2):
                sent[k, half].wait_recv()
            project(order[k], k + 1)
        ends = list(sent.values())
    for k, source in enumerate(order):
        copy = pltpu.make_async_copy(hall.at[source], all_ref.at[source], local_sem.at[2 + groups + k])
        copy.start()
        out.append(copy)
    for copy in ends:
        copy.wait_send()
    for copy in smalls + lists:
        copy.wait()
    mine[0].wait()
    for copy in out:
        copy.wait()


def start(plan, item, hidden_low, shard, small, ids):
    g = plan.groups
    dma = pltpu.SemaphoreType.DMA
    hid = hidden_low.reshape(2, plan.tokens // 2, D)
    return pl.pallas_call(
        partial(start_kernel, plan, item),
        out_shape=[
            jax.ShapeDtypeStruct((g,) + hid.shape, BF),
            jax.ShapeDtypeStruct(plan.x_shape(), BF),
            jax.ShapeDtypeStruct((item,) + small.shape, BF),
            jax.ShapeDtypeStruct(ids.shape, jnp.int32),
        ],
        in_specs=[pl.BlockSpec(memory_space=VMEM)] * 4,
        out_specs=[pl.BlockSpec(memory_space=pl.ANY)] * 2 + [pl.BlockSpec(memory_space=VMEM)] * 2,
        scratch_shapes=[
            VMEM((g,) + hid.shape, BF),
            VMEM((item,) + shard.shape, BF),
            VMEM(plan.x_shape(), BF),
            dma((g - 1, 2)),
            dma((g - 1, 2)),
            dma((g - 1,)),
            dma((g - 1,)),
            dma((item - 1,)),
            dma((item - 1,)),
            dma((item - 1,)),
            dma((item - 1,)),
            dma((2 + 2 * g,)),
        ],
        compiler_params=pltpu.CompilerParams(collective_id=1, has_side_effects=True, vmem_limit_bytes=40 << 20),
        cost_estimate=pl.CostEstimate(flops=55 * 10**9, bytes_accessed=12 * 10**6, transcendentals=0),
        name="start",
    )(hid, shard, small, ids)


def put_own_grad(plan, item, acc_ref, sum_ref, o_ref):
    share, own = D // item, plan.own
    total = jnp.broadcast_to(jnp.sum(sum_ref[...], 0, keepdims=True), (16, own)).astype(BF)
    for r in range(item):
        o_ref[r, :share, :own] = acc_ref[r * share : (r + 1) * share].astype(BF)
        o_ref[r, share:, :own] = total
        o_ref[r, :, own:] = jnp.zeros((share + 16, o_ref.shape[2] - own), BF)


def own_grad_kernel(plan, item, steps, a_ref, d_ref, o_ref, acc_ref, sum_ref):
    n = pl.program_id(0)
    one = Plan.__new__(Plan)
    one.__dict__.update(plan.__dict__)
    one.groups = 1

    @pl.when(n == 0)
    def _():
        acc_ref[...] = jnp.zeros_like(acc_ref)
        sum_ref[...] = jnp.zeros_like(sum_ref)

    d = jnp.concatenate([pick_heads(one, d_ref[:, c]) for c in range(plan.chunks)], 0)
    a = jnp.concatenate([a_ref[0, :, c].reshape(plan.rows, D) for c in range(plan.chunks)], 0)
    acc_ref[...] += dot(a, d, TN)
    sum_ref[...] += jnp.sum(d.astype(F32).reshape(-1, 8, d.shape[1]), 0)

    @pl.when(n == steps - 1)
    def _():
        put_own_grad(plan, item, acc_ref, sum_ref, o_ref)


def own_grad(plan, item, hidden_all, dx):
    a = hidden_all.reshape(plan.groups, 2, plan.chunks, plan.half, D)
    return pl.pallas_call(
        partial(own_grad_kernel, plan, item, plan.groups),
        out_shape=jax.ShapeDtypeStruct((item, D // item + 16, D), BF),
        grid=(plan.groups,),
        in_specs=[
            pl.BlockSpec((1, 2, plan.chunks, plan.half, D), lambda g: (g, 0, 0, 0, 0)),
            pl.BlockSpec((1,) + plan.x_shape()[1:], lambda g: (g, 0, 0, 0, 0, 0)),
        ],
        out_specs=whole((item, D // item + 16, D)),
        scratch_shapes=[VMEM((D, plan.own), F32), VMEM((8, plan.own), F32)],
        compiler_params=pltpu.CompilerParams(vmem_limit_bytes=48 << 20),
        cost_estimate=pl.CostEstimate(flops=7 * 10**9, bytes_accessed=12 * 10**6, transcendentals=0),
        name="own_grad",
    )(a, dx)


def halves(plan, width):
    return pl.BlockSpec((2, plan.half, width), lambda c: (0, c, 0))


def cut(plan, v):
    return v.reshape(2, plan.tokens // 2, v.shape[-1])


def read(ref):
    return ref[...].reshape(-1, ref.shape[-1])


def write(ref, value):
    ref[...] = value.reshape(ref.shape).astype(ref.dtype)


class Packed:
    def __init__(self, ref, ff):
        self.ref = ref
        self.item = ref.shape[0]
        self.share = D // self.item
        self.parts = ff // D

    def rows(self, first):
        return self.ref[:, first : first + self.share].reshape(D, D)

    def out(self):
        return self.rows(0)

    def ffn_in(self, n):
        return self.rows(self.share * (1 + n))

    def ffn_out(self, n):
        ranks = self.item // self.parts
        first = self.share * (1 + self.parts)
        return self.ref[n * ranks : (n + 1) * ranks, first : first + self.share * self.parts].reshape(D, D)


def column_part(ref, n):
    share = D // ref.shape[0]
    return ref[:, n * share : (n + 1) * share].reshape(D, D)


def wide_parts(w):
    return jnp.concatenate([w[:, n : n + D] for n in range(0, w.shape[1], D)])


OUT_BIAS, GAIN1, SHIFT1, FFN_BIAS, GAIN2, SHIFT2 = range(6)


def first_half(plan, ctx, h, w, vec_ref):
    r1 = h + dot(ctx, w.out(), NN) + vec_ref[OUT_BIAS : OUT_BIAS + 1]
    unit1, inv1 = normalise(r1)
    y1 = unit1 * vec_ref[GAIN1 : GAIN1 + 1] + vec_ref[SHIFT1 : SHIFT1 + 1]
    return r1, unit1, inv1, y1, y1.astype(BF)


def part_of(n):
    return slice(n * D, (n + 1) * D)


def put(ref, n, value):
    ref[:, :, part_of(n)] = value.reshape(ref.shape[:2] + (D,)).astype(ref.dtype)


def get(ref, n):
    return ref[:, :, part_of(n)].reshape(-1, D)


class Swap:
    def __init__(self, plan, src, buf, send, recv, own):
        self.plan, self.src, self.buf, self.send, self.recv, self.own = plan, src, buf, send, recv, own
        self.me = lax.axis_index("seq")
        self.rank = lax.axis_index("item")

    def copy(self, c, k):
        peer = lax.rem(self.me + k, self.plan.groups)
        return pltpu.make_async_remote_copy(
            src_ref=self.src.at[peer, c],
            dst_ref=self.buf.at[self.me, c],
            send_sem=self.send.at[c, k - 1],
            recv_sem=self.recv.at[c, k - 1],
            device_id=(peer, self.rank),
            device_id_type=MESH,
        )

    def local(self):
        return pltpu.make_async_copy(self.src.at[self.me], self.buf.at[self.me], self.own.at[0])

    def step(self):
        self.begin()
        return self.arrived()

    def begin(self):
        groups = self.plan.groups

        @pl.when(pl.program_id(0) == 0)
        def _():
            barrier = pltpu.get_barrier_semaphore()
            for k in range(1, groups):
                peer = lax.rem(self.me + k, groups)
                pl.semaphore_signal(barrier, inc=1, device_id=(peer, self.rank), device_id_type=MESH)
            pl.semaphore_wait(barrier, groups - 1)
            self.local().start()
            for n in range(self.plan.chunks):
                for k in range(1, groups):
                    self.copy(n, k).start()
            self.local().wait()

    def arrived(self):
        c = pl.program_id(0)
        for k in range(1, self.plan.groups):
            self.copy(c, k).wait_recv()
        return self.buf[:, c]

    def end(self):
        c = pl.program_id(0)
        for k in range(1, self.plan.groups):
            self.copy(c, k).wait_send()

    @staticmethod
    def scratch(plan, shape):
        sems = (plan.chunks, plan.groups - 1)
        dma = pltpu.SemaphoreType.DMA
        return [VMEM(shape, BF), dma(sems), dma(sems), dma((1,))]


class Give:
    def __init__(self, plan, out, stage, send, recv, own):
        self.plan, self.out, self.stage, self.send, self.recv, self.own = plan, out, stage, send, recv, own
        self.me = lax.axis_index("seq")
        self.rank = lax.axis_index("item")

    def copy(self, c, k):
        peer = lax.rem(self.me + k, self.plan.groups)
        return pltpu.make_async_remote_copy(
            src_ref=self.stage.at[c, peer],
            dst_ref=self.out.at[self.me, c],
            send_sem=self.send.at[c, k - 1],
            recv_sem=self.recv.at[c, k - 1],
            device_id=(peer, self.rank),
            device_id_type=MESH,
        )

    def local(self, c):
        return pltpu.make_async_copy(self.stage.at[c, self.me], self.out.at[self.me, c], self.own.at[c])

    def step(self, fill):
        c = pl.program_id(0)
        fill(self.stage.at[c])
        self.local(c).start()
        for k in range(1, self.plan.groups):
            self.copy(c, k).start()

    def end(self):
        @pl.when(pl.program_id(0) == self.plan.chunks - 1)
        def _():
            for n in range(self.plan.chunks):
                self.local(n).wait()
                for k in range(1, self.plan.groups):
                    self.copy(n, k).wait()

    @staticmethod
    def scratch(plan, shape):
        sems = (plan.chunks, plan.groups - 1)
        dma = pltpu.SemaphoreType.DMA
        return [VMEM((plan.chunks, plan.groups) + shape[2:], BF), dma(sems), dma(sems), dma((plan.chunks,))]


class Spread:
    def __init__(self, plan, out, stage, send, recv, own):
        self.plan, self.out, self.stage, self.send, self.recv, self.own = plan, out, stage, send, recv, own
        self.me = lax.axis_index("seq")
        self.rank = lax.axis_index("item")
        self.passing = plan.groups == 4
        if self.passing:
            self.peers = [self.me + 1 - 2 * lax.rem(self.me, 2), lax.rem(self.me + 2, 4)]
        else:
            self.peers = [lax.rem(self.me + k, plan.groups) for k in range(1, plan.groups)]

    def rows(self, c):
        half = self.plan.half
        return pl.ds(pl.multiple_of(c * half, half), half)

    def remote(self, src, dst, c, n, peer):
        return pltpu.make_async_remote_copy(
            src_ref=src,
            dst_ref=dst,
            send_sem=self.send.at[c, n],
            recv_sem=self.recv.at[c, n],
            device_id=(peer, self.rank),
            device_id_type=MESH,
        )

    def copy(self, c, n):
        return self.remote(self.stage.at[c], self.out.at[self.me, :, self.rows(c)], c, n, self.peers[n])

    def onward(self, c, n):
        part = self.out.at[self.peers[n], n, self.rows(c)]
        return self.remote(part, part, c, 2 + n, self.peers[1 - n])

    def local(self, c):
        return pltpu.make_async_copy(self.stage.at[c], self.out.at[self.me, :, self.rows(c)], self.own.at[c])

    def pass_on(self, c):
        for n in range(2):
            self.copy(c, n).wait_recv()
            self.onward(c, n).start()

    def step(self, value):
        c = pl.program_id(0)
        self.stage[c] = value.reshape(2, self.plan.half, value.shape[-1])
        self.local(c).start()
        for n in range(len(self.peers)):
            self.copy(c, n).start()
        if self.passing:

            @pl.when(c > 0)
            def _():
                self.pass_on(c - 1)

    def end(self):
        @pl.when(pl.program_id(0) == self.plan.chunks - 1)
        def _():
            if self.passing:
                self.pass_on(self.plan.chunks - 1)
            for c in range(self.plan.chunks):
                self.local(c).wait()
                for n in range(len(self.peers)):
                    self.copy(c, n).wait_send()
                    if self.passing:
                        self.onward(c, n).wait()
                    else:
                        self.copy(c, n).wait_recv()

    @staticmethod
    def scratch(plan):
        sems = (plan.chunks, max(plan.groups - 1, 4))
        dma = pltpu.SemaphoreType.DMA
        return [VMEM((plan.chunks, 2, plan.half, D), BF), dma(sems), dma(sems), dma((plan.chunks,))]


def swap_params(number):
    return pltpu.CompilerParams(collective_id=number, has_side_effects=True, vmem_limit_bytes=60 << 20)


def fwd_kernel(plan, ff, c_ref, h_ref, w_ref, vec_ref, inner_ref,
               all_ref, next_ref, r1_ref, r2_ref, u_ref, y_ref, ctx_ref, *swapping):
    swap = Swap(plan, c_ref, *swapping[:4])
    spread = Spread(plan, all_ref, *swapping[4:])
    w = Packed(w_ref, ff)
    ctx = pick_context(plan, swap.step())
    write(ctx_ref, ctx)
    r1, _, _, y1, y1_low = first_half(plan, ctx, read(h_ref), w, vec_ref)
    write(r1_ref, r1)
    write(y_ref, y1_low)
    r2 = y1 + vec_ref[FFN_BIAS : FFN_BIAS + 1]
    for n in range(w.parts):
        u = dot(y1_low, w.ffn_in(n), NN) + inner_ref[:, part_of(n)]
        put(u_ref, n, u)
        r2 = r2 + dot(gelu_parts(u)[0].astype(BF), w.ffn_out(n), NN)
    write(r2_ref, r2)
    unit2, _ = normalise(r2)
    nxt = unit2 * vec_ref[GAIN2 : GAIN2 + 1] + vec_ref[SHIFT2 : SHIFT2 + 1]
    low_ = nxt.astype(BF)
    write(next_ref, nxt)
    spread.step(low_)
    swap.end()
    spread.end()


def own_kernel(plan, a_ref, w_ref, o_ref):
    share = D // w_ref.shape[0]
    weight = w_ref[:, :share, : plan.own].reshape(D, plan.own)
    bias = jnp.sum(w_ref[:, share : share + 1, : plan.own].astype(F32), 0)
    y = (dot(a_ref[...].reshape(plan.rows, D), weight, NN) + bias).astype(BF)
    one = Plan.__new__(Plan)
    one.__dict__.update(plan.__dict__)
    one.groups = 1
    put_heads(one, y, o_ref.at[:, 0])


def own_heads(plan, every, weight):
    return pl.pallas_call(
        partial(own_kernel, plan),
        out_shape=jax.ShapeDtypeStruct(plan.x_shape(), BF),
        grid=(plan.groups, plan.chunks),
        in_specs=[
            pl.BlockSpec((1, 2, 1, plan.half, D), lambda g, c: (g, 0, c, 0, 0)),
            whole(weight.shape),
        ],
        out_specs=pl.BlockSpec((1, 1) + plan.x_shape()[2:], lambda g, c: (g, c, 0, 0, 0, 0)),
        compiler_params=pltpu.CompilerParams(vmem_limit_bytes=48 << 20),
        cost_estimate=pl.CostEstimate(flops=12 * 10**9, bytes_accessed=12 * 10**6, transcendentals=0),
        name="own_heads",
    )(every.reshape(plan.groups, 2, plan.chunks, plan.half, D), weight)


def piece_spec(shape):
    return pl.BlockSpec((shape[0], 1) + shape[2:], lambda c: (0, c, 0, 0, 0, 0))


def layer_fwd(plan, ctx, h, packed, vec, inner):
    t = (2, plan.tokens // 2)
    ff = inner.shape[-1]
    shapes = [(D, F32), (D, F32), (D, F32), (ff, F32), (D, BF), (D, BF)]
    return pl.pallas_call(
        partial(fwd_kernel, plan, ff),
        out_shape=[jax.ShapeDtypeStruct((plan.groups,) + t + (D,), BF)] + [jax.ShapeDtypeStruct(t + (n,), d) for n, d in shapes],
        grid=(plan.chunks,),
        in_specs=[pl.BlockSpec(memory_space=pl.ANY), halves(plan, D)] + [whole(w.shape) for w in (packed, vec, inner)],
        out_specs=[pl.BlockSpec(memory_space=pl.ANY)] + [halves(plan, n) for n, _ in shapes],
        scratch_shapes=Swap.scratch(plan, plan.c_shape()) + Spread.scratch(plan),
        compiler_params=swap_params(2),
        cost_estimate=pl.CostEstimate(flops=24 * 10**9, bytes_accessed=50 * 10**6, transcendentals=3 * 10**6),
        name="layer_fwd",
    )(ctx, cut(plan, h), packed, vec, inner)


SUM_DO, D_GAIN1, D_SHIFT1, SUM_DF, D_GAIN2, D_SHIFT2 = range(6)


def add_sums(ref, at, value):
    ref[at] += jnp.sum(value.reshape(-1, 8, value.shape[-1]), 0)


def back_chunk(plan, gy, unit1, inv1, unit2, inv2, gate, w, vec_ref, sums_ref, inner_sum_ref, du_ref):
    @pl.when(pl.program_id(0) == 0)
    def _():
        sums_ref[...] = jnp.zeros_like(sums_ref)
        inner_sum_ref[...] = jnp.zeros_like(inner_sum_ref)

    dr2 = norm_back(unit2, inv2, vec_ref[GAIN2 : GAIN2 + 1], gy)
    df = dr2.astype(BF)
    dy1 = dr2
    for n in range(w.parts):
        du = (dot(df, w.ffn_out(n), NT) * gate(n)).astype(BF)
        put(du_ref, n, du)
        dy1 = dy1 + dot(du, w.ffn_in(n), NT)
        inner_sum_ref[:, part_of(n)] += jnp.sum(du.astype(F32).reshape(-1, 8, D), 0)
    dr1 = norm_back(unit1, inv1, vec_ref[GAIN1 : GAIN1 + 1], dy1)
    do = dr1.astype(BF)
    dc = dot(do, w.out(), NT).astype(BF)
    add_sums(sums_ref, SUM_DO, do.astype(F32))
    add_sums(sums_ref, D_GAIN1, dy1 * unit1)
    add_sums(sums_ref, D_SHIFT1, dy1)
    add_sums(sums_ref, SUM_DF, df.astype(F32))
    add_sums(sums_ref, D_GAIN2, gy * unit2)
    add_sums(sums_ref, D_SHIFT2, gy)
    return df, dr1, do, dc


def mid_kernel(plan, ff, c_ref, h_ref, gy_ref, w_ref, vec_ref, inner_ref,
               d_ref, out_ref, dr1_ref, gz_ref, du_ref, df_ref, do_ref, y_ref, ctx_ref, sums_ref, inner_sum_ref, gate_ref, *swapping):
    swap = Swap(plan, c_ref, *swapping)
    w = Packed(w_ref, ff)
    ctx = pick_context(plan, swap.step())
    write(ctx_ref, ctx)
    _, unit1, inv1, y1, y1_low = first_half(plan, ctx, read(h_ref), w, vec_ref)
    write(y_ref, y1_low)
    r2 = y1 + vec_ref[FFN_BIAS : FFN_BIAS + 1]
    for n in range(w.parts):
        u = dot(y1_low, w.ffn_in(n), NN) + inner_ref[:, part_of(n)]
        gz, gate_ref[n] = gelu_parts(u)
        gz = gz.astype(BF)
        put(gz_ref, n, gz)
        r2 = r2 + dot(gz, w.ffn_out(n), NN)
    unit2, inv2 = normalise(r2)
    write(out_ref, unit2 * vec_ref[GAIN2 : GAIN2 + 1] + vec_ref[SHIFT2 : SHIFT2 + 1])
    df, dr1, do, dc = back_chunk(plan, read(gy_ref), unit1, inv1, unit2, inv2, lambda n: gate_ref[n],
                                 w, vec_ref, sums_ref, inner_sum_ref, du_ref)
    put_context(plan, dc, d_ref.at[:, 0])
    write(dr1_ref, dr1)
    write(df_ref, df)
    write(do_ref, do)
    swap.end()


def sum_specs(ff):
    return (
        [jax.ShapeDtypeStruct((6, 8, D), F32), jax.ShapeDtypeStruct((8, ff), F32)],
        [pl.BlockSpec((6, 8, D), lambda c: (0, 0, 0)), pl.BlockSpec((8, ff), lambda c: (0, 0))],
    )


def layer_mid(plan, ctx, h, gy, packed, vec, inner):
    t = (2, plan.tokens // 2)
    ff = inner.shape[-1]
    shapes = [(D, F32), (D, F32), (ff, BF), (ff, BF), (D, BF), (D, BF), (D, BF), (D, BF)]
    sums, sums_at = sum_specs(ff)
    return pl.pallas_call(
        partial(mid_kernel, plan, ff),
        out_shape=[jax.ShapeDtypeStruct(plan.c_shape(), BF)] + [jax.ShapeDtypeStruct(t + (n,), d) for n, d in shapes] + sums,
        grid=(plan.chunks,),
        in_specs=[pl.BlockSpec(memory_space=pl.ANY), halves(plan, D), halves(plan, D)]
        + [whole(w.shape) for w in (packed, vec, inner)],
        out_specs=[piece_spec(plan.c_shape())] + [halves(plan, n) for n, _ in shapes] + sums_at,
        scratch_shapes=[VMEM((ff // D, plan.rows, D), F32)] + Swap.scratch(plan, plan.c_shape()),
        compiler_params=swap_params(3),
        cost_estimate=pl.CostEstimate(flops=45 * 10**9, bytes_accessed=50 * 10**6, transcendentals=3 * 10**6),
        name="layer_mid",
    )(ctx, cut(plan, h), cut(plan, gy), packed, vec, inner)


def bwd_kernel(plan, ff, item, dx_ref, up_ref, r1_ref, r2_ref, u_ref, every_ref, own_ref, w_ref, cols_ref, vec_ref,
               d_ref, dr1_ref, gz_ref, du_ref, df_ref, do_ref, own_grad_ref, sums_ref, inner_sum_ref, acc_ref, sum_ref, *swapping):
    swap = Swap(plan, dx_ref, *swapping[:4])
    give = Give(plan, d_ref, *swapping[4:])
    w = Packed(w_ref, ff)
    swap.begin()
    one = Plan.__new__(Plan)
    one.__dict__.update(plan.__dict__)
    one.groups = 1
    c = pl.program_id(0)

    @pl.when(c == 0)
    def _():
        acc_ref[...] = jnp.zeros_like(acc_ref)
        sum_ref[...] = jnp.zeros_like(sum_ref)

    for s in range(plan.groups):
        d = pick_heads(one, own_ref[s : s + 1, 0])
        acc_ref[...] += dot(every_ref[s].reshape(plan.rows, D), d, TN)
        sum_ref[...] += jnp.sum(d.astype(F32).reshape(-1, 8, plan.own), 0)

    @pl.when(c == plan.chunks - 1)
    def _():
        put_own_grad(plan, item, acc_ref, sum_ref, own_grad_ref)

    dqkv = pick_heads(plan, swap.arrived())
    gy = read(up_ref)
    for n in range(plan.cols // D):
        gy = gy + dot(dqkv[:, part_of(n)], column_part(cols_ref, n), NT)

    unit1, inv1 = normalise(read(r1_ref))
    unit2, inv2 = normalise(read(r2_ref))

    def gate(n):
        gz, value = gelu_parts(get(u_ref, n))
        put(gz_ref, n, gz)
        return value

    df, dr1, do, dc = back_chunk(plan, gy, unit1, inv1, unit2, inv2, gate, w, vec_ref, sums_ref, inner_sum_ref, du_ref)
    give.step(lambda ref: put_context(plan, dc, ref))
    write(dr1_ref, dr1)
    write(df_ref, df)
    write(do_ref, do)
    swap.end()
    give.end()


def layer_bwd(plan, item, dx, up, r1, r2, u, every, packed, columns, vec):
    t = (2, plan.tokens // 2)
    ff = u.shape[-1]
    shapes = [(D, F32), (ff, BF), (ff, BF), (D, BF), (D, BF)]
    sums, sums_at = sum_specs(ff)
    own_grad_shape = (item, D // item + 16, D)
    return pl.pallas_call(
        partial(bwd_kernel, plan, ff, item),
        out_shape=[jax.ShapeDtypeStruct(plan.c_shape(), BF)]
        + [jax.ShapeDtypeStruct(t + (n,), d) for n, d in shapes]
        + [jax.ShapeDtypeStruct(own_grad_shape, BF)]
        + sums,
        grid=(plan.chunks,),
        in_specs=[pl.BlockSpec(memory_space=pl.ANY), halves(plan, D), halves(plan, D), halves(plan, D), halves(plan, ff)]
        + [pl.BlockSpec((plan.groups, 2, plan.half, D), lambda c: (0, 0, c, 0)), piece_spec(plan.x_shape())]
        + [whole(w.shape) for w in (packed, columns, vec)],
        out_specs=[pl.BlockSpec(memory_space=pl.ANY)] + [halves(plan, n) for n, _ in shapes] + [whole(own_grad_shape)] + sums_at,
        scratch_shapes=[VMEM((D, plan.own), F32), VMEM((8, plan.own), F32)]
        + Swap.scratch(plan, plan.x_shape())
        + Give.scratch(plan, plan.c_shape()),
        compiler_params=swap_params(4),
        cost_estimate=pl.CostEstimate(flops=70 * 10**9, bytes_accessed=60 * 10**6, transcendentals=3 * 10**6),
        name="layer_bwd",
    )(dx, up, r1, r2, u, every, dx, packed, columns, vec)


def dense_grad_kernel(item, gz_ref, df_ref, y_ref, du_ref, ctx_ref, do_ref, vec_ref, fo_ref, rest_ref):
    n = pl.program_id(0)
    parts = pl.num_programs(0)
    share = D // item
    ranks = item // parts
    fo = dot(gz_ref[...], df_ref[...], TN).astype(BF)
    if len(fo_ref.shape) == 3:
        fo_ref[...] = fo.reshape(fo_ref.shape)
    else:
        count, here, rows = fo_ref.shape[:3]
        for r in range(here):
            for g in range(count):
                first = (r * count + g) * rows
                fo_ref[g, r] = fo[first : first + rows]
    first = pl.multiple_of(n * share, 16)
    rest_ref[:, pl.ds(first, share)] = dot(y_ref[...], du_ref[...], TN).astype(BF).reshape(item, share, D)

    @pl.when(n == parts - 1)
    def _():
        at = parts * share
        rest_ref[:, at : at + share] = dot(ctx_ref[...], do_ref[...], TN).astype(BF).reshape(item, share, D)
        rest_ref[:, at + share : at + share + 16] = vec_ref[:, :16]
        if vec_ref.shape[1] > 16:
            rest_ref[:, at + share + 16 :] = vec_ref[:, 16:]


def dense_grads(item, gz, df, y, du, ctx, do, vecs, cut_for=0):
    tokens, ff = gz.shape
    parts = ff // D
    share = D // item
    rest = parts * share + share + vecs.shape[1]
    column = pl.BlockSpec((tokens, D), lambda n: (0, n))
    fo_shape, fo_spec = (item, ff // item, D), pl.BlockSpec((item // parts, ff // item, D), lambda n: (n, 0, 0))
    if cut_for:
        fo_shape = (cut_for, item, ff // item // cut_for, D)
        fo_spec = pl.BlockSpec((cut_for, item // parts) + fo_shape[2:], lambda n: (0, n, 0, 0))
    return pl.pallas_call(
        partial(dense_grad_kernel, item),
        out_shape=[jax.ShapeDtypeStruct(fo_shape, BF), jax.ShapeDtypeStruct((item, rest, D), BF)],
        grid=(parts,),
        in_specs=[column, whole(df.shape), whole(y.shape), column, whole(ctx.shape), whole(do.shape), whole(vecs.shape)],
        out_specs=[fo_spec, whole((item, rest, D))],
        compiler_params=pltpu.CompilerParams(vmem_limit_bytes=56 << 20),
        cost_estimate=pl.CostEstimate(flops=14 * 10**9, bytes_accessed=30 * 10**6, transcendentals=0),
        name="dense_grads",
    )(gz, df, y, du, ctx, do, vecs)


def tail_kernel(plan, dx_ref, up_ref, w_ref, rows_ref, o_ref, got_ref, *scratch):
    swap = Swap(plan, dx_ref, *scratch[:4])
    send, recv, own = scratch[4:]
    me, rank, groups = swap.me, swap.rank, plan.groups

    def copy(k):
        peer = lax.rem(me + k, groups)
        return pltpu.make_async_remote_copy(
            src_ref=rows_ref.at[peer],
            dst_ref=got_ref.at[me],
            send_sem=send.at[k - 1],
            recv_sem=recv.at[k - 1],
            device_id=(peer, rank),
            device_id_type=MESH,
        )

    def local():
        return pltpu.make_async_copy(rows_ref.at[me], got_ref.at[me], own.at[0])

    swap.begin()

    @pl.when(pl.program_id(0) == 0)
    def _():
        local().start()
        for k in range(1, groups):
            copy(k).start()

    dqkv = pick_heads(plan, swap.arrived())
    out = read(up_ref)
    for n in range(plan.cols // D):
        out = out + dot(dqkv[:, part_of(n)], column_part(w_ref, n), NT)
    write(o_ref, out)
    swap.end()

    @pl.when(pl.program_id(0) == plan.chunks - 1)
    def _():
        local().wait()
        for k in range(1, groups):
            copy(k).wait()


def layer_tail(plan, dx, up, columns, rows):
    dma = pltpu.SemaphoreType.DMA
    return pl.pallas_call(
        partial(tail_kernel, plan),
        out_shape=[jax.ShapeDtypeStruct(up.shape, F32), jax.ShapeDtypeStruct(rows.shape, BF)],
        grid=(plan.chunks,),
        in_specs=[pl.BlockSpec(memory_space=pl.ANY), halves(plan, D), whole(columns.shape), pl.BlockSpec(memory_space=pl.ANY)],
        out_specs=[halves(plan, D), pl.BlockSpec(memory_space=pl.ANY)],
        scratch_shapes=Swap.scratch(plan, plan.x_shape()) + [dma((plan.groups - 1,)), dma((plan.groups - 1,)), dma((1,))],
        compiler_params=swap_params(5),
        cost_estimate=pl.CostEstimate(flops=55 * 10**9, bytes_accessed=12 * 10**6, transcendentals=0),
        name="layer_tail",
    )(dx, up, columns, rows)


def gather_kernel(groups, rows_ref, out_ref, send, recv, own):
    me = lax.axis_index("seq")
    rank = lax.axis_index("item")
    barrier = pltpu.get_barrier_semaphore()
    for k in range(1, groups):
        pl.semaphore_signal(barrier, inc=1, device_id=(lax.rem(me + k, groups), rank), device_id_type=MESH)
    pl.semaphore_wait(barrier, groups - 1)
    count = rows_ref.shape[0]
    first = count // 32 * 16
    parts = [pl.ds(0, first), pl.ds(first, count - first)]
    if groups == 4:
        peers = [me + 1 - 2 * lax.rem(me, 2), lax.rem(me + 2, 4)]
    else:
        peers = [lax.rem(me + k, groups) for k in range(1, groups)]

    def remote(src, dst, n, part, peer):
        return pltpu.make_async_remote_copy(
            src_ref=src, dst_ref=dst, send_sem=send.at[n, part], recv_sem=recv.at[n, part],
            device_id=(peer, rank), device_id_type=MESH,
        )

    def copy(n, part):
        return remote(rows_ref.at[parts[part]], out_ref.at[me, parts[part]], n, part, peers[n])

    def onward(n):
        piece = out_ref.at[peers[n], parts[n]]
        return remote(piece, piece, 2, n, peers[1 - n])

    local = pltpu.make_async_copy(rows_ref, out_ref.at[me], own.at[0])
    if groups == 4:
        order = [(0, 0), (1, 1), (0, 1), (1, 0)]
    else:
        order = [(n, part) for n in range(groups - 1) for part in range(2)]
    for n, part in order:
        copy(n, part).start()
    local.start()
    if groups == 4:
        for n in range(2):
            copy(n, n).wait_recv()
            onward(n).start()
        for n in range(2):
            copy(n, 1 - n).wait_recv()
            onward(n).wait()
        for n, part in order:
            copy(n, part).wait_send()
    else:
        for n, part in order:
            copy(n, part).wait()
    local.wait()


def gather(groups, rows):
    sems = (max(groups - 1, 3), 2)
    dma = pltpu.SemaphoreType.DMA
    return pl.pallas_call(
        partial(gather_kernel, groups),
        out_shape=jax.ShapeDtypeStruct((groups,) + rows.shape, BF),
        in_specs=[pl.BlockSpec(memory_space=pl.ANY)],
        out_specs=pl.BlockSpec(memory_space=pl.ANY),
        scratch_shapes=[dma(sems), dma(sems), dma((1,))],
        compiler_params=swap_params(6),
        cost_estimate=pl.CostEstimate(flops=35 * 10**9, bytes_accessed=6 * 10**6, transcendentals=0),
        name="gather",
    )(rows)


def finish_kernel(plan, share, counts, seq_first, sizes, full_ref, *outs):
    qkv_ref, bias_ref, attn_ref, inner_ref, outer_ref = outs[:5]
    small = outs[5:]
    outer = outer_ref.shape[1]
    parts = inner_ref.shape[2] // D
    hp, groups = plan.hp, plan.groups

    def rest(layer, flat, at):
        for n in range(parts):
            inner_ref[layer, :, part_of(n)] = flat[at : at + share].astype(F32)
            at += share
        attn_ref[layer] = flat[at : at + share].astype(F32)
        at += share
        vecs = flat[at : at + 16].astype(F32)
        first = 0
        for ref, n in zip(small, counts):
            ref[layer : layer + 1, :] = vecs[first // D : first // D + 1, first % D : first % D + n]
            first += n
        return at + 16

    def own(layer, first):
        pieces = {}
        for head in range(H):
            g, i = head // hp, head % hp
            rows = full_ref[g, first : first + share + 16].astype(F32)
            pieces["k", head] = rows[:, i * WIDE : i * WIDE + HD]
            pieces["v", head] = rows[:, i * WIDE + HD : (i + 1) * WIDE]
            pieces["q", head] = rows[:, (2 * hp + i) * HD : (2 * hp + i + 1) * HD]
        value = jnp.concatenate([pieces[kind, head] for kind in "qkv" for head in range(H)], 1)
        qkv_ref[layer] = value[:share]
        bias_ref[layer : layer + 1, :] = value[share : share + 1]

    first, second, third = sizes
    one = full_ref[:, :first].reshape(-1, D)
    outer_ref[1] = one[:outer].astype(F32)
    rest(1, one, outer)
    zero = full_ref[:, first : first + second].reshape(-1, D)
    at = rest(0, zero, 0)
    own(1, first + second)
    own_at = first + second + third
    if seq_first:
        here = outer // groups
        for g in range(groups):
            outer_ref[0, g * here : (g + 1) * here] = full_ref[g, own_at : own_at + here].astype(F32)
        own_at += here
    else:
        outer_ref[0] = zero[at : at + outer].astype(F32)
    own(0, own_at)


def finish(plan, share, ff, item, counts, seq_first, sizes, full):
    out = [(share, 3 * D), (3 * D,), (share, D), (share, ff), (ff // item, D)] + [(n,) for n in counts]
    return pl.pallas_call(
        partial(finish_kernel, plan, share, counts, seq_first, sizes),
        out_shape=[jax.ShapeDtypeStruct((LAYERS,) + s, F32) for s in out],
        in_specs=[pl.BlockSpec(memory_space=VMEM)],
        out_specs=[pl.BlockSpec(memory_space=VMEM)] * len(out),
        compiler_params=pltpu.CompilerParams(vmem_limit_bytes=48 << 20),
        name="finish",
    )(full)


def column_parts(plan, w):
    lead = w.shape[:-1]
    g, hp = plan.groups, plan.hp
    w = w.reshape(lead + (3, H, HD))
    w = jnp.pad(w, [(0, 0)] * (len(lead) + 1) + [(0, g * hp - H), (0, 0)])
    q, k, v = (w[..., n, :, :] for n in range(3))
    kv = jnp.stack([k, v], -2).reshape(lead + (g, hp * WIDE))
    q = q.reshape(lead + (g, hp, HD))
    pairs = q[..., : 2 * plan.pairs, :].reshape(lead + (g, plan.pairs * WIDE))
    last = q[..., 2 * plan.pairs :, :].reshape(lead + (g, plan.odd * HD))
    return kv, pairs, last


def all_columns(plan, w):
    lead = w.shape[:-1]
    return jnp.concatenate([p.reshape(lead + (-1,)) for p in column_parts(plan, w)], -1)


def own_columns(plan, w, rank):
    axis = w.ndim - 1
    return jnp.concatenate(
        [lax.dynamic_index_in_dim(p, rank, axis, False) for p in column_parts(plan, w)], -1
    )


def exchange(x):
    y = x.reshape((x.shape[0], -1, x.shape[-1]))
    return lax.all_to_all(y, "seq", split_axis=0, concat_axis=0, tiled=True).reshape(x.shape)


def tie(*args):
    return lax.optimization_barrier(args)


def key_table(plan, random_ids):
    n = plan.blocks
    here = n // plan.groups
    j = jnp.arange(n, dtype=jnp.int32)
    shared = jnp.stack(
        [jnp.maximum(j - 1, 0), j, jnp.minimum(j + 1, n - 1), jnp.zeros_like(j), jnp.full_like(j, n - 1)], 1
    )
    ids = jnp.concatenate([jnp.broadcast_to(shared[None], (plan.hp, n, 5)), random_ids], 2)
    inside = ids % here
    r = inside % (here // 2)
    head = jnp.arange(plan.hp, dtype=jnp.int32)[:, None, None]
    piece = 2 * head + inside // (here // 2)
    place = (((ids // here) * plan.chunks + r // plan.per) * plan.xp + piece) * plan.per + r % plan.per
    place = place.reshape(plan.hp, plan.groups, 2, here // 2, LISTED).transpose(0, 1, 3, 2, 4)
    return place.reshape(-1)


def local(
    hidden,
    block_lists,
    w_qkv,
    bias_query,
    bias_value,
    w_attn_out,
    bias_attn_out,
    norm1_gain,
    norm1_shift,
    w_ffn_in,
    bias_ffn_in,
    w_ffn_out,
    bias_ffn_out,
    norm2_gain,
    norm2_shift,
    cotangent,
):
    groups = lax.axis_size("seq")
    item = lax.axis_size("item")
    seq_rank = lax.axis_index("seq")
    item_rank = lax.axis_index("item")
    tokens = hidden.shape[1]
    plan = Plan(groups, tokens)
    here = tokens // BLK
    share = D // item
    ids = jnp.pad(block_lists[0], ((0, 0), (0, 0), (0, groups * plan.hp - H), (0, 0)))
    ids = ids.reshape(LAYERS, here, groups, plan.hp * RAND).transpose(2, 0, 1, 3).reshape(groups, -1)
    used = ids.shape[1]
    ids = jnp.pad(ids, ((0, 0), (0, -used % 1024))).reshape(groups, -1, 128)
    small = (bias_query, bias_value, bias_attn_out, norm1_gain, norm1_shift, bias_ffn_in, bias_ffn_out, norm2_gain, norm2_shift)
    flat_small = jnp.concatenate(small, 1).reshape(-1)

    def own_shard(layer):
        bias = lax.dynamic_update_slice(jnp.zeros((3 * D,), BF), bias_query[layer], (item_rank * share,))
        bias = lax.dynamic_update_slice(bias, bias_value[layer], (2 * D + item_rank * share,))
        rows = jnp.concatenate([w_qkv[layer], bias[None], jnp.zeros((15, 3 * D), BF)])
        return own_columns(plan, rows, seq_rank)

    hidden_all, x0, small_all, ids = start(
        plan,
        item,
        hidden[0].astype(BF),
        own_shard(0),
        jnp.pad(flat_small, (0, SMALL * 128 - flat_small.shape[0])).reshape(SMALL, 128),
        ids,
    )
    ids = ids.reshape(groups, -1)[:, :used].reshape(groups, LAYERS, here, plan.hp, RAND)
    ids = ids.transpose(1, 3, 0, 2, 4).reshape(LAYERS, plan.hp, plan.blocks, RAND)
    tables = [key_table(plan, ids[layer]) for layer in range(LAYERS)]
    packed = small_all.reshape(item, -1)[:, : flat_small.shape[0]].reshape(item, LAYERS, -1).astype(F32)
    vectors = []
    for layer in range(LAYERS):
        at, out = 0, []
        for s in small:
            out.append(packed[:, layer, at : at + s.shape[1]].reshape(-1))
            at += s.shape[1]
        vectors.append(out)
    stacked = [jnp.stack(v[2:5] + v[6:9] + [v[2]] * 2) for v in vectors]
    inner = [v[5][None] for v in vectors]

    columns = wide_parts(all_columns(plan, w_qkv[0])), wide_parts(all_columns(plan, w_qkv[1]))

    def dense(layer):
        return [w_attn_out[layer], wide_parts(w_ffn_in[layer]), w_ffn_out[layer]]

    packed0 = lax.all_gather(jnp.concatenate(dense(0)), "item", axis=0)
    own_weight1 = jnp.pad(own_shard(1), ((0, 0), (0, D - plan.own)))
    own_weight1 = lax.all_gather(own_weight1, "item", axis=0)
    packed1 = lax.all_gather(jnp.concatenate(dense(1)), "item", axis=0)
    columns1 = lax.all_gather(columns[1], "item", axis=0)
    columns0 = lax.all_gather(columns[0], "item", axis=0)

    ctx0 = attn_fwd(plan, tables[0], x0)
    h1_all, h1, r1, r2, u, y0, ctx0 = layer_fwd(plan, ctx0, hidden[0], packed0, stacked[0], inner[0])
    x1 = own_heads(plan, h1_all, own_weight1)
    ctx1 = attn_fwd(plan, tables[1], x1)
    d1, output, up1, gz1, du1, df1, do1, y1, ctx1, sums1, inner1 = layer_mid(
        plan, ctx1, h1, cotangent[0], packed1, stacked[1], inner[1]
    )

    def flat(a):
        return a.reshape(tokens, -1)

    def scattered(g):
        return lax.psum_scatter(g, "item", scatter_dimension=0, tiled=False)

    def rows_for(vecs):
        part = jnp.concatenate([v.reshape(item, -1) for v in vecs], 1)
        return jnp.pad(part, ((0, 0), (0, 16 * D - part.shape[1]))).reshape(item, 16, D).astype(BF)

    def grads(gz, du, df, do, y, ctx, sums, inner_sum, cut_for=0, more=()):
        sums = jnp.sum(sums, 1)
        vecs = (sums[SUM_DO], sums[D_GAIN1], sums[D_SHIFT1], jnp.sum(inner_sum, 0), sums[SUM_DF], sums[D_GAIN2], sums[D_SHIFT2])
        rows = jnp.concatenate([rows_for(vecs)] + list(more), 1)
        return dense_grads(item, flat(gz), flat(df), flat(y), flat(du), flat(ctx), flat(do), rows, cut_for)

    def for_groups(shares):
        rows = jnp.concatenate(shares)
        rows = jnp.pad(rows, ((0, -rows.shape[0] % (16 * groups)), (0, 0)))
        return rows.reshape(groups, -1, D)

    def seq_send(shares):
        return exchange(for_groups(shares))

    def seq_sum(sent):
        return jnp.sum(sent.astype(F32), 0).astype(BF)

    counts = [share] * 3 + [w_ffn_in.shape[2] // item] + [share] * 3
    dc1 = exchange(d1)
    fo1, rest1 = grads(gz1, du1, df1, do1, y1, ctx1, sums1, inner1)
    dc1, fo1, rest1 = tie(dc1, fo1, rest1)
    fo1, rest1 = scattered(fo1), scattered(rest1)
    dx1 = attn_bwd(plan, tables[1], x1, dc1)
    dx1, columns0 = tie(dx1, columns0)
    d0, up0, gz0, du0, df0, do0, own1, sums0, inner0 = layer_bwd(
        plan, item, dx1, up1, r1, r2, u, h1_all, packed0, columns1, stacked[0]
    )
    dc0, fo1, rest1, own1 = tie(d0, fo1, rest1, own1)
    sent1 = seq_send([fo1, rest1])
    seq_first = (w_ffn_out.shape[1] // groups) % 16 == 0
    fo0, rest0 = grads(gz0, du0, df0, do0, y0, ctx0, sums0, inner0, groups if seq_first else 0)
    dc0, fo0, rest0, sent1 = tie(dc0, fo0, rest0, sent1)
    part1 = seq_sum(sent1)
    rest0 = scattered(rest0)
    fo0 = exchange(fo0) if seq_first else scattered(fo0)
    dx0 = attn_bwd(plan, tables[0], x0, dc0)
    dx0, fo0, own1 = tie(dx0, fo0, own1)
    own0 = own_grad(plan, item, hidden_all, dx0)
    own0 = jnp.concatenate([own1] + ([seq_sum(fo0)] if seq_first else []) + [own0], 1)
    own_share = scattered(own0)
    dx0, own0 = tie(dx0, own0)
    rows0 = for_groups([rest0] + ([] if seq_first else [fo0]))
    input_grad, rows0 = layer_tail(plan, dx0, up0, columns0, rows0)
    part0 = seq_sum(rows0)
    sizes = part1.shape[0], part0.shape[0], own1.shape[1]
    full = gather(groups, jnp.concatenate([part1, part0, own_share]))
    qkv, bias, attn, inner_grad, outer, *small_grads = finish(
        plan, share, w_ffn_in.shape[2], item, counts, seq_first, sizes, full
    )
    bias_q, bias_v = (lax.dynamic_slice_in_dim(bias, part * D + item_rank * share, share, 1) for part in (0, 2))
    out_bias, gain1, shift1, inner_bias, ffn_bias, gain2, shift2 = small_grads
    return (
        output.reshape(hidden.shape),
        input_grad.reshape(hidden.shape),
        qkv,
        bias_q,
        bias_v,
        attn,
        out_bias,
        gain1,
        shift1,
        inner_grad,
        inner_bias,
        outer,
        ffn_bias,
        gain2,
        shift2,
    )


def solution(mesh):
    placed = (
        P("item", "seq", None),
        P("item", None, "seq", None, None),
        P(None, "item", None),
        P(None, "item"),
        P(None, "item"),
        P(None, "item", None),
        P(None, "item"),
        P(None, "item"),
        P(None, "item"),
        P(None, "item", None),
        P(None, "item"),
        P(None, "item", None),
        P(None, "item"),
        P(None, "item"),
        P(None, "item"),
        P("item", "seq", None),
    )
    return jax.shard_map(
        local,
        mesh=mesh,
        in_specs=placed,
        out_specs=(
            P("item", "seq", None),
            P("item", "seq", None),
            P(None, "item", None),
            P(None, "item"),
            P(None, "item"),
            P(None, "item", None),
            P(None, "item"),
            P(None, "item"),
            P(None, "item"),
            P(None, "item", None),
            P(None, "item"),
            P(None, "item", None),
            P(None, "item"),
            P(None, "item"),
            P(None, "item"),
        ),
        check_vma=False,
    )
```
